32 devices in a mesh: wide: 16 (over z, y, x), narrow: 2 (over core).
Axes of the slice: x: 2, y: 2, z: 4, core: 2. Of those that a mesh axis runs over, the one named last changes fastest.
Arguments:
- tracers: float32 [13, 16, 64, 256], P(None, None, 'wide', 'narrow'), may hold values from -6 to 6
- courant_x: float32 [16, 64, 256], P(None, 'wide', 'narrow'), may hold values from -0.24 to 0.24
- courant_y: float32 [16, 64, 256], P(None, 'wide', 'narrow'), may hold values from -0.24 to 0.24
- physics_ref: float32 [13, 16], replicated, may hold values from -6 to 6
- class_coeffs: float32 [2, 3, 13], replicated, may hold values from 0.1 to 2
- span_target: int32 [64, 256], P('wide', 'narrow'), may hold values from 0 to 8191, as said below
- cloud_class: int32 [64, 256], P('wide', 'narrow'), may hold values from 0 to 2, as said below
Outputs:
- state_out: float32 [13, 16, 64, 256], P(None, None, 'wide', 'narrow')
- span_diag: float32 [64, 256], P('wide', 'narrow')
The draws below stay inside these ranges and needn't reach their ends.
Inputs may be any that keep to these rules, and one draw needn't show every extreme that they name: `span_target`: within each block of 128 grid columns held by one index of narrow, the values are a permutation of 0 .. 8191; v names slot v % 512 of span v // 512, and a device's cell of local index r * 128 + c has grid position (row block start + r, column block start + c), a slot likewise in span order. Each device sends exactly 8 cells to every other span of its column block; its other cells go to its own span. `cloud_class`: A cell's class is that of its slot: slots 0 .. 63 of every span are class 2, the next 128 slots class 1, the rest class 0.
All inputs are finite; a program needn't handle non-finite values.
Results may differ from the reference program's by a relative error of at most 0.0001.
Values sent between devices are 32-bit elements; how exact they have to be, the bound alone decides.
No kernel may reach another device: no remote copies, remote signals or barrier semaphores. Data moves between devices by JAX's collectives and lax.ppermute only.
A program may use at most 64 MiB of HBM per device.

```python
import math
import jax
import jax.numpy as jnp

NF = 13
LEV = 16
R_DEV = 4
C_DEV = 128
DYN_STEPS = 2
CELLS = 512
CAP = 8
DEEP = 64
MID = 128
ROWS = 64
COLS = 256
N_WIDE = 16
N_NARROW = 2


def layout_group(group_key):
    wide_count = N_WIDE
    incoming = (wide_count - 1) * CAP
    keys = jax.random.split(group_key, 4)
    richness = jax.random.randint(keys[0], (wide_count,), 0, 4)
    slots = jnp.arange(CELLS, dtype=jnp.int32)
    slot_class = jnp.where(slots < DEEP, 2, jnp.where(slots < DEEP + MID, 1, 0)).astype(jnp.int32)
    noise = jax.random.randint(keys[1], (wide_count, CELLS), 0, 4096)
    score = (noise + slot_class[None, :] * (3 - richness[:, None]) * 4096) * CELLS + slots[None, :]
    picked = jnp.argsort(-score, axis=1)
    chosen = picked[:, :incoming]
    kept = picked[:, incoming:]
    chosen_class = slot_class[chosen]
    chosen_noise = jnp.take_along_axis(noise, chosen, axis=1)
    second_key = (chosen_class * 4096 + chosen_noise) * CELLS + chosen
    chosen = jnp.take_along_axis(chosen, jnp.argsort(-second_key, axis=1), axis=1)
    devices = jnp.arange(wide_count, dtype=jnp.int32)
    source_noise = jax.random.randint(keys[2], (wide_count, wide_count), 0, 4096)
    source_key = (richness[None, :] * 4096 + source_noise) * wide_count + devices[None, :]
    source_key = jnp.where(devices[:, None] == devices[None, :], -1, source_key)
    source_order = jnp.argsort(-source_key, axis=1)
    source_rank = jnp.argsort(source_order, axis=1)
    cell_score = jax.random.randint(keys[3], (wide_count, CELLS), 0, 65536) * CELLS + slots[None, :]
    cell_perm = jnp.argsort(cell_score, axis=1)
    movers = cell_perm[:, :incoming].reshape(wide_count, wide_count - 1, CAP)
    stayers = cell_perm[:, incoming:]
    peer_rank = jnp.arange(wide_count - 1, dtype=jnp.int32)
    destination = peer_rank[None, :] + (peer_rank[None, :] >= devices[:, None]).astype(jnp.int32)
    sender_rank = source_rank[destination, devices[:, None]]
    position = sender_rank[:, :, None] * CAP + jnp.arange(CAP, dtype=jnp.int32)[None, None, :]
    dest_slot = chosen[destination[:, :, None], position]
    mover_value = destination[:, :, None] * CELLS + dest_slot
    stay_value = devices[:, None] * CELLS + kept
    sender_index = jnp.broadcast_to(devices[:, None, None], movers.shape)
    target = jnp.zeros((wide_count, CELLS), jnp.int32)
    target = target.at[sender_index, movers].set(mover_value)
    target = target.at[jnp.broadcast_to(devices[:, None], stayers.shape), stayers].set(stay_value)
    klass = slot_class[target % CELLS]
    return (target.astype(jnp.int32), klass.astype(jnp.int32))


def joint_layout(key):
    group_keys = jax.random.split(key, N_NARROW)
    targets, classes = jax.vmap(layout_group)(group_keys)

    def arrange(values):
        return values.reshape(N_NARROW, N_WIDE, R_DEV, C_DEV).transpose(1, 2, 0, 3).reshape(N_WIDE * R_DEV, N_NARROW * C_DEV)
    return (arrange(targets), arrange(classes))


def draw_span_target(key, part):
    return joint_layout(jax.random.fold_in(key, 11))[0]


def draw_cloud_class(key, part):
    return joint_layout(jax.random.fold_in(key, 11))[1]


def block_levels(own_key, shape, cuts, smallest, high):
    def one(axis_at, parts):
        draws = jax.random.uniform(jax.random.fold_in(jax.random.fold_in(own_key, 6), axis_at), (parts,), jnp.float32, smallest / len(cuts), high / len(cuts))
        return jnp.repeat(jnp.exp(draws), shape[axis_at] // parts).reshape((-1,) + (1,) * (len(shape) - axis_at - 1))

    level = one(*cuts[0])
    for cut in cuts[1:]:
        level = level * one(*cut)
    return level


def centred(stream_key, shape, spread, reach, cuts=(), kind=jnp.bfloat16):
    result = jax.random.normal(stream_key, shape, jnp.float32) * spread
    if len(cuts) > 0:
        result = block_levels(stream_key, shape, cuts, -0.22, 0.18) * result
    return jnp.clip(result, min=-reach, max=reach).astype(kind)


def setup_inputs(seed: int = 0) -> dict:
    streams_of = jax.random.split(jax.random.key(seed), 8)
    return {
        "tracers": centred(streams_of[0], (NF, LEV, ROWS, COLS), 1.0, 6.0, ((2, 16), (3, 2)), jnp.float32),
        "courant_x": jnp.clip(jax.random.uniform(streams_of[1], (LEV, ROWS, COLS), jnp.float32, -0.24, 0.24) * block_levels(streams_of[1], (LEV, ROWS, COLS), ((1, 16), (2, 2)), -0.4, 0.0), -0.24, 0.24),
        "courant_y": jnp.clip(jax.random.uniform(streams_of[2], (LEV, ROWS, COLS), jnp.float32, -0.24, 0.24) * block_levels(streams_of[2], (LEV, ROWS, COLS), ((1, 16), (2, 2)), -0.4, 0.0), -0.24, 0.24),
        "physics_ref": centred(streams_of[3], (NF, LEV), 1.0, 6.0, (), jnp.float32),
        "class_coeffs": jnp.clip(jnp.exp(jax.random.uniform(streams_of[4], (2, 3, NF), jnp.float32, math.log(0.1), math.log(2.0))), 0.1, 2.0),
        "span_target": draw_span_target(jax.random.fold_in(streams_of[7], 71), 0),
        "cloud_class": draw_cloud_class(jax.random.fold_in(streams_of[7], 71), 0),
    }


def solve_levels(right_side, diffusion, relax_rate):
    levels = right_side.shape[1]
    coupling = -diffusion
    middle = 1.0 + relax_rate + 2.0 * diffusion
    edge_diag = 1.0 + relax_rate + diffusion
    upper_ratio = [coupling / edge_diag]
    partial_value = [right_side[:, 0] / edge_diag]
    for level_index in range(1, levels):
        diagonal = edge_diag if level_index == levels - 1 else middle
        denominator = diagonal - coupling * upper_ratio[-1]
        upper_ratio.append(coupling / denominator)
        partial_value.append((right_side[:, level_index] - coupling * partial_value[-1]) / denominator)
    solved = [partial_value[-1]]
    for level_index in range(levels - 2, -1, -1):
        solved.append(partial_value[level_index] - upper_ratio[level_index] * solved[-1])
    return jnp.stack(solved[::-1], axis=1)


def column_physics(advected, klass, class_coeffs, physics_ref):
    fields = advected.shape[0]
    count = advected.shape[2]
    diff_sel = jnp.zeros((fields, count), jnp.float32)
    rate_sel = jnp.zeros((fields, count), jnp.float32)
    substeps = jnp.zeros((count,), jnp.float32)
    for category, repeats in ((0, 1.0), (1, 2.0), (2, 4.0)):
        picked = (klass == category).astype(jnp.float32)
        diff_sel = diff_sel + picked[None, :] * class_coeffs[0, category][:, None]
        rate_sel = rate_sel + picked[None, :] * class_coeffs[1, category][:, None]
        substeps = substeps + picked * repeats
    diffusion = diff_sel / substeps[None, :]
    relax_rate = rate_sel / substeps[None, :]
    state = advected
    for substep in range(4):
        solved = solve_levels(state + relax_rate[:, None, :] * physics_ref[:, :, None], diffusion, relax_rate)
        state = jnp.where(substeps[None, None, :] > substep, solved, state)
    return state - advected


def advect_once(tracers, courant_x, courant_y):
    east_cell = jnp.roll(tracers, -1, axis=3)
    north_cell = jnp.roll(tracers, -1, axis=2)
    flux_east = jnp.maximum(courant_x, 0.0) * tracers + jnp.minimum(courant_x, 0.0) * east_cell
    flux_north = jnp.maximum(courant_y, 0.0) * tracers + jnp.minimum(courant_y, 0.0) * north_cell
    return tracers - (flux_east - jnp.roll(flux_east, 1, axis=3)) - (flux_north - jnp.roll(flux_north, 1, axis=2))


def reference(tracers, courant_x, courant_y, physics_ref, class_coeffs, span_target, cloud_class):
    advected = tracers
    for step in range(DYN_STEPS):
        advected = advect_once(advected, courant_x, courant_y)
    fields, levels, rows_all, cols_all = tracers.shape
    flat = advected.reshape(fields, levels, rows_all * cols_all)
    tendency = column_physics(flat, cloud_class.reshape(-1), class_coeffs, physics_ref)
    state_out = (flat + tendency).reshape(tracers.shape)
    heat = jnp.mean(tendency * tendency, axis=(0, 1)).reshape(rows_all, cols_all)
    group_start = (jnp.arange(cols_all, dtype=jnp.int32) // C_DEV) * C_DEV
    dest_rows = (span_target // C_DEV).astype(jnp.int32)
    dest_cols = (group_start[None, :] + span_target % C_DEV).astype(jnp.int32)
    span_diag = jnp.zeros((rows_all, cols_all), jnp.float32).at[dest_rows, dest_cols].set(heat)
    return state_out, span_diag
```

```python
import functools

import jax
import jax.numpy as jnp
from jax import lax
from jax.experimental import pallas as pl
from jax.experimental.pallas import tpu as pltpu
from jax.sharding import PartitionSpec as P

VMEM = pl.BlockSpec(memory_space=pltpu.VMEM)
SMEM = pl.BlockSpec(memory_space=pltpu.SMEM)
F32 = jnp.float32


def sub_roll(value, shift):
    shift = shift % value.shape[0]
    return value if shift == 0 else pltpu.roll(value, shift, 0)


def lane_roll(value, shift):
    shift = shift % value.shape[1]
    return value if shift == 0 else pltpu.roll(value, shift, 1)


def iotas(shape):
    return lax.broadcasted_iota(jnp.int32, shape, 0), lax.broadcasted_iota(jnp.int32, shape, 1)


def pack_kernel(levels, tracers, cx, cy, north, south, edge, north_corner, south_corner):
    pairs = levels // 2
    fields = tracers.shape[0] // pairs
    tile = tracers.shape[1:]
    rows = tile[0] // 2
    lanes = tile[1]
    sub, lane = iotas(tile)
    local = sub % rows
    lower = local < rows // 2
    upper = local >= rows // 2
    group = lanes // levels

    def pack_rows(vectors, base):
        for k in range(pairs // 2):
            first, second = vectors[2 * k], vectors[2 * k + 1]
            north[base + k] = jnp.where(upper, first, sub_roll(second, 2))
            south[base + k] = jnp.where(lower, first, sub_roll(second, -2))

    def one_row(vectors, row, step):
        packed = []
        for start in range(0, pairs, rows):
            total = vectors[start]
            for t in range(1, rows):
                total = jnp.where(
                    local == row + step * t, sub_roll(vectors[start + t], step * t), total
                )
            packed.append(total)
        return packed

    def pack_edge(vectors, slot):
        total = lane_roll(vectors[0], 2)
        for k in range(1, pairs):
            total = jnp.where(
                lane // (2 * group) == k, lane_roll(vectors[k], 2 + 2 * group * k), total
            )
        total = jnp.where(
            lane % (2 * group) < group, total, sub_roll(lane_roll(total, group), rows)
        )
        total = jnp.where(lane % group < group // 2, total, lane_roll(total, group // 2))
        edge[slot] = total
        north_corner[pl.ds(slot, 1), :] = total[rows - 1 : rows]
        south_corner[pl.ds(slot, 1), :] = total[0:1]

    half = pairs // 2
    for f in range(fields):
        vectors = [tracers[f * pairs + k] for k in range(pairs)]
        pack_rows(vectors, f * half)
        pack_edge(vectors, f)
    vectors_x = [cx[k] for k in range(pairs)]
    vectors_y = [cy[k] for k in range(pairs)]
    pack_edge(vectors_x, fields)
    pack_edge(vectors_y, fields + 1)
    base = fields * half
    for k in range(half):
        north[base + k] = jnp.where(upper, vectors_y[2 * k], sub_roll(vectors_y[2 * k + 1], 2))
    for k, value in enumerate(one_row(vectors_x, rows - 1, -1)):
        north[base + half + k] = value
    south_rows = one_row(vectors_x, 0, 1) + one_row(vectors_y, 0, 1)
    for k, value in enumerate(south_rows):
        south[base + k] = value


def prep_kernel(coeffs, profile, klass, target, inverse, source, carry, onehot):
    levels, pairs = inverse.shape[:2]
    fields = profile.shape[0]
    tile = inverse.shape[2:]
    rows, lanes = klass.shape
    sub, lane = iotas(tile)
    low = sub < rows
    kind = jnp.concatenate([klass[...], klass[...]], axis=0)
    is_two = kind == 2
    is_one = kind == 1

    def by_class(which, f):
        return jnp.where(
            is_two,
            coeffs[which, 2, f] * 0.25,
            jnp.where(is_one, coeffs[which, 1, f] * 0.5, coeffs[which, 0, f]),
        )

    for p in range(pairs):
        f1 = 2 * p
        f2 = min(2 * p + 1, fields - 1)
        diffusion = jnp.where(low, by_class(0, f1), by_class(0, f2))
        relax = jnp.where(low, by_class(1, f1), by_class(1, f2))
        edge_diag = 1.0 + relax + diffusion
        middle = edge_diag + diffusion
        last = None
        for l in range(levels):
            diagonal = edge_diag if l in (0, levels - 1) else middle
            denominator = diagonal if last is None else diagonal - diffusion * last
            inv = 1.0 / denominator
            last = diffusion * inv
            inverse[l, p] = inv
            carry[l, p] = last
            source[l, p] = relax * jnp.where(low, profile[f1, l], profile[f2, l]) * inv
    low_part = target[...] & (lanes - 1)
    slot, _ = iotas((lanes, lanes))
    for r in range(rows):
        hit = slot == low_part[r : r + 1]
        onehot[r * lanes : (r + 1) * lanes, :] = jnp.where(hit, 1.0, 0.0).astype(jnp.bfloat16)


def main_kernel(
    fields,
    levels,
    tracers,
    cx,
    cy,
    from_south,
    from_north,
    edge,
    edge_west,
    edge_east,
    corner_sw,
    corner_se,
    corner_nw,
    corner_ne,
    inverse,
    source,
    carry,
    klass,
    target,
    onehot,
    state_out,
    placed,
    full_coefs,
    half_coefs,
    edge_raw,
    edge_next,
    start,
    work,
    partial,
):
    pairs = levels // 2
    half = pairs // 2
    tile = tracers.shape[1:]
    rows = tile[0] // 2
    lanes = tile[1]
    group = lanes // levels
    sub, lane = iotas(tile)
    local = sub % rows
    low = sub < rows
    lower = local < rows // 2
    first_lane = lane == 0
    last_lane = lane == lanes - 1
    place = lane % group
    from_east = (place == 2) | (place == 3)
    from_west = (place == 4) | (place == 5)
    east_side = place < group // 2

    def extended_edge(slot):
        value = jnp.where(from_east, edge_east[slot], jnp.where(from_west, edge_west[slot], edge[slot]))
        south = jnp.where(east_side, corner_se[pl.ds(slot, 1), :], corner_sw[pl.ds(slot, 1), :])
        north = jnp.where(east_side, corner_ne[pl.ds(slot, 1), :], corner_nw[pl.ds(slot, 1), :])
        value = jnp.where(sub == 2 * rows - 1, south, value)
        return jnp.where(sub == rows, north, value)

    def side_by_side(value):
        return jnp.where(place == 3, lane_roll(value, -2), value)

    def coefficients(here_x, west_x, here_y, south_y):
        return (
            1.0
            - jnp.maximum(here_x, 0.0)
            + jnp.minimum(west_x, 0.0)
            - jnp.maximum(here_y, 0.0)
            + jnp.minimum(south_y, 0.0),
            jnp.maximum(-here_x, 0.0),
            jnp.maximum(west_x, 0.0),
            jnp.maximum(-here_y, 0.0),
            jnp.maximum(south_y, 0.0),
        )

    def combine(coefs, center, east, west, north, south):
        return (
            coefs[0] * center
            + (coefs[1] * east + coefs[2] * west)
            + (coefs[3] * north + coefs[4] * south)
        )

    edge_x = extended_edge(fields)
    edge_y = extended_edge(fields + 1)
    edge_coefs = coefficients(edge_x, lane_roll(edge_x, 1), edge_y, sub_roll(edge_y, 1))
    for f in range(fields):
        raw = extended_edge(f)
        edge_raw[f] = side_by_side(raw)
        moved = side_by_side(
            combine(
                edge_coefs,
                raw,
                lane_roll(raw, -1),
                lane_roll(raw, 1),
                sub_roll(raw, -1),
                sub_roll(raw, 1),
            )
        )
        edge_next[f] = jnp.where(low, moved, sub_roll(lane_roll(moved, -group), rows))

    sides_x = side_by_side(edge_x)
    sides_x_odd = sub_roll(sides_x, rows)
    base = fields * half
    for k in range(pairs):
        quad, t = k // rows, k % rows
        count = pairs // rows
        row_south = sub_roll(from_south[base + half + quad], rows + t)
        row_north = sub_roll(from_north[base + quad], rows - t)
        halo_x = jnp.where(local == 0, row_north, row_south)
        north_y = sub_roll(from_north[base + count + quad], rows - t)
        south_y = sub_roll(from_south[base + k // 2], rows if k % 2 == 0 else 2)
        halo_y = jnp.where(lower, north_y, south_y)
        own_x = cx[k]
        own_y = cy[k]
        both = []
        for odd in range(2):
            here_x = jnp.where(low, halo_x, own_x) if odd else jnp.where(low, own_x, halo_x)
            here_y = jnp.where(low, halo_y, own_y) if odd else jnp.where(low, own_y, halo_y)
            sides = lane_roll(sides_x_odd if odd else sides_x, -(group * (2 * k + odd) + 3))
            west_x = jnp.where(first_lane, sides, lane_roll(here_x, 1))
            coefs = coefficients(here_x, west_x, here_y, sub_roll(here_y, 1))
            for c in range(5):
                full_coefs[2 * k + odd, c] = coefs[c]
            both.append(coefs)
        for c in range(5):
            half_coefs[k, c] = jnp.where(low, both[0][c], both[1][c])

    north_part = (sub >= 1) & (sub <= rows)
    south_part = (sub < rows - 1) | (sub == 2 * rows - 1)

    def advect(f, k):
        own = tracers[f * pairs + k]
        message_south = from_south[f * half + k // 2]
        message_north = from_north[f * half + k // 2]
        if k % 2 == 0:
            halo = sub_roll(jnp.where(lower, message_north, message_south), rows)
        else:
            halo = jnp.where(lower, sub_roll(message_north, -2), sub_roll(message_south, 2))
        raw_sides = edge_raw[f]
        results = []
        for odd in range(2):
            value = jnp.where(low, halo, own) if odd else jnp.where(low, own, halo)
            sides = sub_roll(raw_sides, rows) if odd else raw_sides
            sides = lane_roll(sides, -(group * (2 * k + odd) + 3))
            results.append(
                combine(
                    [full_coefs[2 * k + odd, c] for c in range(5)],
                    value,
                    jnp.where(last_lane, sides, lane_roll(value, -1)),
                    jnp.where(first_lane, sides, lane_roll(value, 1)),
                    sub_roll(value, -1),
                    sub_roll(value, 1),
                )
            )
        even, odd = results
        center = jnp.where(low, even, odd)
        sides = lane_roll(edge_next[f], -(2 * group * k + 3))
        return combine(
            [half_coefs[k, c] for c in range(5)],
            center,
            jnp.where(last_lane, sides, lane_roll(center, -1)),
            jnp.where(first_lane, sides, lane_roll(center, 1)),
            sub_roll(jnp.where(north_part, even, odd), -1),
            sub_roll(jnp.where(south_part, even, odd), 1),
        )

    def advect_pair(p, carry_in):
        f1 = 2 * p
        f2 = jnp.minimum(2 * p + 1, fields - 1)
        for k in range(pairs):
            one = advect(f1, k)
            two = advect(f2, k)
            start[2 * k, p] = jnp.where(low, one, sub_roll(two, rows))
            start[2 * k + 1, p] = jnp.where(low, sub_roll(one, rows), two)
        return carry_in

    field_pairs = start.shape[1]
    lax.fori_loop(0, field_pairs, advect_pair, 0)

    kind = jnp.concatenate([klass[...], klass[...]], axis=0)
    for step in range(4):
        origin = start if step == 0 else work
        active = None if step == 0 else (kind >= (1 if step == 1 else 2))[None]
        last = None
        for l in range(levels):
            value = origin[l] * inverse[l] + source[l]
            if last is not None:
                value = value + carry[l] * last
            if l < levels - 1:
                partial[l] = value
            last = value
        for l in range(levels - 1, -1, -1):
            if l < levels - 1:
                last = partial[l] + carry[l] * last
            work[l] = last if active is None else jnp.where(active, last, origin[l])

    total = jnp.zeros(tile, F32)
    for p in range(field_pairs):
        f1, f2 = 2 * p, 2 * p + 1
        square = jnp.zeros(tile, F32)
        for k in range(pairs):
            new = []
            for l in (2 * k, 2 * k + 1):
                begin = start[l, p]
                tendency = work[l, p] - begin
                square = square + tendency * tendency
                new.append(begin + tendency)
            state_out[f1 * pairs + k] = jnp.where(low, new[0], sub_roll(new[1], rows))
            if f2 < fields:
                state_out[f2 * pairs + k] = jnp.where(low, sub_roll(new[0], rows), new[1])
        total = total + (square if f2 < fields else jnp.where(low, square, 0.0))
    heat = (total + sub_roll(total, rows)) * (1.0 / (fields * levels))

    first = heat.astype(jnp.bfloat16).astype(F32)
    rest = heat - first
    second = rest.astype(jnp.bfloat16).astype(F32)
    third = rest - second
    spans = placed.shape[0]
    slot_row, _ = iotas((spans, lanes))
    high = lax.shift_right_logical(target[...], lanes.bit_length() - 1)
    result = jnp.zeros((3 * spans, lanes), F32)
    for r in range(rows):
        hit = slot_row == high[r : r + 1]
        left = jnp.concatenate(
            [
                jnp.where(hit, part[r : r + 1], 0.0).astype(jnp.bfloat16)
                for part in (first, second, third)
            ],
            axis=0,
        )
        result = result + lax.dot_general(
            left,
            onehot[r * lanes : (r + 1) * lanes, :],
            (((1,), (1,)), ((), ())),
            preferred_element_type=F32,
        )
    placed[...] = result[:spans] + result[spans : 2 * spans] + result[2 * spans :]


def body(tracers, courant_x, courant_y, physics_ref, class_coeffs, span_target, cloud_class):
    fields, levels, rows, cols = tracers.shape
    wide = lax.axis_size("wide")
    narrow = lax.axis_size("narrow")
    pairs = levels // 2
    half = pairs // 2
    tile = (2 * rows, cols)
    field_pairs = (fields + 1) // 2
    flat = tracers.reshape(fields * pairs, *tile)
    cx = courant_x.reshape(pairs, *tile)
    cy = courant_y.reshape(pairs, *tile)
    quads = pairs // rows
    slots = -(-(fields + 2) // 8) * 8

    def array(*shape, dtype=F32):
        return jax.ShapeDtypeStruct(shape, dtype)

    north, south, edge, north_corner, south_corner = pl.pallas_call(
        functools.partial(pack_kernel, levels),
        out_shape=(
            array(fields * half + half + quads, *tile),
            array(fields * half + 2 * quads, *tile),
            array(fields + 2, *tile),
            array(slots, cols),
            array(slots, cols),
        ),
        in_specs=[VMEM] * 3,
        out_specs=[VMEM] * 5,
    )(flat, cx, cy)

    def send(value, up, right):
        pairs_ = []
        for w in range(wide):
            for n in range(narrow):
                to = ((w + up) % wide) * narrow + (n + right) % narrow
                pairs_.append((w * narrow + n, to))
        return lax.ppermute(value, ("wide", "narrow"), pairs_)

    def to_both_sides(value, up):
        from_west = send(value, up, 1)
        from_east = from_west if narrow == 2 else send(value, up, -1)
        return from_west, from_east

    from_south = send(north, 1, 0)
    from_north = send(south, -1, 0)
    edge_west, edge_east = to_both_sides(edge, 0)
    corner_sw, corner_se = to_both_sides(north_corner, 1)
    corner_nw, corner_ne = to_both_sides(south_corner, -1)

    inverse, source, carry, onehot = pl.pallas_call(
        prep_kernel,
        out_shape=(array(levels, field_pairs, *tile),) * 3
        + (array(rows * cols, cols, dtype=jnp.bfloat16),),
        in_specs=[SMEM, SMEM, VMEM, VMEM],
        out_specs=[VMEM] * 4,
        cost_estimate=pl.CostEstimate(flops=4000000, bytes_accessed=2000000, transcendentals=0),
    )(class_coeffs, physics_ref, cloud_class, span_target)

    state, placed = pl.pallas_call(
        functools.partial(main_kernel, fields, levels),
        out_shape=(array(fields * pairs, *tile), array(wide * rows, cols)),
        in_specs=[VMEM] * 18,
        out_specs=[VMEM] * 2,
        scratch_shapes=[
            pltpu.VMEM((levels, 5) + tile, F32),
            pltpu.VMEM((pairs, 5) + tile, F32),
            pltpu.VMEM((fields,) + tile, F32),
            pltpu.VMEM((fields,) + tile, F32),
            pltpu.VMEM((levels, field_pairs) + tile, F32),
            pltpu.VMEM((levels, field_pairs) + tile, F32),
            pltpu.VMEM((levels, field_pairs) + tile, F32),
        ],
        compiler_params=pltpu.CompilerParams(vmem_limit_bytes=32 * 1024 * 1024),
    )(
        flat,
        cx,
        cy,
        from_south,
        from_north,
        edge,
        edge_west,
        edge_east,
        corner_sw,
        corner_se,
        corner_nw,
        corner_ne,
        inverse,
        source,
        carry,
        cloud_class,
        span_target,
        onehot,
    )
    received = lax.all_to_all(
        placed.reshape(wide, rows, cols), "wide", split_axis=0, concat_axis=0, tiled=True
    )
    return state.reshape(fields, levels, rows, cols), jnp.sum(received, axis=0)


def solution(mesh):
    return jax.shard_map(
        body,
        mesh=mesh,
        in_specs=(
            P(None, None, "wide", "narrow"),
            P(None, "wide", "narrow"),
            P(None, "wide", "narrow"),
            P(),
            P(),
            P("wide", "narrow"),
            P("wide", "narrow"),
        ),
        out_specs=(P(None, None, "wide", "narrow"), P("wide", "narrow")),
        check_vma=False,
    )
```

```python
import functools

import jax
import jax.numpy as jnp
from jax import lax
from jax.experimental import pallas as pl
from jax.experimental.pallas import tpu as pltpu
from jax.sharding import PartitionSpec as P

VMEM = pl.BlockSpec(memory_space=pltpu.VMEM)
SMEM = pl.BlockSpec(memory_space=pltpu.SMEM)
F32 = jnp.float32
PARAMS = pltpu.CompilerParams(vmem_limit_bytes=12 * 1024 * 1024)


def sub_roll(value, shift):
    shift = shift % value.shape[0]
    return value if shift == 0 else pltpu.roll(value, shift, 0)


def lane_roll(value, shift):
    shift = shift % value.shape[1]
    return value if shift == 0 else pltpu.roll(value, shift, 1)


def iotas(shape):
    return lax.broadcasted_iota(jnp.int32, shape, 0), lax.broadcasted_iota(jnp.int32, shape, 1)


def pack_rows_kernel(levels, tracers, cx, cy, north, south):
    pairs = levels // 2
    half = pairs // 2
    fields = tracers.shape[0] // pairs
    tile = tracers.shape[1:]
    rows = tile[0] // 2
    local = iotas(tile)[0] % rows
    lower = local < rows // 2
    upper = local >= rows // 2

    def one_row(vectors, row, step):
        packed = []
        for start in range(0, pairs, rows):
            total = vectors[start]
            for t in range(1, rows):
                total = jnp.where(
                    local == row + step * t, sub_roll(vectors[start + t], step * t), total
                )
            packed.append(total)
        return packed

    for f in range(fields):
        for k in range(half):
            first, second = tracers[f * pairs + 2 * k], tracers[f * pairs + 2 * k + 1]
            north[f * half + k] = jnp.where(upper, first, sub_roll(second, 2))
            south[f * half + k] = jnp.where(lower, first, sub_roll(second, -2))
    vectors_x = [cx[k] for k in range(pairs)]
    vectors_y = [cy[k] for k in range(pairs)]
    base = fields * half
    for k in range(half):
        north[base + k] = jnp.where(upper, vectors_y[2 * k], sub_roll(vectors_y[2 * k + 1], 2))
    for k, value in enumerate(one_row(vectors_x, rows - 1, -1)):
        north[base + half + k] = value
    south_rows = one_row(vectors_x, 0, 1) + one_row(vectors_y, 0, 1)
    for k, value in enumerate(south_rows):
        south[base + k] = value


def pack_edges_kernel(levels, tracers, cx, cy, edge, north_corner, south_corner):
    pairs = levels // 2
    fields = tracers.shape[0] // pairs
    tile = tracers.shape[1:]
    rows = tile[0] // 2
    lanes = tile[1]
    group = lanes // levels
    lane = iotas(tile)[1]

    def pack_edge(vectors, slot):
        total = lane_roll(vectors[0], 2)
        for k in range(1, pairs):
            total = jnp.where(
                lane // (2 * group) == k, lane_roll(vectors[k], 2 + 2 * group * k), total
            )
        total = jnp.where(
            lane % (2 * group) < group, total, sub_roll(lane_roll(total, group), rows)
        )
        total = jnp.where(lane % group < group // 2, total, lane_roll(total, group // 2))
        edge[slot] = total
        north_corner[pl.ds(slot, 1), :] = total[rows - 1 : rows]
        south_corner[pl.ds(slot, 1), :] = total[0:1]

    for f in range(fields):
        pack_edge([tracers[f * pairs + k] for k in range(pairs)], f)
    pack_edge([cx[k] for k in range(pairs)], fields)
    pack_edge([cy[k] for k in range(pairs)], fields + 1)


def prep_kernel(coeffs, profile, klass, target, inverse, source, carry, onehot):
    levels, pairs = inverse.shape[:2]
    fields = profile.shape[0]
    tile = inverse.shape[2:]
    rows, lanes = klass.shape
    sub, lane = iotas(tile)
    low = sub < rows
    kind = jnp.concatenate([klass[...], klass[...]], axis=0)
    is_two = kind == 2
    is_one = kind == 1

    def by_class(which, f):
        return jnp.where(
            is_two,
            coeffs[which, 2, f] * 0.25,
            jnp.where(is_one, coeffs[which, 1, f] * 0.5, coeffs[which, 0, f]),
        )

    for p in range(pairs):
        f1 = 2 * p
        f2 = min(2 * p + 1, fields - 1)
        diffusion = jnp.where(low, by_class(0, f1), by_class(0, f2))
        relax = jnp.where(low, by_class(1, f1), by_class(1, f2))
        edge_diag = 1.0 + relax + diffusion
        middle = edge_diag + diffusion
        last = None
        for l in range(levels):
            diagonal = edge_diag if l in (0, levels - 1) else middle
            denominator = diagonal if last is None else diagonal - diffusion * last
            inv = 1.0 / denominator
            last = diffusion * inv
            inverse[l, p] = inv
            carry[l, p] = last
            source[l, p] = relax * jnp.where(low, profile[f1, l], profile[f2, l]) * inv
    low_part = target[...] & (lanes - 1)
    slot, _ = iotas((lanes, lanes))
    for r in range(rows):
        hit = slot == low_part[r : r + 1]
        onehot[r * lanes : (r + 1) * lanes, :] = jnp.where(hit, 1.0, 0.0).astype(jnp.bfloat16)


def main_kernel(
    fields,
    levels,
    tracers,
    cx,
    cy,
    from_south,
    from_north,
    edge,
    edge_west,
    edge_east,
    corner_sw,
    corner_se,
    corner_nw,
    corner_ne,
    inverse,
    source,
    carry,
    klass,
    target,
    onehot,
    state_out,
    placed,
    full_coefs,
    half_coefs,
    edge_raw,
    edge_next,
    start,
    work,
    partial,
):
    pairs = levels // 2
    half = pairs // 2
    tile = tracers.shape[1:]
    rows = tile[0] // 2
    lanes = tile[1]
    group = lanes // levels
    sub, lane = iotas(tile)
    local = sub % rows
    low = sub < rows
    lower = local < rows // 2
    first_lane = lane == 0
    last_lane = lane == lanes - 1
    place = lane % group
    from_east = (place == 2) | (place == 3)
    from_west = (place == 4) | (place == 5)
    east_side = place < group // 2

    def extended_edge(slot):
        value = jnp.where(from_east, edge_east[slot], jnp.where(from_west, edge_west[slot], edge[slot]))
        south = jnp.where(east_side, corner_se[pl.ds(slot, 1), :], corner_sw[pl.ds(slot, 1), :])
        north = jnp.where(east_side, corner_ne[pl.ds(slot, 1), :], corner_nw[pl.ds(slot, 1), :])
        value = jnp.where(sub == 2 * rows - 1, south, value)
        return jnp.where(sub == rows, north, value)

    def side_by_side(value):
        return jnp.where(place == 3, lane_roll(value, -2), value)

    def coefficients(here_x, west_x, here_y, south_y):
        return (
            1.0
            - jnp.maximum(here_x, 0.0)
            + jnp.minimum(west_x, 0.0)
            - jnp.maximum(here_y, 0.0)
            + jnp.minimum(south_y, 0.0),
            jnp.maximum(-here_x, 0.0),
            jnp.maximum(west_x, 0.0),
            jnp.maximum(-here_y, 0.0),
            jnp.maximum(south_y, 0.0),
        )

    def combine(coefs, center, east, west, north, south):
        return (
            coefs[0] * center
            + (coefs[1] * east + coefs[2] * west)
            + (coefs[3] * north + coefs[4] * south)
        )

    edge_x = extended_edge(fields)
    edge_y = extended_edge(fields + 1)
    edge_coefs = coefficients(edge_x, lane_roll(edge_x, 1), edge_y, sub_roll(edge_y, 1))
    for f in range(fields):
        raw = extended_edge(f)
        edge_raw[f] = side_by_side(raw)
        moved = side_by_side(
            combine(
                edge_coefs,
                raw,
                lane_roll(raw, -1),
                lane_roll(raw, 1),
                sub_roll(raw, -1),
                sub_roll(raw, 1),
            )
        )
        edge_next[f] = jnp.where(low, moved, sub_roll(lane_roll(moved, -group), rows))

    sides_x = side_by_side(edge_x)
    sides_x_odd = sub_roll(sides_x, rows)
    base = fields * half
    for k in range(pairs):
        quad, t = k // rows, k % rows
        count = pairs // rows
        row_south = sub_roll(from_south[base + half + quad], rows + t)
        row_north = sub_roll(from_north[base + quad], rows - t)
        halo_x = jnp.where(local == 0, row_north, row_south)
        north_y = sub_roll(from_north[base + count + quad], rows - t)
        south_y = sub_roll(from_south[base + k // 2], rows if k % 2 == 0 else 2)
        halo_y = jnp.where(lower, north_y, south_y)
        own_x = cx[k]
        own_y = cy[k]
        both = []
        for odd in range(2):
            here_x = jnp.where(low, halo_x, own_x) if odd else jnp.where(low, own_x, halo_x)
            here_y = jnp.where(low, halo_y, own_y) if odd else jnp.where(low, own_y, halo_y)
            sides = lane_roll(sides_x_odd if odd else sides_x, -(group * (2 * k + odd) + 3))
            west_x = jnp.where(first_lane, sides, lane_roll(here_x, 1))
            coefs = coefficients(here_x, west_x, here_y, sub_roll(here_y, 1))
            for c in range(5):
                full_coefs[2 * k + odd, c] = coefs[c]
            both.append(coefs)
        for c in range(5):
            half_coefs[k, c] = jnp.where(low, both[0][c], both[1][c])

    north_part = (sub >= 1) & (sub <= rows)
    south_part = (sub < rows - 1) | (sub == 2 * rows - 1)

    def advect(f, k, first_coefs, second_coefs):
        own = tracers[f * pairs + k]
        message_south = from_south[f * half + k // 2]
        message_north = from_north[f * half + k // 2]
        if k % 2 == 0:
            halo = sub_roll(jnp.where(lower, message_north, message_south), rows)
        else:
            halo = jnp.where(lower, sub_roll(message_north, -2), sub_roll(message_south, 2))
        raw_sides = edge_raw[f]
        results = []
        for odd in range(2):
            value = jnp.where(low, halo, own) if odd else jnp.where(low, own, halo)
            sides = sub_roll(raw_sides, rows) if odd else raw_sides
            sides = lane_roll(sides, -(group * (2 * k + odd) + 3))
            results.append(
                combine(
                    first_coefs[odd],
                    value,
                    jnp.where(last_lane, sides, lane_roll(value, -1)),
                    jnp.where(first_lane, sides, lane_roll(value, 1)),
                    sub_roll(value, -1),
                    sub_roll(value, 1),
                )
            )
        even, odd = results
        center = jnp.where(low, even, odd)
        sides = lane_roll(edge_next[f], -(2 * group * k + 3))
        return combine(
            second_coefs,
            center,
            jnp.where(last_lane, sides, lane_roll(center, -1)),
            jnp.where(first_lane, sides, lane_roll(center, 1)),
            sub_roll(jnp.where(north_part, even, odd), -1),
            sub_roll(jnp.where(south_part, even, odd), 1),
        )

    def advect_pair(p, carry_in):
        f1 = 2 * p
        f2 = jnp.minimum(2 * p + 1, fields - 1)
        for k in range(pairs):
            first_coefs = [[full_coefs[2 * k + odd, c] for c in range(5)] for odd in range(2)]
            second_coefs = [half_coefs[k, c] for c in range(5)]
            one = advect(f1, k, first_coefs, second_coefs)
            two = advect(f2, k, first_coefs, second_coefs)
            start[2 * k, p] = jnp.where(low, one, sub_roll(two, rows))
            start[2 * k + 1, p] = jnp.where(low, sub_roll(one, rows), two)
        return carry_in

    field_pairs = start.shape[1]
    lax.fori_loop(0, field_pairs, advect_pair, 0)

    kind = jnp.concatenate([klass[...], klass[...]], axis=0)
    for step in range(4):
        origin = start if step == 0 else work
        active = None if step == 0 else (kind >= (1 if step == 1 else 2))[None]
        last = None
        for l in range(levels):
            value = origin[l] * inverse[l] + source[l]
            if last is not None:
                value = value + carry[l] * last
            if l < levels - 1:
                partial[l] = value
            last = value
        for l in range(levels - 1, -1, -1):
            if l < levels - 1:
                last = partial[l] + carry[l] * last
            work[l] = last if active is None else jnp.where(active, last, origin[l])

    total = jnp.zeros(tile, F32)
    for p in range(field_pairs):
        f1, f2 = 2 * p, 2 * p + 1
        square = jnp.zeros(tile, F32)
        for k in range(pairs):
            new = []
            for l in (2 * k, 2 * k + 1):
                begin = start[l, p]
                tendency = work[l, p] - begin
                square = square + tendency * tendency
                new.append(begin + tendency)
            state_out[f1 * pairs + k] = jnp.where(low, new[0], sub_roll(new[1], rows))
            if f2 < fields:
                state_out[f2 * pairs + k] = jnp.where(low, sub_roll(new[0], rows), new[1])
        total = total + (square if f2 < fields else jnp.where(low, square, 0.0))
    heat = (total + sub_roll(total, rows)) * (1.0 / (fields * levels))

    first = heat.astype(jnp.bfloat16).astype(F32)
    rest = heat - first
    second = rest.astype(jnp.bfloat16).astype(F32)
    third = rest - second
    spans = placed.shape[0]
    slot_row, _ = iotas((spans, lanes))
    high = lax.shift_right_logical(target[...], lanes.bit_length() - 1)
    result = jnp.zeros((3 * spans, lanes), F32)
    for r in range(rows):
        hit = slot_row == high[r : r + 1]
        left = jnp.concatenate(
            [
                jnp.where(hit, part[r : r + 1], 0.0).astype(jnp.bfloat16)
                for part in (first, second, third)
            ],
            axis=0,
        )
        result = result + lax.dot_general(
            left,
            onehot[r * lanes : (r + 1) * lanes, :],
            (((1,), (1,)), ((), ())),
            preferred_element_type=F32,
        )
    placed[...] = result[:spans] + result[spans : 2 * spans] + result[2 * spans :]


def body(tracers, courant_x, courant_y, physics_ref, class_coeffs, span_target, cloud_class):
    fields, levels, rows, cols = tracers.shape
    wide = lax.axis_size("wide")
    narrow = lax.axis_size("narrow")
    pairs = levels // 2
    half = pairs // 2
    tile = (2 * rows, cols)
    field_pairs = (fields + 1) // 2
    flat = tracers.reshape(fields * pairs, *tile)
    cx = courant_x.reshape(pairs, *tile)
    cy = courant_y.reshape(pairs, *tile)
    quads = pairs // rows
    slots = -(-(fields + 2) // 8) * 8

    def array(*shape, dtype=F32):
        return jax.ShapeDtypeStruct(shape, dtype)

    north, south = pl.pallas_call(
        functools.partial(pack_rows_kernel, levels),
        out_shape=(
            array(fields * half + half + quads, *tile),
            array(fields * half + 2 * quads, *tile),
        ),
        in_specs=[VMEM] * 3,
        out_specs=[VMEM] * 2,
        compiler_params=PARAMS,
    )(flat, cx, cy)
    edge, north_corner, south_corner = pl.pallas_call(
        functools.partial(pack_edges_kernel, levels),
        out_shape=(array(fields + 2, *tile), array(slots, cols), array(slots, cols)),
        in_specs=[VMEM] * 3,
        out_specs=[VMEM] * 3,
        compiler_params=PARAMS,
    )(flat, cx, cy)

    def send(value, up, right):
        pairs_ = []
        for w in range(wide):
            for n in range(narrow):
                to = ((w + up) % wide) * narrow + (n + right) % narrow
                pairs_.append((w * narrow + n, to))
        return lax.ppermute(value, ("wide", "narrow"), pairs_)

    def to_both_sides(value, up):
        from_west = send(value, up, 1)
        from_east = from_west if narrow == 2 else send(value, up, -1)
        return from_west, from_east

    from_south = send(north, 1, 0)
    from_north = send(south, -1, 0)
    edge_west, edge_east = to_both_sides(edge, 0)
    corner_sw, corner_se = to_both_sides(north_corner, 1)
    corner_nw, corner_ne = to_both_sides(south_corner, -1)

    inverse, source, carry, onehot = pl.pallas_call(
        prep_kernel,
        out_shape=(array(levels, field_pairs, *tile),) * 3
        + (array(rows * cols, cols, dtype=jnp.bfloat16),),
        in_specs=[SMEM, SMEM, VMEM, VMEM],
        out_specs=[VMEM] * 4,
        cost_estimate=pl.CostEstimate(flops=4000000, bytes_accessed=2000000, transcendentals=0),
        compiler_params=PARAMS,
    )(class_coeffs, physics_ref, cloud_class, span_target)

    state, placed = pl.pallas_call(
        functools.partial(main_kernel, fields, levels),
        out_shape=(array(fields * pairs, *tile), array(wide * rows, cols)),
        in_specs=[VMEM] * 18,
        out_specs=[VMEM] * 2,
        scratch_shapes=[
            pltpu.VMEM((levels, 5) + tile, F32),
            pltpu.VMEM((pairs, 5) + tile, F32),
            pltpu.VMEM((fields,) + tile, F32),
            pltpu.VMEM((fields,) + tile, F32),
            pltpu.VMEM((levels, field_pairs) + tile, F32),
            pltpu.VMEM((levels, field_pairs) + tile, F32),
            pltpu.VMEM((levels, field_pairs) + tile, F32),
        ],
        compiler_params=PARAMS,
    )(
        flat,
        cx,
        cy,
        from_south,
        from_north,
        edge,
        edge_west,
        edge_east,
        corner_sw,
        corner_se,
        corner_nw,
        corner_ne,
        inverse,
        source,
        carry,
        cloud_class,
        span_target,
        onehot,
    )
    received = lax.all_to_all(
        placed.reshape(wide, rows, cols), "wide", split_axis=0, concat_axis=0, tiled=True
    )
    return state.reshape(fields, levels, rows, cols), jnp.sum(received, axis=0)


def solution(mesh):
    return jax.shard_map(
        body,
        mesh=mesh,
        in_specs=(
            P(None, None, "wide", "narrow"),
            P(None, "wide", "narrow"),
            P(None, "wide", "narrow"),
            P(),
            P(),
            P("wide", "narrow"),
            P("wide", "narrow"),
        ),
        out_specs=(P(None, None, "wide", "narrow"), P("wide", "narrow")),
        check_vma=False,
    )
```

```python
import functools

import jax
import jax.numpy as jnp
from jax import lax
from jax.experimental import pallas as pl
from jax.experimental.pallas import tpu as pltpu
from jax.sharding import PartitionSpec as P

VMEM = pl.BlockSpec(memory_space=pltpu.VMEM)
HBM = pl.BlockSpec(memory_space=pltpu.HBM)
SMEM = pl.BlockSpec(memory_space=pltpu.SMEM)
F32 = jnp.float32
PARAMS = pltpu.CompilerParams(vmem_limit_bytes=12 * 1024 * 1024)


def sub_roll(value, shift):
    shift = shift % value.shape[0]
    return value if shift == 0 else pltpu.roll(value, shift, 0)


def lane_roll(value, shift):
    shift = shift % value.shape[1]
    return value if shift == 0 else pltpu.roll(value, shift, 1)


def iotas(shape):
    return lax.broadcasted_iota(jnp.int32, shape, 0), lax.broadcasted_iota(jnp.int32, shape, 1)


def pack_rows_kernel(
    levels, tracers_in, cx_in, cy_in, tracers, cx, cy, north, south, semaphores
):
    copies = [
        pltpu.make_async_copy(source, into, semaphores.at[i])
        for i, (source, into) in enumerate(((tracers_in, tracers), (cx_in, cx), (cy_in, cy)))
    ]
    for copy in copies:
        copy.start()
    for copy in copies:
        copy.wait()
    pairs = levels // 2
    half = pairs // 2
    fields = tracers.shape[0] // pairs
    tile = tracers.shape[1:]
    rows = tile[0] // 2
    local = iotas(tile)[0] % rows
    lower = local < rows // 2
    upper = local >= rows // 2

    def one_row(vectors, row, step):
        packed = []
        for start in range(0, pairs, rows):
            total = vectors[start]
            for t in range(1, rows):
                total = jnp.where(
                    local == row + step * t, sub_roll(vectors[start + t], step * t), total
                )
            packed.append(total)
        return packed

    for f in range(fields):
        for k in range(half):
            first, second = tracers[f * pairs + 2 * k], tracers[f * pairs + 2 * k + 1]
            north[f * half + k] = jnp.where(upper, first, sub_roll(second, 2))
            south[f * half + k] = jnp.where(lower, first, sub_roll(second, -2))
    vectors_x = [cx[k] for k in range(pairs)]
    vectors_y = [cy[k] for k in range(pairs)]
    base = fields * half
    for k in range(half):
        north[base + k] = jnp.where(upper, vectors_y[2 * k], sub_roll(vectors_y[2 * k + 1], 2))
    for k, value in enumerate(one_row(vectors_x, rows - 1, -1)):
        north[base + half + k] = value
    south_rows = one_row(vectors_x, 0, 1) + one_row(vectors_y, 0, 1)
    for k, value in enumerate(south_rows):
        south[base + k] = value


def pack_edges_kernel(levels, tracers, cx, cy, edge, north_corner, south_corner):
    pairs = levels // 2
    fields = tracers.shape[0] // pairs
    tile = tracers.shape[1:]
    rows = tile[0] // 2
    lanes = tile[1]
    group = lanes // levels
    lane = iotas(tile)[1]

    def pack_edge(vectors, slot):
        total = lane_roll(vectors[0], 2)
        for k in range(1, pairs):
            total = jnp.where(
                lane // (2 * group) == k, lane_roll(vectors[k], 2 + 2 * group * k), total
            )
        total = jnp.where(
            lane % (2 * group) < group, total, sub_roll(lane_roll(total, group), rows)
        )
        total = jnp.where(lane % group < group // 2, total, lane_roll(total, group // 2))
        edge[slot] = total
        north_corner[pl.ds(slot, 1), :] = total[rows - 1 : rows]
        south_corner[pl.ds(slot, 1), :] = total[0:1]

    for f in range(fields):
        pack_edge([tracers[f * pairs + k] for k in range(pairs)], f)
    pack_edge([cx[k] for k in range(pairs)], fields)
    pack_edge([cy[k] for k in range(pairs)], fields + 1)


def prep_kernel(coeffs, profile, klass, target, inverse, source, carry, onehot):
    levels, pairs = inverse.shape[:2]
    fields = profile.shape[0]
    tile = inverse.shape[2:]
    rows, lanes = klass.shape
    sub, lane = iotas(tile)
    low = sub < rows
    kind = jnp.concatenate([klass[...], klass[...]], axis=0)
    is_two = kind == 2
    is_one = kind == 1

    def by_class(which, f):
        return jnp.where(
            is_two,
            coeffs[which, 2, f] * 0.25,
            jnp.where(is_one, coeffs[which, 1, f] * 0.5, coeffs[which, 0, f]),
        )

    for p in range(pairs):
        f1 = 2 * p
        f2 = min(2 * p + 1, fields - 1)
        diffusion = jnp.where(low, by_class(0, f1), by_class(0, f2))
        relax = jnp.where(low, by_class(1, f1), by_class(1, f2))
        edge_diag = 1.0 + relax + diffusion
        middle = edge_diag + diffusion
        last = None
        for l in range(levels):
            diagonal = edge_diag if l in (0, levels - 1) else middle
            denominator = diagonal if last is None else diagonal - diffusion * last
            inv = 1.0 / denominator
            last = diffusion * inv
            inverse[l, p] = inv
            carry[l, p] = last
            source[l, p] = relax * jnp.where(low, profile[f1, l], profile[f2, l]) * inv
    low_part = target[...] & (lanes - 1)
    slot, _ = iotas((lanes, lanes))
    for r in range(rows):
        hit = slot == low_part[r : r + 1]
        onehot[r * lanes : (r + 1) * lanes, :] = jnp.where(hit, 1.0, 0.0).astype(jnp.bfloat16)


def main_kernel(
    fields,
    levels,
    tracers,
    cx,
    cy,
    from_south,
    from_north,
    edge,
    edge_west,
    edge_east,
    corner_sw,
    corner_se,
    corner_nw,
    corner_ne,
    inverse,
    source,
    carry,
    klass,
    target,
    onehot,
    state_out,
    placed,
    full_coefs,
    half_coefs,
    edge_raw,
    edge_next,
    start,
    work,
    partial,
):
    pairs = levels // 2
    half = pairs // 2
    tile = tracers.shape[1:]
    rows = tile[0] // 2
    lanes = tile[1]
    group = lanes // levels
    sub, lane = iotas(tile)
    local = sub % rows
    low = sub < rows
    lower = local < rows // 2
    first_lane = lane == 0
    last_lane = lane == lanes - 1
    place = lane % group
    from_east = (place == 2) | (place == 3)
    from_west = (place == 4) | (place == 5)
    east_side = place < group // 2

    def extended_edge(slot):
        value = jnp.where(from_east, edge_east[slot], jnp.where(from_west, edge_west[slot], edge[slot]))
        south = jnp.where(east_side, corner_se[pl.ds(slot, 1), :], corner_sw[pl.ds(slot, 1), :])
        north = jnp.where(east_side, corner_ne[pl.ds(slot, 1), :], corner_nw[pl.ds(slot, 1), :])
        value = jnp.where(sub == 2 * rows - 1, south, value)
        return jnp.where(sub == rows, north, value)

    def side_by_side(value):
        return jnp.where(place == 3, lane_roll(value, -2), value)

    def coefficients(here_x, west_x, here_y, south_y):
        return (
            1.0
            - jnp.maximum(here_x, 0.0)
            + jnp.minimum(west_x, 0.0)
            - jnp.maximum(here_y, 0.0)
            + jnp.minimum(south_y, 0.0),
            jnp.maximum(-here_x, 0.0),
            jnp.maximum(west_x, 0.0),
            jnp.maximum(-here_y, 0.0),
            jnp.maximum(south_y, 0.0),
        )

    def combine(coefs, center, east, west, north, south):
        return (
            coefs[0] * center
            + (coefs[1] * east + coefs[2] * west)
            + (coefs[3] * north + coefs[4] * south)
        )

    edge_x = extended_edge(fields)
    edge_y = extended_edge(fields + 1)
    edge_coefs = coefficients(edge_x, lane_roll(edge_x, 1), edge_y, sub_roll(edge_y, 1))
    for f in range(fields):
        raw = extended_edge(f)
        edge_raw[f] = side_by_side(raw)
        moved = side_by_side(
            combine(
                edge_coefs,
                raw,
                lane_roll(raw, -1),
                lane_roll(raw, 1),
                sub_roll(raw, -1),
                sub_roll(raw, 1),
            )
        )
        edge_next[f] = jnp.where(low, moved, sub_roll(lane_roll(moved, -group), rows))

    sides_x = side_by_side(edge_x)
    sides_x_odd = sub_roll(sides_x, rows)
    base = fields * half
    for k in range(pairs):
        quad, t = k // rows, k % rows
        count = pairs // rows
        row_south = sub_roll(from_south[base + half + quad], rows + t)
        row_north = sub_roll(from_north[base + quad], rows - t)
        halo_x = jnp.where(local == 0, row_north, row_south)
        north_y = sub_roll(from_north[base + count + quad], rows - t)
        south_y = sub_roll(from_south[base + k // 2], rows if k % 2 == 0 else 2)
        halo_y = jnp.where(lower, north_y, south_y)
        own_x = cx[k]
        own_y = cy[k]
        both = []
        for odd in range(2):
            here_x = jnp.where(low, halo_x, own_x) if odd else jnp.where(low, own_x, halo_x)
            here_y = jnp.where(low, halo_y, own_y) if odd else jnp.where(low, own_y, halo_y)
            sides = lane_roll(sides_x_odd if odd else sides_x, -(group * (2 * k + odd) + 3))
            west_x = jnp.where(first_lane, sides, lane_roll(here_x, 1))
            coefs = coefficients(here_x, west_x, here_y, sub_roll(here_y, 1))
            for c in range(5):
                full_coefs[2 * k + odd, c] = coefs[c]
            both.append(coefs)
        for c in range(5):
            half_coefs[k, c] = jnp.where(low, both[0][c], both[1][c])

    north_part = (sub >= 1) & (sub <= rows)
    south_part = (sub < rows - 1) | (sub == 2 * rows - 1)

    def advect(f, k, first_coefs, second_coefs):
        own = tracers[f * pairs + k]
        message_south = from_south[f * half + k // 2]
        message_north = from_north[f * half + k // 2]
        if k % 2 == 0:
            halo = sub_roll(jnp.where(lower, message_north, message_south), rows)
        else:
            halo = jnp.where(lower, sub_roll(message_north, -2), sub_roll(message_south, 2))
        raw_sides = edge_raw[f]
        results = []
        for odd in range(2):
            value = jnp.where(low, halo, own) if odd else jnp.where(low, own, halo)
            sides = sub_roll(raw_sides, rows) if odd else raw_sides
            sides = lane_roll(sides, -(group * (2 * k + odd) + 3))
            results.append(
                combine(
                    first_coefs[odd],
                    value,
                    jnp.where(last_lane, sides, lane_roll(value, -1)),
                    jnp.where(first_lane, sides, lane_roll(value, 1)),
                    sub_roll(value, -1),
                    sub_roll(value, 1),
                )
            )
        even, odd = results
        center = jnp.where(low, even, odd)
        sides = lane_roll(edge_next[f], -(2 * group * k + 3))
        return combine(
            second_coefs,
            center,
            jnp.where(last_lane, sides, lane_roll(center, -1)),
            jnp.where(first_lane, sides, lane_roll(center, 1)),
            sub_roll(jnp.where(north_part, even, odd), -1),
            sub_roll(jnp.where(south_part, even, odd), 1),
        )

    def advect_pair(p, carry_in):
        f1 = 2 * p
        f2 = jnp.minimum(2 * p + 1, fields - 1)
        for k in range(pairs):
            first_coefs = [[full_coefs[2 * k + odd, c] for c in range(5)] for odd in range(2)]
            second_coefs = [half_coefs[k, c] for c in range(5)]
            one = advect(f1, k, first_coefs, second_coefs)
            two = advect(f2, k, first_coefs, second_coefs)
            start[2 * k, p] = jnp.where(low, one, sub_roll(two, rows))
            start[2 * k + 1, p] = jnp.where(low, sub_roll(one, rows), two)
        return carry_in

    field_pairs = start.shape[1]
    lax.fori_loop(0, field_pairs, advect_pair, 0)

    kind = jnp.concatenate([klass[...], klass[...]], axis=0)
    for step in range(4):
        origin = start if step == 0 else work
        active = None if step == 0 else (kind >= (1 if step == 1 else 2))[None]
        last = None
        for l in range(levels):
            value = origin[l] * inverse[l] + source[l]
            if last is not None:
                value = value + carry[l] * last
            if l < levels - 1:
                partial[l] = value
            last = value
        for l in range(levels - 1, -1, -1):
            if l < levels - 1:
                last = partial[l] + carry[l] * last
            work[l] = last if active is None else jnp.where(active, last, origin[l])

    total = jnp.zeros(tile, F32)
    for p in range(field_pairs):
        f1, f2 = 2 * p, 2 * p + 1
        square = jnp.zeros(tile, F32)
        for k in range(pairs):
            new = []
            for l in (2 * k, 2 * k + 1):
                begin = start[l, p]
                tendency = work[l, p] - begin
                square = square + tendency * tendency
                new.append(begin + tendency)
            state_out[f1 * pairs + k] = jnp.where(low, new[0], sub_roll(new[1], rows))
            if f2 < fields:
                state_out[f2 * pairs + k] = jnp.where(low, sub_roll(new[0], rows), new[1])
        total = total + (square if f2 < fields else jnp.where(low, square, 0.0))
    heat = (total + sub_roll(total, rows)) * (1.0 / (fields * levels))

    first = heat.astype(jnp.bfloat16).astype(F32)
    rest = heat - first
    second = rest.astype(jnp.bfloat16).astype(F32)
    third = rest - second
    spans = placed.shape[0]
    slot_row, _ = iotas((spans, lanes))
    high = lax.shift_right_logical(target[...], lanes.bit_length() - 1)
    result = jnp.zeros((3 * spans, lanes), F32)
    for r in range(rows):
        hit = slot_row == high[r : r + 1]
        left = jnp.concatenate(
            [
                jnp.where(hit, part[r : r + 1], 0.0).astype(jnp.bfloat16)
                for part in (first, second, third)
            ],
            axis=0,
        )
        result = result + lax.dot_general(
            left,
            onehot[r * lanes : (r + 1) * lanes, :],
            (((1,), (1,)), ((), ())),
            preferred_element_type=F32,
        )
    placed[...] = result[:spans] + result[spans : 2 * spans] + result[2 * spans :]


def body(tracers, courant_x, courant_y, physics_ref, class_coeffs, span_target, cloud_class):
    fields, levels, rows, cols = tracers.shape
    wide = lax.axis_size("wide")
    narrow = lax.axis_size("narrow")
    pairs = levels // 2
    half = pairs // 2
    tile = (2 * rows, cols)
    field_pairs = (fields + 1) // 2
    flat = tracers.reshape(fields * pairs, *tile)
    cx = courant_x.reshape(pairs, *tile)
    cy = courant_y.reshape(pairs, *tile)
    quads = pairs // rows
    slots = -(-(fields + 2) // 8) * 8

    def array(*shape, dtype=F32):
        return jax.ShapeDtypeStruct(shape, dtype)

    flat, cx, cy, north, south = pl.pallas_call(
        functools.partial(pack_rows_kernel, levels),
        out_shape=(
            array(fields * pairs, *tile),
            array(pairs, *tile),
            array(pairs, *tile),
            array(fields * half + half + quads, *tile),
            array(fields * half + 2 * quads, *tile),
        ),
        in_specs=[HBM] * 3,
        out_specs=[VMEM] * 5,
        scratch_shapes=[pltpu.SemaphoreType.DMA((3,))],
        compiler_params=PARAMS,
    )(flat, cx, cy)
    edge, north_corner, south_corner = pl.pallas_call(
        functools.partial(pack_edges_kernel, levels),
        out_shape=(array(fields + 2, *tile), array(slots, cols), array(slots, cols)),
        in_specs=[VMEM] * 3,
        out_specs=[VMEM] * 3,
        compiler_params=PARAMS,
    )(flat, cx, cy)

    def send(value, up, right):
        pairs_ = []
        for w in range(wide):
            for n in range(narrow):
                to = ((w + up) % wide) * narrow + (n + right) % narrow
                pairs_.append((w * narrow + n, to))
        return lax.ppermute(value, ("wide", "narrow"), pairs_)

    def to_both_sides(value, up):
        from_west = send(value, up, 1)
        from_east = from_west if narrow == 2 else send(value, up, -1)
        return from_west, from_east

    from_south = send(north, 1, 0)
    from_north = send(south, -1, 0)
    edge_west, edge_east = to_both_sides(edge, 0)
    corner_sw, corner_se = to_both_sides(north_corner, 1)
    corner_nw, corner_ne = to_both_sides(south_corner, -1)

    inverse, source, carry, onehot = pl.pallas_call(
        prep_kernel,
        out_shape=(array(levels, field_pairs, *tile),) * 3
        + (array(rows * cols, cols, dtype=jnp.bfloat16),),
        in_specs=[SMEM, SMEM, VMEM, VMEM],
        out_specs=[VMEM] * 4,
        cost_estimate=pl.CostEstimate(flops=4000000, bytes_accessed=2000000, transcendentals=0),
        compiler_params=PARAMS,
    )(class_coeffs, physics_ref, cloud_class, span_target)

    state, placed = pl.pallas_call(
        functools.partial(main_kernel, fields, levels),
        out_shape=(array(fields * pairs, *tile), array(wide * rows, cols)),
        in_specs=[VMEM] * 18,
        out_specs=[VMEM] * 2,
        scratch_shapes=[
            pltpu.VMEM((levels, 5) + tile, F32),
            pltpu.VMEM((pairs, 5) + tile, F32),
            pltpu.VMEM((fields,) + tile, F32),
            pltpu.VMEM((fields,) + tile, F32),
            pltpu.VMEM((levels, field_pairs) + tile, F32),
            pltpu.VMEM((levels, field_pairs) + tile, F32),
            pltpu.VMEM((levels, field_pairs) + tile, F32),
        ],
        compiler_params=PARAMS,
    )(
        flat,
        cx,
        cy,
        from_south,
        from_north,
        edge,
        edge_west,
        edge_east,
        corner_sw,
        corner_se,
        corner_nw,
        corner_ne,
        inverse,
        source,
        carry,
        cloud_class,
        span_target,
        onehot,
    )
    span_diag = lax.psum_scatter(placed, "wide", scatter_dimension=0, tiled=True)
    return state.reshape(fields, levels, rows, cols), span_diag


def solution(mesh):
    return jax.shard_map(
        body,
        mesh=mesh,
        in_specs=(
            P(None, None, "wide", "narrow"),
            P(None, "wide", "narrow"),
            P(None, "wide", "narrow"),
            P(),
            P(),
            P("wide", "narrow"),
            P("wide", "narrow"),
        ),
        out_specs=(P(None, None, "wide", "narrow"), P("wide", "narrow")),
        check_vma=False,
    )
```

```python
import functools

import jax
import jax.numpy as jnp
from jax import lax
from jax.experimental import pallas as pl
from jax.experimental.pallas import tpu as pltpu
from jax.sharding import PartitionSpec as P

VMEM = pl.BlockSpec(memory_space=pltpu.VMEM)
HBM = pl.BlockSpec(memory_space=pltpu.HBM)
SMEM = pl.BlockSpec(memory_space=pltpu.SMEM)
F32 = jnp.float32
PARAMS = pltpu.CompilerParams(vmem_limit_bytes=12 * 1024 * 1024)


def sub_roll(value, shift):
    shift = shift % value.shape[0]
    return value if shift == 0 else pltpu.roll(value, shift, 0)


def lane_roll(value, shift):
    shift = shift % value.shape[1]
    return value if shift == 0 else pltpu.roll(value, shift, 1)


def iotas(shape):
    return lax.broadcasted_iota(jnp.int32, shape, 0), lax.broadcasted_iota(jnp.int32, shape, 1)


def pack_rows_kernel(
    levels, tracers_in, cx_in, cy_in, tracers, cx, cy, north, south, semaphores
):
    copies = [
        pltpu.make_async_copy(source, into, semaphores.at[i])
        for i, (source, into) in enumerate(((tracers_in, tracers), (cx_in, cx), (cy_in, cy)))
    ]
    for copy in copies:
        copy.start()
    for copy in copies:
        copy.wait()
    pairs = levels // 2
    half = pairs // 2
    fields = tracers.shape[0] // pairs
    tile = tracers.shape[1:]
    rows = tile[0] // 2
    local = iotas(tile)[0] % rows
    lower = local < rows // 2
    upper = local >= rows // 2

    def one_row(vectors, row, step):
        packed = []
        for start in range(0, pairs, rows):
            total = vectors[start]
            for t in range(1, rows):
                total = jnp.where(
                    local == row + step * t, sub_roll(vectors[start + t], step * t), total
                )
            packed.append(total)
        return packed

    for f in range(fields):
        for k in range(half):
            first, second = tracers[f * pairs + 2 * k], tracers[f * pairs + 2 * k + 1]
            north[f * half + k] = jnp.where(upper, first, sub_roll(second, 2))
            south[f * half + k] = jnp.where(lower, first, sub_roll(second, -2))
    vectors_x = [cx[k] for k in range(pairs)]
    vectors_y = [cy[k] for k in range(pairs)]
    base = fields * half
    for k in range(half):
        north[base + k] = jnp.where(upper, vectors_y[2 * k], sub_roll(vectors_y[2 * k + 1], 2))
    for k, value in enumerate(one_row(vectors_x, rows - 1, -1)):
        north[base + half + k] = value
    south_rows = one_row(vectors_x, 0, 1) + one_row(vectors_y, 0, 1)
    for k, value in enumerate(south_rows):
        south[base + k] = value


def pack_edges_kernel(levels, tracers, cx, cy, edge, north_corner, south_corner):
    pairs = levels // 2
    fields = tracers.shape[0] // pairs
    tile = tracers.shape[1:]
    rows = tile[0] // 2
    lanes = tile[1]
    group = lanes // levels
    lane = iotas(tile)[1]

    def pack_edge(vectors, slot):
        total = lane_roll(vectors[0], 2)
        for k in range(1, pairs):
            total = jnp.where(
                lane // (2 * group) == k, lane_roll(vectors[k], 2 + 2 * group * k), total
            )
        total = jnp.where(
            lane % (2 * group) < group, total, sub_roll(lane_roll(total, group), rows)
        )
        total = jnp.where(lane % group < group // 2, total, lane_roll(total, group // 2))
        edge[slot] = total
        north_corner[pl.ds(slot, 1), :] = total[rows - 1 : rows]
        south_corner[pl.ds(slot, 1), :] = total[0:1]

    for f in range(fields):
        pack_edge([tracers[f * pairs + k] for k in range(pairs)], f)
    pack_edge([cx[k] for k in range(pairs)], fields)
    pack_edge([cy[k] for k in range(pairs)], fields + 1)


def prep_kernel(coeffs, profile, klass, target, inverse, source, carry, onehot):
    levels, pairs = inverse.shape[:2]
    fields = profile.shape[0]
    tile = inverse.shape[2:]
    rows, lanes = klass.shape
    sub, lane = iotas(tile)
    low = sub < rows
    kind = jnp.concatenate([klass[...], klass[...]], axis=0)
    is_two = kind == 2
    is_one = kind == 1

    def by_class(which, f):
        return jnp.where(
            is_two,
            coeffs[which, 2, f] * 0.25,
            jnp.where(is_one, coeffs[which, 1, f] * 0.5, coeffs[which, 0, f]),
        )

    for p in range(pairs):
        f1 = 2 * p
        f2 = min(2 * p + 1, fields - 1)
        diffusion = jnp.where(low, by_class(0, f1), by_class(0, f2))
        relax = jnp.where(low, by_class(1, f1), by_class(1, f2))
        edge_diag = 1.0 + relax + diffusion
        middle = edge_diag + diffusion
        last = None
        for l in range(levels):
            diagonal = edge_diag if l in (0, levels - 1) else middle
            denominator = diagonal if last is None else diagonal - diffusion * last
            inv = 1.0 / denominator
            last = diffusion * inv
            inverse[l, p] = inv
            carry[l, p] = last
            source[l, p] = relax * jnp.where(low, profile[f1, l], profile[f2, l]) * inv
    low_part = target[...] & (lanes - 1)
    slot, _ = iotas((lanes, lanes))
    for r in range(rows):
        hit = slot == low_part[r : r + 1]
        onehot[r * lanes : (r + 1) * lanes, :] = jnp.where(hit, 1.0, 0.0).astype(jnp.bfloat16)


def main_kernel(
    fields,
    levels,
    tracers,
    cx,
    cy,
    from_south,
    from_north,
    edge,
    edge_west,
    edge_east,
    corner_sw,
    corner_se,
    corner_nw,
    corner_ne,
    inverse,
    source,
    carry,
    klass,
    target,
    onehot,
    state_out,
    placed,
    full_coefs,
    half_coefs,
    edge_raw,
    edge_next,
    start,
    work,
    partial,
):
    pairs = levels // 2
    half = pairs // 2
    tile = tracers.shape[1:]
    rows = tile[0] // 2
    lanes = tile[1]
    group = lanes // levels
    sub, lane = iotas(tile)
    local = sub % rows
    low = sub < rows
    lower = local < rows // 2
    first_lane = lane == 0
    last_lane = lane == lanes - 1
    place = lane % group
    from_east = (place == 2) | (place == 3)
    from_west = (place == 4) | (place == 5)
    east_side = place < group // 2

    def extended_edge(slot):
        value = jnp.where(from_east, edge_east[slot], jnp.where(from_west, edge_west[slot], edge[slot]))
        south = jnp.where(east_side, corner_se[pl.ds(slot, 1), :], corner_sw[pl.ds(slot, 1), :])
        north = jnp.where(east_side, corner_ne[pl.ds(slot, 1), :], corner_nw[pl.ds(slot, 1), :])
        value = jnp.where(sub == 2 * rows - 1, south, value)
        return jnp.where(sub == rows, north, value)

    def side_by_side(value):
        return jnp.where(place == 3, lane_roll(value, -2), value)

    def coefficients(here_x, west_x, here_y, south_y):
        return (
            1.0
            - jnp.maximum(here_x, 0.0)
            + jnp.minimum(west_x, 0.0)
            - jnp.maximum(here_y, 0.0)
            + jnp.minimum(south_y, 0.0),
            jnp.maximum(-here_x, 0.0),
            jnp.maximum(west_x, 0.0),
            jnp.maximum(-here_y, 0.0),
            jnp.maximum(south_y, 0.0),
        )

    def combine(coefs, center, east, west, north, south):
        return (
            coefs[0] * center
            + (coefs[1] * east + coefs[2] * west)
            + (coefs[3] * north + coefs[4] * south)
        )

    edge_x = extended_edge(fields)
    edge_y = extended_edge(fields + 1)
    edge_coefs = coefficients(edge_x, lane_roll(edge_x, 1), edge_y, sub_roll(edge_y, 1))
    for f in range(fields):
        raw = extended_edge(f)
        edge_raw[f] = side_by_side(raw)
        moved = side_by_side(
            combine(
                edge_coefs,
                raw,
                lane_roll(raw, -1),
                lane_roll(raw, 1),
                sub_roll(raw, -1),
                sub_roll(raw, 1),
            )
        )
        edge_next[f] = jnp.where(low, moved, sub_roll(lane_roll(moved, -group), rows))

    sides_x = side_by_side(edge_x)
    sides_x_odd = sub_roll(sides_x, rows)
    base = fields * half
    for k in range(pairs):
        quad, t = k // rows, k % rows
        count = pairs // rows
        row_south = sub_roll(from_south[base + half + quad], rows + t)
        row_north = sub_roll(from_north[base + quad], rows - t)
        halo_x = jnp.where(local == 0, row_north, row_south)
        north_y = sub_roll(from_north[base + count + quad], rows - t)
        south_y = sub_roll(from_south[base + k // 2], rows if k % 2 == 0 else 2)
        halo_y = jnp.where(lower, north_y, south_y)
        own_x = cx[k]
        own_y = cy[k]
        both = []
        for odd in range(2):
            here_x = jnp.where(low, halo_x, own_x) if odd else jnp.where(low, own_x, halo_x)
            here_y = jnp.where(low, halo_y, own_y) if odd else jnp.where(low, own_y, halo_y)
            sides = lane_roll(sides_x_odd if odd else sides_x, -(group * (2 * k + odd) + 3))
            west_x = jnp.where(first_lane, sides, lane_roll(here_x, 1))
            coefs = coefficients(here_x, west_x, here_y, sub_roll(here_y, 1))
            for c in range(5):
                full_coefs[2 * k + odd, c] = coefs[c]
            both.append(coefs)
        for c in range(5):
            half_coefs[k, c] = jnp.where(low, both[0][c], both[1][c])

    north_part = (sub >= 1) & (sub <= rows)
    south_part = (sub < rows - 1) | (sub == 2 * rows - 1)

    def advect(f, k, first_coefs, second_coefs):
        own = tracers[f * pairs + k]
        message_south = from_south[f * half + k // 2]
        message_north = from_north[f * half + k // 2]
        if k % 2 == 0:
            halo = sub_roll(jnp.where(lower, message_north, message_south), rows)
        else:
            halo = jnp.where(lower, sub_roll(message_north, -2), sub_roll(message_south, 2))
        raw_sides = edge_raw[f]
        results = []
        for odd in range(2):
            value = jnp.where(low, halo, own) if odd else jnp.where(low, own, halo)
            sides = sub_roll(raw_sides, rows) if odd else raw_sides
            sides = lane_roll(sides, -(group * (2 * k + odd) + 3))
            results.append(
                combine(
                    first_coefs[odd],
                    value,
                    jnp.where(last_lane, sides, lane_roll(value, -1)),
                    jnp.where(first_lane, sides, lane_roll(value, 1)),
                    sub_roll(value, -1),
                    sub_roll(value, 1),
                )
            )
        even, odd = results
        center = jnp.where(low, even, odd)
        sides = lane_roll(edge_next[f], -(2 * group * k + 3))
        return combine(
            second_coefs,
            center,
            jnp.where(last_lane, sides, lane_roll(center, -1)),
            jnp.where(first_lane, sides, lane_roll(center, 1)),
            sub_roll(jnp.where(north_part, even, odd), -1),
            sub_roll(jnp.where(south_part, even, odd), 1),
        )

    def advect_pair(p, carry_in):
        f1 = 2 * p
        f2 = jnp.minimum(2 * p + 1, fields - 1)
        for k in range(pairs):
            first_coefs = [[full_coefs[2 * k + odd, c] for c in range(5)] for odd in range(2)]
            second_coefs = [half_coefs[k, c] for c in range(5)]
            one = advect(f1, k, first_coefs, second_coefs)
            two = advect(f2, k, first_coefs, second_coefs)
            start[2 * k, p] = jnp.where(low, one, sub_roll(two, rows))
            start[2 * k + 1, p] = jnp.where(low, sub_roll(one, rows), two)
        return carry_in

    field_pairs = start.shape[1]
    lax.fori_loop(0, field_pairs, advect_pair, 0)

    kind = jnp.concatenate([klass[...], klass[...]], axis=0)
    for step in range(4):
        origin = start if step == 0 else work
        active = None if step == 0 else (kind >= (1 if step == 1 else 2))[None]
        last = None
        for l in range(levels):
            value = origin[l] * inverse[l] + source[l]
            if last is not None:
                value = value + carry[l] * last
            if l < levels - 1:
                partial[l] = value
            last = value
        for l in range(levels - 1, -1, -1):
            if l < levels - 1:
                last = partial[l] + carry[l] * last
            work[l] = last if active is None else jnp.where(active, last, origin[l])

    total = jnp.zeros(tile, F32)
    for p in range(field_pairs):
        f1, f2 = 2 * p, 2 * p + 1
        square = jnp.zeros(tile, F32)
        for k in range(pairs):
            new = []
            for l in (2 * k, 2 * k + 1):
                begin = start[l, p]
                tendency = work[l, p] - begin
                square = square + tendency * tendency
                new.append(begin + tendency)
            state_out[f1 * pairs + k] = jnp.where(low, new[0], sub_roll(new[1], rows))
            if f2 < fields:
                state_out[f2 * pairs + k] = jnp.where(low, sub_roll(new[0], rows), new[1])
        total = total + (square if f2 < fields else jnp.where(low, square, 0.0))
    heat = (total + sub_roll(total, rows)) * (1.0 / (fields * levels))

    first = heat.astype(jnp.bfloat16).astype(F32)
    rest = heat - first
    second = rest.astype(jnp.bfloat16).astype(F32)
    third = rest - second
    spans = placed.shape[0]
    place_row, _ = iotas((spans, lanes))
    inner = split_of(spans // rows)
    outer = spans // rows // inner
    span = (place_row // rows % outer) * inner + place_row // (rows * outer)
    slot_row = span * rows + place_row % rows
    high = lax.shift_right_logical(target[...], lanes.bit_length() - 1)
    result = jnp.zeros((3 * spans, lanes), F32)
    for r in range(rows):
        hit = slot_row == high[r : r + 1]
        left = jnp.concatenate(
            [
                jnp.where(hit, part[r : r + 1], 0.0).astype(jnp.bfloat16)
                for part in (first, second, third)
            ],
            axis=0,
        )
        result = result + lax.dot_general(
            left,
            onehot[r * lanes : (r + 1) * lanes, :],
            (((1,), (1,)), ((), ())),
            preferred_element_type=F32,
        )
    placed[...] = result[:spans] + result[spans : 2 * spans] + result[2 * spans :]


def split_of(count):
    inner = 1
    while inner * inner * 4 <= count and count % (inner * 2) == 0:
        inner *= 2
    return inner


def add_kernel(parts, total):
    value = parts[0]
    for i in range(1, parts.shape[0]):
        value = value + parts[i]
    total[...] = value


def add_up(parts):
    return pl.pallas_call(
        add_kernel,
        out_shape=jax.ShapeDtypeStruct(parts.shape[1:], F32),
        in_specs=[VMEM],
        out_specs=VMEM,
        compiler_params=PARAMS,
    )(parts)


def body(tracers, courant_x, courant_y, physics_ref, class_coeffs, span_target, cloud_class):
    fields, levels, rows, cols = tracers.shape
    wide = lax.axis_size("wide")
    narrow = lax.axis_size("narrow")
    pairs = levels // 2
    half = pairs // 2
    tile = (2 * rows, cols)
    field_pairs = (fields + 1) // 2
    flat = tracers.reshape(fields * pairs, *tile)
    cx = courant_x.reshape(pairs, *tile)
    cy = courant_y.reshape(pairs, *tile)
    quads = pairs // rows
    slots = -(-(fields + 2) // 8) * 8

    def array(*shape, dtype=F32):
        return jax.ShapeDtypeStruct(shape, dtype)

    flat, cx, cy, north, south = pl.pallas_call(
        functools.partial(pack_rows_kernel, levels),
        out_shape=(
            array(fields * pairs, *tile),
            array(pairs, *tile),
            array(pairs, *tile),
            array(fields * half + half + quads, *tile),
            array(fields * half + 2 * quads, *tile),
        ),
        in_specs=[HBM] * 3,
        out_specs=[VMEM] * 5,
        scratch_shapes=[pltpu.SemaphoreType.DMA((3,))],
        compiler_params=PARAMS,
    )(*(pltpu.with_memory_space_constraint(x, pltpu.HBM) for x in (flat, cx, cy)))
    edge, north_corner, south_corner = pl.pallas_call(
        functools.partial(pack_edges_kernel, levels),
        out_shape=(array(fields + 2, *tile), array(slots, cols), array(slots, cols)),
        in_specs=[VMEM] * 3,
        out_specs=[VMEM] * 3,
        compiler_params=PARAMS,
    )(flat, cx, cy)

    def send(value, up, right):
        pairs_ = []
        for w in range(wide):
            for n in range(narrow):
                to = ((w + up) % wide) * narrow + (n + right) % narrow
                pairs_.append((w * narrow + n, to))
        return lax.ppermute(value, ("wide", "narrow"), pairs_)

    def to_both_sides(value, up):
        from_west = send(value, up, 1)
        from_east = from_west if narrow == 2 else send(value, up, -1)
        return from_west, from_east

    from_south = send(north, 1, 0)
    from_north = send(south, -1, 0)
    edge_west, edge_east = to_both_sides(edge, 0)
    corner_sw, corner_se = to_both_sides(north_corner, 1)
    corner_nw, corner_ne = to_both_sides(south_corner, -1)

    inverse, source, carry, onehot = pl.pallas_call(
        prep_kernel,
        out_shape=(array(levels, field_pairs, *tile),) * 3
        + (array(rows * cols, cols, dtype=jnp.bfloat16),),
        in_specs=[SMEM, SMEM, VMEM, VMEM],
        out_specs=[VMEM] * 4,
        cost_estimate=pl.CostEstimate(flops=4000000, bytes_accessed=2000000, transcendentals=0),
        compiler_params=PARAMS,
    )(class_coeffs, physics_ref, cloud_class, span_target)

    state, placed = pl.pallas_call(
        functools.partial(main_kernel, fields, levels),
        out_shape=(array(fields * pairs, *tile), array(wide * rows, cols)),
        in_specs=[VMEM] * 18,
        out_specs=[VMEM] * 2,
        scratch_shapes=[
            pltpu.VMEM((levels, 5) + tile, F32),
            pltpu.VMEM((pairs, 5) + tile, F32),
            pltpu.VMEM((fields,) + tile, F32),
            pltpu.VMEM((fields,) + tile, F32),
            pltpu.VMEM((levels, field_pairs) + tile, F32),
            pltpu.VMEM((levels, field_pairs) + tile, F32),
            pltpu.VMEM((levels, field_pairs) + tile, F32),
        ],
        compiler_params=PARAMS,
    )(
        flat,
        cx,
        cy,
        from_south,
        from_north,
        edge,
        edge_west,
        edge_east,
        corner_sw,
        corner_se,
        corner_nw,
        corner_ne,
        inverse,
        source,
        carry,
        cloud_class,
        span_target,
        onehot,
    )
    inner = split_of(wide)
    outer = wide // inner
    planes = [[o * inner + i for i in range(inner)] for o in range(outer)]
    columns = [[o * inner + i for o in range(outer)] for i in range(inner)]
    placed = placed.reshape(inner, outer * rows, cols)
    placed = lax.all_to_all(placed, "wide", 0, 0, axis_index_groups=planes, tiled=True)
    placed = add_up(placed).reshape(outer, rows, cols)
    placed = lax.all_to_all(placed, "wide", 0, 0, axis_index_groups=columns, tiled=True)
    return state.reshape(fields, levels, rows, cols), add_up(placed)


def solution(mesh):
    return jax.shard_map(
        body,
        mesh=mesh,
        in_specs=(
            P(None, None, "wide", "narrow"),
            P(None, "wide", "narrow"),
            P(None, "wide", "narrow"),
            P(),
            P(),
            P("wide", "narrow"),
            P("wide", "narrow"),
        ),
        out_specs=(P(None, None, "wide", "narrow"), P("wide", "narrow")),
        check_vma=False,
    )
```

```python
import functools

import jax
import jax.numpy as jnp
from jax import lax
from jax.experimental import pallas as pl
from jax.experimental.pallas import tpu as pltpu
from jax.sharding import PartitionSpec as P

VMEM = pl.BlockSpec(memory_space=pltpu.VMEM)
HBM = pl.BlockSpec(memory_space=pltpu.HBM)
SMEM = pl.BlockSpec(memory_space=pltpu.SMEM)
F32 = jnp.float32
PARAMS = pltpu.CompilerParams(vmem_limit_bytes=12 * 1024 * 1024)


def sub_roll(value, shift):
    shift = shift % value.shape[0]
    return value if shift == 0 else pltpu.roll(value, shift, 0)


def lane_roll(value, shift):
    shift = shift % value.shape[1]
    return value if shift == 0 else pltpu.roll(value, shift, 1)


def iotas(shape):
    return lax.broadcasted_iota(jnp.int32, shape, 0), lax.broadcasted_iota(jnp.int32, shape, 1)


def pack_rows_kernel(
    levels, tracers_in, cx_in, cy_in, tracers, cx, cy, north, south, semaphores
):
    copies = [
        pltpu.make_async_copy(source, into, semaphores.at[i])
        for i, (source, into) in enumerate(((tracers_in, tracers), (cx_in, cx), (cy_in, cy)))
    ]
    for copy in copies:
        copy.start()
    for copy in copies:
        copy.wait()
    pairs = levels // 2
    half = pairs // 2
    fields = tracers.shape[0] // pairs
    tile = tracers.shape[1:]
    rows = tile[0] // 2
    local = iotas(tile)[0] % rows
    lower = local < rows // 2
    upper = local >= rows // 2

    def one_row(vectors, row, step):
        packed = []
        for start in range(0, pairs, rows):
            total = vectors[start]
            for t in range(1, rows):
                total = jnp.where(
                    local == row + step * t, sub_roll(vectors[start + t], step * t), total
                )
            packed.append(total)
        return packed

    for f in range(fields):
        for k in range(half):
            first, second = tracers[f * pairs + 2 * k], tracers[f * pairs + 2 * k + 1]
            north[f * half + k] = jnp.where(upper, first, sub_roll(second, 2))
            south[f * half + k] = jnp.where(lower, first, sub_roll(second, -2))
    vectors_x = [cx[k] for k in range(pairs)]
    vectors_y = [cy[k] for k in range(pairs)]
    base = fields * half
    for k in range(half):
        north[base + k] = jnp.where(upper, vectors_y[2 * k], sub_roll(vectors_y[2 * k + 1], 2))
    for k, value in enumerate(one_row(vectors_x, rows - 1, -1)):
        north[base + half + k] = value
    south_rows = one_row(vectors_x, 0, 1) + one_row(vectors_y, 0, 1)
    for k, value in enumerate(south_rows):
        south[base + k] = value


def pack_edges_kernel(levels, tracers, cx, cy, edge, north_corner, south_corner):
    pairs = levels // 2
    fields = tracers.shape[0] // pairs
    tile = tracers.shape[1:]
    rows = tile[0] // 2
    lanes = tile[1]
    group = lanes // levels
    lane = iotas(tile)[1]

    def pack_edge(vectors, slot):
        total = lane_roll(vectors[0], 2)
        for k in range(1, pairs):
            total = jnp.where(
                lane // (2 * group) == k, lane_roll(vectors[k], 2 + 2 * group * k), total
            )
        total = jnp.where(
            lane % (2 * group) < group, total, sub_roll(lane_roll(total, group), rows)
        )
        total = jnp.where(lane % group < group // 2, total, lane_roll(total, group // 2))
        edge[slot] = total
        north_corner[pl.ds(slot, 1), :] = total[rows - 1 : rows]
        south_corner[pl.ds(slot, 1), :] = total[0:1]

    for f in range(fields):
        pack_edge([tracers[f * pairs + k] for k in range(pairs)], f)
    pack_edge([cx[k] for k in range(pairs)], fields)
    pack_edge([cy[k] for k in range(pairs)], fields + 1)


def prep_kernel(coeffs, profile, klass, target, inverse, source, carry, onehot):
    levels, pairs = inverse.shape[:2]
    fields = profile.shape[0]
    tile = inverse.shape[2:]
    rows, lanes = klass.shape
    sub, lane = iotas(tile)
    low = sub < rows
    kind = jnp.concatenate([klass[...], klass[...]], axis=0)
    is_two = kind == 2
    is_one = kind == 1

    def by_class(which, f):
        return jnp.where(
            is_two,
            coeffs[which, 2, f] * 0.25,
            jnp.where(is_one, coeffs[which, 1, f] * 0.5, coeffs[which, 0, f]),
        )

    for p in range(pairs):
        f1 = 2 * p
        f2 = min(2 * p + 1, fields - 1)
        diffusion = jnp.where(low, by_class(0, f1), by_class(0, f2))
        relax = jnp.where(low, by_class(1, f1), by_class(1, f2))
        edge_diag = 1.0 + relax + diffusion
        middle = edge_diag + diffusion
        last = None
        for l in range(levels):
            diagonal = edge_diag if l in (0, levels - 1) else middle
            denominator = diagonal if last is None else diagonal - diffusion * last
            inv = 1.0 / denominator
            last = diffusion * inv
            inverse[l, p] = inv
            carry[l, p] = last
            source[l, p] = relax * jnp.where(low, profile[f1, l], profile[f2, l]) * inv
    low_part = target[...] & (lanes - 1)
    slot, _ = iotas((lanes, lanes))
    for r in range(rows):
        hit = slot == low_part[r : r + 1]
        onehot[r * lanes : (r + 1) * lanes, :] = jnp.where(hit, 1.0, 0.0).astype(jnp.bfloat16)


def main_kernel(
    fields,
    levels,
    tracers,
    cx,
    cy,
    from_south,
    from_north,
    edge,
    edge_west,
    edge_east,
    corner_sw,
    corner_se,
    corner_nw,
    corner_ne,
    inverse,
    source,
    carry,
    klass,
    target,
    onehot,
    state_out,
    kept,
    sent,
    full_coefs,
    half_coefs,
    edge_raw,
    edge_next,
    start,
    work,
    partial,
):
    pairs = levels // 2
    half = pairs // 2
    tile = tracers.shape[1:]
    rows = tile[0] // 2
    lanes = tile[1]
    group = lanes // levels
    sub, lane = iotas(tile)
    local = sub % rows
    low = sub < rows
    lower = local < rows // 2
    first_lane = lane == 0
    last_lane = lane == lanes - 1
    place = lane % group
    from_east = (place == 2) | (place == 3)
    from_west = (place == 4) | (place == 5)
    east_side = place < group // 2

    def extended_edge(slot):
        value = jnp.where(from_east, edge_east[slot], jnp.where(from_west, edge_west[slot], edge[slot]))
        south = jnp.where(east_side, corner_se[pl.ds(slot, 1), :], corner_sw[pl.ds(slot, 1), :])
        north = jnp.where(east_side, corner_ne[pl.ds(slot, 1), :], corner_nw[pl.ds(slot, 1), :])
        value = jnp.where(sub == 2 * rows - 1, south, value)
        return jnp.where(sub == rows, north, value)

    def side_by_side(value):
        return jnp.where(place == 3, lane_roll(value, -2), value)

    def coefficients(here_x, west_x, here_y, south_y):
        return (
            1.0
            - jnp.maximum(here_x, 0.0)
            + jnp.minimum(west_x, 0.0)
            - jnp.maximum(here_y, 0.0)
            + jnp.minimum(south_y, 0.0),
            jnp.maximum(-here_x, 0.0),
            jnp.maximum(west_x, 0.0),
            jnp.maximum(-here_y, 0.0),
            jnp.maximum(south_y, 0.0),
        )

    def combine(coefs, center, east, west, north, south):
        return (
            coefs[0] * center
            + (coefs[1] * east + coefs[2] * west)
            + (coefs[3] * north + coefs[4] * south)
        )

    edge_x = extended_edge(fields)
    edge_y = extended_edge(fields + 1)
    edge_coefs = coefficients(edge_x, lane_roll(edge_x, 1), edge_y, sub_roll(edge_y, 1))
    for f in range(fields):
        raw = extended_edge(f)
        edge_raw[f] = side_by_side(raw)
        moved = side_by_side(
            combine(
                edge_coefs,
                raw,
                lane_roll(raw, -1),
                lane_roll(raw, 1),
                sub_roll(raw, -1),
                sub_roll(raw, 1),
            )
        )
        edge_next[f] = jnp.where(low, moved, sub_roll(lane_roll(moved, -group), rows))

    sides_x = side_by_side(edge_x)
    sides_x_odd = sub_roll(sides_x, rows)
    base = fields * half
    for k in range(pairs):
        quad, t = k // rows, k % rows
        count = pairs // rows
        row_south = sub_roll(from_south[base + half + quad], rows + t)
        row_north = sub_roll(from_north[base + quad], rows - t)
        halo_x = jnp.where(local == 0, row_north, row_south)
        north_y = sub_roll(from_north[base + count + quad], rows - t)
        south_y = sub_roll(from_south[base + k // 2], rows if k % 2 == 0 else 2)
        halo_y = jnp.where(lower, north_y, south_y)
        own_x = cx[k]
        own_y = cy[k]
        both = []
        for odd in range(2):
            here_x = jnp.where(low, halo_x, own_x) if odd else jnp.where(low, own_x, halo_x)
            here_y = jnp.where(low, halo_y, own_y) if odd else jnp.where(low, own_y, halo_y)
            sides = lane_roll(sides_x_odd if odd else sides_x, -(group * (2 * k + odd) + 3))
            west_x = jnp.where(first_lane, sides, lane_roll(here_x, 1))
            coefs = coefficients(here_x, west_x, here_y, sub_roll(here_y, 1))
            for c in range(5):
                full_coefs[2 * k + odd, c] = coefs[c]
            both.append(coefs)
        for c in range(5):
            half_coefs[k, c] = jnp.where(low, both[0][c], both[1][c])

    north_part = (sub >= 1) & (sub <= rows)
    south_part = (sub < rows - 1) | (sub == 2 * rows - 1)

    def advect(f, k, first_coefs, second_coefs):
        own = tracers[f * pairs + k]
        message_south = from_south[f * half + k // 2]
        message_north = from_north[f * half + k // 2]
        if k % 2 == 0:
            halo = sub_roll(jnp.where(lower, message_north, message_south), rows)
        else:
            halo = jnp.where(lower, sub_roll(message_north, -2), sub_roll(message_south, 2))
        raw_sides = edge_raw[f]
        results = []
        for odd in range(2):
            value = jnp.where(low, halo, own) if odd else jnp.where(low, own, halo)
            sides = sub_roll(raw_sides, rows) if odd else raw_sides
            sides = lane_roll(sides, -(group * (2 * k + odd) + 3))
            results.append(
                combine(
                    first_coefs[odd],
                    value,
                    jnp.where(last_lane, sides, lane_roll(value, -1)),
                    jnp.where(first_lane, sides, lane_roll(value, 1)),
                    sub_roll(value, -1),
                    sub_roll(value, 1),
                )
            )
        even, odd = results
        center = jnp.where(low, even, odd)
        sides = lane_roll(edge_next[f], -(2 * group * k + 3))
        return combine(
            second_coefs,
            center,
            jnp.where(last_lane, sides, lane_roll(center, -1)),
            jnp.where(first_lane, sides, lane_roll(center, 1)),
            sub_roll(jnp.where(north_part, even, odd), -1),
            sub_roll(jnp.where(south_part, even, odd), 1),
        )

    def advect_pair(p, carry_in):
        f1 = 2 * p
        f2 = jnp.minimum(2 * p + 1, fields - 1)
        for k in range(pairs):
            first_coefs = [[full_coefs[2 * k + odd, c] for c in range(5)] for odd in range(2)]
            second_coefs = [half_coefs[k, c] for c in range(5)]
            one = advect(f1, k, first_coefs, second_coefs)
            two = advect(f2, k, first_coefs, second_coefs)
            start[2 * k, p] = jnp.where(low, one, sub_roll(two, rows))
            start[2 * k + 1, p] = jnp.where(low, sub_roll(one, rows), two)
        return carry_in

    field_pairs = start.shape[1]
    lax.fori_loop(0, field_pairs, advect_pair, 0)

    kind = jnp.concatenate([klass[...], klass[...]], axis=0)
    for step in range(4):
        origin = start if step == 0 else work
        active = None if step == 0 else (kind >= (1 if step == 1 else 2))[None]
        last = None
        for l in range(levels):
            value = origin[l] * inverse[l] + source[l]
            if last is not None:
                value = value + carry[l] * last
            if l < levels - 1:
                partial[l] = value
            last = value
        for l in range(levels - 1, -1, -1):
            if l < levels - 1:
                last = partial[l] + carry[l] * last
            work[l] = last if active is None else jnp.where(active, last, origin[l])

    total = jnp.zeros(tile, F32)
    for p in range(field_pairs):
        f1, f2 = 2 * p, 2 * p + 1
        square = jnp.zeros(tile, F32)
        for k in range(pairs):
            new = []
            for l in (2 * k, 2 * k + 1):
                begin = start[l, p]
                tendency = work[l, p] - begin
                square = square + tendency * tendency
                new.append(begin + tendency)
            state_out[f1 * pairs + k] = jnp.where(low, new[0], sub_roll(new[1], rows))
            if f2 < fields:
                state_out[f2 * pairs + k] = jnp.where(low, sub_roll(new[0], rows), new[1])
        total = total + (square if f2 < fields else jnp.where(low, square, 0.0))
    heat = (total + sub_roll(total, rows)) * (1.0 / (fields * levels))

    first = heat.astype(jnp.bfloat16).astype(F32)
    rest = heat - first
    second = rest.astype(jnp.bfloat16).astype(F32)
    third = rest - second
    spans = kept.shape[0] * 2
    slot_row, _ = iotas((spans, lanes))
    own_rows = lax.axis_index("wide") * rows
    high = lax.shift_right_logical(target[...], lanes.bit_length() - 1) ^ own_rows
    result = jnp.zeros((3 * spans, lanes), F32)
    for r in range(rows):
        hit = slot_row == high[r : r + 1]
        left = jnp.concatenate(
            [
                jnp.where(hit, part[r : r + 1], 0.0).astype(jnp.bfloat16)
                for part in (first, second, third)
            ],
            axis=0,
        )
        result = result + lax.dot_general(
            left,
            onehot[r * lanes : (r + 1) * lanes, :],
            (((1,), (1,)), ((), ())),
            preferred_element_type=F32,
        )
    placed = result[:spans] + result[spans : 2 * spans] + result[2 * spans :]
    kept[...] = placed[: spans // 2]
    sent[...] = placed[spans // 2 :]


def fold_kernel(mine, other, kept, *sent):
    count = kept.shape[0]
    kept[...] = mine[:count] + other[:count]
    if sent:
        sent[0][...] = mine[count:] + other[count:]


def fold(mine, other, count):
    last = count == 0
    shape = jax.ShapeDtypeStruct((mine.shape[0] if last else count, mine.shape[1]), F32)
    results = pl.pallas_call(
        fold_kernel,
        out_shape=(shape,) if last else (shape, shape),
        in_specs=[VMEM, VMEM],
        out_specs=[VMEM] if last else [VMEM, VMEM],
        compiler_params=PARAMS,
    )(mine, other)
    return results[0], None if last else results[1]


def body(tracers, courant_x, courant_y, physics_ref, class_coeffs, span_target, cloud_class):
    fields, levels, rows, cols = tracers.shape
    wide = lax.axis_size("wide")
    narrow = lax.axis_size("narrow")
    pairs = levels // 2
    half = pairs // 2
    tile = (2 * rows, cols)
    field_pairs = (fields + 1) // 2
    flat = tracers.reshape(fields * pairs, *tile)
    cx = courant_x.reshape(pairs, *tile)
    cy = courant_y.reshape(pairs, *tile)
    quads = pairs // rows
    slots = -(-(fields + 2) // 8) * 8

    def array(*shape, dtype=F32):
        return jax.ShapeDtypeStruct(shape, dtype)

    flat, cx, cy, north, south = pl.pallas_call(
        functools.partial(pack_rows_kernel, levels),
        out_shape=(
            array(fields * pairs, *tile),
            array(pairs, *tile),
            array(pairs, *tile),
            array(fields * half + half + quads, *tile),
            array(fields * half + 2 * quads, *tile),
        ),
        in_specs=[HBM] * 3,
        out_specs=[VMEM] * 5,
        scratch_shapes=[pltpu.SemaphoreType.DMA((3,))],
        compiler_params=PARAMS,
    )(*(pltpu.with_memory_space_constraint(x, pltpu.HBM) for x in (flat, cx, cy)))
    edge, north_corner, south_corner = pl.pallas_call(
        functools.partial(pack_edges_kernel, levels),
        out_shape=(array(fields + 2, *tile), array(slots, cols), array(slots, cols)),
        in_specs=[VMEM] * 3,
        out_specs=[VMEM] * 3,
        compiler_params=PARAMS,
    )(flat, cx, cy)

    def send(value, up, right):
        pairs_ = []
        for w in range(wide):
            for n in range(narrow):
                to = ((w + up) % wide) * narrow + (n + right) % narrow
                pairs_.append((w * narrow + n, to))
        return lax.ppermute(value, ("wide", "narrow"), pairs_)

    def to_both_sides(value, up):
        from_west = send(value, up, 1)
        from_east = from_west if narrow == 2 else send(value, up, -1)
        return from_west, from_east

    from_south = send(north, 1, 0)
    from_north = send(south, -1, 0)
    edge_west, edge_east = to_both_sides(edge, 0)
    corner_sw, corner_se = to_both_sides(north_corner, 1)
    corner_nw, corner_ne = to_both_sides(south_corner, -1)

    inverse, source, carry, onehot = pl.pallas_call(
        prep_kernel,
        out_shape=(array(levels, field_pairs, *tile),) * 3
        + (array(rows * cols, cols, dtype=jnp.bfloat16),),
        in_specs=[SMEM, SMEM, VMEM, VMEM],
        out_specs=[VMEM] * 4,
        cost_estimate=pl.CostEstimate(flops=4000000, bytes_accessed=2000000, transcendentals=0),
        compiler_params=PARAMS,
    )(class_coeffs, physics_ref, cloud_class, span_target)

    state, kept, sent = pl.pallas_call(
        functools.partial(main_kernel, fields, levels),
        out_shape=(
            array(fields * pairs, *tile),
            array(wide // 2 * rows, cols),
            array(wide // 2 * rows, cols),
        ),
        in_specs=[VMEM] * 18,
        out_specs=[VMEM] * 3,
        scratch_shapes=[
            pltpu.VMEM((levels, 5) + tile, F32),
            pltpu.VMEM((pairs, 5) + tile, F32),
            pltpu.VMEM((fields,) + tile, F32),
            pltpu.VMEM((fields,) + tile, F32),
            pltpu.VMEM((levels, field_pairs) + tile, F32),
            pltpu.VMEM((levels, field_pairs) + tile, F32),
            pltpu.VMEM((levels, field_pairs) + tile, F32),
        ],
        compiler_params=PARAMS,
    )(
        flat,
        cx,
        cy,
        from_south,
        from_north,
        edge,
        edge_west,
        edge_east,
        corner_sw,
        corner_se,
        corner_nw,
        corner_ne,
        inverse,
        source,
        carry,
        cloud_class,
        span_target,
        onehot,
    )
    span = wide // 2
    while span >= 1:
        pairs_ = [
            (w * narrow + n, (w ^ span) * narrow + n) for w in range(wide) for n in range(narrow)
        ]
        received = lax.ppermute(sent, ("wide", "narrow"), pairs_)
        span //= 2
        kept, sent = fold(kept, received, span * rows)
    return state.reshape(fields, levels, rows, cols), kept


def solution(mesh):
    return jax.shard_map(
        body,
        mesh=mesh,
        in_specs=(
            P(None, None, "wide", "narrow"),
            P(None, "wide", "narrow"),
            P(None, "wide", "narrow"),
            P(),
            P(),
            P("wide", "narrow"),
            P("wide", "narrow"),
        ),
        out_specs=(P(None, None, "wide", "narrow"), P("wide", "narrow")),
        check_vma=False,
    )
```

```python
import functools
import math

import jax
import jax.numpy as jnp
from jax import lax
from jax.experimental import pallas as pl
from jax.experimental.pallas import tpu as pltpu
from jax.sharding import PartitionSpec as P

VMEM = pl.BlockSpec(memory_space=pltpu.VMEM)
HBM = pl.BlockSpec(memory_space=pltpu.HBM)
SMEM = pl.BlockSpec(memory_space=pltpu.SMEM)
F32 = jnp.float32
PARAMS = pltpu.CompilerParams(vmem_limit_bytes=12 * 1024 * 1024)


def sub_roll(value, shift):
    shift = shift % value.shape[0]
    return value if shift == 0 else pltpu.roll(value, shift, 0)


def lane_roll(value, shift):
    shift = shift % value.shape[1]
    return value if shift == 0 else pltpu.roll(value, shift, 1)


def iotas(shape):
    return lax.broadcasted_iota(jnp.int32, shape, 0), lax.broadcasted_iota(jnp.int32, shape, 1)


def pack_rows(tracers, f, pairs, north, south, slot):
    local = iotas(tracers.shape[1:])[0] % (tracers.shape[1] // 2)
    lower = local < tracers.shape[1] // 4
    for k in range(pairs // 2):
        first, second = tracers[f * pairs + 2 * k], tracers[f * pairs + 2 * k + 1]
        north[slot + k] = jnp.where(lower, sub_roll(second, 2), first)
        south[slot + k] = jnp.where(lower, first, sub_roll(second, -2))


def pack_rows_kernel(
    levels, tracers_in, cx_in, cy_in, tracers, cx, cy, north, south, semaphores
):
    copies = [
        pltpu.make_async_copy(source, into, semaphores.at[i])
        for i, (source, into) in enumerate(((tracers_in, tracers), (cx_in, cx), (cy_in, cy)))
    ]
    for copy in copies:
        copy.start()
    for copy in copies:
        copy.wait()
    pairs = levels // 2
    half = pairs // 2
    tile = tracers.shape[1:]
    rows = tile[0] // 2
    local = iotas(tile)[0] % rows
    upper = local >= rows // 2

    def one_row(vectors, row, step):
        packed = []
        for start in range(0, pairs, rows):
            total = vectors[start]
            for t in range(1, rows):
                total = jnp.where(
                    local == row + step * t, sub_roll(vectors[start + t], step * t), total
                )
            packed.append(total)
        return packed

    fields = tracers.shape[0] // pairs
    for f in range(fields):
        pack_rows(tracers, f, pairs, north, south, f * half)
    vectors_x = [cx[k] for k in range(pairs)]
    vectors_y = [cy[k] for k in range(pairs)]
    base = fields * half
    for k in range(half):
        north[base + k] = jnp.where(upper, vectors_y[2 * k], sub_roll(vectors_y[2 * k + 1], 2))
    for k, value in enumerate(one_row(vectors_x, rows - 1, -1)):
        north[base + half + k] = value
    south_rows = one_row(vectors_x, 0, 1) + one_row(vectors_y, 0, 1)
    for k, value in enumerate(south_rows):
        south[base + k] = value


def pack_edges_kernel(levels, tracers, cx, cy, edge, north_corner, south_corner):
    pairs = levels // 2
    fields = tracers.shape[0] // pairs
    tile = tracers.shape[1:]
    rows = tile[0] // 2
    lanes = tile[1]
    group = lanes // levels
    lane = iotas(tile)[1]

    def pack_edge(vectors, slot):
        total = lane_roll(vectors[0], 2)
        for k in range(1, pairs):
            total = jnp.where(
                lane // (2 * group) == k, lane_roll(vectors[k], 2 + 2 * group * k), total
            )
        total = jnp.where(
            lane % (2 * group) < group, total, sub_roll(lane_roll(total, group), rows)
        )
        total = jnp.where(lane % group < group // 2, total, lane_roll(total, group // 2))
        edge[slot] = total
        north_corner[pl.ds(slot, 1), :] = total[rows - 1 : rows]
        south_corner[pl.ds(slot, 1), :] = total[0:1]

    for f in range(fields):
        pack_edge([tracers[f * pairs + k] for k in range(pairs)], f)
    pack_edge([cx[k] for k in range(pairs)], fields)
    pack_edge([cy[k] for k in range(pairs)], fields + 1)


def cosine_sums(values):
    count = len(values)
    if count == 1:
        return values
    half = count // 2
    plus = [values[n] + values[count - 1 - n] for n in range(half)]
    minus = [
        (values[n] - values[count - 1 - n])
        * (0.5 / math.cos(math.pi * (2 * n + 1) / (2 * count)))
        for n in range(half)
    ]
    even = cosine_sums(plus)
    odd = cosine_sums(minus)
    result = []
    for k in range(half):
        result.append(even[k])
        result.append(odd[k] + odd[k + 1] if k + 1 < half else odd[k])
    return result


def cosine_series(values):
    count = len(values)
    if count == 1:
        return values
    half = count // 2
    odd_in = [values[2 * k + 1] + values[2 * k - 1] if k else values[1] for k in range(half)]
    even = cosine_series(values[0::2])
    odd = cosine_series(odd_in)
    odd = [
        odd[n] * (0.5 / math.cos(math.pi * (2 * n + 1) / (2 * count))) for n in range(half)
    ]
    return [even[n] + odd[n] for n in range(half)] + [
        even[n] - odd[n] for n in range(half - 1, -1, -1)
    ]


def prep_kernel(coeffs, profile, klass, target, decay, source, onehot):
    levels, pairs = decay.shape[:2]
    fields = profile.shape[0]
    tile = decay.shape[2:]
    rows, lanes = klass.shape
    sub, lane = iotas(tile)
    low = sub < rows
    kind = jnp.concatenate([klass[...], klass[...]], axis=0)
    is_two = kind == 2
    is_one = kind == 1

    def by_class(which, f):
        return jnp.where(
            is_two,
            coeffs[which, 2, f] * 0.25,
            jnp.where(is_one, coeffs[which, 1, f] * 0.5, coeffs[which, 0, f]),
        )

    for p in range(pairs):
        f1 = 2 * p
        f2 = min(2 * p + 1, fields - 1)
        diffusion = jnp.where(low, by_class(0, f1), by_class(0, f2))
        relax = jnp.where(low, by_class(1, f1), by_class(1, f2))
        waves = cosine_sums([jnp.where(low, profile[f1, l], profile[f2, l]) for l in range(levels)])
        for m in range(levels):
            rate = relax + diffusion * (2.0 - 2.0 * math.cos(math.pi * m / levels))
            once = 1.0 / (1.0 + rate)
            square = once * once
            twice = once + square
            steps = jnp.where(is_two, twice + twice * square, jnp.where(is_one, twice, once))
            steps = steps * ((1.0 if m == 0 else 2.0) / levels)
            decay[m, p] = steps * rate
            source[m, p] = steps * relax * waves[m]
    low_part = target[...] & (lanes - 1)
    slot, _ = iotas((lanes, lanes))
    for r in range(rows):
        hit = slot == low_part[r : r + 1]
        onehot[r * lanes : (r + 1) * lanes, :] = jnp.where(hit, 1.0, 0.0).astype(jnp.bfloat16)


def combine(coefs, center, east, west, north, south):
    return (
        coefs[0] * center
        + (coefs[1] * east + coefs[2] * west)
        + (coefs[3] * north + coefs[4] * south)
    )


def coefficients(here_x, west_x, here_y, south_y):
    return (
        1.0
        - jnp.maximum(here_x, 0.0)
        + jnp.minimum(west_x, 0.0)
        - jnp.maximum(here_y, 0.0)
        + jnp.minimum(south_y, 0.0),
        jnp.maximum(-here_x, 0.0),
        jnp.maximum(west_x, 0.0),
        jnp.maximum(-here_y, 0.0),
        jnp.maximum(south_y, 0.0),
    )


def edge_kernel(
    levels,
    edge,
    edge_west,
    edge_east,
    corner_sw,
    corner_se,
    corner_nw,
    corner_ne,
    edge_raw,
    edge_next,
    edge_courant,
):
    fields = edge_raw.shape[0]
    tile = edge.shape[1:]
    rows = tile[0] // 2
    lanes = tile[1]
    group = lanes // levels
    sub, lane = iotas(tile)
    low = sub < rows
    place = lane % group
    from_east = (place == 2) | (place == 3)
    from_west = (place == 4) | (place == 5)
    east_side = place < group // 2

    def extended_edge(slot):
        value = jnp.where(
            from_east, edge_east[slot], jnp.where(from_west, edge_west[slot], edge[slot])
        )
        south = jnp.where(east_side, corner_se[pl.ds(slot, 1), :], corner_sw[pl.ds(slot, 1), :])
        north = jnp.where(east_side, corner_ne[pl.ds(slot, 1), :], corner_nw[pl.ds(slot, 1), :])
        value = jnp.where(sub == 2 * rows - 1, south, value)
        return jnp.where(sub == rows, north, value)

    def side_by_side(value):
        return jnp.where(place == 3, lane_roll(value, -2), value)

    edge_x = extended_edge(fields)
    edge_y = extended_edge(fields + 1)
    edge_coefs = coefficients(edge_x, lane_roll(edge_x, 1), edge_y, sub_roll(edge_y, 1))
    for f in range(fields):
        raw = extended_edge(f)
        edge_raw[f] = side_by_side(raw)
        moved = side_by_side(
            combine(
                edge_coefs,
                raw,
                lane_roll(raw, -1),
                lane_roll(raw, 1),
                sub_roll(raw, -1),
                sub_roll(raw, 1),
            )
        )
        edge_next[f] = jnp.where(low, moved, sub_roll(lane_roll(moved, -group), rows))
    edge_courant[...] = side_by_side(edge_x)


def transport_and_solve(
    fields,
    levels,
    tracers,
    cx,
    cy,
    from_south,
    from_north,
    edge_raw,
    edge_next,
    edge_courant,
    decay,
    source,
    state,
    full_coefs,
    half_coefs,
):
    pairs = levels // 2
    half = pairs // 2
    tile = tracers.shape[1:]
    rows = tile[0] // 2
    lanes = tile[1]
    group = lanes // levels
    sub, lane = iotas(tile)
    local = sub % rows
    low = sub < rows
    lower = local < rows // 2
    first_lane = lane == 0
    last_lane = lane == lanes - 1
    north_part = (sub >= 1) & (sub <= rows)
    south_part = (sub < rows - 1) | (sub == 2 * rows - 1)

    sides_x = edge_courant[...]
    sides_x_odd = sub_roll(sides_x, rows)
    base = fields * half
    count = pairs // rows
    for k in range(pairs):
        quad, t = k // rows, k % rows
        row_south = sub_roll(from_south[base + half + quad], rows + t)
        row_north = sub_roll(from_north[base + quad], rows - t)
        halo_x = jnp.where(local == 0, row_north, row_south)
        north_y = sub_roll(from_north[base + count + quad], rows - t)
        south_y = sub_roll(from_south[base + k // 2], rows if k % 2 == 0 else 2)
        halo_y = jnp.where(lower, north_y, south_y)
        own_x = cx[k]
        own_y = cy[k]
        both = []
        for odd in range(2):
            here_x = jnp.where(low, halo_x, own_x) if odd else jnp.where(low, own_x, halo_x)
            here_y = jnp.where(low, halo_y, own_y) if odd else jnp.where(low, own_y, halo_y)
            sides = lane_roll(sides_x_odd if odd else sides_x, -(group * (2 * k + odd) + 3))
            west_x = jnp.where(first_lane, sides, lane_roll(here_x, 1))
            coefs = coefficients(here_x, west_x, here_y, sub_roll(here_y, 1))
            for c in range(5):
                full_coefs[2 * k + odd, c] = coefs[c]
            both.append(coefs)
        for c in range(5):
            half_coefs[k, c] = jnp.where(low, both[0][c], both[1][c])


    def advect(f, k, first_coefs, second_coefs):
        own = tracers[f * pairs + k]
        message_south = from_south[f * half + k // 2]
        message_north = from_north[f * half + k // 2]
        if k % 2 == 0:
            halo = sub_roll(jnp.where(lower, message_north, message_south), rows)
        else:
            halo = jnp.where(lower, sub_roll(message_north, -2), sub_roll(message_south, 2))
        raw_sides = edge_raw[f]
        results = []
        for odd in range(2):
            value = jnp.where(low, halo, own) if odd else jnp.where(low, own, halo)
            sides = sub_roll(raw_sides, rows) if odd else raw_sides
            sides = lane_roll(sides, -(group * (2 * k + odd) + 3))
            results.append(
                combine(
                    first_coefs[odd],
                    value,
                    jnp.where(last_lane, sides, lane_roll(value, -1)),
                    jnp.where(first_lane, sides, lane_roll(value, 1)),
                    sub_roll(value, -1),
                    sub_roll(value, 1),
                )
            )
        even, odd = results
        center = jnp.where(low, even, odd)
        sides = lane_roll(edge_next[f], -(2 * group * k + 3))
        return combine(
            second_coefs,
            center,
            jnp.where(last_lane, sides, lane_roll(center, -1)),
            jnp.where(first_lane, sides, lane_roll(center, 1)),
            sub_roll(jnp.where(north_part, even, odd), -1),
            sub_roll(jnp.where(south_part, even, odd), 1),
        )

    def pair_step(p, total):
        f1 = 2 * p
        f2 = jnp.minimum(f1 + 1, fields - 1)
        columns = []
        for k in range(pairs):
            first_coefs = [[full_coefs[2 * k + odd, c] for c in range(5)] for odd in range(2)]
            second_coefs = [half_coefs[k, c] for c in range(5)]
            one = advect(f1, k, first_coefs, second_coefs)
            two = advect(f2, k, first_coefs, second_coefs)
            columns.append(jnp.where(low, one, sub_roll(two, rows)))
            columns.append(jnp.where(low, sub_roll(one, rows), two))
        waves = cosine_sums(columns)
        change = cosine_series([source[m, p] - decay[m, p] * waves[m] for m in range(levels)])
        square = change[0] * change[0]
        for l in range(1, levels):
            square = square + change[l] * change[l]
        for k in range(pairs):
            even, odd = (columns[l] + change[l] for l in (2 * k, 2 * k + 1))
            state[f1 * pairs + k] = jnp.where(low, even, sub_roll(odd, rows))
            state[f2 * pairs + k] = jnp.where(low, sub_roll(even, rows), odd)
        return total + jnp.where(low | (f1 + 1 < fields), square, 0.0)

    return lax.fori_loop(0, (fields + 1) // 2, pair_step, jnp.zeros(tile, F32))


def main_kernel(fields, levels, *refs):
    inputs, (target, onehot), (state, placed), coefs = refs[:10], refs[10:12], refs[12:14], refs[14:]
    rows, lanes = target.shape
    total = transport_and_solve(fields, levels, *inputs, state, *coefs)

    heat = (total + sub_roll(total, rows)) * (1.0 / (fields * levels))
    first = heat.astype(jnp.bfloat16).astype(F32)
    rest = heat - first
    second = rest.astype(jnp.bfloat16).astype(F32)
    third = rest - second
    spans = placed.shape[0]
    slot_row, _ = iotas((spans, lanes))
    high = lax.shift_right_logical(target[...], lanes.bit_length() - 1)
    result = jnp.zeros((3 * spans, lanes), F32)
    for r in range(rows):
        hit = slot_row == high[r : r + 1]
        left = jnp.concatenate(
            [
                jnp.where(hit, part[r : r + 1], 0.0).astype(jnp.bfloat16)
                for part in (first, second, third)
            ],
            axis=0,
        )
        result = result + lax.dot_general(
            left,
            onehot[r * lanes : (r + 1) * lanes, :],
            (((1,), (1,)), ((), ())),
            preferred_element_type=F32,
        )
    placed[...] = result[:spans] + result[spans : 2 * spans] + result[2 * spans :]


def finish_kernel(parts, state, total_out, state_out, total, semaphores):
    copy_state = pltpu.make_async_copy(state, state_out, semaphores.at[0])
    copy_state.start()
    value = parts[0]
    for i in range(1, parts.shape[0]):
        value = value + parts[i]
    total[...] = value
    copy_total = pltpu.make_async_copy(total, total_out, semaphores.at[1])
    copy_total.start()
    copy_state.wait()
    copy_total.wait()


def body(tracers, courant_x, courant_y, physics_ref, class_coeffs, span_target, cloud_class):
    fields, levels, rows, cols = tracers.shape
    wide = lax.axis_size("wide")
    narrow = lax.axis_size("narrow")
    pairs = levels // 2
    half = pairs // 2
    tile = (2 * rows, cols)
    field_pairs = (fields + 1) // 2
    flat = tracers.reshape(fields * pairs, *tile)
    cx = courant_x.reshape(pairs, *tile)
    cy = courant_y.reshape(pairs, *tile)
    quads = pairs // rows
    slots = -(-(fields + 2) // 8) * 8

    def array(*shape, dtype=F32):
        return jax.ShapeDtypeStruct(shape, dtype)

    flat, cx, cy, north, south = pl.pallas_call(
        functools.partial(pack_rows_kernel, levels),
        out_shape=(
            array(fields * pairs, *tile),
            array(pairs, *tile),
            array(pairs, *tile),
            array(fields * half + half + quads, *tile),
            array(fields * half + 2 * quads, *tile),
        ),
        in_specs=[HBM] * 3,
        out_specs=[VMEM] * 5,
        scratch_shapes=[pltpu.SemaphoreType.DMA((3,))],
        compiler_params=PARAMS,
    )(*(pltpu.with_memory_space_constraint(x, pltpu.HBM) for x in (flat, cx, cy)))
    edge, north_corner, south_corner = pl.pallas_call(
        functools.partial(pack_edges_kernel, levels),
        out_shape=(array(fields + 2, *tile), array(slots, cols), array(slots, cols)),
        in_specs=[VMEM] * 3,
        out_specs=[VMEM] * 3,
        compiler_params=PARAMS,
    )(flat, cx, cy)

    def send(value, up, right):
        pairs_ = []
        for w in range(wide):
            for n in range(narrow):
                to = ((w + up) % wide) * narrow + (n + right) % narrow
                pairs_.append((w * narrow + n, to))
        return lax.ppermute(value, ("wide", "narrow"), pairs_)

    def to_both_sides(value, up):
        from_west = send(value, up, 1)
        from_east = from_west if narrow == 2 else send(value, up, -1)
        return from_west, from_east

    from_south = send(north, 1, 0)
    from_north = send(south, -1, 0)
    edge_west, edge_east = to_both_sides(edge, 0)
    corner_sw, corner_se = to_both_sides(north_corner, 1)
    corner_nw, corner_ne = to_both_sides(south_corner, -1)

    decay, source, onehot = pl.pallas_call(
        prep_kernel,
        out_shape=(array(levels, field_pairs, *tile),) * 2
        + (array(rows * cols, cols, dtype=jnp.bfloat16),),
        in_specs=[SMEM, SMEM, VMEM, VMEM],
        out_specs=[VMEM] * 3,
        cost_estimate=pl.CostEstimate(flops=4000000, bytes_accessed=2000000, transcendentals=0),
        compiler_params=PARAMS,
    )(class_coeffs, physics_ref, cloud_class, span_target)

    edges = pl.pallas_call(
        functools.partial(edge_kernel, levels),
        out_shape=(array(fields, *tile), array(fields, *tile), array(*tile)),
        in_specs=[VMEM] * 7,
        out_specs=[VMEM] * 3,
        compiler_params=PARAMS,
    )(edge, edge_west, edge_east, corner_sw, corner_se, corner_nw, corner_ne)
    state, placed = pl.pallas_call(
        functools.partial(main_kernel, fields, levels),
        out_shape=(array(fields * pairs, *tile), array(wide * rows, cols)),
        in_specs=[VMEM] * 12,
        out_specs=[VMEM] * 2,
        scratch_shapes=[
            pltpu.VMEM((levels, 5) + tile, F32),
            pltpu.VMEM((pairs, 5) + tile, F32),
        ],
        compiler_params=PARAMS,
    )(
        flat,
        cx,
        cy,
        from_south,
        from_north,
        *edges,
        decay,
        source,
        span_target,
        onehot,
    )
    received = lax.all_to_all(
        placed.reshape(wide, rows, cols), "wide", split_axis=0, concat_axis=0, tiled=True
    )
    span_diag, state = pl.pallas_call(
        finish_kernel,
        out_shape=(array(rows, cols), array(fields * pairs, *tile)),
        in_specs=[VMEM] * 2,
        out_specs=[HBM] * 2,
        scratch_shapes=[pltpu.VMEM((rows, cols), F32), pltpu.SemaphoreType.DMA((2,))],
        compiler_params=PARAMS,
    )(received, state)
    return state.reshape(fields, levels, rows, cols), span_diag


def solution(mesh):
    return jax.shard_map(
        body,
        mesh=mesh,
        in_specs=(
            P(None, None, "wide", "narrow"),
            P(None, "wide", "narrow"),
            P(None, "wide", "narrow"),
            P(),
            P(),
            P("wide", "narrow"),
            P("wide", "narrow"),
        ),
        out_specs=(P(None, None, "wide", "narrow"), P("wide", "narrow")),
        check_vma=False,
    )
```

```python
import functools
import math

import jax
import jax.numpy as jnp
from jax import lax
from jax.experimental import pallas as pl
from jax.experimental.pallas import tpu as pltpu
from jax.sharding import PartitionSpec as P

VMEM = pl.BlockSpec(memory_space=pltpu.VMEM)
HBM = pl.BlockSpec(memory_space=pltpu.HBM)
SMEM = pl.BlockSpec(memory_space=pltpu.SMEM)
F32 = jnp.float32
PARAMS = pltpu.CompilerParams(vmem_limit_bytes=12 * 1024 * 1024)


def sub_roll(value, shift):
    shift = shift % value.shape[0]
    return value if shift == 0 else pltpu.roll(value, shift, 0)


def lane_roll(value, shift):
    shift = shift % value.shape[1]
    return value if shift == 0 else pltpu.roll(value, shift, 1)


def iotas(shape):
    return lax.broadcasted_iota(jnp.int32, shape, 0), lax.broadcasted_iota(jnp.int32, shape, 1)


def pack_rows_kernel(
    levels, split, tracers_in, cx_in, cy_in, tracers, cx, cy, north, south, semaphores
):
    copies = [
        pltpu.make_async_copy(source, into, semaphores.at[i])
        for i, (source, into) in enumerate(((tracers_in, tracers), (cx_in, cx), (cy_in, cy)))
    ]
    for copy in copies:
        copy.start()
    for copy in copies:
        copy.wait()
    pairs = levels // 2
    half = pairs // 2
    tile = tracers.shape[1:]
    rows = tile[0] // 2
    local = iotas(tile)[0] % rows
    upper = local >= rows // 2

    def one_row(vectors, row, step):
        packed = []
        for start in range(0, pairs, rows):
            total = vectors[start]
            for t in range(1, rows):
                total = jnp.where(
                    local == row + step * t, sub_roll(vectors[start + t], step * t), total
                )
            packed.append(total)
        return packed

    fields = tracers.shape[0] // pairs
    for f in range(fields):
        for k in range(half):
            one, two = tracers[f * pairs + 2 * k], tracers[f * pairs + 2 * k + 1]
            north[f * half + k] = jnp.where(upper, one, sub_roll(two, 2))
            if f < split:
                south[f * half + k] = jnp.where(upper, sub_roll(two, -2), one)
    vectors_x = [cx[k] for k in range(pairs)]
    vectors_y = [cy[k] for k in range(pairs)]
    base = fields * half
    for k in range(half):
        north[base + k] = jnp.where(upper, vectors_y[2 * k], sub_roll(vectors_y[2 * k + 1], 2))
    for k, value in enumerate(one_row(vectors_x, rows - 1, -1)):
        north[base + half + k] = value
    base = split * half
    south_rows = one_row(vectors_x, 0, 1) + one_row(vectors_y, 0, 1)
    for k, value in enumerate(south_rows):
        south[base + k] = value


def pack_edges_kernel(levels, tracers, cx, cy, edge, north_corner, south_corner):
    pairs = levels // 2
    fields = tracers.shape[0] // pairs
    tile = tracers.shape[1:]
    rows = tile[0] // 2
    lanes = tile[1]
    group = lanes // levels
    lane = iotas(tile)[1]

    def pack_edge(vectors, slot):
        total = lane_roll(vectors[0], 2)
        for k in range(1, pairs):
            total = jnp.where(
                lane // (2 * group) == k, lane_roll(vectors[k], 2 + 2 * group * k), total
            )
        total = jnp.where(
            lane % (2 * group) < group, total, sub_roll(lane_roll(total, group), rows)
        )
        total = jnp.where(lane % group < group // 2, total, lane_roll(total, group // 2))
        edge[slot] = total
        north_corner[pl.ds(slot, 1), :] = total[rows - 1 : rows]
        south_corner[pl.ds(slot, 1), :] = total[0:1]

    for f in range(fields):
        pack_edge([tracers[f * pairs + k] for k in range(pairs)], f)
    pack_edge([cx[k] for k in range(pairs)], fields)
    pack_edge([cy[k] for k in range(pairs)], fields + 1)


def pack_late_kernel(levels, split, tracers, edge, edge_west, edge_east, wide_edge, south):
    pairs = levels // 2
    half = pairs // 2
    tile = tracers.shape[1:]
    rows = tile[0] // 2
    fields = tracers.shape[0] // pairs
    group = tile[1] // levels
    sub, lane = iotas(tile)
    upper = sub % rows >= rows // 2
    place = lane % group
    from_east = (place == 2) | (place == 3)
    from_west = (place == 4) | (place == 5)
    for f in range(split, fields):
        for k in range(half):
            one, two = tracers[f * pairs + 2 * k], tracers[f * pairs + 2 * k + 1]
            south[(f - split) * half + k] = jnp.where(upper, sub_roll(two, -2), one)
    for slot in range(edge.shape[0]):
        wide_edge[slot] = jnp.where(
            from_east, edge_east[slot], jnp.where(from_west, edge_west[slot], edge[slot])
        )


def cosine_sums(values):
    count = len(values)
    if count == 1:
        return values
    half = count // 2
    plus = [values[n] + values[count - 1 - n] for n in range(half)]
    minus = [
        (values[n] - values[count - 1 - n])
        * (0.5 / math.cos(math.pi * (2 * n + 1) / (2 * count)))
        for n in range(half)
    ]
    even = cosine_sums(plus)
    odd = cosine_sums(minus)
    result = []
    for k in range(half):
        result.append(even[k])
        result.append(odd[k] + odd[k + 1] if k + 1 < half else odd[k])
    return result


def cosine_series(values):
    count = len(values)
    if count == 1:
        return values
    half = count // 2
    odd_in = [values[2 * k + 1] + values[2 * k - 1] if k else values[1] for k in range(half)]
    even = cosine_series(values[0::2])
    odd = cosine_series(odd_in)
    odd = [
        odd[n] * (0.5 / math.cos(math.pi * (2 * n + 1) / (2 * count))) for n in range(half)
    ]
    return [even[n] + odd[n] for n in range(half)] + [
        even[n] - odd[n] for n in range(half - 1, -1, -1)
    ]


def prep_kernel(coeffs, profile, klass, target, decay, source, onehot):
    levels, pairs = decay.shape[:2]
    fields = profile.shape[0]
    tile = decay.shape[2:]
    rows, lanes = klass.shape
    sub, lane = iotas(tile)
    low = sub < rows
    kind = jnp.concatenate([klass[...], klass[...]], axis=0)
    is_two = kind == 2
    is_one = kind == 1

    def by_class(which, f):
        return jnp.where(
            is_two,
            coeffs[which, 2, f] * 0.25,
            jnp.where(is_one, coeffs[which, 1, f] * 0.5, coeffs[which, 0, f]),
        )

    for p in range(pairs):
        f1 = 2 * p
        f2 = min(2 * p + 1, fields - 1)
        diffusion = jnp.where(low, by_class(0, f1), by_class(0, f2))
        relax = jnp.where(low, by_class(1, f1), by_class(1, f2))
        waves = cosine_sums([jnp.where(low, profile[f1, l], profile[f2, l]) for l in range(levels)])
        for m in range(levels):
            rate = relax + diffusion * (2.0 - 2.0 * math.cos(math.pi * m / levels))
            once = 1.0 / (1.0 + rate)
            square = once * once
            twice = once + square
            steps = jnp.where(is_two, twice + twice * square, jnp.where(is_one, twice, once))
            steps = steps * ((1.0 if m == 0 else 2.0) / levels)
            decay[m, p] = steps * rate
            source[m, p] = steps * relax * waves[m]
    low_part = target[...] & (lanes - 1)
    slot, _ = iotas((lanes, lanes))
    for r in range(rows):
        hit = slot == low_part[r : r + 1]
        onehot[r * lanes : (r + 1) * lanes, :] = jnp.where(hit, 1.0, 0.0).astype(jnp.bfloat16)


def combine(coefs, center, east, west, north, south):
    return (
        coefs[0] * center
        + (coefs[1] * east + coefs[2] * west)
        + (coefs[3] * north + coefs[4] * south)
    )


def coefficients(here_x, west_x, here_y, south_y):
    return (
        1.0
        - jnp.maximum(here_x, 0.0)
        + jnp.minimum(west_x, 0.0)
        - jnp.maximum(here_y, 0.0)
        + jnp.minimum(south_y, 0.0),
        jnp.maximum(-here_x, 0.0),
        jnp.maximum(west_x, 0.0),
        jnp.maximum(-here_y, 0.0),
        jnp.maximum(south_y, 0.0),
    )


def edge_kernel(
    levels,
    wide_edge,
    corner_sw,
    corner_se,
    corner_nw,
    corner_ne,
    edge_raw,
    edge_next,
    edge_courant,
):
    fields = edge_raw.shape[0]
    tile = wide_edge.shape[1:]
    rows = tile[0] // 2
    group = tile[1] // levels
    sub, lane = iotas(tile)
    low = sub < rows
    place = lane % group
    east_side = place < group // 2

    def extended_edge(slot):
        south = jnp.where(east_side, corner_se[pl.ds(slot, 1), :], corner_sw[pl.ds(slot, 1), :])
        north = jnp.where(east_side, corner_ne[pl.ds(slot, 1), :], corner_nw[pl.ds(slot, 1), :])
        value = jnp.where(sub == 2 * rows - 1, south, wide_edge[slot])
        return jnp.where(sub == rows, north, value)

    def side_by_side(value):
        return jnp.where(place == 3, lane_roll(value, -2), value)

    edge_x = extended_edge(fields)
    edge_y = extended_edge(fields + 1)
    edge_coefs = coefficients(edge_x, lane_roll(edge_x, 1), edge_y, sub_roll(edge_y, 1))
    for f in range(fields):
        raw = extended_edge(f)
        edge_raw[f] = side_by_side(raw)
        moved = side_by_side(
            combine(
                edge_coefs,
                raw,
                lane_roll(raw, -1),
                lane_roll(raw, 1),
                sub_roll(raw, -1),
                sub_roll(raw, 1),
            )
        )
        edge_next[f] = jnp.where(low, moved, sub_roll(lane_roll(moved, -group), rows))
    edge_courant[...] = side_by_side(edge_x)


def set_coefficients(
    fields, levels, split, cx, cy, from_south, from_north, edge_courant, full_coefs, half_coefs
):
    pairs = levels // 2
    half = pairs // 2
    tile = cx.shape[1:]
    rows = tile[0] // 2
    lanes = tile[1]
    group = lanes // levels
    sub, lane = iotas(tile)
    local = sub % rows
    low = sub < rows
    lower = local < rows // 2
    first_lane = lane == 0

    sides_x = edge_courant[...]
    sides_x_odd = sub_roll(sides_x, rows)
    base_south = fields * half
    base_north = split * half
    count = pairs // rows
    for k in range(pairs):
        quad, t = k // rows, k % rows
        row_south = sub_roll(from_south[base_south + half + quad], rows + t)
        row_north = sub_roll(from_north[base_north + quad], rows - t)
        halo_x = jnp.where(local == 0, row_north, row_south)
        north_y = sub_roll(from_north[base_north + count + quad], rows - t)
        south_y = sub_roll(from_south[base_south + k // 2], rows if k % 2 == 0 else 2)
        halo_y = jnp.where(lower, north_y, south_y)
        own_x = cx[k]
        own_y = cy[k]
        both = []
        for odd in range(2):
            here_x = jnp.where(low, halo_x, own_x) if odd else jnp.where(low, own_x, halo_x)
            here_y = jnp.where(low, halo_y, own_y) if odd else jnp.where(low, own_y, halo_y)
            sides = lane_roll(sides_x_odd if odd else sides_x, -(group * (2 * k + odd) + 3))
            west_x = jnp.where(first_lane, sides, lane_roll(here_x, 1))
            coefs = coefficients(here_x, west_x, here_y, sub_roll(here_y, 1))
            for c in range(5):
                full_coefs[2 * k + odd, c] = coefs[c]
            both.append(coefs)
        for c in range(5):
            half_coefs[k, c] = jnp.where(low, both[0][c], both[1][c])


def transport_and_solve(
    fields,
    levels,
    begin,
    end,
    tracers,
    from_south,
    from_north,
    edge_raw,
    edge_next,
    full_coefs,
    half_coefs,
    decay,
    source,
    state,
):
    pairs = levels // 2
    half = pairs // 2
    tile = tracers.shape[1:]
    rows = tile[0] // 2
    lanes = tile[1]
    group = lanes // levels
    sub, lane = iotas(tile)
    local = sub % rows
    low = sub < rows
    lower = local < rows // 2
    first_lane = lane == 0
    last_lane = lane == lanes - 1
    north_part = (sub >= 1) & (sub <= rows)
    south_part = (sub < rows - 1) | (sub == 2 * rows - 1)

    def advect(f, k, first_coefs, second_coefs):
        own = tracers[f * pairs + k]
        message_south = from_south[f * half + k // 2]
        message_north = from_north[(f - begin) * half + k // 2]
        if k % 2 == 0:
            halo = sub_roll(jnp.where(lower, message_north, message_south), rows)
        else:
            halo = jnp.where(lower, sub_roll(message_north, -2), sub_roll(message_south, 2))
        raw_sides = edge_raw[f]
        results = []
        for odd in range(2):
            value = jnp.where(low, halo, own) if odd else jnp.where(low, own, halo)
            sides = sub_roll(raw_sides, rows) if odd else raw_sides
            sides = lane_roll(sides, -(group * (2 * k + odd) + 3))
            results.append(
                combine(
                    first_coefs[odd],
                    value,
                    jnp.where(last_lane, sides, lane_roll(value, -1)),
                    jnp.where(first_lane, sides, lane_roll(value, 1)),
                    sub_roll(value, -1),
                    sub_roll(value, 1),
                )
            )
        even, odd = results
        center = jnp.where(low, even, odd)
        sides = lane_roll(edge_next[f], -(2 * group * k + 3))
        return combine(
            second_coefs,
            center,
            jnp.where(last_lane, sides, lane_roll(center, -1)),
            jnp.where(first_lane, sides, lane_roll(center, 1)),
            sub_roll(jnp.where(north_part, even, odd), -1),
            sub_roll(jnp.where(south_part, even, odd), 1),
        )

    def pair_step(p, total):
        f1 = 2 * p
        f2 = jnp.minimum(f1 + 1, fields - 1)
        columns = []
        for k in range(pairs):
            first_coefs = [[full_coefs[2 * k + odd, c] for c in range(5)] for odd in range(2)]
            second_coefs = [half_coefs[k, c] for c in range(5)]
            one = advect(f1, k, first_coefs, second_coefs)
            two = advect(f2, k, first_coefs, second_coefs)
            columns.append(jnp.where(low, one, sub_roll(two, rows)))
            columns.append(jnp.where(low, sub_roll(one, rows), two))
        waves = cosine_sums(columns)
        change = cosine_series([source[m, p] - decay[m, p] * waves[m] for m in range(levels)])
        square = change[0] * change[0]
        for l in range(1, levels):
            square = square + change[l] * change[l]
        for k in range(pairs):
            even, odd = (columns[l] + change[l] for l in (2 * k, 2 * k + 1))
            state[(f1 - begin) * pairs + k] = jnp.where(low, even, sub_roll(odd, rows))
            state[(f2 - begin) * pairs + k] = jnp.where(low, sub_roll(even, rows), odd)
        return total + jnp.where(low | (f1 + 1 < fields), square, 0.0)

    return lax.fori_loop(begin // 2, (end + 1) // 2, pair_step, jnp.zeros(tile, F32))


def first_kernel(
    fields,
    levels,
    split,
    tracers,
    cx,
    cy,
    from_south,
    from_north,
    edge_raw,
    edge_next,
    edge_courant,
    decay,
    source,
    state,
    heat,
    full_coefs,
    half_coefs,
):
    set_coefficients(
        fields, levels, split, cx, cy, from_south, from_north, edge_courant, full_coefs, half_coefs
    )
    heat[...] = transport_and_solve(
        fields,
        levels,
        0,
        split,
        tracers,
        from_south,
        from_north,
        edge_raw,
        edge_next,
        full_coefs,
        half_coefs,
        decay,
        source,
        state,
    )


def second_kernel(fields, levels, split, *refs):
    inputs, (heat_first, target, onehot), (state, placed) = refs[:9], refs[9:12], refs[12:]
    rows, lanes = target.shape
    total = heat_first[...] + transport_and_solve(fields, levels, split, fields, *inputs, state)

    heat = (total + sub_roll(total, rows)) * (1.0 / (fields * levels))
    first = heat.astype(jnp.bfloat16).astype(F32)
    rest = heat - first
    second = rest.astype(jnp.bfloat16).astype(F32)
    third = rest - second
    spans = placed.shape[0]
    slot_row, _ = iotas((spans, lanes))
    high = lax.shift_right_logical(target[...], lanes.bit_length() - 1)
    result = jnp.zeros((3 * spans, lanes), F32)
    for r in range(rows):
        hit = slot_row == high[r : r + 1]
        left = jnp.concatenate(
            [
                jnp.where(hit, part[r : r + 1], 0.0).astype(jnp.bfloat16)
                for part in (first, second, third)
            ],
            axis=0,
        )
        result = result + lax.dot_general(
            left,
            onehot[r * lanes : (r + 1) * lanes, :],
            (((1,), (1,)), ((), ())),
            preferred_element_type=F32,
        )
    placed[...] = result[:spans] + result[spans : 2 * spans] + result[2 * spans :]


def finish_kernel(parts, state_first, state_second, total_out, state_out, total, semaphores):
    split = state_first.shape[0]
    copies = [
        pltpu.make_async_copy(state_first, state_out.at[pl.ds(0, split)], semaphores.at[0]),
        pltpu.make_async_copy(
            state_second, state_out.at[pl.ds(split, state_second.shape[0])], semaphores.at[1]
        ),
        pltpu.make_async_copy(total, total_out, semaphores.at[2]),
    ]
    copies[0].start()
    copies[1].start()
    value = parts[0]
    for i in range(1, parts.shape[0]):
        value = value + parts[i]
    total[...] = value
    copies[2].start()
    for copy in copies:
        copy.wait()


def body(tracers, courant_x, courant_y, physics_ref, class_coeffs, span_target, cloud_class):
    fields, levels, rows, cols = tracers.shape
    wide = lax.axis_size("wide")
    narrow = lax.axis_size("narrow")
    pairs = levels // 2
    half = pairs // 2
    tile = (2 * rows, cols)
    field_pairs = (fields + 1) // 2
    flat = tracers.reshape(fields * pairs, *tile)
    cx = courant_x.reshape(pairs, *tile)
    cy = courant_y.reshape(pairs, *tile)
    quads = pairs // rows
    slots = -(-(fields + 2) // 8) * 8

    def array(*shape, dtype=F32):
        return jax.ShapeDtypeStruct(shape, dtype)

    split = 4 * ((fields + 6) // 7)
    flat, cx, cy, north, south = pl.pallas_call(
        functools.partial(pack_rows_kernel, levels, split),
        out_shape=(
            array(fields * pairs, *tile),
            array(pairs, *tile),
            array(pairs, *tile),
            array(fields * half + half + quads, *tile),
            array(split * half + 2 * quads, *tile),
        ),
        in_specs=[HBM] * 3,
        out_specs=[VMEM] * 5,
        scratch_shapes=[pltpu.SemaphoreType.DMA((3,))],
        compiler_params=PARAMS,
    )(*(pltpu.with_memory_space_constraint(x, pltpu.HBM) for x in (flat, cx, cy)))
    edge, north_corner, south_corner = pl.pallas_call(
        functools.partial(pack_edges_kernel, levels),
        out_shape=(array(fields + 2, *tile), array(slots, cols), array(slots, cols)),
        in_specs=[VMEM] * 3,
        out_specs=[VMEM] * 3,
        compiler_params=PARAMS,
    )(flat, cx, cy)

    def send(value, up, right):
        pairs_ = []
        for w in range(wide):
            for n in range(narrow):
                to = ((w + up) % wide) * narrow + (n + right) % narrow
                pairs_.append((w * narrow + n, to))
        return lax.ppermute(value, ("wide", "narrow"), pairs_)

    def to_both_sides(value, up):
        from_west = send(value, up, 1)
        from_east = from_west if narrow == 2 else send(value, up, -1)
        return from_west, from_east

    from_south = send(north, 1, 0)
    from_north = send(south, -1, 0)
    edge_west, edge_east = to_both_sides(edge, 0)
    corner_sw, corner_se = to_both_sides(north_corner, 1)
    corner_nw, corner_ne = to_both_sides(south_corner, -1)
    wide_edge, south_late = pl.pallas_call(
        functools.partial(pack_late_kernel, levels, split),
        out_shape=(array(fields + 2, *tile), array((fields - split) * half, *tile)),
        in_specs=[VMEM] * 4,
        out_specs=[VMEM] * 2,
        compiler_params=PARAMS,
    )(flat, edge, edge_west, edge_east)
    from_north_late = send(south_late, -1, 0)

    decay, source, onehot = pl.pallas_call(
        prep_kernel,
        out_shape=(array(levels, field_pairs, *tile),) * 2
        + (array(rows * cols, cols, dtype=jnp.bfloat16),),
        in_specs=[SMEM, SMEM, VMEM, VMEM],
        out_specs=[VMEM] * 3,
        cost_estimate=pl.CostEstimate(flops=4000000, bytes_accessed=2000000, transcendentals=0),
        compiler_params=PARAMS,
    )(class_coeffs, physics_ref, cloud_class, span_target)

    edge_raw, edge_next, edge_courant = pl.pallas_call(
        functools.partial(edge_kernel, levels),
        out_shape=(array(fields, *tile), array(fields, *tile), array(*tile)),
        in_specs=[VMEM] * 5,
        out_specs=[VMEM] * 3,
        compiler_params=PARAMS,
    )(wide_edge, corner_sw, corner_se, corner_nw, corner_ne)
    state_first, heat_first, full_coefs, half_coefs = pl.pallas_call(
        functools.partial(first_kernel, fields, levels, split),
        out_shape=(
            array(split * pairs, *tile),
            array(*tile),
            array(levels, 5, *tile),
            array(pairs, 5, *tile),
        ),
        in_specs=[VMEM] * 10,
        out_specs=[VMEM] * 4,
        cost_estimate=pl.CostEstimate(flops=1000000000, bytes_accessed=2000000, transcendentals=0),
        compiler_params=PARAMS,
    )(flat, cx, cy, from_south, from_north, edge_raw, edge_next, edge_courant, decay, source)
    state_second, placed = pl.pallas_call(
        functools.partial(second_kernel, fields, levels, split),
        out_shape=(array((fields - split) * pairs, *tile), array(wide * rows, cols)),
        in_specs=[VMEM] * 12,
        out_specs=[VMEM] * 2,
        compiler_params=PARAMS,
    )(
        flat,
        from_south,
        from_north_late,
        edge_raw,
        edge_next,
        full_coefs,
        half_coefs,
        decay,
        source,
        heat_first,
        span_target,
        onehot,
    )
    received = lax.all_to_all(
        placed.reshape(wide, rows, cols), "wide", split_axis=0, concat_axis=0, tiled=True
    )
    span_diag, state = pl.pallas_call(
        finish_kernel,
        out_shape=(array(rows, cols), array(fields * pairs, *tile)),
        in_specs=[VMEM] * 3,
        out_specs=[HBM] * 2,
        scratch_shapes=[pltpu.VMEM((rows, cols), F32), pltpu.SemaphoreType.DMA((3,))],
        compiler_params=PARAMS,
    )(received, state_first, state_second)
    return state.reshape(fields, levels, rows, cols), span_diag


def solution(mesh):
    return jax.shard_map(
        body,
        mesh=mesh,
        in_specs=(
            P(None, None, "wide", "narrow"),
            P(None, "wide", "narrow"),
            P(None, "wide", "narrow"),
            P(),
            P(),
            P("wide", "narrow"),
            P("wide", "narrow"),
        ),
        out_specs=(P(None, None, "wide", "narrow"), P("wide", "narrow")),
        check_vma=False,
    )
```

```python
import functools
import math

import jax
import jax.numpy as jnp
from jax import lax
from jax.experimental import pallas as pl
from jax.experimental.pallas import tpu as pltpu
from jax.sharding import PartitionSpec as P

VMEM = pl.BlockSpec(memory_space=pltpu.VMEM)
HBM = pl.BlockSpec(memory_space=pltpu.HBM)
SMEM = pl.BlockSpec(memory_space=pltpu.SMEM)
F32 = jnp.float32
PARAMS = pltpu.CompilerParams(vmem_limit_bytes=12 * 1024 * 1024)


def sub_roll(value, shift):
    shift = shift % value.shape[0]
    return value if shift == 0 else pltpu.roll(value, shift, 0)


def lane_roll(value, shift):
    shift = shift % value.shape[1]
    return value if shift == 0 else pltpu.roll(value, shift, 1)


def iotas(shape):
    return lax.broadcasted_iota(jnp.int32, shape, 0), lax.broadcasted_iota(jnp.int32, shape, 1)


def one_row(vectors, row, step):
    rows = vectors[0].shape[0] // 2
    local = iotas(vectors[0].shape)[0] % rows
    packed = []
    for start in range(0, len(vectors), rows):
        total = vectors[start]
        for t in range(1, rows):
            total = jnp.where(
                local == row + step * t, sub_roll(vectors[start + t], step * t), total
            )
        packed.append(total)
    return packed


def pack_north_kernel(levels, tracers_in, cx_in, cy_in, tracers, cx, cy, north, semaphores):
    copies = [
        pltpu.make_async_copy(source, into, semaphores.at[i])
        for i, (source, into) in enumerate(((tracers_in, tracers), (cx_in, cx), (cy_in, cy)))
    ]
    for copy in copies:
        copy.start()
    for copy in copies:
        copy.wait()
    pairs = levels // 2
    half = pairs // 2
    tile = tracers.shape[1:]
    rows = tile[0] // 2
    upper = iotas(tile)[0] % rows >= rows // 2
    fields = tracers.shape[0] // pairs
    for f in range(fields):
        for k in range(half):
            one, two = tracers[f * pairs + 2 * k], tracers[f * pairs + 2 * k + 1]
            north[f * half + k] = jnp.where(upper, one, sub_roll(two, 2))
    base = fields * half
    for k in range(half):
        north[base + k] = jnp.where(upper, cy[2 * k], sub_roll(cy[2 * k + 1], 2))
    for k, value in enumerate(one_row([cx[k] for k in range(pairs)], rows - 1, -1)):
        north[base + half + k] = value


def pack_edges_kernel(levels, tracers, cx, cy, edge, north_corner, south_corner):
    pairs = levels // 2
    fields = tracers.shape[0] // pairs
    tile = tracers.shape[1:]
    rows = tile[0] // 2
    lanes = tile[1]
    group = lanes // levels
    lane = iotas(tile)[1]

    def pack_edge(vectors, slot):
        total = lane_roll(vectors[0], 2)
        for k in range(1, pairs):
            total = jnp.where(
                lane // (2 * group) == k, lane_roll(vectors[k], 2 + 2 * group * k), total
            )
        total = jnp.where(
            lane % (2 * group) < group, total, sub_roll(lane_roll(total, group), rows)
        )
        total = jnp.where(lane % group < group // 2, total, lane_roll(total, group // 2))
        edge[slot] = total
        north_corner[pl.ds(slot, 1), :] = total[rows - 1 : rows]
        south_corner[pl.ds(slot, 1), :] = total[0:1]

    for f in range(fields):
        pack_edge([tracers[f * pairs + k] for k in range(pairs)], f)
    pack_edge([cx[k] for k in range(pairs)], fields)
    pack_edge([cy[k] for k in range(pairs)], fields + 1)


def pack_south_kernel(
    levels, split, tracers, cx, cy, edge, edge_west, edge_east, wide_edge, first
):
    pairs = levels // 2
    half = pairs // 2
    tile = tracers.shape[1:]
    rows = tile[0] // 2
    fields = tracers.shape[0] // pairs
    group = tile[1] // levels
    sub, lane = iotas(tile)
    upper = sub % rows >= rows // 2
    place = lane % group
    from_east = (place == 2) | (place == 3)
    from_west = (place == 4) | (place == 5)
    for f in range(split):
        for k in range(half):
            one, two = tracers[f * pairs + 2 * k], tracers[f * pairs + 2 * k + 1]
            first[f * half + k] = jnp.where(upper, sub_roll(two, -2), one)
    courant = one_row([cx[k] for k in range(pairs)], 0, 1)
    courant += one_row([cy[k] for k in range(pairs)], 0, 1)
    for k, value in enumerate(courant):
        first[split * half + k] = value
    for slot in range(edge.shape[0]):
        wide_edge[slot] = jnp.where(
            from_east, edge_east[slot], jnp.where(from_west, edge_west[slot], edge[slot])
        )


def cosine_sums(values):
    count = len(values)
    if count == 1:
        return values
    half = count // 2
    plus = [values[n] + values[count - 1 - n] for n in range(half)]
    minus = [
        (values[n] - values[count - 1 - n])
        * (0.5 / math.cos(math.pi * (2 * n + 1) / (2 * count)))
        for n in range(half)
    ]
    even = cosine_sums(plus)
    odd = cosine_sums(minus)
    result = []
    for k in range(half):
        result.append(even[k])
        result.append(odd[k] + odd[k + 1] if k + 1 < half else odd[k])
    return result


def cosine_series(values):
    count = len(values)
    if count == 1:
        return values
    half = count // 2
    odd_in = [values[2 * k + 1] + values[2 * k - 1] if k else values[1] for k in range(half)]
    even = cosine_series(values[0::2])
    odd = cosine_series(odd_in)
    odd = [
        odd[n] * (0.5 / math.cos(math.pi * (2 * n + 1) / (2 * count))) for n in range(half)
    ]
    return [even[n] + odd[n] for n in range(half)] + [
        even[n] - odd[n] for n in range(half - 1, -1, -1)
    ]


def prep_kernel(coeffs, profile, klass, target, _, decay, source, onehot):
    levels, pairs = decay.shape[:2]
    fields = profile.shape[0]
    tile = decay.shape[2:]
    rows, lanes = klass.shape
    sub, lane = iotas(tile)
    low = sub < rows
    kind = jnp.concatenate([klass[...], klass[...]], axis=0)
    is_two = kind == 2
    is_one = kind == 1

    def by_class(which, f):
        return jnp.where(
            is_two,
            coeffs[which, 2, f] * 0.25,
            jnp.where(is_one, coeffs[which, 1, f] * 0.5, coeffs[which, 0, f]),
        )

    for p in range(pairs):
        f1 = 2 * p
        f2 = min(2 * p + 1, fields - 1)
        diffusion = jnp.where(low, by_class(0, f1), by_class(0, f2))
        relax = jnp.where(low, by_class(1, f1), by_class(1, f2))
        waves = cosine_sums([jnp.where(low, profile[f1, l], profile[f2, l]) for l in range(levels)])
        for m in range(levels):
            rate = relax + diffusion * (2.0 - 2.0 * math.cos(math.pi * m / levels))
            once = 1.0 / (1.0 + rate)
            square = once * once
            twice = once + square
            steps = jnp.where(is_two, twice + twice * square, jnp.where(is_one, twice, once))
            steps = steps * ((1.0 if m == 0 else 2.0) / levels)
            decay[m, p] = steps * rate
            source[m, p] = steps * relax * waves[m]
    low_part = target[...] & (lanes - 1)
    slot, _ = iotas((lanes, lanes))
    for r in range(rows):
        hit = slot == low_part[r : r + 1]
        onehot[r * lanes : (r + 1) * lanes, :] = jnp.where(hit, 1.0, 0.0).astype(jnp.bfloat16)


def combine(coefs, center, east, west, north, south):
    return (
        coefs[0] * center
        + (coefs[1] * east + coefs[2] * west)
        + (coefs[3] * north + coefs[4] * south)
    )


def coefficients(here_x, west_x, here_y, south_y):
    return (
        1.0
        - jnp.maximum(here_x, 0.0)
        + jnp.minimum(west_x, 0.0)
        - jnp.maximum(here_y, 0.0)
        + jnp.minimum(south_y, 0.0),
        jnp.maximum(-here_x, 0.0),
        jnp.maximum(west_x, 0.0),
        jnp.maximum(-here_y, 0.0),
        jnp.maximum(south_y, 0.0),
    )


def edge_kernel(
    levels,
    split,
    tracers,
    wide_edge,
    corner_sw,
    corner_se,
    corner_nw,
    corner_ne,
    edge_raw,
    edge_next,
    edge_courant,
    second,
):
    fields = edge_raw.shape[0]
    tile = wide_edge.shape[1:]
    pairs = levels // 2
    half = pairs // 2
    rows = tile[0] // 2
    group = tile[1] // levels
    sub, lane = iotas(tile)
    low = sub < rows
    place = lane % group
    east_side = place < group // 2
    upper = sub % rows >= rows // 2

    for f in range(split, fields):
        for k in range(half):
            one, two = tracers[f * pairs + 2 * k], tracers[f * pairs + 2 * k + 1]
            second[(f - split) * half + k] = jnp.where(upper, sub_roll(two, -2), one)

    def extended_edge(slot):
        south = jnp.where(east_side, corner_se[pl.ds(slot, 1), :], corner_sw[pl.ds(slot, 1), :])
        north = jnp.where(east_side, corner_ne[pl.ds(slot, 1), :], corner_nw[pl.ds(slot, 1), :])
        value = jnp.where(sub == 2 * rows - 1, south, wide_edge[slot])
        return jnp.where(sub == rows, north, value)

    def side_by_side(value):
        return jnp.where(place == 3, lane_roll(value, -2), value)

    edge_x = extended_edge(fields)
    edge_y = extended_edge(fields + 1)
    edge_coefs = coefficients(edge_x, lane_roll(edge_x, 1), edge_y, sub_roll(edge_y, 1))
    for f in range(fields):
        raw = extended_edge(f)
        edge_raw[f] = side_by_side(raw)
        moved = side_by_side(
            combine(
                edge_coefs,
                raw,
                lane_roll(raw, -1),
                lane_roll(raw, 1),
                sub_roll(raw, -1),
                sub_roll(raw, 1),
            )
        )
        edge_next[f] = jnp.where(low, moved, sub_roll(lane_roll(moved, -group), rows))
    edge_courant[...] = side_by_side(edge_x)


def set_coefficients(
    fields, levels, split, cx, cy, from_south, from_north, edge_courant, full_coefs, half_coefs
):
    pairs = levels // 2
    half = pairs // 2
    tile = cx.shape[1:]
    rows = tile[0] // 2
    lanes = tile[1]
    group = lanes // levels
    sub, lane = iotas(tile)
    local = sub % rows
    low = sub < rows
    lower = local < rows // 2
    first_lane = lane == 0

    sides_x = edge_courant[...]
    sides_x_odd = sub_roll(sides_x, rows)
    base_south = fields * half
    base_north = split * half
    count = pairs // rows
    for k in range(pairs):
        quad, t = k // rows, k % rows
        row_south = sub_roll(from_south[base_south + half + quad], rows + t)
        row_north = sub_roll(from_north[base_north + quad], rows - t)
        halo_x = jnp.where(local == 0, row_north, row_south)
        north_y = sub_roll(from_north[base_north + count + quad], rows - t)
        south_y = sub_roll(from_south[base_south + k // 2], rows if k % 2 == 0 else 2)
        halo_y = jnp.where(lower, north_y, south_y)
        own_x = cx[k]
        own_y = cy[k]
        both = []
        for odd in range(2):
            here_x = jnp.where(low, halo_x, own_x) if odd else jnp.where(low, own_x, halo_x)
            here_y = jnp.where(low, halo_y, own_y) if odd else jnp.where(low, own_y, halo_y)
            sides = lane_roll(sides_x_odd if odd else sides_x, -(group * (2 * k + odd) + 3))
            west_x = jnp.where(first_lane, sides, lane_roll(here_x, 1))
            coefs = coefficients(here_x, west_x, here_y, sub_roll(here_y, 1))
            for c in range(5):
                full_coefs[2 * k + odd, c] = coefs[c]
            both.append(coefs)
        for c in range(5):
            half_coefs[k, c] = jnp.where(low, both[0][c], both[1][c])


def transport_and_solve(
    fields,
    levels,
    begin,
    end,
    tracers,
    from_south,
    from_north,
    edge_raw,
    edge_next,
    full_coefs,
    half_coefs,
    decay,
    source,
    state,
):
    pairs = levels // 2
    half = pairs // 2
    tile = tracers.shape[1:]
    rows = tile[0] // 2
    lanes = tile[1]
    group = lanes // levels
    sub, lane = iotas(tile)
    local = sub % rows
    low = sub < rows
    lower = local < rows // 2
    first_lane = lane == 0
    last_lane = lane == lanes - 1
    north_part = (sub >= 1) & (sub <= rows)
    south_part = (sub < rows - 1) | (sub == 2 * rows - 1)

    def advect(f, k, first_coefs, second_coefs):
        own = tracers[f * pairs + k]
        message_south = from_south[f * half + k // 2]
        message_north = from_north[(f - begin) * half + k // 2]
        if k % 2 == 0:
            halo = sub_roll(jnp.where(lower, message_north, message_south), rows)
        else:
            halo = jnp.where(lower, sub_roll(message_north, -2), sub_roll(message_south, 2))
        raw_sides = edge_raw[f]
        results = []
        for odd in range(2):
            value = jnp.where(low, halo, own) if odd else jnp.where(low, own, halo)
            sides = sub_roll(raw_sides, rows) if odd else raw_sides
            sides = lane_roll(sides, -(group * (2 * k + odd) + 3))
            results.append(
                combine(
                    first_coefs[odd],
                    value,
                    jnp.where(last_lane, sides, lane_roll(value, -1)),
                    jnp.where(first_lane, sides, lane_roll(value, 1)),
                    sub_roll(value, -1),
                    sub_roll(value, 1),
                )
            )
        even, odd = results
        center = jnp.where(low, even, odd)
        sides = lane_roll(edge_next[f], -(2 * group * k + 3))
        return combine(
            second_coefs,
            center,
            jnp.where(last_lane, sides, lane_roll(center, -1)),
            jnp.where(first_lane, sides, lane_roll(center, 1)),
            sub_roll(jnp.where(north_part, even, odd), -1),
            sub_roll(jnp.where(south_part, even, odd), 1),
        )

    def pair_step(p, total):
        f1 = 2 * p
        f2 = jnp.minimum(f1 + 1, fields - 1)
        columns = []
        for k in range(pairs):
            first_coefs = [[full_coefs[2 * k + odd, c] for c in range(5)] for odd in range(2)]
            second_coefs = [half_coefs[k, c] for c in range(5)]
            one = advect(f1, k, first_coefs, second_coefs)
            two = advect(f2, k, first_coefs, second_coefs)
            columns.append(jnp.where(low, one, sub_roll(two, rows)))
            columns.append(jnp.where(low, sub_roll(one, rows), two))
        waves = cosine_sums(columns)
        change = cosine_series([source[m, p] - decay[m, p] * waves[m] for m in range(levels)])
        square = change[0] * change[0]
        for l in range(1, levels):
            square = square + change[l] * change[l]
        for k in range(pairs):
            even, odd = (columns[l] + change[l] for l in (2 * k, 2 * k + 1))
            state[(f1 - begin) * pairs + k] = jnp.where(low, even, sub_roll(odd, rows))
            state[(f2 - begin) * pairs + k] = jnp.where(low, sub_roll(even, rows), odd)
        return total + jnp.where(low | (f1 + 1 < fields), square, 0.0)

    return lax.fori_loop(begin // 2, (end + 1) // 2, pair_step, jnp.zeros(tile, F32))


def first_kernel(
    fields,
    levels,
    split,
    tracers,
    cx,
    cy,
    from_south,
    from_north,
    edge_raw,
    edge_next,
    edge_courant,
    decay,
    source,
    state,
    heat,
    full_coefs,
    half_coefs,
):
    set_coefficients(
        fields, levels, split, cx, cy, from_south, from_north, edge_courant, full_coefs, half_coefs
    )
    heat[...] = transport_and_solve(
        fields,
        levels,
        0,
        split,
        tracers,
        from_south,
        from_north,
        edge_raw,
        edge_next,
        full_coefs,
        half_coefs,
        decay,
        source,
        state,
    )


def second_kernel(fields, levels, split, *refs):
    inputs, (heat_first, target, onehot), (state, placed) = refs[:9], refs[9:12], refs[12:]
    rows, lanes = target.shape
    total = heat_first[...] + transport_and_solve(fields, levels, split, fields, *inputs, state)

    heat = (total + sub_roll(total, rows)) * (1.0 / (fields * levels))
    first = heat.astype(jnp.bfloat16).astype(F32)
    rest = heat - first
    second = rest.astype(jnp.bfloat16).astype(F32)
    third = rest - second
    spans = placed.shape[0]
    slot_row, _ = iotas((spans, lanes))
    high = lax.shift_right_logical(target[...], lanes.bit_length() - 1)
    result = jnp.zeros((3 * spans, lanes), F32)
    for r in range(rows):
        hit = slot_row == high[r : r + 1]
        left = jnp.concatenate(
            [
                jnp.where(hit, part[r : r + 1], 0.0).astype(jnp.bfloat16)
                for part in (first, second, third)
            ],
            axis=0,
        )
        result = result + lax.dot_general(
            left,
            onehot[r * lanes : (r + 1) * lanes, :],
            (((1,), (1,)), ((), ())),
            preferred_element_type=F32,
        )
    placed[...] = result[:spans] + result[spans : 2 * spans] + result[2 * spans :]


def finish_kernel(parts, state_first, state_second, total_out, state_out, total, semaphores):
    split = state_first.shape[0]
    copies = [
        pltpu.make_async_copy(state_first, state_out.at[pl.ds(0, split)], semaphores.at[0]),
        pltpu.make_async_copy(
            state_second, state_out.at[pl.ds(split, state_second.shape[0])], semaphores.at[1]
        ),
        pltpu.make_async_copy(total, total_out, semaphores.at[2]),
    ]
    copies[0].start()
    copies[1].start()
    value = parts[0]
    for i in range(1, parts.shape[0]):
        value = value + parts[i]
    total[...] = value
    copies[2].start()
    for copy in copies:
        copy.wait()


def body(tracers, courant_x, courant_y, physics_ref, class_coeffs, span_target, cloud_class):
    fields, levels, rows, cols = tracers.shape
    wide = lax.axis_size("wide")
    narrow = lax.axis_size("narrow")
    pairs = levels // 2
    half = pairs // 2
    tile = (2 * rows, cols)
    field_pairs = (fields + 1) // 2
    flat = tracers.reshape(fields * pairs, *tile)
    cx = courant_x.reshape(pairs, *tile)
    cy = courant_y.reshape(pairs, *tile)
    quads = pairs // rows
    slots = -(-(fields + 2) // 8) * 8

    def array(*shape, dtype=F32):
        return jax.ShapeDtypeStruct(shape, dtype)

    split = 4 * ((fields + 6) // 7)
    flat, cx, cy, north = pl.pallas_call(
        functools.partial(pack_north_kernel, levels),
        out_shape=(
            array(fields * pairs, *tile),
            array(pairs, *tile),
            array(pairs, *tile),
            array(fields * half + half + quads, *tile),
        ),
        in_specs=[HBM] * 3,
        out_specs=[VMEM] * 4,
        scratch_shapes=[pltpu.SemaphoreType.DMA((3,))],
        compiler_params=PARAMS,
    )(*(pltpu.with_memory_space_constraint(x, pltpu.HBM) for x in (flat, cx, cy)))
    edge, north_corner, south_corner = pl.pallas_call(
        functools.partial(pack_edges_kernel, levels),
        out_shape=(array(fields + 2, *tile), array(slots, cols), array(slots, cols)),
        in_specs=[VMEM] * 3,
        out_specs=[VMEM] * 3,
        compiler_params=PARAMS,
    )(flat, cx, cy)

    def send(value, up, right):
        pairs_ = []
        for w in range(wide):
            for n in range(narrow):
                to = ((w + up) % wide) * narrow + (n + right) % narrow
                pairs_.append((w * narrow + n, to))
        return lax.ppermute(value, ("wide", "narrow"), pairs_)

    def to_both_sides(value, up):
        from_west = send(value, up, 1)
        from_east = from_west if narrow == 2 else send(value, up, -1)
        return from_west, from_east

    from_south = send(north, 1, 0)
    edge_west, edge_east = to_both_sides(edge, 0)
    corner_sw, corner_se = to_both_sides(north_corner, 1)
    corner_nw, corner_ne = to_both_sides(south_corner, -1)
    wide_edge, south_first = pl.pallas_call(
        functools.partial(pack_south_kernel, levels, split),
        out_shape=(
            array(fields + 2, *tile),
            array(split * half + 2 * quads, *tile),
        ),
        in_specs=[VMEM] * 6,
        out_specs=[VMEM] * 2,
        compiler_params=PARAMS,
    )(flat, cx, cy, edge, edge_west, edge_east)
    from_north = send(south_first, -1, 0)
    edge_raw, edge_next, edge_courant, south_second = pl.pallas_call(
        functools.partial(edge_kernel, levels, split),
        out_shape=(
            array(fields, *tile),
            array(fields, *tile),
            array(*tile),
            array((fields - split) * half, *tile),
        ),
        in_specs=[VMEM] * 6,
        out_specs=[VMEM] * 4,
        cost_estimate=pl.CostEstimate(flops=1500000000, bytes_accessed=1000000, transcendentals=0),
        compiler_params=PARAMS,
    )(flat, wide_edge, corner_sw, corner_se, corner_nw, corner_ne)
    from_north_late = send(south_second, -1, 0)

    decay, source, onehot = pl.pallas_call(
        prep_kernel,
        out_shape=(array(levels, field_pairs, *tile),) * 2
        + (array(rows * cols, cols, dtype=jnp.bfloat16),),
        in_specs=[SMEM, SMEM, VMEM, VMEM, VMEM],
        out_specs=[VMEM] * 3,
        cost_estimate=pl.CostEstimate(flops=4000000, bytes_accessed=2000000, transcendentals=0),
        compiler_params=PARAMS,
    )(class_coeffs, physics_ref, cloud_class, span_target, south_second)

    state_first, heat_first, full_coefs, half_coefs = pl.pallas_call(
        functools.partial(first_kernel, fields, levels, split),
        out_shape=(
            array(split * pairs, *tile),
            array(*tile),
            array(levels, 5, *tile),
            array(pairs, 5, *tile),
        ),
        in_specs=[VMEM] * 10,
        out_specs=[VMEM] * 4,
        cost_estimate=pl.CostEstimate(flops=1000000000, bytes_accessed=2000000, transcendentals=0),
        compiler_params=PARAMS,
    )(flat, cx, cy, from_south, from_north, edge_raw, edge_next, edge_courant, decay, source)
    state_second, placed = pl.pallas_call(
        functools.partial(second_kernel, fields, levels, split),
        out_shape=(array((fields - split) * pairs, *tile), array(wide * rows, cols)),
        in_specs=[VMEM] * 12,
        out_specs=[VMEM] * 2,
        compiler_params=PARAMS,
    )(
        flat,
        from_south,
        from_north_late,
        edge_raw,
        edge_next,
        full_coefs,
        half_coefs,
        decay,
        source,
        heat_first,
        span_target,
        onehot,
    )
    received = lax.all_to_all(
        placed.reshape(wide, rows, cols), "wide", split_axis=0, concat_axis=0, tiled=True
    )
    span_diag, state = pl.pallas_call(
        finish_kernel,
        out_shape=(array(rows, cols), array(fields * pairs, *tile)),
        in_specs=[VMEM] * 3,
        out_specs=[HBM] * 2,
        scratch_shapes=[pltpu.VMEM((rows, cols), F32), pltpu.SemaphoreType.DMA((3,))],
        compiler_params=PARAMS,
    )(received, state_first, state_second)
    return state.reshape(fields, levels, rows, cols), span_diag


def solution(mesh):
    return jax.shard_map(
        body,
        mesh=mesh,
        in_specs=(
            P(None, None, "wide", "narrow"),
            P(None, "wide", "narrow"),
            P(None, "wide", "narrow"),
            P(),
            P(),
            P("wide", "narrow"),
            P("wide", "narrow"),
        ),
        out_specs=(P(None, None, "wide", "narrow"), P("wide", "narrow")),
        check_vma=False,
    )
```

```python
import functools
import math

import jax
import jax.numpy as jnp
from jax import lax
from jax.experimental import pallas as pl
from jax.experimental.pallas import tpu as pltpu
from jax.sharding import PartitionSpec as P

VMEM = pl.BlockSpec(memory_space=pltpu.VMEM)
HBM = pl.BlockSpec(memory_space=pltpu.HBM)
SMEM = pl.BlockSpec(memory_space=pltpu.SMEM)
F32 = jnp.float32
PARAMS = pltpu.CompilerParams(vmem_limit_bytes=12 * 1024 * 1024)


def sub_roll(value, shift):
    shift = shift % value.shape[0]
    return value if shift == 0 else pltpu.roll(value, shift, 0)


def lane_roll(value, shift):
    shift = shift % value.shape[1]
    return value if shift == 0 else pltpu.roll(value, shift, 1)


def iotas(shape):
    return lax.broadcasted_iota(jnp.int32, shape, 0), lax.broadcasted_iota(jnp.int32, shape, 1)


def pack_rows(tracers, f, pairs, north, south, slot):
    local = iotas(tracers.shape[1:])[0] % (tracers.shape[1] // 2)
    lower = local < tracers.shape[1] // 4
    for k in range(pairs // 2):
        first, second = tracers[f * pairs + 2 * k], tracers[f * pairs + 2 * k + 1]
        north[slot + k] = jnp.where(lower, sub_roll(second, 2), first)
        south[slot + k] = jnp.where(lower, first, sub_roll(second, -2))


def pack_rows_kernel(
    levels, tracers_in, cx_in, cy_in, tracers, cx, cy, north, south, semaphores
):
    copies = [
        pltpu.make_async_copy(source, into, semaphores.at[i])
        for i, (source, into) in enumerate(((tracers_in, tracers), (cx_in, cx), (cy_in, cy)))
    ]
    for copy in copies:
        copy.start()
    for copy in copies:
        copy.wait()
    pairs = levels // 2
    half = pairs // 2
    tile = tracers.shape[1:]
    rows = tile[0] // 2
    local = iotas(tile)[0] % rows
    upper = local >= rows // 2

    def one_row(vectors, row, step):
        packed = []
        for start in range(0, pairs, rows):
            total = vectors[start]
            for t in range(1, rows):
                total = jnp.where(
                    local == row + step * t, sub_roll(vectors[start + t], step * t), total
                )
            packed.append(total)
        return packed

    fields = tracers.shape[0] // pairs
    for f in range(fields):
        pack_rows(tracers, f, pairs, north, south, f * half)
    vectors_x = [cx[k] for k in range(pairs)]
    vectors_y = [cy[k] for k in range(pairs)]
    base = fields * half
    for k in range(half):
        north[base + k] = jnp.where(upper, vectors_y[2 * k], sub_roll(vectors_y[2 * k + 1], 2))
    for k, value in enumerate(one_row(vectors_x, rows - 1, -1)):
        north[base + half + k] = value
    south_rows = one_row(vectors_x, 0, 1) + one_row(vectors_y, 0, 1)
    for k, value in enumerate(south_rows):
        south[base + k] = value


def pack_edges_kernel(levels, tracers, cx, cy, edge, north_corner, south_corner):
    pairs = levels // 2
    fields = tracers.shape[0] // pairs
    tile = tracers.shape[1:]
    rows = tile[0] // 2
    lanes = tile[1]
    group = lanes // levels
    lane = iotas(tile)[1]

    def pack_edge(vectors, slot):
        total = lane_roll(vectors[0], 2)
        for k in range(1, pairs):
            total = jnp.where(
                lane // (2 * group) == k, lane_roll(vectors[k], 2 + 2 * group * k), total
            )
        total = jnp.where(
            lane % (2 * group) < group, total, sub_roll(lane_roll(total, group), rows)
        )
        total = jnp.where(lane % group < group // 2, total, lane_roll(total, group // 2))
        edge[slot] = total
        north_corner[pl.ds(slot, 1), :] = total[rows - 1 : rows]
        south_corner[pl.ds(slot, 1), :] = total[0:1]

    for f in range(fields):
        pack_edge([tracers[f * pairs + k] for k in range(pairs)], f)
    pack_edge([cx[k] for k in range(pairs)], fields)
    pack_edge([cy[k] for k in range(pairs)], fields + 1)


def cosine_sums(values):
    count = len(values)
    if count == 1:
        return values
    half = count // 2
    plus = [values[n] + values[count - 1 - n] for n in range(half)]
    minus = [
        (values[n] - values[count - 1 - n])
        * (0.5 / math.cos(math.pi * (2 * n + 1) / (2 * count)))
        for n in range(half)
    ]
    even = cosine_sums(plus)
    odd = cosine_sums(minus)
    result = []
    for k in range(half):
        result.append(even[k])
        result.append(odd[k] + odd[k + 1] if k + 1 < half else odd[k])
    return result


def cosine_series(values):
    count = len(values)
    if count == 1:
        return values
    half = count // 2
    odd_in = [values[2 * k + 1] + values[2 * k - 1] if k else values[1] for k in range(half)]
    even = cosine_series(values[0::2])
    odd = cosine_series(odd_in)
    odd = [
        odd[n] * (0.5 / math.cos(math.pi * (2 * n + 1) / (2 * count))) for n in range(half)
    ]
    return [even[n] + odd[n] for n in range(half)] + [
        even[n] - odd[n] for n in range(half - 1, -1, -1)
    ]


def prep_kernel(coeffs, profile, klass, target, decay, source, onehot):
    levels, pairs = decay.shape[:2]
    fields = profile.shape[0]
    tile = decay.shape[2:]
    rows, lanes = klass.shape
    sub, lane = iotas(tile)
    low = sub < rows
    kind = jnp.concatenate([klass[...], klass[...]], axis=0)
    is_two = kind == 2
    is_one = kind == 1

    def by_class(which, f):
        return jnp.where(
            is_two,
            coeffs[which, 2, f] * 0.25,
            jnp.where(is_one, coeffs[which, 1, f] * 0.5, coeffs[which, 0, f]),
        )

    for p in range(pairs):
        f1 = 2 * p
        f2 = min(2 * p + 1, fields - 1)
        diffusion = jnp.where(low, by_class(0, f1), by_class(0, f2))
        relax = jnp.where(low, by_class(1, f1), by_class(1, f2))
        waves = cosine_sums([jnp.where(low, profile[f1, l], profile[f2, l]) for l in range(levels)])
        for m in range(levels):
            rate = relax + diffusion * (2.0 - 2.0 * math.cos(math.pi * m / levels))
            once = 1.0 / (1.0 + rate)
            square = once * once
            twice = once + square
            steps = jnp.where(is_two, twice + twice * square, jnp.where(is_one, twice, once))
            steps = steps * ((1.0 if m == 0 else 2.0) / levels)
            decay[m, p] = steps * rate
            source[m, p] = steps * relax * waves[m]
    low_part = target[...] & (lanes - 1)
    slot, _ = iotas((lanes, lanes))
    for r in range(rows):
        hit = jnp.where(slot == low_part[r : r + 1], 1.0, 0.0)
        onehot[r * lanes : (r + 1) * lanes, :] = jnp.transpose(hit).astype(jnp.bfloat16)


def combine(coefs, center, east, west, north, south):
    return (
        coefs[0] * center
        + (coefs[1] * east + coefs[2] * west)
        + (coefs[3] * north + coefs[4] * south)
    )


def coefficients(here_x, west_x, here_y, south_y):
    return (
        1.0
        - jnp.maximum(here_x, 0.0)
        + jnp.minimum(west_x, 0.0)
        - jnp.maximum(here_y, 0.0)
        + jnp.minimum(south_y, 0.0),
        jnp.maximum(-here_x, 0.0),
        jnp.maximum(west_x, 0.0),
        jnp.maximum(-here_y, 0.0),
        jnp.maximum(south_y, 0.0),
    )


def edge_kernel(
    levels,
    edge,
    edge_west,
    edge_east,
    corner_sw,
    corner_se,
    corner_nw,
    corner_ne,
    edge_raw,
    edge_next,
    edge_courant,
):
    fields = edge_raw.shape[0]
    tile = edge.shape[1:]
    rows = tile[0] // 2
    lanes = tile[1]
    group = lanes // levels
    sub, lane = iotas(tile)
    low = sub < rows
    place = lane % group
    from_east = (place == 2) | (place == 3)
    from_west = (place == 4) | (place == 5)
    east_side = place < group // 2

    def extended_edge(slot):
        value = jnp.where(
            from_east, edge_east[slot], jnp.where(from_west, edge_west[slot], edge[slot])
        )
        south = jnp.where(east_side, corner_se[pl.ds(slot, 1), :], corner_sw[pl.ds(slot, 1), :])
        north = jnp.where(east_side, corner_ne[pl.ds(slot, 1), :], corner_nw[pl.ds(slot, 1), :])
        value = jnp.where(sub == 2 * rows - 1, south, value)
        return jnp.where(sub == rows, north, value)

    def side_by_side(value):
        return jnp.where(place == 3, lane_roll(value, -2), value)

    edge_x = extended_edge(fields)
    edge_y = extended_edge(fields + 1)
    edge_coefs = coefficients(edge_x, lane_roll(edge_x, 1), edge_y, sub_roll(edge_y, 1))
    for f in range(fields):
        raw = extended_edge(f)
        edge_raw[f] = side_by_side(raw)
        moved = side_by_side(
            combine(
                edge_coefs,
                raw,
                lane_roll(raw, -1),
                lane_roll(raw, 1),
                sub_roll(raw, -1),
                sub_roll(raw, 1),
            )
        )
        edge_next[f] = jnp.where(low, moved, sub_roll(lane_roll(moved, -group), rows))
    edge_courant[...] = side_by_side(edge_x)


def transport_and_solve(
    fields,
    levels,
    tracers,
    cx,
    cy,
    from_south,
    from_north,
    edge_raw,
    edge_next,
    edge_courant,
    decay,
    source,
    state,
    full_coefs,
    half_coefs,
):
    pairs = levels // 2
    half = pairs // 2
    tile = tracers.shape[1:]
    rows = tile[0] // 2
    lanes = tile[1]
    group = lanes // levels
    sub, lane = iotas(tile)
    local = sub % rows
    low = sub < rows
    lower = local < rows // 2
    first_lane = lane == 0
    last_lane = lane == lanes - 1
    north_part = (sub >= 1) & (sub <= rows)
    south_part = (sub < rows - 1) | (sub == 2 * rows - 1)

    sides_x = edge_courant[...]
    sides_x_odd = sub_roll(sides_x, rows)
    base = fields * half
    count = pairs // rows
    for k in range(pairs):
        quad, t = k // rows, k % rows
        row_south = sub_roll(from_south[base + half + quad], rows + t)
        row_north = sub_roll(from_north[base + quad], rows - t)
        halo_x = jnp.where(local == 0, row_north, row_south)
        north_y = sub_roll(from_north[base + count + quad], rows - t)
        south_y = sub_roll(from_south[base + k // 2], rows if k % 2 == 0 else 2)
        halo_y = jnp.where(lower, north_y, south_y)
        own_x = cx[k]
        own_y = cy[k]
        both = []
        for odd in range(2):
            here_x = jnp.where(low, halo_x, own_x) if odd else jnp.where(low, own_x, halo_x)
            here_y = jnp.where(low, halo_y, own_y) if odd else jnp.where(low, own_y, halo_y)
            sides = lane_roll(sides_x_odd if odd else sides_x, -(group * (2 * k + odd) + 3))
            west_x = jnp.where(first_lane, sides, lane_roll(here_x, 1))
            coefs = coefficients(here_x, west_x, here_y, sub_roll(here_y, 1))
            for c in range(5):
                full_coefs[2 * k + odd, c] = coefs[c]
            both.append(coefs)
        for c in range(5):
            half_coefs[k, c] = jnp.where(low, both[0][c], both[1][c])


    def advect(f, k, first_coefs, second_coefs):
        own = tracers[f * pairs + k]
        message_south = from_south[f * half + k // 2]
        message_north = from_north[f * half + k // 2]
        if k % 2 == 0:
            halo = sub_roll(jnp.where(lower, message_north, message_south), rows)
        else:
            halo = jnp.where(lower, sub_roll(message_north, -2), sub_roll(message_south, 2))
        raw_sides = edge_raw[f]
        results = []
        for odd in range(2):
            value = jnp.where(low, halo, own) if odd else jnp.where(low, own, halo)
            sides = sub_roll(raw_sides, rows) if odd else raw_sides
            sides = lane_roll(sides, -(group * (2 * k + odd) + 3))
            results.append(
                combine(
                    first_coefs[odd],
                    value,
                    jnp.where(last_lane, sides, lane_roll(value, -1)),
                    jnp.where(first_lane, sides, lane_roll(value, 1)),
                    sub_roll(value, -1),
                    sub_roll(value, 1),
                )
            )
        even, odd = results
        center = jnp.where(low, even, odd)
        sides = lane_roll(edge_next[f], -(2 * group * k + 3))
        return combine(
            second_coefs,
            center,
            jnp.where(last_lane, sides, lane_roll(center, -1)),
            jnp.where(first_lane, sides, lane_roll(center, 1)),
            sub_roll(jnp.where(north_part, even, odd), -1),
            sub_roll(jnp.where(south_part, even, odd), 1),
        )

    def pair_step(p, total):
        f1 = 2 * p
        f2 = jnp.minimum(f1 + 1, fields - 1)
        columns = []
        for k in range(pairs):
            first_coefs = [[full_coefs[2 * k + odd, c] for c in range(5)] for odd in range(2)]
            second_coefs = [half_coefs[k, c] for c in range(5)]
            one = advect(f1, k, first_coefs, second_coefs)
            two = advect(f2, k, first_coefs, second_coefs)
            columns.append(jnp.where(low, one, sub_roll(two, rows)))
            columns.append(jnp.where(low, sub_roll(one, rows), two))
        waves = cosine_sums(columns)
        change = cosine_series([source[m, p] - decay[m, p] * waves[m] for m in range(levels)])
        square = change[0] * change[0]
        for l in range(1, levels):
            square = square + change[l] * change[l]
        for k in range(pairs):
            even, odd = (columns[l] + change[l] for l in (2 * k, 2 * k + 1))
            state[f1 * pairs + k] = jnp.where(low, even, sub_roll(odd, rows))
            state[f2 * pairs + k] = jnp.where(low, sub_roll(even, rows), odd)
        return total + jnp.where(low | (f1 + 1 < fields), square, 0.0)

    return lax.fori_loop(0, (fields + 1) // 2, pair_step, jnp.zeros(tile, F32), unroll=True)


def main_kernel(fields, levels, *refs):
    inputs, (target, onehot), (state, placed), coefs = refs[:10], refs[10:12], refs[12:14], refs[14:]
    rows, lanes = target.shape
    total = transport_and_solve(fields, levels, *inputs, state, *coefs)

    heat = (total + sub_roll(total, rows)) * (1.0 / (fields * levels))
    first = heat.astype(jnp.bfloat16).astype(F32)
    rest = heat - first
    second = rest.astype(jnp.bfloat16).astype(F32)
    third = rest - second
    spans = placed.shape[0]
    slot_row, _ = iotas((spans, lanes))
    high = lax.shift_right_logical(target[...], lanes.bit_length() - 1)
    hits = [slot_row == high[r : r + 1] for r in range(rows)]
    left = jnp.concatenate(
        [
            jnp.concatenate(
                [
                    jnp.where(hits[r], part[r : r + 1], 0.0).astype(jnp.bfloat16)
                    for r in range(rows)
                ],
                axis=1,
            )
            for part in (first, second, third)
        ],
        axis=0,
    )
    result = jnp.dot(left, onehot[...], preferred_element_type=F32)
    placed[...] = result[:spans] + result[spans : 2 * spans] + result[2 * spans :]


def finish_kernel(parts, state, total_out, state_out, total, semaphores):
    copy_state = pltpu.make_async_copy(state, state_out, semaphores.at[0])
    copy_state.start()
    value = parts[0]
    for i in range(1, parts.shape[0]):
        value = value + parts[i]
    total[...] = value
    copy_total = pltpu.make_async_copy(total, total_out, semaphores.at[1])
    copy_total.start()
    copy_state.wait()
    copy_total.wait()


def body(tracers, courant_x, courant_y, physics_ref, class_coeffs, span_target, cloud_class):
    fields, levels, rows, cols = tracers.shape
    wide = lax.axis_size("wide")
    narrow = lax.axis_size("narrow")
    pairs = levels // 2
    half = pairs // 2
    tile = (2 * rows, cols)
    field_pairs = (fields + 1) // 2
    flat = tracers.reshape(fields * pairs, *tile)
    cx = courant_x.reshape(pairs, *tile)
    cy = courant_y.reshape(pairs, *tile)
    quads = pairs // rows
    slots = -(-(fields + 2) // 8) * 8

    def array(*shape, dtype=F32):
        return jax.ShapeDtypeStruct(shape, dtype)

    flat, cx, cy, north, south = pl.pallas_call(
        functools.partial(pack_rows_kernel, levels),
        out_shape=(
            array(fields * pairs, *tile),
            array(pairs, *tile),
            array(pairs, *tile),
            array(fields * half + half + quads, *tile),
            array(fields * half + 2 * quads, *tile),
        ),
        in_specs=[HBM] * 3,
        out_specs=[VMEM] * 5,
        scratch_shapes=[pltpu.SemaphoreType.DMA((3,))],
        compiler_params=PARAMS,
    )(*(pltpu.with_memory_space_constraint(x, pltpu.HBM) for x in (flat, cx, cy)))
    edge, north_corner, south_corner = pl.pallas_call(
        functools.partial(pack_edges_kernel, levels),
        out_shape=(array(fields + 2, *tile), array(slots, cols), array(slots, cols)),
        in_specs=[VMEM] * 3,
        out_specs=[VMEM] * 3,
        compiler_params=PARAMS,
    )(flat, cx, cy)

    def send(value, up, right):
        pairs_ = []
        for w in range(wide):
            for n in range(narrow):
                to = ((w + up) % wide) * narrow + (n + right) % narrow
                pairs_.append((w * narrow + n, to))
        return lax.ppermute(value, ("wide", "narrow"), pairs_)

    def to_both_sides(value, up):
        from_west = send(value, up, 1)
        from_east = from_west if narrow == 2 else send(value, up, -1)
        return from_west, from_east

    from_south = send(north, 1, 0)
    from_north = send(south, -1, 0)
    edge_west, edge_east = to_both_sides(edge, 0)
    corner_sw, corner_se = to_both_sides(north_corner, 1)
    corner_nw, corner_ne = to_both_sides(south_corner, -1)

    decay, source, onehot = pl.pallas_call(
        prep_kernel,
        out_shape=(array(levels, field_pairs, *tile),) * 2
        + (array(rows * cols, cols, dtype=jnp.bfloat16),),
        in_specs=[SMEM, SMEM, VMEM, VMEM],
        out_specs=[VMEM] * 3,
        cost_estimate=pl.CostEstimate(flops=4000000, bytes_accessed=2000000, transcendentals=0),
        compiler_params=PARAMS,
    )(class_coeffs, physics_ref, cloud_class, span_target)

    edges = pl.pallas_call(
        functools.partial(edge_kernel, levels),
        out_shape=(array(fields, *tile), array(fields, *tile), array(*tile)),
        in_specs=[VMEM] * 7,
        out_specs=[VMEM] * 3,
        compiler_params=PARAMS,
    )(edge, edge_west, edge_east, corner_sw, corner_se, corner_nw, corner_ne)
    state, placed = pl.pallas_call(
        functools.partial(main_kernel, fields, levels),
        out_shape=(array(fields * pairs, *tile), array(wide * rows, cols)),
        in_specs=[VMEM] * 12,
        out_specs=[VMEM] * 2,
        scratch_shapes=[
            pltpu.VMEM((levels, 5) + tile, F32),
            pltpu.VMEM((pairs, 5) + tile, F32),
        ],
        compiler_params=PARAMS,
    )(
        flat,
        cx,
        cy,
        from_south,
        from_north,
        *edges,
        decay,
        source,
        span_target,
        onehot,
    )
    received = lax.all_to_all(
        placed.reshape(wide, rows, cols), "wide", split_axis=0, concat_axis=0, tiled=True
    )
    span_diag, state = pl.pallas_call(
        finish_kernel,
        out_shape=(array(rows, cols), array(fields * pairs, *tile)),
        in_specs=[VMEM] * 2,
        out_specs=[HBM] * 2,
        scratch_shapes=[pltpu.VMEM((rows, cols), F32), pltpu.SemaphoreType.DMA((2,))],
        compiler_params=PARAMS,
    )(received, state)
    return state.reshape(fields, levels, rows, cols), span_diag


def solution(mesh):
    return jax.shard_map(
        body,
        mesh=mesh,
        in_specs=(
            P(None, None, "wide", "narrow"),
            P(None, "wide", "narrow"),
            P(None, "wide", "narrow"),
            P(),
            P(),
            P("wide", "narrow"),
            P("wide", "narrow"),
        ),
        out_specs=(P(None, None, "wide", "narrow"), P("wide", "narrow")),
        check_vma=False,
    )
```

```python
import functools
import math

import jax
import jax.numpy as jnp
from jax import lax
from jax.experimental import pallas as pl
from jax.experimental.pallas import tpu as pltpu
from jax.sharding import PartitionSpec as P

VMEM = pl.BlockSpec(memory_space=pltpu.VMEM)
HBM = pl.BlockSpec(memory_space=pltpu.HBM)
SMEM = pl.BlockSpec(memory_space=pltpu.SMEM)
F32 = jnp.float32
PARAMS = pltpu.CompilerParams(vmem_limit_bytes=12 * 1024 * 1024)


def sub_roll(value, shift):
    shift = shift % value.shape[0]
    return value if shift == 0 else pltpu.roll(value, shift, 0)


def lane_roll(value, shift):
    shift = shift % value.shape[1]
    return value if shift == 0 else pltpu.roll(value, shift, 1)


def iotas(shape):
    return lax.broadcasted_iota(jnp.int32, shape, 0), lax.broadcasted_iota(jnp.int32, shape, 1)


def pack_rows(tracers, f, pairs, north, south, slot):
    local = iotas(tracers.shape[1:])[0] % (tracers.shape[1] // 2)
    lower = local < tracers.shape[1] // 4
    for k in range(pairs // 2):
        first, second = tracers[f * pairs + 2 * k], tracers[f * pairs + 2 * k + 1]
        north[slot + k] = jnp.where(lower, sub_roll(second, 2), first)
        south[slot + k] = jnp.where(lower, first, sub_roll(second, -2))


def pack_rows_kernel(
    levels, tracers_in, cx_in, cy_in, tracers, cx, cy, north, south, semaphores
):
    copies = [
        pltpu.make_async_copy(source, into, semaphores.at[i])
        for i, (source, into) in enumerate(((tracers_in, tracers), (cx_in, cx), (cy_in, cy)))
    ]
    for copy in copies:
        copy.start()
    for copy in copies:
        copy.wait()
    pairs = levels // 2
    half = pairs // 2
    tile = tracers.shape[1:]
    rows = tile[0] // 2
    local = iotas(tile)[0] % rows
    upper = local >= rows // 2

    def one_row(vectors, row, step):
        packed = []
        for start in range(0, pairs, rows):
            total = vectors[start]
            for t in range(1, rows):
                total = jnp.where(
                    local == row + step * t, sub_roll(vectors[start + t], step * t), total
                )
            packed.append(total)
        return packed

    fields = tracers.shape[0] // pairs
    for f in range(fields):
        pack_rows(tracers, f, pairs, north, south, f * half)
    vectors_x = [cx[k] for k in range(pairs)]
    vectors_y = [cy[k] for k in range(pairs)]
    base = fields * half
    for k in range(half):
        north[base + k] = jnp.where(upper, vectors_y[2 * k], sub_roll(vectors_y[2 * k + 1], 2))
    for k, value in enumerate(one_row(vectors_x, rows - 1, -1)):
        north[base + half + k] = value
    south_rows = one_row(vectors_x, 0, 1) + one_row(vectors_y, 0, 1)
    for k, value in enumerate(south_rows):
        south[base + k] = value


def pack_edges_kernel(levels, tracers, cx, cy, edge, north_corner, south_corner):
    pairs = levels // 2
    fields = tracers.shape[0] // pairs
    tile = tracers.shape[1:]
    rows = tile[0] // 2
    lanes = tile[1]
    group = lanes // levels
    lane = iotas(tile)[1]

    def pack_edge(vectors, slot):
        total = lane_roll(vectors[0], 2)
        for k in range(1, pairs):
            total = jnp.where(
                lane // (2 * group) == k, lane_roll(vectors[k], 2 + 2 * group * k), total
            )
        total = jnp.where(
            lane % (2 * group) < group, total, sub_roll(lane_roll(total, group), rows)
        )
        total = jnp.where(lane % group < group // 2, total, lane_roll(total, group // 2))
        edge[slot] = total
        north_corner[pl.ds(slot, 1), :] = total[rows - 1 : rows]
        south_corner[pl.ds(slot, 1), :] = total[0:1]

    for f in range(fields):
        pack_edge([tracers[f * pairs + k] for k in range(pairs)], f)
    pack_edge([cx[k] for k in range(pairs)], fields)
    pack_edge([cy[k] for k in range(pairs)], fields + 1)


def cosine_sums(values):
    count = len(values)
    if count == 1:
        return values
    half = count // 2
    plus = [values[n] + values[count - 1 - n] for n in range(half)]
    minus = [
        (values[n] - values[count - 1 - n])
        * (0.5 / math.cos(math.pi * (2 * n + 1) / (2 * count)))
        for n in range(half)
    ]
    even = cosine_sums(plus)
    odd = cosine_sums(minus)
    result = []
    for k in range(half):
        result.append(even[k])
        result.append(odd[k] + odd[k + 1] if k + 1 < half else odd[k])
    return result


def cosine_series(values):
    count = len(values)
    if count == 1:
        return values
    half = count // 2
    odd_in = [values[2 * k + 1] + values[2 * k - 1] if k else values[1] for k in range(half)]
    even = cosine_series(values[0::2])
    odd = cosine_series(odd_in)
    odd = [
        odd[n] * (0.5 / math.cos(math.pi * (2 * n + 1) / (2 * count))) for n in range(half)
    ]
    return [even[n] + odd[n] for n in range(half)] + [
        even[n] - odd[n] for n in range(half - 1, -1, -1)
    ]


def prep_kernel(coeffs, profile, klass, target, decay, source, onehot):
    levels, pairs = decay.shape[:2]
    fields = profile.shape[0]
    tile = decay.shape[2:]
    rows, lanes = klass.shape
    sub, lane = iotas(tile)
    low = sub < rows
    kind = jnp.concatenate([klass[...], klass[...]], axis=0)
    is_two = kind == 2
    is_one = kind == 1

    def by_class(which, f):
        return jnp.where(
            is_two,
            coeffs[which, 2, f] * 0.25,
            jnp.where(is_one, coeffs[which, 1, f] * 0.5, coeffs[which, 0, f]),
        )

    for p in range(pairs):
        f1 = 2 * p
        f2 = min(2 * p + 1, fields - 1)
        diffusion = jnp.where(low, by_class(0, f1), by_class(0, f2))
        relax = jnp.where(low, by_class(1, f1), by_class(1, f2))
        waves = cosine_sums([jnp.where(low, profile[f1, l], profile[f2, l]) for l in range(levels)])
        for m in range(levels):
            rate = relax + diffusion * (2.0 - 2.0 * math.cos(math.pi * m / levels))
            once = 1.0 / (1.0 + rate)
            square = once * once
            twice = once + square
            steps = jnp.where(is_two, twice + twice * square, jnp.where(is_one, twice, once))
            steps = steps * ((1.0 if m == 0 else 2.0) / levels)
            decay[m, p] = steps * rate
            source[m, p] = steps * relax * waves[m]
    low_part = target[...] & (lanes - 1)
    slot, _ = iotas((lanes, lanes))
    for r in range(rows):
        hit = jnp.where(slot == low_part[r : r + 1], 1.0, 0.0)
        onehot[r * lanes : (r + 1) * lanes, :] = jnp.transpose(hit).astype(jnp.bfloat16)


def combine(coefs, center, east, west, north, south):
    return (
        coefs[0] * center
        + (coefs[1] * east + coefs[2] * west)
        + (coefs[3] * north + coefs[4] * south)
    )


def coefficients(here_x, west_x, here_y, south_y):
    return (
        1.0
        - jnp.maximum(here_x, 0.0)
        + jnp.minimum(west_x, 0.0)
        - jnp.maximum(here_y, 0.0)
        + jnp.minimum(south_y, 0.0),
        jnp.maximum(-here_x, 0.0),
        jnp.maximum(west_x, 0.0),
        jnp.maximum(-here_y, 0.0),
        jnp.maximum(south_y, 0.0),
    )


def edge_kernel(
    levels,
    edge,
    edge_west,
    edge_east,
    corner_sw,
    corner_se,
    corner_nw,
    corner_ne,
    edge_raw,
    edge_next,
    edge_courant,
):
    fields = edge_raw.shape[0]
    tile = edge.shape[1:]
    rows = tile[0] // 2
    lanes = tile[1]
    group = lanes // levels
    sub, lane = iotas(tile)
    low = sub < rows
    place = lane % group
    from_east = (place == 2) | (place == 3)
    from_west = (place == 4) | (place == 5)
    east_side = place < group // 2

    def extended_edge(slot):
        value = jnp.where(
            from_east, edge_east[slot], jnp.where(from_west, edge_west[slot], edge[slot])
        )
        south = jnp.where(east_side, corner_se[pl.ds(slot, 1), :], corner_sw[pl.ds(slot, 1), :])
        north = jnp.where(east_side, corner_ne[pl.ds(slot, 1), :], corner_nw[pl.ds(slot, 1), :])
        value = jnp.where(sub == 2 * rows - 1, south, value)
        return jnp.where(sub == rows, north, value)

    def side_by_side(value):
        return jnp.where(place == 3, lane_roll(value, -2), value)

    edge_x = extended_edge(fields)
    edge_y = extended_edge(fields + 1)
    edge_coefs = coefficients(edge_x, lane_roll(edge_x, 1), edge_y, sub_roll(edge_y, 1))
    for f in range(fields):
        raw = extended_edge(f)
        edge_raw[f] = side_by_side(raw)
        moved = side_by_side(
            combine(
                edge_coefs,
                raw,
                lane_roll(raw, -1),
                lane_roll(raw, 1),
                sub_roll(raw, -1),
                sub_roll(raw, 1),
            )
        )
        edge_next[f] = jnp.where(low, moved, sub_roll(lane_roll(moved, -group), rows))
    edge_courant[...] = side_by_side(edge_x)


def transport_and_solve(
    fields,
    levels,
    tracers,
    cx,
    cy,
    from_south,
    from_north,
    edge_raw,
    edge_next,
    edge_courant,
    decay,
    source,
    state,
    full_coefs,
    half_coefs,
):
    pairs = levels // 2
    half = pairs // 2
    tile = tracers.shape[1:]
    rows = tile[0] // 2
    lanes = tile[1]
    group = lanes // levels
    sub, lane = iotas(tile)
    local = sub % rows
    low = sub < rows
    lower = local < rows // 2
    first_lane = lane == 0
    last_lane = lane == lanes - 1
    north_part = (sub >= 1) & (sub <= rows)
    south_part = (sub < rows - 1) | (sub == 2 * rows - 1)

    sides_x = edge_courant[...]
    sides_x_odd = sub_roll(sides_x, rows)
    base = fields * half
    count = pairs // rows
    for k in range(pairs):
        quad, t = k // rows, k % rows
        row_south = sub_roll(from_south[base + half + quad], rows + t)
        row_north = sub_roll(from_north[base + quad], rows - t)
        halo_x = jnp.where(local == 0, row_north, row_south)
        north_y = sub_roll(from_north[base + count + quad], rows - t)
        south_y = sub_roll(from_south[base + k // 2], rows if k % 2 == 0 else 2)
        halo_y = jnp.where(lower, north_y, south_y)
        own_x = cx[k]
        own_y = cy[k]
        both = []
        for odd in range(2):
            here_x = jnp.where(low, halo_x, own_x) if odd else jnp.where(low, own_x, halo_x)
            here_y = jnp.where(low, halo_y, own_y) if odd else jnp.where(low, own_y, halo_y)
            sides = lane_roll(sides_x_odd if odd else sides_x, -(group * (2 * k + odd) + 3))
            west_x = jnp.where(first_lane, sides, lane_roll(here_x, 1))
            coefs = coefficients(here_x, west_x, here_y, sub_roll(here_y, 1))
            for c in range(5):
                full_coefs[2 * k + odd, c] = coefs[c]
            both.append(coefs)
        for c in range(5):
            half_coefs[k, c] = jnp.where(low, both[0][c], both[1][c])


    def advect(f, k, first_coefs, second_coefs):
        own = tracers[f * pairs + k]
        message_south = from_south[f * half + k // 2]
        message_north = from_north[f * half + k // 2]
        if k % 2 == 0:
            halo = sub_roll(jnp.where(lower, message_north, message_south), rows)
        else:
            halo = jnp.where(lower, sub_roll(message_north, -2), sub_roll(message_south, 2))
        raw_sides = edge_raw[f]
        results = []
        for odd in range(2):
            value = jnp.where(low, halo, own) if odd else jnp.where(low, own, halo)
            sides = sub_roll(raw_sides, rows) if odd else raw_sides
            sides = lane_roll(sides, -(group * (2 * k + odd) + 3))
            results.append(
                combine(
                    first_coefs[odd],
                    value,
                    jnp.where(last_lane, sides, lane_roll(value, -1)),
                    jnp.where(first_lane, sides, lane_roll(value, 1)),
                    sub_roll(value, -1),
                    sub_roll(value, 1),
                )
            )
        even, odd = results
        center = jnp.where(low, even, odd)
        sides = lane_roll(edge_next[f], -(2 * group * k + 3))
        return combine(
            second_coefs,
            center,
            jnp.where(last_lane, sides, lane_roll(center, -1)),
            jnp.where(first_lane, sides, lane_roll(center, 1)),
            sub_roll(jnp.where(north_part, even, odd), -1),
            sub_roll(jnp.where(south_part, even, odd), 1),
        )

    def transport(p):
        f1 = 2 * p
        f2 = jnp.minimum(f1 + 1, fields - 1)
        columns = []
        for k in range(pairs):
            first_coefs = [[full_coefs[2 * k + odd, c] for c in range(5)] for odd in range(2)]
            second_coefs = [half_coefs[k, c] for c in range(5)]
            one = advect(f1, k, first_coefs, second_coefs)
            two = advect(f2, k, first_coefs, second_coefs)
            columns.append(jnp.where(low, one, sub_roll(two, rows)))
            columns.append(jnp.where(low, sub_roll(one, rows), two))
        return tuple(columns)

    def solve(p, columns):
        f1 = 2 * p
        f2 = jnp.minimum(f1 + 1, fields - 1)
        waves = cosine_sums(columns)
        change = cosine_series([source[m, p] - decay[m, p] * waves[m] for m in range(levels)])
        square = change[0] * change[0]
        for l in range(1, levels):
            square = square + change[l] * change[l]
        for k in range(pairs):
            even, odd = (columns[l] + change[l] for l in (2 * k, 2 * k + 1))
            state[f1 * pairs + k] = jnp.where(low, even, sub_roll(odd, rows))
            state[f2 * pairs + k] = jnp.where(low, sub_roll(even, rows), odd)
        return jnp.where(low | (f1 + 1 < fields), square, 0.0)

    def pair_step(p, carried):
        total, columns = carried
        following = transport(p)
        return total + solve(p - 1, columns), following

    field_pairs = (fields + 1) // 2
    total, columns = lax.fori_loop(
        1, field_pairs, pair_step, (jnp.zeros(tile, F32), transport(0))
    )
    return total + solve(field_pairs - 1, columns)


def main_kernel(fields, levels, *refs):
    inputs, (target, onehot), (state, placed), coefs = refs[:10], refs[10:12], refs[12:14], refs[14:]
    rows, lanes = target.shape
    total = transport_and_solve(fields, levels, *inputs, state, *coefs)

    heat = (total + sub_roll(total, rows)) * (1.0 / (fields * levels))
    first = heat.astype(jnp.bfloat16).astype(F32)
    rest = heat - first
    second = rest.astype(jnp.bfloat16).astype(F32)
    third = rest - second
    spans = placed.shape[0]
    slot_row, _ = iotas((spans, lanes))
    high = lax.shift_right_logical(target[...], lanes.bit_length() - 1)
    hits = [slot_row == high[r : r + 1] for r in range(rows)]
    left = jnp.concatenate(
        [
            jnp.concatenate(
                [
                    jnp.where(hits[r], part[r : r + 1], 0.0).astype(jnp.bfloat16)
                    for r in range(rows)
                ],
                axis=1,
            )
            for part in (first, second, third)
        ],
        axis=0,
    )
    result = jnp.dot(left, onehot[...], preferred_element_type=F32)
    placed[...] = result[:spans] + result[spans : 2 * spans] + result[2 * spans :]


def finish_kernel(parts, state, total_out, state_out, total, semaphores):
    copy_state = pltpu.make_async_copy(state, state_out, semaphores.at[0])
    copy_state.start()
    value = parts[0]
    for i in range(1, parts.shape[0]):
        value = value + parts[i]
    total[...] = value
    copy_total = pltpu.make_async_copy(total, total_out, semaphores.at[1])
    copy_total.start()
    copy_state.wait()
    copy_total.wait()


def body(tracers, courant_x, courant_y, physics_ref, class_coeffs, span_target, cloud_class):
    fields, levels, rows, cols = tracers.shape
    wide = lax.axis_size("wide")
    narrow = lax.axis_size("narrow")
    pairs = levels // 2
    half = pairs // 2
    tile = (2 * rows, cols)
    field_pairs = (fields + 1) // 2
    flat = tracers.reshape(fields * pairs, *tile)
    cx = courant_x.reshape(pairs, *tile)
    cy = courant_y.reshape(pairs, *tile)
    quads = pairs // rows
    slots = -(-(fields + 2) // 8) * 8

    def array(*shape, dtype=F32):
        return jax.ShapeDtypeStruct(shape, dtype)

    flat, cx, cy, north, south = pl.pallas_call(
        functools.partial(pack_rows_kernel, levels),
        out_shape=(
            array(fields * pairs, *tile),
            array(pairs, *tile),
            array(pairs, *tile),
            array(fields * half + half + quads, *tile),
            array(fields * half + 2 * quads, *tile),
        ),
        in_specs=[HBM] * 3,
        out_specs=[VMEM] * 5,
        scratch_shapes=[pltpu.SemaphoreType.DMA((3,))],
        compiler_params=PARAMS,
    )(*(pltpu.with_memory_space_constraint(x, pltpu.HBM) for x in (flat, cx, cy)))
    edge, north_corner, south_corner = pl.pallas_call(
        functools.partial(pack_edges_kernel, levels),
        out_shape=(array(fields + 2, *tile), array(slots, cols), array(slots, cols)),
        in_specs=[VMEM] * 3,
        out_specs=[VMEM] * 3,
        compiler_params=PARAMS,
    )(flat, cx, cy)

    def send(value, up, right):
        pairs_ = []
        for w in range(wide):
            for n in range(narrow):
                to = ((w + up) % wide) * narrow + (n + right) % narrow
                pairs_.append((w * narrow + n, to))
        return lax.ppermute(value, ("wide", "narrow"), pairs_)

    def to_both_sides(value, up):
        from_west = send(value, up, 1)
        from_east = from_west if narrow == 2 else send(value, up, -1)
        return from_west, from_east

    from_south = send(north, 1, 0)
    from_north = send(south, -1, 0)
    edge_west, edge_east = to_both_sides(edge, 0)
    corner_sw, corner_se = to_both_sides(north_corner, 1)
    corner_nw, corner_ne = to_both_sides(south_corner, -1)

    decay, source, onehot = pl.pallas_call(
        prep_kernel,
        out_shape=(array(levels, field_pairs, *tile),) * 2
        + (array(rows * cols, cols, dtype=jnp.bfloat16),),
        in_specs=[SMEM, SMEM, VMEM, VMEM],
        out_specs=[VMEM] * 3,
        cost_estimate=pl.CostEstimate(flops=4000000, bytes_accessed=2000000, transcendentals=0),
        compiler_params=PARAMS,
    )(class_coeffs, physics_ref, cloud_class, span_target)

    edges = pl.pallas_call(
        functools.partial(edge_kernel, levels),
        out_shape=(array(fields, *tile), array(fields, *tile), array(*tile)),
        in_specs=[VMEM] * 7,
        out_specs=[VMEM] * 3,
        compiler_params=PARAMS,
    )(edge, edge_west, edge_east, corner_sw, corner_se, corner_nw, corner_ne)
    state, placed = pl.pallas_call(
        functools.partial(main_kernel, fields, levels),
        out_shape=(array(fields * pairs, *tile), array(wide * rows, cols)),
        in_specs=[VMEM] * 12,
        out_specs=[VMEM] * 2,
        scratch_shapes=[
            pltpu.VMEM((levels, 5) + tile, F32),
            pltpu.VMEM((pairs, 5) + tile, F32),
        ],
        compiler_params=PARAMS,
    )(
        flat,
        cx,
        cy,
        from_south,
        from_north,
        *edges,
        decay,
        source,
        span_target,
        onehot,
    )
    received = lax.all_to_all(
        placed.reshape(wide, rows, cols), "wide", split_axis=0, concat_axis=0, tiled=True
    )
    span_diag, state = pl.pallas_call(
        finish_kernel,
        out_shape=(array(rows, cols), array(fields * pairs, *tile)),
        in_specs=[VMEM] * 2,
        out_specs=[HBM] * 2,
        scratch_shapes=[pltpu.VMEM((rows, cols), F32), pltpu.SemaphoreType.DMA((2,))],
        compiler_params=PARAMS,
    )(received, state)
    return state.reshape(fields, levels, rows, cols), span_diag


def solution(mesh):
    return jax.shard_map(
        body,
        mesh=mesh,
        in_specs=(
            P(None, None, "wide", "narrow"),
            P(None, "wide", "narrow"),
            P(None, "wide", "narrow"),
            P(),
            P(),
            P("wide", "narrow"),
            P("wide", "narrow"),
        ),
        out_specs=(P(None, None, "wide", "narrow"), P("wide", "narrow")),
        check_vma=False,
    )
```

```python
import functools
import math

import jax
import jax.numpy as jnp
from jax import lax
from jax.experimental import pallas as pl
from jax.experimental.pallas import tpu as pltpu
from jax.sharding import PartitionSpec as P

VMEM = pl.BlockSpec(memory_space=pltpu.VMEM)
HBM = pl.BlockSpec(memory_space=pltpu.HBM)
SMEM = pl.BlockSpec(memory_space=pltpu.SMEM)
F32 = jnp.float32
PARAMS = pltpu.CompilerParams(vmem_limit_bytes=12 * 1024 * 1024)


def sub_roll(value, shift):
    shift = shift % value.shape[0]
    return value if shift == 0 else pltpu.roll(value, shift, 0)


def lane_roll(value, shift):
    shift = shift % value.shape[1]
    return value if shift == 0 else pltpu.roll(value, shift, 1)


def iotas(shape):
    return lax.broadcasted_iota(jnp.int32, shape, 0), lax.broadcasted_iota(jnp.int32, shape, 1)


def pack_rows(tracers, f, pairs, north, south, slot):
    local = iotas(tracers.shape[1:])[0] % (tracers.shape[1] // 2)
    lower = local < tracers.shape[1] // 4
    for k in range(pairs // 2):
        first, second = tracers[f * pairs + 2 * k], tracers[f * pairs + 2 * k + 1]
        north[slot + k] = jnp.where(lower, sub_roll(second, 2), first)
        south[slot + k] = jnp.where(lower, first, sub_roll(second, -2))


def pack_rows_kernel(
    levels, tracers_in, cx_in, cy_in, tracers, cx, cy, north, south, semaphores
):
    copies = [
        pltpu.make_async_copy(source, into, semaphores.at[i])
        for i, (source, into) in enumerate(((tracers_in, tracers), (cx_in, cx), (cy_in, cy)))
    ]
    for copy in copies:
        copy.start()
    for copy in copies:
        copy.wait()
    pairs = levels // 2
    half = pairs // 2
    tile = tracers.shape[1:]
    rows = tile[0] // 2
    local = iotas(tile)[0] % rows
    upper = local >= rows // 2

    def one_row(vectors, row, step):
        packed = []
        for start in range(0, pairs, rows):
            total = vectors[start]
            for t in range(1, rows):
                total = jnp.where(
                    local == row + step * t, sub_roll(vectors[start + t], step * t), total
                )
            packed.append(total)
        return packed

    fields = tracers.shape[0] // pairs
    for f in range(fields):
        pack_rows(tracers, f, pairs, north, south, f * half)
    vectors_x = [cx[k] for k in range(pairs)]
    vectors_y = [cy[k] for k in range(pairs)]
    base = fields * half
    for k in range(half):
        north[base + k] = jnp.where(upper, vectors_y[2 * k], sub_roll(vectors_y[2 * k + 1], 2))
    for k, value in enumerate(one_row(vectors_x, rows - 1, -1)):
        north[base + half + k] = value
    south_rows = one_row(vectors_x, 0, 1) + one_row(vectors_y, 0, 1)
    for k, value in enumerate(south_rows):
        south[base + k] = value


def pack_edges_kernel(levels, tracers, cx, cy, edge, north_corner, south_corner):
    pairs = levels // 2
    fields = tracers.shape[0] // pairs
    tile = tracers.shape[1:]
    rows = tile[0] // 2
    lanes = tile[1]
    group = lanes // levels
    lane = iotas(tile)[1]

    def pack_edge(vectors, slot):
        total = lane_roll(vectors[0], 2)
        for k in range(1, pairs):
            total = jnp.where(
                lane // (2 * group) == k, lane_roll(vectors[k], 2 + 2 * group * k), total
            )
        total = jnp.where(
            lane % (2 * group) < group, total, sub_roll(lane_roll(total, group), rows)
        )
        total = jnp.where(lane % group < group // 2, total, lane_roll(total, group // 2))
        edge[slot] = total
        north_corner[pl.ds(slot, 1), :] = total[rows - 1 : rows]
        south_corner[pl.ds(slot, 1), :] = total[0:1]

    for f in range(fields):
        pack_edge([tracers[f * pairs + k] for k in range(pairs)], f)
    pack_edge([cx[k] for k in range(pairs)], fields)
    pack_edge([cy[k] for k in range(pairs)], fields + 1)


def cosine_sums(values):
    count = len(values)
    if count == 1:
        return values
    half = count // 2
    plus = [values[n] + values[count - 1 - n] for n in range(half)]
    minus = [
        (values[n] - values[count - 1 - n])
        * (0.5 / math.cos(math.pi * (2 * n + 1) / (2 * count)))
        for n in range(half)
    ]
    even = cosine_sums(plus)
    odd = cosine_sums(minus)
    result = []
    for k in range(half):
        result.append(even[k])
        result.append(odd[k] + odd[k + 1] if k + 1 < half else odd[k])
    return result


def cosine_series(values):
    count = len(values)
    if count == 1:
        return values
    half = count // 2
    odd_in = [values[2 * k + 1] + values[2 * k - 1] if k else values[1] for k in range(half)]
    even = cosine_series(values[0::2])
    odd = cosine_series(odd_in)
    odd = [
        odd[n] * (0.5 / math.cos(math.pi * (2 * n + 1) / (2 * count))) for n in range(half)
    ]
    return [even[n] + odd[n] for n in range(half)] + [
        even[n] - odd[n] for n in range(half - 1, -1, -1)
    ]


def prep_kernel(coeffs, profile, klass, target, decay, source, onehot):
    levels, pairs = decay.shape[:2]
    fields = profile.shape[0]
    tile = decay.shape[2:]
    rows, lanes = klass.shape
    sub, lane = iotas(tile)
    low = sub < rows
    kind = jnp.concatenate([klass[...], klass[...]], axis=0)
    is_two = kind == 2
    is_one = kind == 1

    def by_class(which, f):
        return jnp.where(
            is_two,
            coeffs[which, 2, f] * 0.25,
            jnp.where(is_one, coeffs[which, 1, f] * 0.5, coeffs[which, 0, f]),
        )

    for p in range(pairs):
        f1 = 2 * p
        f2 = min(2 * p + 1, fields - 1)
        diffusion = jnp.where(low, by_class(0, f1), by_class(0, f2))
        relax = jnp.where(low, by_class(1, f1), by_class(1, f2))
        waves = cosine_sums([jnp.where(low, profile[f1, l], profile[f2, l]) for l in range(levels)])
        for m in range(levels):
            rate = relax + diffusion * (2.0 - 2.0 * math.cos(math.pi * m / levels))
            once = 1.0 / (1.0 + rate)
            square = once * once
            twice = once + square
            steps = jnp.where(is_two, twice + twice * square, jnp.where(is_one, twice, once))
            steps = steps * ((1.0 if m == 0 else 2.0) / levels)
            decay[m, p] = steps * rate
            source[m, p] = steps * relax * waves[m]
    low_part = target[...] & (lanes - 1)
    slot, _ = iotas((lanes, lanes))
    for r in range(rows):
        hit = jnp.where(slot == low_part[r : r + 1], 1.0, 0.0)
        onehot[r * lanes : (r + 1) * lanes, :] = jnp.transpose(hit).astype(jnp.bfloat16)


def combine(coefs, center, east, west, north, south):
    return (
        coefs[0] * center
        + (coefs[1] * east + coefs[2] * west)
        + (coefs[3] * north + coefs[4] * south)
    )


def coefficients(here_x, west_x, here_y, south_y):
    return (
        1.0
        - jnp.maximum(here_x, 0.0)
        + jnp.minimum(west_x, 0.0)
        - jnp.maximum(here_y, 0.0)
        + jnp.minimum(south_y, 0.0),
        jnp.maximum(-here_x, 0.0),
        jnp.maximum(west_x, 0.0),
        jnp.maximum(-here_y, 0.0),
        jnp.maximum(south_y, 0.0),
    )


def edge_kernel(
    levels,
    edge,
    edge_west,
    edge_east,
    corner_sw,
    corner_se,
    corner_nw,
    corner_ne,
    edge_raw,
    edge_next,
    edge_courant,
):
    fields = edge_raw.shape[0]
    tile = edge.shape[1:]
    rows = tile[0] // 2
    lanes = tile[1]
    group = lanes // levels
    sub, lane = iotas(tile)
    low = sub < rows
    place = lane % group
    from_east = (place == 2) | (place == 3)
    from_west = (place == 4) | (place == 5)
    east_side = place < group // 2

    def extended_edge(slot):
        value = jnp.where(
            from_east, edge_east[slot], jnp.where(from_west, edge_west[slot], edge[slot])
        )
        south = jnp.where(east_side, corner_se[pl.ds(slot, 1), :], corner_sw[pl.ds(slot, 1), :])
        north = jnp.where(east_side, corner_ne[pl.ds(slot, 1), :], corner_nw[pl.ds(slot, 1), :])
        value = jnp.where(sub == 2 * rows - 1, south, value)
        return jnp.where(sub == rows, north, value)

    def side_by_side(value):
        return jnp.where(place == 3, lane_roll(value, -2), value)

    edge_x = extended_edge(fields)
    edge_y = extended_edge(fields + 1)
    edge_coefs = coefficients(edge_x, lane_roll(edge_x, 1), edge_y, sub_roll(edge_y, 1))
    for f in range(fields):
        raw = extended_edge(f)
        edge_raw[f] = side_by_side(raw)
        moved = side_by_side(
            combine(
                edge_coefs,
                raw,
                lane_roll(raw, -1),
                lane_roll(raw, 1),
                sub_roll(raw, -1),
                sub_roll(raw, 1),
            )
        )
        edge_next[f] = jnp.where(low, moved, sub_roll(lane_roll(moved, -group), rows))
    edge_courant[...] = side_by_side(edge_x)


def transport_and_solve(
    fields,
    levels,
    tracers,
    cx,
    cy,
    from_south,
    from_north,
    edge_raw,
    edge_next,
    edge_courant,
    decay,
    source,
    state,
    full_coefs,
    half_coefs,
):
    pairs = levels // 2
    half = pairs // 2
    tile = tracers.shape[1:]
    rows = tile[0] // 2
    lanes = tile[1]
    group = lanes // levels
    sub, lane = iotas(tile)
    local = sub % rows
    low = sub < rows
    lower = local < rows // 2
    first_lane = lane == 0
    last_lane = lane == lanes - 1
    north_part = (sub >= 1) & (sub <= rows)
    south_part = (sub < rows - 1) | (sub == 2 * rows - 1)

    sides_x = edge_courant[...]
    sides_x_odd = sub_roll(sides_x, rows)
    base = fields * half
    count = pairs // rows
    def set_quad(quad, sides_both):
        for t in range(rows):
            k = quad * rows + t
            row_south = sub_roll(from_south[base + half + quad], rows + t)
            row_north = sub_roll(from_north[base + quad], rows - t)
            halo_x = jnp.where(local == 0, row_north, row_south)
            north_y = sub_roll(from_north[base + count + quad], rows - t)
            south_y = from_south[base + quad * (rows // 2) + t // 2]
            south_y = sub_roll(south_y, rows if t % 2 == 0 else 2)
            halo_y = jnp.where(lower, north_y, south_y)
            own_x = cx[k]
            own_y = cy[k]
            both = []
            for odd in range(2):
                here_x = jnp.where(low, halo_x, own_x) if odd else jnp.where(low, own_x, halo_x)
                here_y = jnp.where(low, halo_y, own_y) if odd else jnp.where(low, own_y, halo_y)
                sides = lane_roll(sides_both[odd], -(group * (2 * t + odd) + 3))
                west_x = jnp.where(first_lane, sides, lane_roll(here_x, 1))
                coefs = coefficients(here_x, west_x, here_y, sub_roll(here_y, 1))
                for c in range(5):
                    full_coefs[2 * k + odd, c] = coefs[c]
                both.append(coefs)
            for c in range(5):
                half_coefs[k, c] = jnp.where(low, both[0][c], both[1][c])
        return tuple(lane_roll(sides, -group * 2 * rows) for sides in sides_both)

    lax.fori_loop(0, count, set_quad, (sides_x, sides_x_odd))

    def advect(f, k, first_coefs, second_coefs):
        own = tracers[f * pairs + k]
        message_south = from_south[f * half + k // 2]
        message_north = from_north[f * half + k // 2]
        if k % 2 == 0:
            halo = sub_roll(jnp.where(lower, message_north, message_south), rows)
        else:
            halo = jnp.where(lower, sub_roll(message_north, -2), sub_roll(message_south, 2))
        raw_sides = edge_raw[f]
        results = []
        for odd in range(2):
            value = jnp.where(low, halo, own) if odd else jnp.where(low, own, halo)
            sides = sub_roll(raw_sides, rows) if odd else raw_sides
            sides = lane_roll(sides, -(group * (2 * k + odd) + 3))
            results.append(
                combine(
                    first_coefs[odd],
                    value,
                    jnp.where(last_lane, sides, lane_roll(value, -1)),
                    jnp.where(first_lane, sides, lane_roll(value, 1)),
                    sub_roll(value, -1),
                    sub_roll(value, 1),
                )
            )
        even, odd = results
        center = jnp.where(low, even, odd)
        sides = lane_roll(edge_next[f], -(2 * group * k + 3))
        return combine(
            second_coefs,
            center,
            jnp.where(last_lane, sides, lane_roll(center, -1)),
            jnp.where(first_lane, sides, lane_roll(center, 1)),
            sub_roll(jnp.where(north_part, even, odd), -1),
            sub_roll(jnp.where(south_part, even, odd), 1),
        )

    def transport(p):
        f1 = 2 * p
        f2 = jnp.minimum(f1 + 1, fields - 1)
        columns = []
        for k in range(pairs):
            first_coefs = [[full_coefs[2 * k + odd, c] for c in range(5)] for odd in range(2)]
            second_coefs = [half_coefs[k, c] for c in range(5)]
            one = advect(f1, k, first_coefs, second_coefs)
            two = advect(f2, k, first_coefs, second_coefs)
            columns.append(jnp.where(low, one, sub_roll(two, rows)))
            columns.append(jnp.where(low, sub_roll(one, rows), two))
        return tuple(columns)

    def solve(p, columns):
        f1 = 2 * p
        f2 = jnp.minimum(f1 + 1, fields - 1)
        waves = cosine_sums(columns)
        change = cosine_series([source[m, p] - decay[m, p] * waves[m] for m in range(levels)])
        square = change[0] * change[0]
        for l in range(1, levels):
            square = square + change[l] * change[l]
        for k in range(pairs):
            even, odd = (columns[l] + change[l] for l in (2 * k, 2 * k + 1))
            state[f1 * pairs + k] = jnp.where(low, even, sub_roll(odd, rows))
            state[f2 * pairs + k] = jnp.where(low, sub_roll(even, rows), odd)
        return jnp.where(low | (f1 + 1 < fields), square, 0.0)

    def pair_step(p, carried):
        total, columns = carried
        following = transport(jnp.minimum(p, field_pairs - 1))
        square = solve(jnp.maximum(p - 1, 0), columns)
        return total + jnp.where(p > 0, square, 0.0), following

    field_pairs = (fields + 1) // 2
    nothing = jnp.zeros(tile, F32)
    total, _ = lax.fori_loop(0, field_pairs + 1, pair_step, (nothing, (nothing,) * levels))
    return total


def main_kernel(fields, levels, *refs):
    inputs, (target, onehot), (state, placed), coefs = refs[:10], refs[10:12], refs[12:14], refs[14:]
    rows, lanes = target.shape
    total = transport_and_solve(fields, levels, *inputs, state, *coefs)

    heat = (total + sub_roll(total, rows)) * (1.0 / (fields * levels))
    first = heat.astype(jnp.bfloat16).astype(F32)
    rest = heat - first
    second = rest.astype(jnp.bfloat16).astype(F32)
    third = rest - second
    spans = placed.shape[0]
    slot_row, _ = iotas((spans, lanes))
    high = lax.shift_right_logical(target[...], lanes.bit_length() - 1)
    hits = [slot_row == high[r : r + 1] for r in range(rows)]
    left = jnp.concatenate(
        [
            jnp.concatenate(
                [
                    jnp.where(hits[r], part[r : r + 1], 0.0).astype(jnp.bfloat16)
                    for r in range(rows)
                ],
                axis=1,
            )
            for part in (first, second, third)
        ],
        axis=0,
    )
    result = jnp.dot(left, onehot[...], preferred_element_type=F32)
    placed[...] = result[:spans] + result[spans : 2 * spans] + result[2 * spans :]


def finish_kernel(parts, state, total_out, state_out, total, semaphores):
    copy_state = pltpu.make_async_copy(state, state_out, semaphores.at[0])
    copy_state.start()
    value = parts[0]
    for i in range(1, parts.shape[0]):
        value = value + parts[i]
    total[...] = value
    copy_total = pltpu.make_async_copy(total, total_out, semaphores.at[1])
    copy_total.start()
    copy_state.wait()
    copy_total.wait()


def body(tracers, courant_x, courant_y, physics_ref, class_coeffs, span_target, cloud_class):
    fields, levels, rows, cols = tracers.shape
    wide = lax.axis_size("wide")
    narrow = lax.axis_size("narrow")
    pairs = levels // 2
    half = pairs // 2
    tile = (2 * rows, cols)
    field_pairs = (fields + 1) // 2
    flat = tracers.reshape(fields * pairs, *tile)
    cx = courant_x.reshape(pairs, *tile)
    cy = courant_y.reshape(pairs, *tile)
    quads = pairs // rows
    slots = -(-(fields + 2) // 8) * 8

    def array(*shape, dtype=F32):
        return jax.ShapeDtypeStruct(shape, dtype)

    flat, cx, cy, north, south = pl.pallas_call(
        functools.partial(pack_rows_kernel, levels),
        out_shape=(
            array(fields * pairs, *tile),
            array(pairs, *tile),
            array(pairs, *tile),
            array(fields * half + half + quads, *tile),
            array(fields * half + 2 * quads, *tile),
        ),
        in_specs=[HBM] * 3,
        out_specs=[VMEM] * 5,
        scratch_shapes=[pltpu.SemaphoreType.DMA((3,))],
        compiler_params=PARAMS,
    )(*(pltpu.with_memory_space_constraint(x, pltpu.HBM) for x in (flat, cx, cy)))
    edge, north_corner, south_corner = pl.pallas_call(
        functools.partial(pack_edges_kernel, levels),
        out_shape=(array(fields + 2, *tile), array(slots, cols), array(slots, cols)),
        in_specs=[VMEM] * 3,
        out_specs=[VMEM] * 3,
        compiler_params=PARAMS,
    )(flat, cx, cy)

    def send(value, up, right):
        pairs_ = []
        for w in range(wide):
            for n in range(narrow):
                to = ((w + up) % wide) * narrow + (n + right) % narrow
                pairs_.append((w * narrow + n, to))
        return lax.ppermute(value, ("wide", "narrow"), pairs_)

    def to_both_sides(value, up):
        from_west = send(value, up, 1)
        from_east = from_west if narrow == 2 else send(value, up, -1)
        return from_west, from_east

    from_south = send(north, 1, 0)
    from_north = send(south, -1, 0)
    edge_west, edge_east = to_both_sides(edge, 0)
    corner_sw, corner_se = to_both_sides(north_corner, 1)
    corner_nw, corner_ne = to_both_sides(south_corner, -1)

    decay, source, onehot = pl.pallas_call(
        prep_kernel,
        out_shape=(array(levels, field_pairs, *tile),) * 2
        + (array(rows * cols, cols, dtype=jnp.bfloat16),),
        in_specs=[SMEM, SMEM, VMEM, VMEM],
        out_specs=[VMEM] * 3,
        cost_estimate=pl.CostEstimate(flops=4000000, bytes_accessed=2000000, transcendentals=0),
        compiler_params=PARAMS,
    )(class_coeffs, physics_ref, cloud_class, span_target)

    edges = pl.pallas_call(
        functools.partial(edge_kernel, levels),
        out_shape=(array(fields, *tile), array(fields, *tile), array(*tile)),
        in_specs=[VMEM] * 7,
        out_specs=[VMEM] * 3,
        compiler_params=PARAMS,
    )(edge, edge_west, edge_east, corner_sw, corner_se, corner_nw, corner_ne)
    state, placed = pl.pallas_call(
        functools.partial(main_kernel, fields, levels),
        out_shape=(array(fields * pairs, *tile), array(wide * rows, cols)),
        in_specs=[VMEM] * 12,
        out_specs=[VMEM] * 2,
        scratch_shapes=[
            pltpu.VMEM((levels, 5) + tile, F32),
            pltpu.VMEM((pairs, 5) + tile, F32),
        ],
        compiler_params=PARAMS,
    )(
        flat,
        cx,
        cy,
        from_south,
        from_north,
        *edges,
        decay,
        source,
        span_target,
        onehot,
    )
    received = lax.all_to_all(
        placed.reshape(wide, rows, cols), "wide", split_axis=0, concat_axis=0, tiled=True
    )
    span_diag, state = pl.pallas_call(
        finish_kernel,
        out_shape=(array(rows, cols), array(fields * pairs, *tile)),
        in_specs=[VMEM] * 2,
        out_specs=[HBM] * 2,
        scratch_shapes=[pltpu.VMEM((rows, cols), F32), pltpu.SemaphoreType.DMA((2,))],
        compiler_params=PARAMS,
    )(received, state)
    return state.reshape(fields, levels, rows, cols), span_diag


def solution(mesh):
    return jax.shard_map(
        body,
        mesh=mesh,
        in_specs=(
            P(None, None, "wide", "narrow"),
            P(None, "wide", "narrow"),
            P(None, "wide", "narrow"),
            P(),
            P(),
            P("wide", "narrow"),
            P("wide", "narrow"),
        ),
        out_specs=(P(None, None, "wide", "narrow"), P("wide", "narrow")),
        check_vma=False,
    )
```

```python
import functools
import math

import jax
import jax.numpy as jnp
from jax import lax
from jax.experimental import pallas as pl
from jax.experimental.pallas import tpu as pltpu
from jax.sharding import PartitionSpec as P

VMEM = pl.BlockSpec(memory_space=pltpu.VMEM)
HBM = pl.BlockSpec(memory_space=pltpu.HBM)
SMEM = pl.BlockSpec(memory_space=pltpu.SMEM)
F32 = jnp.float32
PARAMS = pltpu.CompilerParams(vmem_limit_bytes=12 * 1024 * 1024)


def sub_roll(value, shift):
    shift = shift % value.shape[0]
    return value if shift == 0 else pltpu.roll(value, shift, 0)


def lane_roll(value, shift):
    shift = shift % value.shape[1]
    return value if shift == 0 else pltpu.roll(value, shift, 1)


def iotas(shape):
    return lax.broadcasted_iota(jnp.int32, shape, 0), lax.broadcasted_iota(jnp.int32, shape, 1)


def pack_rows(tracers, f, pairs, north, south, slot):
    local = iotas(tracers.shape[1:])[0] % (tracers.shape[1] // 2)
    lower = local < tracers.shape[1] // 4
    for k in range(pairs // 2):
        first, second = tracers[f * pairs + 2 * k], tracers[f * pairs + 2 * k + 1]
        north[slot + k] = jnp.where(lower, sub_roll(second, 2), first)
        south[slot + k] = jnp.where(lower, first, sub_roll(second, -2))


def pack_rows_kernel(
    levels, tracers_in, cx_in, cy_in, tracers, cx, cy, north, south, semaphores
):
    copies = [
        pltpu.make_async_copy(source, into, semaphores.at[i])
        for i, (source, into) in enumerate(((tracers_in, tracers), (cx_in, cx), (cy_in, cy)))
    ]
    for copy in copies:
        copy.start()
    for copy in copies:
        copy.wait()
    pairs = levels // 2
    half = pairs // 2
    tile = tracers.shape[1:]
    rows = tile[0] // 2
    local = iotas(tile)[0] % rows
    upper = local >= rows // 2

    def one_row(vectors, row, step):
        packed = []
        for start in range(0, pairs, rows):
            total = vectors[start]
            for t in range(1, rows):
                total = jnp.where(
                    local == row + step * t, sub_roll(vectors[start + t], step * t), total
                )
            packed.append(total)
        return packed

    fields = tracers.shape[0] // pairs
    for f in range(fields):
        pack_rows(tracers, f, pairs, north, south, f * half)
    vectors_x = [cx[k] for k in range(pairs)]
    vectors_y = [cy[k] for k in range(pairs)]
    base = fields * half
    for k in range(half):
        north[base + k] = jnp.where(upper, vectors_y[2 * k], sub_roll(vectors_y[2 * k + 1], 2))
    for k, value in enumerate(one_row(vectors_x, rows - 1, -1)):
        north[base + half + k] = value
    south_rows = one_row(vectors_x, 0, 1) + one_row(vectors_y, 0, 1)
    for k, value in enumerate(south_rows):
        south[base + k] = value


def pack_edges_kernel(levels, tracers, cx, cy, edge, north_corner, south_corner):
    pairs = levels // 2
    fields = tracers.shape[0] // pairs
    tile = tracers.shape[1:]
    rows = tile[0] // 2
    lanes = tile[1]
    group = lanes // levels
    lane = iotas(tile)[1]

    def pack_edge(vectors, slot):
        total = lane_roll(vectors[0], 2)
        for k in range(1, pairs):
            total = jnp.where(
                lane // (2 * group) == k, lane_roll(vectors[k], 2 + 2 * group * k), total
            )
        total = jnp.where(
            lane % (2 * group) < group, total, sub_roll(lane_roll(total, group), rows)
        )
        total = jnp.where(lane % group < group // 2, total, lane_roll(total, group // 2))
        edge[slot] = total
        north_corner[pl.ds(slot, 1), :] = total[rows - 1 : rows]
        south_corner[pl.ds(slot, 1), :] = total[0:1]

    for f in range(fields):
        pack_edge([tracers[f * pairs + k] for k in range(pairs)], f)
    pack_edge([cx[k] for k in range(pairs)], fields)
    pack_edge([cy[k] for k in range(pairs)], fields + 1)


def cosine_sums(values):
    count = len(values)
    if count == 1:
        return values
    half = count // 2
    plus = [values[n] + values[count - 1 - n] for n in range(half)]
    minus = [
        (values[n] - values[count - 1 - n])
        * (0.5 / math.cos(math.pi * (2 * n + 1) / (2 * count)))
        for n in range(half)
    ]
    even = cosine_sums(plus)
    odd = cosine_sums(minus)
    result = []
    for k in range(half):
        result.append(even[k])
        result.append(odd[k] + odd[k + 1] if k + 1 < half else odd[k])
    return result


def cosine_series(values):
    count = len(values)
    if count == 1:
        return values
    half = count // 2
    odd_in = [values[2 * k + 1] + values[2 * k - 1] if k else values[1] for k in range(half)]
    even = cosine_series(values[0::2])
    odd = cosine_series(odd_in)
    odd = [
        odd[n] * (0.5 / math.cos(math.pi * (2 * n + 1) / (2 * count))) for n in range(half)
    ]
    return [even[n] + odd[n] for n in range(half)] + [
        even[n] - odd[n] for n in range(half - 1, -1, -1)
    ]


def prep_kernel(coeffs, profile, klass, target, decay, source, onehot):
    levels, pairs = decay.shape[:2]
    fields = profile.shape[0]
    tile = decay.shape[2:]
    rows, lanes = klass.shape
    sub, lane = iotas(tile)
    low = sub < rows
    kind = jnp.concatenate([klass[...], klass[...]], axis=0)
    is_two = kind == 2
    is_one = kind == 1

    def by_class(which, f):
        return jnp.where(
            is_two,
            coeffs[which, 2, f] * 0.25,
            jnp.where(is_one, coeffs[which, 1, f] * 0.5, coeffs[which, 0, f]),
        )

    for p in range(pairs):
        f1 = 2 * p
        f2 = min(2 * p + 1, fields - 1)
        diffusion = jnp.where(low, by_class(0, f1), by_class(0, f2))
        relax = jnp.where(low, by_class(1, f1), by_class(1, f2))
        waves = cosine_sums([jnp.where(low, profile[f1, l], profile[f2, l]) for l in range(levels)])
        for m in range(levels):
            rate = relax + diffusion * (2.0 - 2.0 * math.cos(math.pi * m / levels))
            once = 1.0 / (1.0 + rate)
            square = once * once
            twice = once + square
            steps = jnp.where(is_two, twice + twice * square, jnp.where(is_one, twice, once))
            steps = steps * ((1.0 if m == 0 else 2.0) / levels)
            decay[m, p] = steps * rate
            source[m, p] = steps * relax * waves[m]
    low_part = target[...] & (lanes - 1)
    slot, _ = iotas((lanes, lanes))
    for r in range(rows):
        hit = jnp.where(slot == low_part[r : r + 1], 1.0, 0.0)
        onehot[r * lanes : (r + 1) * lanes, :] = jnp.transpose(hit).astype(jnp.bfloat16)


def combine(coefs, center, east, west, north, south):
    return (
        coefs[0] * center
        + (coefs[1] * east + coefs[2] * west)
        + (coefs[3] * north + coefs[4] * south)
    )


def coefficients(here_x, west_x, here_y, south_y):
    return (
        1.0
        - jnp.maximum(here_x, 0.0)
        + jnp.minimum(west_x, 0.0)
        - jnp.maximum(here_y, 0.0)
        + jnp.minimum(south_y, 0.0),
        jnp.maximum(-here_x, 0.0),
        jnp.maximum(west_x, 0.0),
        jnp.maximum(-here_y, 0.0),
        jnp.maximum(south_y, 0.0),
    )


def side_by_side(value, place):
    return jnp.where(place == 3, lane_roll(value, -2), value)


def beside(edge, edge_west, edge_east, slot, place):
    from_east = (place == 2) | (place == 3)
    from_west = (place == 4) | (place == 5)
    return jnp.where(
        from_east, edge_east[slot], jnp.where(from_west, edge_west[slot], edge[slot])
    )


def shift_kernel(levels, tracers, edge, edge_west, edge_east, east, west):
    pairs = levels // 2
    tile = tracers.shape[1:]
    rows = tile[0] // 2
    lanes = tile[1]
    group = lanes // levels
    sub, lane = iotas(tile)
    place = lane % group

    def shift_field(f, carried):
        sides = side_by_side(beside(edge, edge_west, edge_east, f, place), place)
        sides = jnp.where(sub < rows, sides, sub_roll(lane_roll(sides, -group), rows))
        for k in range(pairs):
            own = tracers[f * pairs + k]
            here = lane_roll(sides, -(2 * group * k + 3))
            east[f * pairs + k] = jnp.where(lane == lanes - 1, here, lane_roll(own, -1))
            west[f * pairs + k] = jnp.where(lane == 0, here, lane_roll(own, 1))
        return carried

    lax.fori_loop(0, tracers.shape[0] // pairs, shift_field, 0)


def edge_kernel(
    levels,
    edge,
    edge_west,
    edge_east,
    corner_sw,
    corner_se,
    corner_nw,
    corner_ne,
    halo_sides,
    next_sides,
    courant_sides,
):
    tile = edge.shape[1:]
    fields = edge.shape[0] - 2
    pairs = levels // 2
    half = pairs // 2
    rows = tile[0] // 2
    lanes = tile[1]
    group = lanes // levels
    sub, lane = iotas(tile)
    low = sub < rows
    place = lane % group
    east_side = place < group // 2
    odd_sub = sub % 2 == 1
    level_one = (sub == 4) | (sub == 7)
    level_two = (sub == 5) | (sub == 6)
    level_three = (sub == 1) | (sub == 2)

    def corner_rows(slot):
        south = jnp.where(east_side, corner_se[pl.ds(slot, 1), :], corner_sw[pl.ds(slot, 1), :])
        north = jnp.where(east_side, corner_ne[pl.ds(slot, 1), :], corner_nw[pl.ds(slot, 1), :])
        return south, north

    def extended_edge(slot, south, north):
        value = beside(edge, edge_west, edge_east, slot, place)
        value = jnp.where(sub == 2 * rows - 1, south, value)
        return jnp.where(sub == rows, north, value)

    edge_x = extended_edge(fields, *corner_rows(fields))
    edge_y = extended_edge(fields + 1, *corner_rows(fields + 1))
    courant_sides[...] = side_by_side(edge_x, place)
    edge_coefs = coefficients(edge_x, lane_roll(edge_x, 1), edge_y, sub_roll(edge_y, 1))

    def one_field(f, carried):
        south, north = corner_rows(f)
        halo = side_by_side(jnp.where(odd_sub, south, north), place)
        halo = jnp.where(
            level_one,
            lane_roll(halo, -group),
            jnp.where(
                level_two,
                lane_roll(halo, -2 * group),
                jnp.where(level_three, lane_roll(halo, -3 * group), halo),
            ),
        )
        for k in range(half):
            halo_sides[f * half + k] = lane_roll(halo, -(4 * group * k + 3))
        raw = extended_edge(f, south, north)
        moved = side_by_side(
            combine(
                edge_coefs,
                raw,
                lane_roll(raw, -1),
                lane_roll(raw, 1),
                sub_roll(raw, -1),
                sub_roll(raw, 1),
            ),
            place,
        )
        moved = jnp.where(low, moved, sub_roll(lane_roll(moved, -group), rows))
        for k in range(pairs):
            next_sides[f * pairs + k] = lane_roll(moved, -(2 * group * k + 3))
        return carried

    lax.fori_loop(0, fields, one_field, 0)


def transport_and_solve(
    fields,
    levels,
    tracers,
    cx,
    cy,
    from_south,
    from_north,
    east,
    west,
    halo_sides,
    next_sides,
    courant_sides,
    decay,
    source,
    state,
    full_coefs,
    half_coefs,
):
    pairs = levels // 2
    half = pairs // 2
    tile = tracers.shape[1:]
    rows = tile[0] // 2
    lanes = tile[1]
    group = lanes // levels
    sub, lane = iotas(tile)
    local = sub % rows
    low = sub < rows
    lower = local < rows // 2
    first_lane = lane == 0
    last_lane = lane == lanes - 1
    odd_sub = sub % 2 == 1
    north_even = (sub < rows - 1) | (sub == 2 * rows - 1)
    south_even = (sub >= 1) & (sub <= rows)
    north_part = (sub >= 1) & (sub <= rows)
    south_part = (sub < rows - 1) | (sub == 2 * rows - 1)

    sides_x = courant_sides[...]
    sides_x_odd = sub_roll(sides_x, rows)
    base = fields * half
    count = pairs // rows
    for k in range(pairs):
        quad, t = k // rows, k % rows
        row_south = sub_roll(from_south[base + half + quad], rows + t)
        row_north = sub_roll(from_north[base + quad], rows - t)
        halo_x = jnp.where(local == 0, row_north, row_south)
        north_y = sub_roll(from_north[base + count + quad], rows - t)
        south_y = sub_roll(from_south[base + k // 2], rows if k % 2 == 0 else 2)
        halo_y = jnp.where(lower, north_y, south_y)
        own_x = cx[k]
        own_y = cy[k]
        both = []
        for odd in range(2):
            here_x = jnp.where(low, halo_x, own_x) if odd else jnp.where(low, own_x, halo_x)
            here_y = jnp.where(low, halo_y, own_y) if odd else jnp.where(low, own_y, halo_y)
            sides = lane_roll(sides_x_odd if odd else sides_x, -(group * (2 * k + odd) + 3))
            west_x = jnp.where(first_lane, sides, lane_roll(here_x, 1))
            coefs = coefficients(here_x, west_x, here_y, sub_roll(here_y, 1))
            for c in range(5):
                full_coefs[2 * k + odd, c] = coefs[c]
            both.append(coefs)
        for c in range(5):
            half_coefs[k, c] = jnp.where(low, both[0][c], both[1][c])


    def halos(f, k):
        message_south = from_south[f * half + k]
        message_north = from_north[f * half + k]
        center = jnp.where(odd_sub, message_south, message_north)
        sides = halo_sides[f * half + k]
        shifted = (
            jnp.where(last_lane, sides, lane_roll(center, -1)),
            jnp.where(first_lane, sides, lane_roll(center, 1)),
        )
        first = sub_roll(jnp.where(lower, message_north, message_south), rows)
        second = jnp.where(lower, sub_roll(message_north, -2), sub_roll(message_south, 2))
        return (
            (first, *(sub_roll(value, rows) for value in shifted)),
            (
                second,
                *(
                    jnp.where(local == 0, sub_roll(value, -2), sub_roll(value, 2))
                    for value in shifted
                ),
            ),
        )

    def advect(f, k, halo, first_coefs, second_coefs):
        slot = f * pairs + k
        own = (tracers[slot], east[slot], west[slot])
        own_north, own_south = sub_roll(own[0], -1), sub_roll(own[0], 1)
        halo_north, halo_south = sub_roll(halo[0], -1), sub_roll(halo[0], 1)
        even = combine(
            first_coefs[0],
            *(jnp.where(low, mine, other) for mine, other in zip(own, halo)),
            jnp.where(north_even, own_north, halo_north),
            jnp.where(south_even, own_south, halo_south),
        )
        odd = combine(
            first_coefs[1],
            *(jnp.where(low, other, mine) for mine, other in zip(own, halo)),
            jnp.where(north_even, halo_north, own_north),
            jnp.where(south_even, halo_south, own_south),
        )
        center = jnp.where(low, even, odd)
        sides = next_sides[slot]
        return combine(
            second_coefs,
            center,
            jnp.where(last_lane, sides, lane_roll(center, -1)),
            jnp.where(first_lane, sides, lane_roll(center, 1)),
            sub_roll(jnp.where(north_part, even, odd), -1),
            sub_roll(jnp.where(south_part, even, odd), 1),
        )

    def pair_step(p, total):
        f1 = 2 * p
        f2 = jnp.minimum(f1 + 1, fields - 1)
        columns = []
        for k in range(half):
            halo_one, halo_two = halos(f1, k), halos(f2, k)
            for i in range(2):
                j = 2 * k + i
                first_coefs = [[full_coefs[2 * j + odd, c] for c in range(5)] for odd in range(2)]
                second_coefs = [half_coefs[j, c] for c in range(5)]
                one = advect(f1, j, halo_one[i], first_coefs, second_coefs)
                two = advect(f2, j, halo_two[i], first_coefs, second_coefs)
                columns.append(jnp.where(low, one, sub_roll(two, rows)))
                columns.append(jnp.where(low, sub_roll(one, rows), two))
        waves = cosine_sums(columns)
        change = cosine_series([source[m, p] - decay[m, p] * waves[m] for m in range(levels)])
        square = change[0] * change[0]
        for l in range(1, levels):
            square = square + change[l] * change[l]
        for k in range(pairs):
            even, odd = (columns[l] + change[l] for l in (2 * k, 2 * k + 1))
            state[f1 * pairs + k] = jnp.where(low, even, sub_roll(odd, rows))
            state[f2 * pairs + k] = jnp.where(low, sub_roll(even, rows), odd)
        return total + jnp.where(low | (f1 + 1 < fields), square, 0.0)

    return lax.fori_loop(0, (fields + 1) // 2, pair_step, jnp.zeros(tile, F32))


def main_kernel(fields, levels, *refs):
    inputs, (target, onehot), (state, placed), coefs = refs[:12], refs[12:14], refs[14:16], refs[16:]
    rows, lanes = target.shape
    total = transport_and_solve(fields, levels, *inputs, state, *coefs)

    heat = (total + sub_roll(total, rows)) * (1.0 / (fields * levels))
    first = heat.astype(jnp.bfloat16).astype(F32)
    rest = heat - first
    second = rest.astype(jnp.bfloat16).astype(F32)
    third = rest - second
    spans = placed.shape[0]
    slot_row, _ = iotas((spans, lanes))
    high = lax.shift_right_logical(target[...], lanes.bit_length() - 1)
    hits = [slot_row == high[r : r + 1] for r in range(rows)]
    left = jnp.concatenate(
        [
            jnp.concatenate(
                [
                    jnp.where(hits[r], part[r : r + 1], 0.0).astype(jnp.bfloat16)
                    for r in range(rows)
                ],
                axis=1,
            )
            for part in (first, second, third)
        ],
        axis=0,
    )
    result = jnp.dot(left, onehot[...], preferred_element_type=F32)
    placed[...] = result[:spans] + result[spans : 2 * spans] + result[2 * spans :]


def finish_kernel(parts, state, total_out, state_out, total, semaphores):
    copy_state = pltpu.make_async_copy(state, state_out, semaphores.at[0])
    copy_state.start()
    value = parts[0]
    for i in range(1, parts.shape[0]):
        value = value + parts[i]
    total[...] = value
    copy_total = pltpu.make_async_copy(total, total_out, semaphores.at[1])
    copy_total.start()
    copy_state.wait()
    copy_total.wait()


def body(tracers, courant_x, courant_y, physics_ref, class_coeffs, span_target, cloud_class):
    fields, levels, rows, cols = tracers.shape
    wide = lax.axis_size("wide")
    narrow = lax.axis_size("narrow")
    pairs = levels // 2
    half = pairs // 2
    tile = (2 * rows, cols)
    field_pairs = (fields + 1) // 2
    flat = tracers.reshape(fields * pairs, *tile)
    cx = courant_x.reshape(pairs, *tile)
    cy = courant_y.reshape(pairs, *tile)
    quads = pairs // rows
    slots = -(-(fields + 2) // 8) * 8

    def array(*shape, dtype=F32):
        return jax.ShapeDtypeStruct(shape, dtype)

    flat, cx, cy, north, south = pl.pallas_call(
        functools.partial(pack_rows_kernel, levels),
        out_shape=(
            array(fields * pairs, *tile),
            array(pairs, *tile),
            array(pairs, *tile),
            array(fields * half + half + quads, *tile),
            array(fields * half + 2 * quads, *tile),
        ),
        in_specs=[HBM] * 3,
        out_specs=[VMEM] * 5,
        scratch_shapes=[pltpu.SemaphoreType.DMA((3,))],
        compiler_params=PARAMS,
    )(*(pltpu.with_memory_space_constraint(x, pltpu.HBM) for x in (flat, cx, cy)))
    edge, north_corner, south_corner = pl.pallas_call(
        functools.partial(pack_edges_kernel, levels),
        out_shape=(array(fields + 2, *tile), array(slots, cols), array(slots, cols)),
        in_specs=[VMEM] * 3,
        out_specs=[VMEM] * 3,
        compiler_params=PARAMS,
    )(flat, cx, cy)

    def send(value, up, right):
        pairs_ = []
        for w in range(wide):
            for n in range(narrow):
                to = ((w + up) % wide) * narrow + (n + right) % narrow
                pairs_.append((w * narrow + n, to))
        return lax.ppermute(value, ("wide", "narrow"), pairs_)

    def to_both_sides(value, up):
        from_west = send(value, up, 1)
        from_east = from_west if narrow == 2 else send(value, up, -1)
        return from_west, from_east

    from_south = send(north, 1, 0)
    from_north = send(south, -1, 0)
    edge_west, edge_east = to_both_sides(edge, 0)
    corner_sw, corner_se = to_both_sides(north_corner, 1)
    corner_nw, corner_ne = to_both_sides(south_corner, -1)

    decay, source, onehot = pl.pallas_call(
        prep_kernel,
        out_shape=(array(levels, field_pairs, *tile),) * 2
        + (array(rows * cols, cols, dtype=jnp.bfloat16),),
        in_specs=[SMEM, SMEM, VMEM, VMEM],
        out_specs=[VMEM] * 3,
        cost_estimate=pl.CostEstimate(flops=4000000, bytes_accessed=2000000, transcendentals=0),
        compiler_params=PARAMS,
    )(class_coeffs, physics_ref, cloud_class, span_target)

    shifted = pl.pallas_call(
        functools.partial(shift_kernel, levels),
        out_shape=(array(fields * pairs, *tile),) * 2,
        in_specs=[VMEM] * 4,
        out_specs=[VMEM] * 2,
        compiler_params=PARAMS,
    )(flat, edge, edge_west, edge_east)
    sides = pl.pallas_call(
        functools.partial(edge_kernel, levels),
        out_shape=(
            array(fields * half, *tile),
            array(fields * pairs, *tile),
            array(*tile),
        ),
        in_specs=[VMEM] * 7,
        out_specs=[VMEM] * 3,
        compiler_params=PARAMS,
    )(edge, edge_west, edge_east, corner_sw, corner_se, corner_nw, corner_ne)
    state, placed = pl.pallas_call(
        functools.partial(main_kernel, fields, levels),
        out_shape=(array(fields * pairs, *tile), array(wide * rows, cols)),
        in_specs=[VMEM] * 14,
        out_specs=[VMEM] * 2,
        scratch_shapes=[
            pltpu.VMEM((levels, 5) + tile, F32),
            pltpu.VMEM((pairs, 5) + tile, F32),
        ],
        compiler_params=PARAMS,
    )(
        flat,
        cx,
        cy,
        from_south,
        from_north,
        *shifted,
        *sides,
        decay,
        source,
        span_target,
        onehot,
    )
    received = lax.all_to_all(
        placed.reshape(wide, rows, cols), "wide", split_axis=0, concat_axis=0, tiled=True
    )
    span_diag, state = pl.pallas_call(
        finish_kernel,
        out_shape=(array(rows, cols), array(fields * pairs, *tile)),
        in_specs=[VMEM] * 2,
        out_specs=[HBM] * 2,
        scratch_shapes=[pltpu.VMEM((rows, cols), F32), pltpu.SemaphoreType.DMA((2,))],
        compiler_params=PARAMS,
    )(received, state)
    return state.reshape(fields, levels, rows, cols), span_diag


def solution(mesh):
    return jax.shard_map(
        body,
        mesh=mesh,
        in_specs=(
            P(None, None, "wide", "narrow"),
            P(None, "wide", "narrow"),
            P(None, "wide", "narrow"),
            P(),
            P(),
            P("wide", "narrow"),
            P("wide", "narrow"),
        ),
        out_specs=(P(None, None, "wide", "narrow"), P("wide", "narrow")),
        check_vma=False,
    )
```

```python
import functools
import math

import jax
import jax.numpy as jnp
from jax import lax
from jax.experimental import pallas as pl
from jax.experimental.pallas import tpu as pltpu
from jax.sharding import PartitionSpec as P

VMEM = pl.BlockSpec(memory_space=pltpu.VMEM)
HBM = pl.BlockSpec(memory_space=pltpu.HBM)
SMEM = pl.BlockSpec(memory_space=pltpu.SMEM)
F32 = jnp.float32
PARAMS = pltpu.CompilerParams(vmem_limit_bytes=12 * 1024 * 1024)


def sub_roll(value, shift):
    shift = shift % value.shape[0]
    return value if shift == 0 else pltpu.roll(value, shift, 0)


def lane_roll(value, shift):
    shift = shift % value.shape[1]
    return value if shift == 0 else pltpu.roll(value, shift, 1)


def iotas(shape):
    return lax.broadcasted_iota(jnp.int32, shape, 0), lax.broadcasted_iota(jnp.int32, shape, 1)


def pack_rows(tracers, f, pairs, north, south, slot):
    local = iotas(tracers.shape[1:])[0] % (tracers.shape[1] // 2)
    lower = local < tracers.shape[1] // 4
    for k in range(pairs // 2):
        first, second = tracers[f * pairs + 2 * k], tracers[f * pairs + 2 * k + 1]
        north[slot + k] = jnp.where(lower, sub_roll(second, 2), first)
        south[slot + k] = jnp.where(lower, first, sub_roll(second, -2))


def pack_rows_kernel(
    levels, tracers_in, cx_in, cy_in, tracers, cx, cy, north, south, semaphores
):
    copies = [
        pltpu.make_async_copy(source, into, semaphores.at[i])
        for i, (source, into) in enumerate(((tracers_in, tracers), (cx_in, cx), (cy_in, cy)))
    ]
    for copy in copies:
        copy.start()
    for copy in copies:
        copy.wait()
    pairs = levels // 2
    half = pairs // 2
    tile = tracers.shape[1:]
    rows = tile[0] // 2
    local = iotas(tile)[0] % rows
    upper = local >= rows // 2

    def one_row(vectors, row, step):
        packed = []
        for start in range(0, pairs, rows):
            total = vectors[start]
            for t in range(1, rows):
                total = jnp.where(
                    local == row + step * t, sub_roll(vectors[start + t], step * t), total
                )
            packed.append(total)
        return packed

    fields = tracers.shape[0] // pairs
    for f in range(fields):
        pack_rows(tracers, f, pairs, north, south, f * half)
    vectors_x = [cx[k] for k in range(pairs)]
    vectors_y = [cy[k] for k in range(pairs)]
    base = fields * half
    for k in range(half):
        north[base + k] = jnp.where(upper, vectors_y[2 * k], sub_roll(vectors_y[2 * k + 1], 2))
    for k, value in enumerate(one_row(vectors_x, rows - 1, -1)):
        north[base + half + k] = value
    south_rows = one_row(vectors_x, 0, 1) + one_row(vectors_y, 0, 1)
    for k, value in enumerate(south_rows):
        south[base + k] = value


def pack_edges_kernel(levels, tracers, cx, cy, edge, north_corner, south_corner):
    pairs = levels // 2
    fields = tracers.shape[0] // pairs
    tile = tracers.shape[1:]
    rows = tile[0] // 2
    lanes = tile[1]
    group = lanes // levels
    lane = iotas(tile)[1]

    def pack_edge(vectors, slot):
        total = lane_roll(vectors[0], 2)
        for k in range(1, pairs):
            total = jnp.where(
                lane // (2 * group) == k, lane_roll(vectors[k], 2 + 2 * group * k), total
            )
        total = jnp.where(
            lane % (2 * group) < group, total, sub_roll(lane_roll(total, group), rows)
        )
        total = jnp.where(lane % group < group // 2, total, lane_roll(total, group // 2))
        edge[slot] = total
        north_corner[pl.ds(slot, 1), :] = total[rows - 1 : rows]
        south_corner[pl.ds(slot, 1), :] = total[0:1]

    for f in range(fields):
        pack_edge([tracers[f * pairs + k] for k in range(pairs)], f)
    pack_edge([cx[k] for k in range(pairs)], fields)
    pack_edge([cy[k] for k in range(pairs)], fields + 1)


def cosine_sums(values):
    count = len(values)
    if count == 1:
        return values
    half = count // 2
    plus = [values[n] + values[count - 1 - n] for n in range(half)]
    minus = [
        (values[n] - values[count - 1 - n])
        * (0.5 / math.cos(math.pi * (2 * n + 1) / (2 * count)))
        for n in range(half)
    ]
    even = cosine_sums(plus)
    odd = cosine_sums(minus)
    result = []
    for k in range(half):
        result.append(even[k])
        result.append(odd[k] + odd[k + 1] if k + 1 < half else odd[k])
    return result


def cosine_series(values):
    count = len(values)
    if count == 1:
        return values
    half = count // 2
    odd_in = [values[2 * k + 1] + values[2 * k - 1] if k else values[1] for k in range(half)]
    even = cosine_series(values[0::2])
    odd = cosine_series(odd_in)
    odd = [
        odd[n] * (0.5 / math.cos(math.pi * (2 * n + 1) / (2 * count))) for n in range(half)
    ]
    return [even[n] + odd[n] for n in range(half)] + [
        even[n] - odd[n] for n in range(half - 1, -1, -1)
    ]


def prep_kernel(coeffs, profile, klass, target, decay, source, onehot):
    levels, pairs = decay.shape[:2]
    fields = profile.shape[0]
    tile = decay.shape[2:]
    rows, lanes = klass.shape
    sub, lane = iotas(tile)
    low = sub < rows
    kind = jnp.concatenate([klass[...], klass[...]], axis=0)
    is_two = kind == 2
    is_one = kind == 1

    def by_class(which, f):
        return jnp.where(
            is_two,
            coeffs[which, 2, f] * 0.25,
            jnp.where(is_one, coeffs[which, 1, f] * 0.5, coeffs[which, 0, f]),
        )

    for p in range(pairs):
        f1 = 2 * p
        f2 = min(2 * p + 1, fields - 1)
        diffusion = jnp.where(low, by_class(0, f1), by_class(0, f2))
        relax = jnp.where(low, by_class(1, f1), by_class(1, f2))
        waves = cosine_sums([jnp.where(low, profile[f1, l], profile[f2, l]) for l in range(levels)])
        for m in range(levels):
            rate = relax + diffusion * (2.0 - 2.0 * math.cos(math.pi * m / levels))
            once = 1.0 / (1.0 + rate)
            square = once * once
            twice = once + square
            steps = jnp.where(is_two, twice + twice * square, jnp.where(is_one, twice, once))
            steps = steps * ((1.0 if m == 0 else 2.0) / levels)
            decay[m, p] = steps * rate
            source[m, p] = steps * relax * waves[m]
    low_part = target[...] & (lanes - 1)
    slot, _ = iotas((lanes, lanes))
    for r in range(rows):
        hit = jnp.where(slot == low_part[r : r + 1], 1.0, 0.0)
        onehot[r * lanes : (r + 1) * lanes, :] = jnp.transpose(hit).astype(jnp.bfloat16)


def combine(coefs, center, east, west, north, south):
    return (
        coefs[0] * center
        + (coefs[1] * east + coefs[2] * west)
        + (coefs[3] * north + coefs[4] * south)
    )


def coefficients(here_x, west_x, here_y, south_y):
    return (
        1.0
        - jnp.maximum(here_x, 0.0)
        + jnp.minimum(west_x, 0.0)
        - jnp.maximum(here_y, 0.0)
        + jnp.minimum(south_y, 0.0),
        jnp.maximum(-here_x, 0.0),
        jnp.maximum(west_x, 0.0),
        jnp.maximum(-here_y, 0.0),
        jnp.maximum(south_y, 0.0),
    )


def side_by_side(value, place):
    return jnp.where(place == 3, lane_roll(value, -2), value)


def beside(edge, edge_west, edge_east, slot, place):
    from_east = (place == 2) | (place == 3)
    from_west = (place == 4) | (place == 5)
    return jnp.where(
        from_east, edge_east[slot], jnp.where(from_west, edge_west[slot], edge[slot])
    )


def shift_kernel(levels, tracers, edge, edge_west, edge_east, east, west):
    pairs = levels // 2
    tile = tracers.shape[1:]
    rows = tile[0] // 2
    lanes = tile[1]
    group = lanes // levels
    sub, lane = iotas(tile)
    place = lane % group

    def shift_field(f, carried):
        sides = side_by_side(beside(edge, edge_west, edge_east, f, place), place)
        sides = jnp.where(sub < rows, sides, sub_roll(lane_roll(sides, -group), rows))
        for k in range(pairs):
            own = tracers[f * pairs + k]
            here = lane_roll(sides, -(2 * group * k + 3))
            east[f * pairs + k] = jnp.where(lane == lanes - 1, here, lane_roll(own, -1))
            west[f * pairs + k] = jnp.where(lane == 0, here, lane_roll(own, 1))
        return carried

    lax.fori_loop(0, tracers.shape[0] // pairs, shift_field, 0, unroll=True)


def edge_kernel(
    levels,
    edge,
    edge_west,
    edge_east,
    corner_sw,
    corner_se,
    corner_nw,
    corner_ne,
    halo_sides,
    next_sides,
    courant_sides,
):
    tile = edge.shape[1:]
    fields = edge.shape[0] - 2
    pairs = levels // 2
    half = pairs // 2
    rows = tile[0] // 2
    lanes = tile[1]
    group = lanes // levels
    sub, lane = iotas(tile)
    low = sub < rows
    place = lane % group
    east_side = place < group // 2
    odd_sub = sub % 2 == 1
    level_one = (sub == 4) | (sub == 7)
    level_two = (sub == 5) | (sub == 6)
    level_three = (sub == 1) | (sub == 2)

    def corner_rows(slot):
        south = jnp.where(east_side, corner_se[pl.ds(slot, 1), :], corner_sw[pl.ds(slot, 1), :])
        north = jnp.where(east_side, corner_ne[pl.ds(slot, 1), :], corner_nw[pl.ds(slot, 1), :])
        return south, north

    def extended_edge(slot, south, north):
        value = beside(edge, edge_west, edge_east, slot, place)
        value = jnp.where(sub == 2 * rows - 1, south, value)
        return jnp.where(sub == rows, north, value)

    edge_x = extended_edge(fields, *corner_rows(fields))
    edge_y = extended_edge(fields + 1, *corner_rows(fields + 1))
    courant_sides[...] = side_by_side(edge_x, place)
    edge_coefs = coefficients(edge_x, lane_roll(edge_x, 1), edge_y, sub_roll(edge_y, 1))

    def one_field(f, carried):
        south, north = corner_rows(f)
        halo = side_by_side(jnp.where(odd_sub, south, north), place)
        halo = jnp.where(
            level_one,
            lane_roll(halo, -group),
            jnp.where(
                level_two,
                lane_roll(halo, -2 * group),
                jnp.where(level_three, lane_roll(halo, -3 * group), halo),
            ),
        )
        for k in range(half):
            halo_sides[f * half + k] = lane_roll(halo, -(4 * group * k + 3))
        raw = extended_edge(f, south, north)
        moved = side_by_side(
            combine(
                edge_coefs,
                raw,
                lane_roll(raw, -1),
                lane_roll(raw, 1),
                sub_roll(raw, -1),
                sub_roll(raw, 1),
            ),
            place,
        )
        moved = jnp.where(low, moved, sub_roll(lane_roll(moved, -group), rows))
        for k in range(pairs):
            next_sides[f * pairs + k] = lane_roll(moved, -(2 * group * k + 3))
        return carried

    lax.fori_loop(0, fields, one_field, 0, unroll=True)


def transport_and_solve(
    fields,
    levels,
    tracers,
    cx,
    cy,
    from_south,
    from_north,
    east,
    west,
    halo_sides,
    next_sides,
    courant_sides,
    decay,
    source,
    state,
    full_coefs,
    half_coefs,
):
    pairs = levels // 2
    half = pairs // 2
    tile = tracers.shape[1:]
    rows = tile[0] // 2
    lanes = tile[1]
    group = lanes // levels
    sub, lane = iotas(tile)
    local = sub % rows
    low = sub < rows
    lower = local < rows // 2
    first_lane = lane == 0
    last_lane = lane == lanes - 1
    odd_sub = sub % 2 == 1
    north_even = (sub < rows - 1) | (sub == 2 * rows - 1)
    south_even = (sub >= 1) & (sub <= rows)
    north_part = (sub >= 1) & (sub <= rows)
    south_part = (sub < rows - 1) | (sub == 2 * rows - 1)

    sides_x = courant_sides[...]
    sides_x_odd = sub_roll(sides_x, rows)
    base = fields * half
    count = pairs // rows
    for k in range(pairs):
        quad, t = k // rows, k % rows
        row_south = sub_roll(from_south[base + half + quad], rows + t)
        row_north = sub_roll(from_north[base + quad], rows - t)
        halo_x = jnp.where(local == 0, row_north, row_south)
        north_y = sub_roll(from_north[base + count + quad], rows - t)
        south_y = sub_roll(from_south[base + k // 2], rows if k % 2 == 0 else 2)
        halo_y = jnp.where(lower, north_y, south_y)
        own_x = cx[k]
        own_y = cy[k]
        both = []
        for odd in range(2):
            here_x = jnp.where(low, halo_x, own_x) if odd else jnp.where(low, own_x, halo_x)
            here_y = jnp.where(low, halo_y, own_y) if odd else jnp.where(low, own_y, halo_y)
            sides = lane_roll(sides_x_odd if odd else sides_x, -(group * (2 * k + odd) + 3))
            west_x = jnp.where(first_lane, sides, lane_roll(here_x, 1))
            coefs = coefficients(here_x, west_x, here_y, sub_roll(here_y, 1))
            for c in range(5):
                full_coefs[2 * k + odd, c] = coefs[c]
            both.append(coefs)
        for c in range(5):
            half_coefs[k, c] = jnp.where(low, both[0][c], both[1][c])


    def halos(f, k):
        message_south = from_south[f * half + k]
        message_north = from_north[f * half + k]
        center = jnp.where(odd_sub, message_south, message_north)
        sides = halo_sides[f * half + k]
        shifted = (
            jnp.where(last_lane, sides, lane_roll(center, -1)),
            jnp.where(first_lane, sides, lane_roll(center, 1)),
        )
        first = sub_roll(jnp.where(lower, message_north, message_south), rows)
        second = jnp.where(lower, sub_roll(message_north, -2), sub_roll(message_south, 2))
        return (
            (first, *(sub_roll(value, rows) for value in shifted)),
            (
                second,
                *(
                    jnp.where(local == 0, sub_roll(value, -2), sub_roll(value, 2))
                    for value in shifted
                ),
            ),
        )

    def advect(f, k, halo, first_coefs, second_coefs):
        slot = f * pairs + k
        own = (tracers[slot], east[slot], west[slot])
        own_north, own_south = sub_roll(own[0], -1), sub_roll(own[0], 1)
        halo_north, halo_south = sub_roll(halo[0], -1), sub_roll(halo[0], 1)
        even = combine(
            first_coefs[0],
            *(jnp.where(low, mine, other) for mine, other in zip(own, halo)),
            jnp.where(north_even, own_north, halo_north),
            jnp.where(south_even, own_south, halo_south),
        )
        odd = combine(
            first_coefs[1],
            *(jnp.where(low, other, mine) for mine, other in zip(own, halo)),
            jnp.where(north_even, halo_north, own_north),
            jnp.where(south_even, halo_south, own_south),
        )
        center = jnp.where(low, even, odd)
        sides = next_sides[slot]
        return combine(
            second_coefs,
            center,
            jnp.where(last_lane, sides, lane_roll(center, -1)),
            jnp.where(first_lane, sides, lane_roll(center, 1)),
            sub_roll(jnp.where(north_part, even, odd), -1),
            sub_roll(jnp.where(south_part, even, odd), 1),
        )

    def pair_step(p, total):
        f1 = 2 * p
        f2 = jnp.minimum(f1 + 1, fields - 1)
        columns = []
        for k in range(half):
            halo_one, halo_two = halos(f1, k), halos(f2, k)
            for i in range(2):
                j = 2 * k + i
                first_coefs = [[full_coefs[2 * j + odd, c] for c in range(5)] for odd in range(2)]
                second_coefs = [half_coefs[j, c] for c in range(5)]
                one = advect(f1, j, halo_one[i], first_coefs, second_coefs)
                two = advect(f2, j, halo_two[i], first_coefs, second_coefs)
                columns.append(jnp.where(low, one, sub_roll(two, rows)))
                columns.append(jnp.where(low, sub_roll(one, rows), two))
        waves = cosine_sums(columns)
        change = cosine_series([source[m, p] - decay[m, p] * waves[m] for m in range(levels)])
        square = change[0] * change[0]
        for l in range(1, levels):
            square = square + change[l] * change[l]
        for k in range(pairs):
            even, odd = (columns[l] + change[l] for l in (2 * k, 2 * k + 1))
            state[f1 * pairs + k] = jnp.where(low, even, sub_roll(odd, rows))
            state[f2 * pairs + k] = jnp.where(low, sub_roll(even, rows), odd)
        return total + jnp.where(low | (f1 + 1 < fields), square, 0.0)

    return lax.fori_loop(0, (fields + 1) // 2, pair_step, jnp.zeros(tile, F32))


def main_kernel(fields, levels, *refs):
    inputs, (target, onehot), (state, placed), coefs = refs[:12], refs[12:14], refs[14:16], refs[16:]
    rows, lanes = target.shape
    total = transport_and_solve(fields, levels, *inputs, state, *coefs)

    heat = (total + sub_roll(total, rows)) * (1.0 / (fields * levels))
    first = heat.astype(jnp.bfloat16).astype(F32)
    rest = heat - first
    second = rest.astype(jnp.bfloat16).astype(F32)
    third = rest - second
    spans = placed.shape[0]
    slot_row, _ = iotas((spans, lanes))
    high = lax.shift_right_logical(target[...], lanes.bit_length() - 1)
    hits = [slot_row == high[r : r + 1] for r in range(rows)]
    left = jnp.concatenate(
        [
            jnp.concatenate(
                [
                    jnp.where(hits[r], part[r : r + 1], 0.0).astype(jnp.bfloat16)
                    for r in range(rows)
                ],
                axis=1,
            )
            for part in (first, second, third)
        ],
        axis=0,
    )
    result = jnp.dot(left, onehot[...], preferred_element_type=F32)
    placed[...] = result[:spans] + result[spans : 2 * spans] + result[2 * spans :]


def finish_kernel(parts, state, total_out, state_out, total, semaphores):
    copy_state = pltpu.make_async_copy(state, state_out, semaphores.at[0])
    copy_state.start()
    value = parts[0]
    for i in range(1, parts.shape[0]):
        value = value + parts[i]
    total[...] = value
    copy_total = pltpu.make_async_copy(total, total_out, semaphores.at[1])
    copy_total.start()
    copy_state.wait()
    copy_total.wait()


def body(tracers, courant_x, courant_y, physics_ref, class_coeffs, span_target, cloud_class):
    fields, levels, rows, cols = tracers.shape
    wide = lax.axis_size("wide")
    narrow = lax.axis_size("narrow")
    pairs = levels // 2
    half = pairs // 2
    tile = (2 * rows, cols)
    field_pairs = (fields + 1) // 2
    flat = tracers.reshape(fields * pairs, *tile)
    cx = courant_x.reshape(pairs, *tile)
    cy = courant_y.reshape(pairs, *tile)
    quads = pairs // rows
    slots = -(-(fields + 2) // 8) * 8

    def array(*shape, dtype=F32):
        return jax.ShapeDtypeStruct(shape, dtype)

    flat, cx, cy, north, south = pl.pallas_call(
        functools.partial(pack_rows_kernel, levels),
        out_shape=(
            array(fields * pairs, *tile),
            array(pairs, *tile),
            array(pairs, *tile),
            array(fields * half + half + quads, *tile),
            array(fields * half + 2 * quads, *tile),
        ),
        in_specs=[HBM] * 3,
        out_specs=[VMEM] * 5,
        scratch_shapes=[pltpu.SemaphoreType.DMA((3,))],
        compiler_params=PARAMS,
    )(*(pltpu.with_memory_space_constraint(x, pltpu.HBM) for x in (flat, cx, cy)))
    edge, north_corner, south_corner = pl.pallas_call(
        functools.partial(pack_edges_kernel, levels),
        out_shape=(array(fields + 2, *tile), array(slots, cols), array(slots, cols)),
        in_specs=[VMEM] * 3,
        out_specs=[VMEM] * 3,
        compiler_params=PARAMS,
    )(flat, cx, cy)

    def send(value, up, right):
        pairs_ = []
        for w in range(wide):
            for n in range(narrow):
                to = ((w + up) % wide) * narrow + (n + right) % narrow
                pairs_.append((w * narrow + n, to))
        return lax.ppermute(value, ("wide", "narrow"), pairs_)

    def to_both_sides(value, up):
        from_west = send(value, up, 1)
        from_east = from_west if narrow == 2 else send(value, up, -1)
        return from_west, from_east

    from_south = send(north, 1, 0)
    from_north = send(south, -1, 0)
    edge_west, edge_east = to_both_sides(edge, 0)
    corner_sw, corner_se = to_both_sides(north_corner, 1)
    corner_nw, corner_ne = to_both_sides(south_corner, -1)

    decay, source, onehot = pl.pallas_call(
        prep_kernel,
        out_shape=(array(levels, field_pairs, *tile),) * 2
        + (array(rows * cols, cols, dtype=jnp.bfloat16),),
        in_specs=[SMEM, SMEM, VMEM, VMEM],
        out_specs=[VMEM] * 3,
        cost_estimate=pl.CostEstimate(flops=4000000, bytes_accessed=2000000, transcendentals=0),
        compiler_params=PARAMS,
    )(class_coeffs, physics_ref, cloud_class, span_target)

    shifted = pl.pallas_call(
        functools.partial(shift_kernel, levels),
        out_shape=(array(fields * pairs, *tile),) * 2,
        in_specs=[VMEM] * 4,
        out_specs=[VMEM] * 2,
        compiler_params=PARAMS,
    )(flat, edge, edge_west, edge_east)
    sides = pl.pallas_call(
        functools.partial(edge_kernel, levels),
        out_shape=(
            array(fields * half, *tile),
            array(fields * pairs, *tile),
            array(*tile),
        ),
        in_specs=[VMEM] * 7,
        out_specs=[VMEM] * 3,
        compiler_params=PARAMS,
    )(edge, edge_west, edge_east, corner_sw, corner_se, corner_nw, corner_ne)
    state, placed = pl.pallas_call(
        functools.partial(main_kernel, fields, levels),
        out_shape=(array(fields * pairs, *tile), array(wide * rows, cols)),
        in_specs=[VMEM] * 14,
        out_specs=[VMEM] * 2,
        scratch_shapes=[
            pltpu.VMEM((levels, 5) + tile, F32),
            pltpu.VMEM((pairs, 5) + tile, F32),
        ],
        compiler_params=PARAMS,
    )(
        flat,
        cx,
        cy,
        from_south,
        from_north,
        *shifted,
        *sides,
        decay,
        source,
        span_target,
        onehot,
    )
    received = lax.all_to_all(
        placed.reshape(wide, rows, cols), "wide", split_axis=0, concat_axis=0, tiled=True
    )
    span_diag, state = pl.pallas_call(
        finish_kernel,
        out_shape=(array(rows, cols), array(fields * pairs, *tile)),
        in_specs=[VMEM] * 2,
        out_specs=[HBM] * 2,
        scratch_shapes=[pltpu.VMEM((rows, cols), F32), pltpu.SemaphoreType.DMA((2,))],
        compiler_params=PARAMS,
    )(received, state)
    return state.reshape(fields, levels, rows, cols), span_diag


def solution(mesh):
    return jax.shard_map(
        body,
        mesh=mesh,
        in_specs=(
            P(None, None, "wide", "narrow"),
            P(None, "wide", "narrow"),
            P(None, "wide", "narrow"),
            P(),
            P(),
            P("wide", "narrow"),
            P("wide", "narrow"),
        ),
        out_specs=(P(None, None, "wide", "narrow"), P("wide", "narrow")),
        check_vma=False,
    )
```

```python
import functools
import math

import jax
import jax.numpy as jnp
from jax import lax
from jax.experimental import pallas as pl
from jax.experimental.pallas import tpu as pltpu
from jax.sharding import PartitionSpec as P

VMEM = pl.BlockSpec(memory_space=pltpu.VMEM)
HBM = pl.BlockSpec(memory_space=pltpu.HBM)
SMEM = pl.BlockSpec(memory_space=pltpu.SMEM)
F32 = jnp.float32
PARAMS = pltpu.CompilerParams(vmem_limit_bytes=12 * 1024 * 1024)


def sub_roll(value, shift):
    shift = shift % value.shape[0]
    return value if shift == 0 else pltpu.roll(value, shift, 0)


def lane_roll(value, shift):
    shift = shift % value.shape[1]
    return value if shift == 0 else pltpu.roll(value, shift, 1)


def iotas(shape):
    return lax.broadcasted_iota(jnp.int32, shape, 0), lax.broadcasted_iota(jnp.int32, shape, 1)


def pack_rows(tracers, f, pairs, north, south, slot):
    local = iotas(tracers.shape[1:])[0] % (tracers.shape[1] // 2)
    lower = local < tracers.shape[1] // 4
    for k in range(pairs // 2):
        first, second = tracers[f * pairs + 2 * k], tracers[f * pairs + 2 * k + 1]
        north[slot + k] = jnp.where(lower, sub_roll(second, 2), first)
        south[slot + k] = jnp.where(lower, first, sub_roll(second, -2))


def pack_rows_kernel(
    levels, tracers_in, cx_in, cy_in, tracers, cx, cy, north, south, semaphores
):
    copies = [
        pltpu.make_async_copy(source, into, semaphores.at[i])
        for i, (source, into) in enumerate(((tracers_in, tracers), (cx_in, cx), (cy_in, cy)))
    ]
    for copy in copies:
        copy.start()
    for copy in copies:
        copy.wait()
    pairs = levels // 2
    half = pairs // 2
    tile = tracers.shape[1:]
    rows = tile[0] // 2
    local = iotas(tile)[0] % rows
    upper = local >= rows // 2

    def one_row(vectors, row, step):
        packed = []
        for start in range(0, pairs, rows):
            total = vectors[start]
            for t in range(1, rows):
                total = jnp.where(
                    local == row + step * t, sub_roll(vectors[start + t], step * t), total
                )
            packed.append(total)
        return packed

    fields = tracers.shape[0] // pairs
    for f in range(fields):
        pack_rows(tracers, f, pairs, north, south, f * half)
    vectors_x = [cx[k] for k in range(pairs)]
    vectors_y = [cy[k] for k in range(pairs)]
    base = fields * half
    for k in range(half):
        north[base + k] = jnp.where(upper, vectors_y[2 * k], sub_roll(vectors_y[2 * k + 1], 2))
    for k, value in enumerate(one_row(vectors_x, rows - 1, -1)):
        north[base + half + k] = value
    south_rows = one_row(vectors_x, 0, 1) + one_row(vectors_y, 0, 1)
    for k, value in enumerate(south_rows):
        south[base + k] = value


def pack_edges_kernel(levels, tracers, cx, cy, edge, north_corner, south_corner):
    pairs = levels // 2
    half = pairs // 2
    fields = tracers.shape[0] // pairs
    tile = tracers.shape[1:]
    rows = tile[0] // 2
    lanes = tile[1]
    group = lanes // levels
    sub, lane = iotas(tile)
    upper = sub % rows >= rows // 2
    corners = [jnp.zeros(tile, F32), jnp.zeros(tile, F32)]

    def pack_edge(vectors, slot):
        total = lane_roll(vectors[0], 2)
        for k in range(1, pairs):
            total = jnp.where(
                lane // (2 * group) == k, lane_roll(vectors[k], 2 + 2 * group * k), total
            )
        total = jnp.where(
            lane % (2 * group) < group, total, sub_roll(lane_roll(total, group), rows)
        )
        edge[slot] = jnp.where(lane % group < group // 2, total, lane_roll(total, group // 2))
        for k in range(half):
            one, two = vectors[2 * k], vectors[2 * k + 1]
            place = slot * half + k
            north = jnp.where(upper, one, sub_roll(two, 2))
            south = jnp.where(upper, sub_roll(two, -2), one)
            for i, value in enumerate((north, south)):
                corners[i] = jnp.where(
                    lane // 2 == place, lane_roll(value, 2 * place + 1), corners[i]
                )

    for f in range(fields):
        pack_edge([tracers[f * pairs + k] for k in range(pairs)], f)
    pack_edge([cx[k] for k in range(pairs)], fields)
    pack_edge([cy[k] for k in range(pairs)], fields + 1)
    north_corner[...] = corners[0]
    south_corner[...] = corners[1]


def cosine_sums(values):
    count = len(values)
    if count == 1:
        return values
    half = count // 2
    plus = [values[n] + values[count - 1 - n] for n in range(half)]
    minus = [
        (values[n] - values[count - 1 - n])
        * (0.5 / math.cos(math.pi * (2 * n + 1) / (2 * count)))
        for n in range(half)
    ]
    even = cosine_sums(plus)
    odd = cosine_sums(minus)
    result = []
    for k in range(half):
        result.append(even[k])
        result.append(odd[k] + odd[k + 1] if k + 1 < half else odd[k])
    return result


def cosine_series(values):
    count = len(values)
    if count == 1:
        return values
    half = count // 2
    odd_in = [values[2 * k + 1] + values[2 * k - 1] if k else values[1] for k in range(half)]
    even = cosine_series(values[0::2])
    odd = cosine_series(odd_in)
    odd = [
        odd[n] * (0.5 / math.cos(math.pi * (2 * n + 1) / (2 * count))) for n in range(half)
    ]
    return [even[n] + odd[n] for n in range(half)] + [
        even[n] - odd[n] for n in range(half - 1, -1, -1)
    ]


def prep_kernel(coeffs, profile, klass, target, decay, source, onehot):
    levels, pairs = decay.shape[:2]
    fields = profile.shape[0]
    tile = decay.shape[2:]
    rows, lanes = klass.shape
    sub, lane = iotas(tile)
    low = sub < rows
    kind = jnp.concatenate([klass[...], klass[...]], axis=0)
    is_two = kind == 2
    is_one = kind == 1

    def by_class(which, f):
        return jnp.where(
            is_two,
            coeffs[which, 2, f] * 0.25,
            jnp.where(is_one, coeffs[which, 1, f] * 0.5, coeffs[which, 0, f]),
        )

    for p in range(pairs):
        f1 = 2 * p
        f2 = min(2 * p + 1, fields - 1)
        diffusion = jnp.where(low, by_class(0, f1), by_class(0, f2))
        relax = jnp.where(low, by_class(1, f1), by_class(1, f2))
        waves = cosine_sums([jnp.where(low, profile[f1, l], profile[f2, l]) for l in range(levels)])
        for m in range(levels):
            rate = relax + diffusion * (2.0 - 2.0 * math.cos(math.pi * m / levels))
            once = 1.0 / (1.0 + rate)
            square = once * once
            twice = once + square
            steps = jnp.where(is_two, twice + twice * square, jnp.where(is_one, twice, once))
            steps = steps * ((1.0 if m == 0 else 2.0) / levels)
            decay[m, p] = steps * rate
            source[m, p] = steps * relax * waves[m]
    low_part = target[...] & (lanes - 1)
    slot, _ = iotas((lanes, lanes))
    for r in range(rows):
        hit = jnp.where(slot == low_part[r : r + 1], 1.0, 0.0)
        onehot[r * lanes : (r + 1) * lanes, :] = jnp.transpose(hit).astype(jnp.bfloat16)


def combine(coefs, center, east, west, north, south):
    return (
        coefs[0] * center
        + (coefs[1] * east + coefs[2] * west)
        + (coefs[3] * north + coefs[4] * south)
    )


def coefficients(here_x, west_x, here_y, south_y):
    return (
        1.0
        - jnp.maximum(here_x, 0.0)
        + jnp.minimum(west_x, 0.0)
        - jnp.maximum(here_y, 0.0)
        + jnp.minimum(south_y, 0.0),
        jnp.maximum(-here_x, 0.0),
        jnp.maximum(west_x, 0.0),
        jnp.maximum(-here_y, 0.0),
        jnp.maximum(south_y, 0.0),
    )


def side_by_side(value, place):
    return jnp.where(place == 3, lane_roll(value, -2), value)


def beside(edge, edge_west, edge_east, slot, place):
    from_east = (place == 2) | (place == 3)
    from_west = (place == 4) | (place == 5)
    return jnp.where(
        from_east, edge_east[slot], jnp.where(from_west, edge_west[slot], edge[slot])
    )


def shift_kernel(
    levels,
    tracers,
    cx,
    cy,
    edge,
    edge_west,
    edge_east,
    east,
    west,
    next_sides,
    west_x,
    sides_y,
):
    pairs = levels // 2
    fields = tracers.shape[0] // pairs
    tile = tracers.shape[1:]
    rows = tile[0] // 2
    lanes = tile[1]
    group = lanes // levels
    sub, lane = iotas(tile)
    low = sub < rows
    place = lane % group

    def own_rows(slot):
        return jnp.where(low, beside(edge, edge_west, edge_east, slot, place), 0.0)

    def spread(value):
        value = side_by_side(value, place)
        value = jnp.where(low, value, sub_roll(lane_roll(value, -group), rows))
        return [lane_roll(value, -(2 * group * k + 3)) for k in range(pairs)]

    edge_x = own_rows(fields)
    edge_y = own_rows(fields + 1)
    coefs = coefficients(edge_x, lane_roll(edge_x, 1), edge_y, sub_roll(edge_y, 1))
    for k, sides in enumerate(spread(edge_x)):
        west_x[k] = jnp.where(lane == 0, sides, lane_roll(cx[k], 1))
    for k, sides in enumerate(spread(edge_y)):
        sides_y[k] = sides
    for f in range(fields):
        raw = own_rows(f)
        for k, sides in enumerate(spread(raw)):
            own = tracers[f * pairs + k]
            east[f * pairs + k] = jnp.where(lane == lanes - 1, sides, lane_roll(own, -1))
            west[f * pairs + k] = jnp.where(lane == 0, sides, lane_roll(own, 1))
        moved = combine(
            coefs,
            raw,
            lane_roll(raw, -1),
            lane_roll(raw, 1),
            sub_roll(raw, -1),
            sub_roll(raw, 1),
        )
        for k, sides in enumerate(spread(moved)):
            next_sides[f * pairs + k] = sides


def transport_and_solve(
    fields,
    levels,
    tracers,
    cx,
    cy,
    from_south,
    from_north,
    east,
    west,
    next_sides,
    west_x,
    sides_y,
    corner_sw,
    corner_se,
    corner_nw,
    corner_ne,
    decay,
    source,
    state,
    full_coefs,
    half_coefs,
):
    pairs = levels // 2
    half = pairs // 2
    tile = tracers.shape[1:]
    rows = tile[0] // 2
    lanes = tile[1]
    group = lanes // levels
    sub, lane = iotas(tile)
    local = sub % rows
    low = sub < rows
    lower = local < rows // 2
    first_lane = lane == 0
    last_lane = lane == lanes - 1
    odd_sub = sub % 2 == 1
    north_even = (sub < rows - 1) | (sub == 2 * rows - 1)
    south_even = (sub >= 1) & (sub <= rows)
    north_part = (sub >= 1) & (sub <= rows)
    south_part = (sub < rows - 1) | (sub == 2 * rows - 1)

    even_lane = lane % 2 == 0
    dense = jnp.where(
        odd_sub,
        jnp.where(even_lane, lane_roll(corner_se[...], -1), lane_roll(corner_sw[...], 1)),
        jnp.where(even_lane, lane_roll(corner_ne[...], -1), lane_roll(corner_nw[...], 1)),
    )

    def corner(slot, k):
        return pltpu.roll(dense, lanes - 2 * (slot * half + k) - 1, 1)

    def to_halo(value, k):
        if k % 2 == 0:
            return sub_roll(value, rows)
        return jnp.where(local == 0, sub_roll(value, -2), sub_roll(value, 2))

    def to_ends(value, k):
        down, up = sub_roll(value, 1 - rows), sub_roll(value, rows - 1)
        return jnp.where(local == 0, down, up) if k % 2 == 0 else jnp.where(local == 0, up, down)

    base = fields * half
    count = pairs // rows
    for k in range(pairs):
        quad, t = k // rows, k % rows
        row_south = sub_roll(from_south[base + half + quad], rows + t)
        row_north = sub_roll(from_north[base + quad], rows - t)
        halo_x = jnp.where(local == 0, row_north, row_south)
        north_y = sub_roll(from_north[base + count + quad], rows - t)
        south_y = sub_roll(from_south[base + k // 2], rows if k % 2 == 0 else 2)
        halo_y = jnp.where(lower, north_y, south_y)
        own_x = cx[k]
        own_y = cy[k]
        own_west = west_x[k]
        halo_west = jnp.where(
            first_lane, to_halo(corner(fields, k // 2), k), lane_roll(halo_x, 1)
        )
        both = []
        for odd in range(2):
            here_x = jnp.where(low, halo_x, own_x) if odd else jnp.where(low, own_x, halo_x)
            here_y = jnp.where(low, halo_y, own_y) if odd else jnp.where(low, own_y, halo_y)
            west_face = (
                jnp.where(low, halo_west, own_west) if odd else jnp.where(low, own_west, halo_west)
            )
            coefs = coefficients(here_x, west_face, here_y, sub_roll(here_y, 1))
            for c in range(5):
                full_coefs[2 * k + odd, c] = coefs[c]
            both.append(coefs)
        for c in range(5):
            half_coefs[k, c] = jnp.where(low, both[0][c], both[1][c])
        south_face = to_ends(corner(fields + 1, k // 2), k)
        half_coefs[k, 5] = jnp.where(local == 0, jnp.minimum(south_face, 0.0), 0.0)
        half_coefs[k, 6] = jnp.where(
            local == 0,
            jnp.maximum(south_face, 0.0),
            jnp.where(local == rows - 1, jnp.maximum(-sides_y[k], 0.0), 0.0),
        )

    def halos(f, k):
        message_south = from_south[f * half + k]
        message_north = from_north[f * half + k]
        center = jnp.where(odd_sub, message_south, message_north)
        sides = corner(f, k)
        shifted = (
            jnp.where(last_lane, sides, lane_roll(center, -1)),
            jnp.where(first_lane, sides, lane_roll(center, 1)),
        )
        first = sub_roll(jnp.where(lower, message_north, message_south), rows)
        second = jnp.where(lower, sub_roll(message_north, -2), sub_roll(message_south, 2))
        return tuple(
            (here, *(to_halo(value, i) for value in shifted), to_ends(sides, i))
            for i, here in enumerate((first, second))
        )

    def advect(f, k, halo, first_coefs, second_coefs):
        slot = f * pairs + k
        own = (tracers[slot], east[slot], west[slot])
        own_north, own_south = sub_roll(own[0], -1), sub_roll(own[0], 1)
        halo_north, halo_south = sub_roll(halo[0], -1), sub_roll(halo[0], 1)
        even = combine(
            first_coefs[0],
            *(jnp.where(low, mine, other) for mine, other in zip(own, halo[:3])),
            jnp.where(north_even, own_north, halo_north),
            jnp.where(south_even, own_south, halo_south),
        )
        odd = combine(
            first_coefs[1],
            *(jnp.where(low, other, mine) for mine, other in zip(own, halo[:3])),
            jnp.where(north_even, halo_north, own_north),
            jnp.where(south_even, halo_south, own_south),
        )
        center = jnp.where(low, even, odd)
        sides = (
            next_sides[slot]
            + second_coefs[5] * jnp.where(first_lane, own[2], own[1])
            + second_coefs[6] * halo[3]
        )
        return combine(
            second_coefs,
            center,
            jnp.where(last_lane, sides, lane_roll(center, -1)),
            jnp.where(first_lane, sides, lane_roll(center, 1)),
            sub_roll(jnp.where(north_part, even, odd), -1),
            sub_roll(jnp.where(south_part, even, odd), 1),
        )

    def pair_step(p, total):
        f1 = 2 * p
        f2 = jnp.minimum(f1 + 1, fields - 1)
        columns = []
        for k in range(half):
            halo_one, halo_two = halos(f1, k), halos(f2, k)
            for i in range(2):
                j = 2 * k + i
                first_coefs = [[full_coefs[2 * j + odd, c] for c in range(5)] for odd in range(2)]
                second_coefs = [half_coefs[j, c] for c in range(7)]
                one = advect(f1, j, halo_one[i], first_coefs, second_coefs)
                two = advect(f2, j, halo_two[i], first_coefs, second_coefs)
                columns.append(jnp.where(low, one, sub_roll(two, rows)))
                columns.append(jnp.where(low, sub_roll(one, rows), two))
        waves = cosine_sums(columns)
        change = cosine_series([source[m, p] - decay[m, p] * waves[m] for m in range(levels)])
        square = change[0] * change[0]
        for l in range(1, levels):
            square = square + change[l] * change[l]
        for k in range(pairs):
            even, odd = (columns[l] + change[l] for l in (2 * k, 2 * k + 1))
            state[f1 * pairs + k] = jnp.where(low, even, sub_roll(odd, rows))
            state[f2 * pairs + k] = jnp.where(low, sub_roll(even, rows), odd)
        return total + jnp.where(low | (f1 + 1 < fields), square, 0.0)

    return lax.fori_loop(0, (fields + 1) // 2, pair_step, jnp.zeros(tile, F32))


def main_kernel(fields, levels, *refs):
    inputs, (target, onehot), (state, placed), coefs = refs[:16], refs[16:18], refs[18:20], refs[20:]
    rows, lanes = target.shape
    total = transport_and_solve(fields, levels, *inputs, state, *coefs)

    heat = (total + sub_roll(total, rows)) * (1.0 / (fields * levels))
    first = heat.astype(jnp.bfloat16).astype(F32)
    rest = heat - first
    second = rest.astype(jnp.bfloat16).astype(F32)
    third = rest - second
    spans = placed.shape[0]
    slot_row, _ = iotas((spans, lanes))
    high = lax.shift_right_logical(target[...], lanes.bit_length() - 1)
    hits = [slot_row == high[r : r + 1] for r in range(rows)]
    left = jnp.concatenate(
        [
            jnp.concatenate(
                [
                    jnp.where(hits[r], part[r : r + 1], 0.0).astype(jnp.bfloat16)
                    for r in range(rows)
                ],
                axis=1,
            )
            for part in (first, second, third)
        ],
        axis=0,
    )
    result = jnp.dot(left, onehot[...], preferred_element_type=F32)
    placed[...] = result[:spans] + result[spans : 2 * spans] + result[2 * spans :]


def finish_kernel(parts, state, total_out, state_out, total, semaphores):
    copy_state = pltpu.make_async_copy(state, state_out, semaphores.at[0])
    copy_state.start()
    value = parts[0]
    for i in range(1, parts.shape[0]):
        value = value + parts[i]
    total[...] = value
    copy_total = pltpu.make_async_copy(total, total_out, semaphores.at[1])
    copy_total.start()
    copy_state.wait()
    copy_total.wait()


def body(tracers, courant_x, courant_y, physics_ref, class_coeffs, span_target, cloud_class):
    fields, levels, rows, cols = tracers.shape
    wide = lax.axis_size("wide")
    narrow = lax.axis_size("narrow")
    pairs = levels // 2
    half = pairs // 2
    tile = (2 * rows, cols)
    field_pairs = (fields + 1) // 2
    flat = tracers.reshape(fields * pairs, *tile)
    cx = courant_x.reshape(pairs, *tile)
    cy = courant_y.reshape(pairs, *tile)
    quads = pairs // rows

    def array(*shape, dtype=F32):
        return jax.ShapeDtypeStruct(shape, dtype)

    flat, cx, cy, north, south = pl.pallas_call(
        functools.partial(pack_rows_kernel, levels),
        out_shape=(
            array(fields * pairs, *tile),
            array(pairs, *tile),
            array(pairs, *tile),
            array(fields * half + half + quads, *tile),
            array(fields * half + 2 * quads, *tile),
        ),
        in_specs=[HBM] * 3,
        out_specs=[VMEM] * 5,
        scratch_shapes=[pltpu.SemaphoreType.DMA((3,))],
        compiler_params=PARAMS,
    )(*(pltpu.with_memory_space_constraint(x, pltpu.HBM) for x in (flat, cx, cy)))
    edge, north_corner, south_corner = pl.pallas_call(
        functools.partial(pack_edges_kernel, levels),
        out_shape=(array(fields + 2, *tile), array(*tile), array(*tile)),
        in_specs=[VMEM] * 3,
        out_specs=[VMEM] * 3,
        compiler_params=PARAMS,
    )(flat, cx, cy)

    def send(value, up, right):
        pairs_ = []
        for w in range(wide):
            for n in range(narrow):
                to = ((w + up) % wide) * narrow + (n + right) % narrow
                pairs_.append((w * narrow + n, to))
        return lax.ppermute(value, ("wide", "narrow"), pairs_)

    def to_both_sides(value, up):
        from_west = send(value, up, 1)
        from_east = from_west if narrow == 2 else send(value, up, -1)
        return from_west, from_east

    from_south = send(north, 1, 0)
    from_north = send(south, -1, 0)
    edge_west, edge_east = to_both_sides(edge, 0)
    corner_sw, corner_se = to_both_sides(north_corner, 1)
    corner_nw, corner_ne = to_both_sides(south_corner, -1)

    decay, source, onehot = pl.pallas_call(
        prep_kernel,
        out_shape=(array(levels, field_pairs, *tile),) * 2
        + (array(rows * cols, cols, dtype=jnp.bfloat16),),
        in_specs=[SMEM, SMEM, VMEM, VMEM],
        out_specs=[VMEM] * 3,
        cost_estimate=pl.CostEstimate(flops=4000000, bytes_accessed=2000000, transcendentals=0),
        compiler_params=PARAMS,
    )(class_coeffs, physics_ref, cloud_class, span_target)

    beside_own = pl.pallas_call(
        functools.partial(shift_kernel, levels),
        out_shape=(array(fields * pairs, *tile),) * 3 + (array(pairs, *tile),) * 2,
        in_specs=[VMEM] * 6,
        out_specs=[VMEM] * 5,
        compiler_params=PARAMS,
    )(flat, cx, cy, edge, edge_west, edge_east)
    state, placed = pl.pallas_call(
        functools.partial(main_kernel, fields, levels),
        out_shape=(array(fields * pairs, *tile), array(wide * rows, cols)),
        in_specs=[VMEM] * 18,
        out_specs=[VMEM] * 2,
        scratch_shapes=[
            pltpu.VMEM((levels, 5) + tile, F32),
            pltpu.VMEM((pairs, 7) + tile, F32),
        ],
        compiler_params=PARAMS,
    )(
        flat,
        cx,
        cy,
        from_south,
        from_north,
        *beside_own,
        corner_sw,
        corner_se,
        corner_nw,
        corner_ne,
        decay,
        source,
        span_target,
        onehot,
    )
    received = lax.all_to_all(
        placed.reshape(wide, rows, cols), "wide", split_axis=0, concat_axis=0, tiled=True
    )
    span_diag, state = pl.pallas_call(
        finish_kernel,
        out_shape=(array(rows, cols), array(fields * pairs, *tile)),
        in_specs=[VMEM] * 2,
        out_specs=[HBM] * 2,
        scratch_shapes=[pltpu.VMEM((rows, cols), F32), pltpu.SemaphoreType.DMA((2,))],
        compiler_params=PARAMS,
    )(received, state)
    return state.reshape(fields, levels, rows, cols), span_diag


def solution(mesh):
    return jax.shard_map(
        body,
        mesh=mesh,
        in_specs=(
            P(None, None, "wide", "narrow"),
            P(None, "wide", "narrow"),
            P(None, "wide", "narrow"),
            P(),
            P(),
            P("wide", "narrow"),
            P("wide", "narrow"),
        ),
        out_specs=(P(None, None, "wide", "narrow"), P("wide", "narrow")),
        check_vma=False,
    )
```

```python
import functools
import math

import jax
import jax.numpy as jnp
from jax import lax
from jax.experimental import pallas as pl
from jax.experimental.pallas import tpu as pltpu
from jax.sharding import PartitionSpec as P

VMEM = pl.BlockSpec(memory_space=pltpu.VMEM)
HBM = pl.BlockSpec(memory_space=pltpu.HBM)
SMEM = pl.BlockSpec(memory_space=pltpu.SMEM)
F32 = jnp.float32
PARAMS = pltpu.CompilerParams(vmem_limit_bytes=12 * 1024 * 1024)


def sub_roll(value, shift):
    shift = shift % value.shape[0]
    return value if shift == 0 else pltpu.roll(value, shift, 0)


def lane_roll(value, shift):
    shift = shift % value.shape[1]
    return value if shift == 0 else pltpu.roll(value, shift, 1)


def iotas(shape):
    return lax.broadcasted_iota(jnp.int32, shape, 0), lax.broadcasted_iota(jnp.int32, shape, 1)


def pack_rows(tracers, f, pairs, north, south, slot):
    local = iotas(tracers.shape[1:])[0] % (tracers.shape[1] // 2)
    lower = local < tracers.shape[1] // 4
    for k in range(pairs // 2):
        first, second = tracers[f * pairs + 2 * k], tracers[f * pairs + 2 * k + 1]
        north[slot + k] = jnp.where(lower, sub_roll(second, 2), first)
        south[slot + k] = jnp.where(lower, first, sub_roll(second, -2))


def pack_rows_kernel(
    levels, tracers_in, cx_in, cy_in, tracers, cx, cy, north, south, semaphores
):
    copies = [
        pltpu.make_async_copy(source, into, semaphores.at[i])
        for i, (source, into) in enumerate(((tracers_in, tracers), (cx_in, cx), (cy_in, cy)))
    ]
    for copy in copies:
        copy.start()
    for copy in copies:
        copy.wait()
    pairs = levels // 2
    half = pairs // 2
    tile = tracers.shape[1:]
    rows = tile[0] // 2
    local = iotas(tile)[0] % rows
    upper = local >= rows // 2

    def one_row(vectors, row, step):
        packed = []
        for start in range(0, pairs, rows):
            total = vectors[start]
            for t in range(1, rows):
                total = jnp.where(
                    local == row + step * t, sub_roll(vectors[start + t], step * t), total
                )
            packed.append(total)
        return packed

    fields = tracers.shape[0] // pairs
    for f in range(fields):
        pack_rows(tracers, f, pairs, north, south, f * half)
    vectors_x = [cx[k] for k in range(pairs)]
    vectors_y = [cy[k] for k in range(pairs)]
    base = fields * half
    for k in range(half):
        north[base + k] = jnp.where(upper, vectors_y[2 * k], sub_roll(vectors_y[2 * k + 1], 2))
    for k, value in enumerate(one_row(vectors_x, rows - 1, -1)):
        north[base + half + k] = value
    south_rows = one_row(vectors_x, 0, 1) + one_row(vectors_y, 0, 1)
    for k, value in enumerate(south_rows):
        south[base + k] = value


def pack_edges_kernel(levels, tracers, cx, cy, edge, corner):
    pairs = levels // 2
    half = pairs // 2
    fields = tracers.shape[0] // pairs
    tile = tracers.shape[1:]
    rows = tile[0] // 2
    lanes = tile[1]
    group = lanes // levels
    sub, lane = iotas(tile)
    upper = sub % rows >= rows // 2
    odd_sub = sub % 2 == 1
    corners = [jnp.zeros(tile, F32)]

    def pack_edge(vectors, slot):
        total = lane_roll(vectors[0], 2)
        for k in range(1, pairs):
            total = jnp.where(
                lane // (2 * group) == k, lane_roll(vectors[k], 2 + 2 * group * k), total
            )
        total = jnp.where(
            lane % (2 * group) < group, total, sub_roll(lane_roll(total, group), rows)
        )
        edge[slot] = jnp.where(lane % group < group // 2, total, lane_roll(total, group // 2))
        for k in range(half):
            one, two = vectors[2 * k], vectors[2 * k + 1]
            place = slot * half + k
            north = jnp.where(upper, one, sub_roll(two, 2))
            south = jnp.where(upper, sub_roll(two, -2), one)
            value = lane_roll(jnp.where(odd_sub, north, south), 2 * place + 1)
            corners[0] = jnp.where(lane // 2 == place, value, corners[0])

    for f in range(fields):
        pack_edge([tracers[f * pairs + k] for k in range(pairs)], f)
    pack_edge([cx[k] for k in range(pairs)], fields)
    pack_edge([cy[k] for k in range(pairs)], fields + 1)
    corner[...] = corners[0]


def cosine_sums(values):
    count = len(values)
    if count == 1:
        return values
    half = count // 2
    plus = [values[n] + values[count - 1 - n] for n in range(half)]
    minus = [
        (values[n] - values[count - 1 - n])
        * (0.5 / math.cos(math.pi * (2 * n + 1) / (2 * count)))
        for n in range(half)
    ]
    even = cosine_sums(plus)
    odd = cosine_sums(minus)
    result = []
    for k in range(half):
        result.append(even[k])
        result.append(odd[k] + odd[k + 1] if k + 1 < half else odd[k])
    return result


def cosine_series(values):
    count = len(values)
    if count == 1:
        return values
    half = count // 2
    odd_in = [values[2 * k + 1] + values[2 * k - 1] if k else values[1] for k in range(half)]
    even = cosine_series(values[0::2])
    odd = cosine_series(odd_in)
    odd = [
        odd[n] * (0.5 / math.cos(math.pi * (2 * n + 1) / (2 * count))) for n in range(half)
    ]
    return [even[n] + odd[n] for n in range(half)] + [
        even[n] - odd[n] for n in range(half - 1, -1, -1)
    ]


def prep_kernel(coeffs, profile, klass, target, decay, source, onehot):
    levels, pairs = decay.shape[:2]
    fields = profile.shape[0]
    tile = decay.shape[2:]
    rows, lanes = klass.shape
    sub, lane = iotas(tile)
    low = sub < rows
    kind = jnp.concatenate([klass[...], klass[...]], axis=0)
    is_two = kind == 2
    is_one = kind == 1

    def by_class(which, f):
        return jnp.where(
            is_two,
            coeffs[which, 2, f] * 0.25,
            jnp.where(is_one, coeffs[which, 1, f] * 0.5, coeffs[which, 0, f]),
        )

    for p in range(pairs):
        f1 = 2 * p
        f2 = min(2 * p + 1, fields - 1)
        diffusion = jnp.where(low, by_class(0, f1), by_class(0, f2))
        relax = jnp.where(low, by_class(1, f1), by_class(1, f2))
        waves = cosine_sums([jnp.where(low, profile[f1, l], profile[f2, l]) for l in range(levels)])
        for m in range(levels):
            rate = relax + diffusion * (2.0 - 2.0 * math.cos(math.pi * m / levels))
            once = 1.0 / (1.0 + rate)
            square = once * once
            twice = once + square
            steps = jnp.where(is_two, twice + twice * square, jnp.where(is_one, twice, once))
            steps = steps * ((1.0 if m == 0 else 2.0) / levels)
            decay[m, p] = steps * rate
            source[m, p] = steps * relax * waves[m]
    low_part = target[...] & (lanes - 1)
    slot, _ = iotas((lanes, lanes))
    for r in range(rows):
        hit = jnp.where(slot == low_part[r : r + 1], 1.0, 0.0)
        onehot[r * lanes : (r + 1) * lanes, :] = jnp.transpose(hit).astype(jnp.bfloat16)


def combine(coefs, center, east, west, north, south):
    return (
        coefs[0] * center
        + (coefs[1] * east + coefs[2] * west)
        + (coefs[3] * north + coefs[4] * south)
    )


def coefficients(here_x, west_x, here_y, south_y):
    return (
        1.0
        - jnp.maximum(here_x, 0.0)
        + jnp.minimum(west_x, 0.0)
        - jnp.maximum(here_y, 0.0)
        + jnp.minimum(south_y, 0.0),
        jnp.maximum(-here_x, 0.0),
        jnp.maximum(west_x, 0.0),
        jnp.maximum(-here_y, 0.0),
        jnp.maximum(south_y, 0.0),
    )


def side_by_side(value, place):
    return jnp.where(place == 3, lane_roll(value, -2), value)


def beside(edge, edge_west, edge_east, slot, place):
    from_east = (place == 2) | (place == 3)
    from_west = (place == 4) | (place == 5)
    return jnp.where(
        from_east, edge_east[slot], jnp.where(from_west, edge_west[slot], edge[slot])
    )


def spread(value, levels):
    lanes = value.shape[1]
    rows = value.shape[0] // 2
    group = lanes // levels
    sub, lane = iotas(value.shape)
    value = side_by_side(value, lane % group)
    value = jnp.where(sub < rows, value, sub_roll(lane_roll(value, -group), rows))
    return [lane_roll(value, -(2 * group * k + 3)) for k in range(levels // 2)]


def shift_kernel(levels, tracers, edge, edge_west, edge_east, east, west):
    pairs = levels // 2
    tile = tracers.shape[1:]
    lanes = tile[1]
    lane = iotas(tile)[1]
    place = lane % (lanes // levels)
    for f in range(tracers.shape[0] // pairs):
        for k, sides in enumerate(spread(beside(edge, edge_west, edge_east, f, place), levels)):
            own = tracers[f * pairs + k]
            east[f * pairs + k] = jnp.where(lane == lanes - 1, sides, lane_roll(own, -1))
            west[f * pairs + k] = jnp.where(lane == 0, sides, lane_roll(own, 1))


def next_kernel(levels, cx, edge, edge_west, edge_east, next_sides, west_x, sides_y):
    pairs = levels // 2
    fields = next_sides.shape[0] // pairs
    tile = cx.shape[1:]
    rows = tile[0] // 2
    sub, lane = iotas(tile)
    place = lane % (tile[1] // levels)

    def own_rows(slot):
        value = beside(edge, edge_west, edge_east, slot, place)
        return jnp.where(sub < rows, value, 0.0)

    edge_x = own_rows(fields)
    edge_y = own_rows(fields + 1)
    coefs = coefficients(edge_x, lane_roll(edge_x, 1), edge_y, sub_roll(edge_y, 1))
    for k, sides in enumerate(spread(edge_x, levels)):
        west_x[k] = jnp.where(lane == 0, sides, lane_roll(cx[k], 1))
    for k, sides in enumerate(spread(edge_y, levels)):
        sides_y[k] = sides
    for f in range(fields):
        raw = own_rows(f)
        moved = combine(
            coefs,
            raw,
            lane_roll(raw, -1),
            lane_roll(raw, 1),
            sub_roll(raw, -1),
            sub_roll(raw, 1),
        )
        for k, sides in enumerate(spread(moved, levels)):
            next_sides[f * pairs + k] = sides


def transport_and_solve(
    fields,
    levels,
    tracers,
    cx,
    cy,
    from_south,
    from_north,
    east,
    west,
    next_sides,
    west_x,
    sides_y,
    corner_sw,
    corner_se,
    corner_nw,
    corner_ne,
    decay,
    source,
    state,
    full_coefs,
    half_coefs,
):
    pairs = levels // 2
    half = pairs // 2
    tile = tracers.shape[1:]
    rows = tile[0] // 2
    lanes = tile[1]
    group = lanes // levels
    sub, lane = iotas(tile)
    local = sub % rows
    low = sub < rows
    lower = local < rows // 2
    first_lane = lane == 0
    last_lane = lane == lanes - 1
    odd_sub = sub % 2 == 1
    north_even = (sub < rows - 1) | (sub == 2 * rows - 1)
    south_even = (sub >= 1) & (sub <= rows)
    north_part = (sub >= 1) & (sub <= rows)
    south_part = (sub < rows - 1) | (sub == 2 * rows - 1)

    even_lane = lane % 2 == 0
    dense = jnp.where(
        odd_sub,
        jnp.where(even_lane, lane_roll(corner_se[...], -1), lane_roll(corner_sw[...], 1)),
        jnp.where(even_lane, lane_roll(corner_ne[...], -1), lane_roll(corner_nw[...], 1)),
    )

    def corner(slot, k):
        return pltpu.roll(dense, lanes - 2 * (slot * half + k) - 1, 1)

    def to_halo(value, k):
        if k % 2 == 0:
            return sub_roll(value, rows)
        return jnp.where(local == 0, sub_roll(value, -2), sub_roll(value, 2))

    def to_ends(value, k):
        down, up = sub_roll(value, 1 - rows), sub_roll(value, rows - 1)
        return jnp.where(local == 0, down, up) if k % 2 == 0 else jnp.where(local == 0, up, down)

    base = fields * half
    count = pairs // rows
    for k in range(pairs):
        quad, t = k // rows, k % rows
        row_south = sub_roll(from_south[base + half + quad], rows + t)
        row_north = sub_roll(from_north[base + quad], rows - t)
        halo_x = jnp.where(local == 0, row_north, row_south)
        north_y = sub_roll(from_north[base + count + quad], rows - t)
        south_y = sub_roll(from_south[base + k // 2], rows if k % 2 == 0 else 2)
        halo_y = jnp.where(lower, north_y, south_y)
        own_x = cx[k]
        own_y = cy[k]
        own_west = west_x[k]
        halo_west = jnp.where(
            first_lane, to_halo(corner(fields, k // 2), k), lane_roll(halo_x, 1)
        )
        both = []
        for odd in range(2):
            here_x = jnp.where(low, halo_x, own_x) if odd else jnp.where(low, own_x, halo_x)
            here_y = jnp.where(low, halo_y, own_y) if odd else jnp.where(low, own_y, halo_y)
            west_face = (
                jnp.where(low, halo_west, own_west) if odd else jnp.where(low, own_west, halo_west)
            )
            coefs = coefficients(here_x, west_face, here_y, sub_roll(here_y, 1))
            for c in range(5):
                full_coefs[2 * k + odd, c] = coefs[c]
            both.append(coefs)
        for c in range(5):
            half_coefs[k, c] = jnp.where(low, both[0][c], both[1][c])
        south_face = to_ends(corner(fields + 1, k // 2), k)
        half_coefs[k, 5] = jnp.where(local == 0, jnp.minimum(south_face, 0.0), 0.0)
        half_coefs[k, 6] = jnp.where(
            local == 0,
            jnp.maximum(south_face, 0.0),
            jnp.where(local == rows - 1, jnp.maximum(-sides_y[k], 0.0), 0.0),
        )

    def halos(f, k):
        message_south = from_south[f * half + k]
        message_north = from_north[f * half + k]
        center = jnp.where(odd_sub, message_south, message_north)
        sides = corner(f, k)
        shifted = (
            jnp.where(last_lane, sides, lane_roll(center, -1)),
            jnp.where(first_lane, sides, lane_roll(center, 1)),
        )
        first = sub_roll(jnp.where(lower, message_north, message_south), rows)
        second = jnp.where(lower, sub_roll(message_north, -2), sub_roll(message_south, 2))
        return tuple(
            (here, *(to_halo(value, i) for value in shifted), to_ends(sides, i))
            for i, here in enumerate((first, second))
        )

    def advect(f, k, halo, first_coefs, second_coefs):
        slot = f * pairs + k
        own = (tracers[slot], east[slot], west[slot])
        own_north, own_south = sub_roll(own[0], -1), sub_roll(own[0], 1)
        halo_north, halo_south = sub_roll(halo[0], -1), sub_roll(halo[0], 1)
        even = combine(
            first_coefs[0],
            *(jnp.where(low, mine, other) for mine, other in zip(own, halo[:3])),
            jnp.where(north_even, own_north, halo_north),
            jnp.where(south_even, own_south, halo_south),
        )
        odd = combine(
            first_coefs[1],
            *(jnp.where(low, other, mine) for mine, other in zip(own, halo[:3])),
            jnp.where(north_even, halo_north, own_north),
            jnp.where(south_even, halo_south, own_south),
        )
        center = jnp.where(low, even, odd)
        sides = (
            next_sides[slot]
            + second_coefs[5] * jnp.where(first_lane, own[2], own[1])
            + second_coefs[6] * halo[3]
        )
        return combine(
            second_coefs,
            center,
            jnp.where(last_lane, sides, lane_roll(center, -1)),
            jnp.where(first_lane, sides, lane_roll(center, 1)),
            sub_roll(jnp.where(north_part, even, odd), -1),
            sub_roll(jnp.where(south_part, even, odd), 1),
        )

    def transport(p):
        f1 = 2 * p
        f2 = jnp.minimum(f1 + 1, fields - 1)
        columns = []
        for k in range(half):
            halo_one, halo_two = halos(f1, k), halos(f2, k)
            for i in range(2):
                j = 2 * k + i
                first_coefs = [[full_coefs[2 * j + odd, c] for c in range(5)] for odd in range(2)]
                second_coefs = [half_coefs[j, c] for c in range(7)]
                one = advect(f1, j, halo_one[i], first_coefs, second_coefs)
                two = advect(f2, j, halo_two[i], first_coefs, second_coefs)
                columns.append(jnp.where(low, one, sub_roll(two, rows)))
                columns.append(jnp.where(low, sub_roll(one, rows), two))
        return tuple(columns)

    def solve(p, columns):
        f1 = 2 * p
        f2 = jnp.minimum(f1 + 1, fields - 1)
        waves = cosine_sums(columns)
        change = cosine_series([source[m, p] - decay[m, p] * waves[m] for m in range(levels)])
        square = change[0] * change[0]
        for l in range(1, levels):
            square = square + change[l] * change[l]
        for k in range(pairs):
            even, odd = (columns[l] + change[l] for l in (2 * k, 2 * k + 1))
            state[f1 * pairs + k] = jnp.where(low, even, sub_roll(odd, rows))
            state[f2 * pairs + k] = jnp.where(low, sub_roll(even, rows), odd)
        return jnp.where(low | (f1 + 1 < fields), square, 0.0)

    def pair_step(p, carried):
        total, columns = carried
        following = transport(p)
        return total + solve(p - 1, columns), following

    field_pairs = (fields + 1) // 2
    total, columns = lax.fori_loop(
        1, field_pairs, pair_step, (jnp.zeros(tile, F32), transport(0))
    )
    return total + solve(field_pairs - 1, columns)


def main_kernel(fields, levels, *refs):
    inputs, (target, onehot), (state, placed), coefs = refs[:16], refs[16:18], refs[18:20], refs[20:]
    rows, lanes = target.shape
    total = transport_and_solve(fields, levels, *inputs, state, *coefs)

    heat = (total + sub_roll(total, rows)) * (1.0 / (fields * levels))
    first = heat.astype(jnp.bfloat16).astype(F32)
    rest = heat - first
    second = rest.astype(jnp.bfloat16).astype(F32)
    third = rest - second
    spans = placed.shape[0]
    slot_row, _ = iotas((spans, lanes))
    high = lax.shift_right_logical(target[...], lanes.bit_length() - 1)
    hits = [slot_row == high[r : r + 1] for r in range(rows)]
    left = jnp.concatenate(
        [
            jnp.concatenate(
                [
                    jnp.where(hits[r], part[r : r + 1], 0.0).astype(jnp.bfloat16)
                    for r in range(rows)
                ],
                axis=1,
            )
            for part in (first, second, third)
        ],
        axis=0,
    )
    result = jnp.dot(left, onehot[...], preferred_element_type=F32)
    placed[...] = result[:spans] + result[spans : 2 * spans] + result[2 * spans :]


def finish_kernel(parts, state, total_out, state_out, total, semaphores):
    copy_state = pltpu.make_async_copy(state, state_out, semaphores.at[0])
    copy_state.start()
    value = parts[0]
    for i in range(1, parts.shape[0]):
        value = value + parts[i]
    total[...] = value
    copy_total = pltpu.make_async_copy(total, total_out, semaphores.at[1])
    copy_total.start()
    copy_state.wait()
    copy_total.wait()


def body(tracers, courant_x, courant_y, physics_ref, class_coeffs, span_target, cloud_class):
    fields, levels, rows, cols = tracers.shape
    wide = lax.axis_size("wide")
    narrow = lax.axis_size("narrow")
    pairs = levels // 2
    half = pairs // 2
    tile = (2 * rows, cols)
    field_pairs = (fields + 1) // 2
    flat = tracers.reshape(fields * pairs, *tile)
    cx = courant_x.reshape(pairs, *tile)
    cy = courant_y.reshape(pairs, *tile)
    quads = pairs // rows

    def array(*shape, dtype=F32):
        return jax.ShapeDtypeStruct(shape, dtype)

    flat, cx, cy, north, south = pl.pallas_call(
        functools.partial(pack_rows_kernel, levels),
        out_shape=(
            array(fields * pairs, *tile),
            array(pairs, *tile),
            array(pairs, *tile),
            array(fields * half + half + quads, *tile),
            array(fields * half + 2 * quads, *tile),
        ),
        in_specs=[HBM] * 3,
        out_specs=[VMEM] * 5,
        scratch_shapes=[pltpu.SemaphoreType.DMA((3,))],
        compiler_params=PARAMS,
    )(*(pltpu.with_memory_space_constraint(x, pltpu.HBM) for x in (flat, cx, cy)))
    edge, corner = pl.pallas_call(
        functools.partial(pack_edges_kernel, levels),
        out_shape=(array(fields + 2, *tile), array(*tile)),
        in_specs=[VMEM] * 3,
        out_specs=[VMEM] * 2,
        compiler_params=PARAMS,
    )(flat, cx, cy)

    def send(value, up, right):
        pairs_ = []
        for w in range(wide):
            for n in range(narrow):
                to = ((w + up) % wide) * narrow + (n + right) % narrow
                pairs_.append((w * narrow + n, to))
        return lax.ppermute(value, ("wide", "narrow"), pairs_)

    def to_both_sides(value, up):
        from_west = send(value, up, 1)
        from_east = from_west if narrow == 2 else send(value, up, -1)
        return from_west, from_east

    from_south = send(north, 1, 0)
    from_north = send(south, -1, 0)
    edge_west, edge_east = to_both_sides(edge, 0)
    corner_sw, corner_se = to_both_sides(corner, 1)
    corner_nw, corner_ne = to_both_sides(corner, -1)

    decay, source, onehot = pl.pallas_call(
        prep_kernel,
        out_shape=(array(levels, field_pairs, *tile),) * 2
        + (array(rows * cols, cols, dtype=jnp.bfloat16),),
        in_specs=[SMEM, SMEM, VMEM, VMEM],
        out_specs=[VMEM] * 3,
        cost_estimate=pl.CostEstimate(flops=4000000, bytes_accessed=2000000, transcendentals=0),
        compiler_params=PARAMS,
    )(class_coeffs, physics_ref, cloud_class, span_target)

    shifted = pl.pallas_call(
        functools.partial(shift_kernel, levels),
        out_shape=(array(fields * pairs, *tile),) * 2,
        in_specs=[VMEM] * 4,
        out_specs=[VMEM] * 2,
        compiler_params=PARAMS,
    )(flat, edge, edge_west, edge_east)
    edge_columns = pl.pallas_call(
        functools.partial(next_kernel, levels),
        out_shape=(array(fields * pairs, *tile),) + (array(pairs, *tile),) * 2,
        in_specs=[VMEM] * 4,
        out_specs=[VMEM] * 3,
        compiler_params=PARAMS,
    )(cx, edge, edge_west, edge_east)
    state, placed = pl.pallas_call(
        functools.partial(main_kernel, fields, levels),
        out_shape=(array(fields * pairs, *tile), array(wide * rows, cols)),
        in_specs=[VMEM] * 18,
        out_specs=[VMEM] * 2,
        scratch_shapes=[
            pltpu.VMEM((levels, 5) + tile, F32),
            pltpu.VMEM((pairs, 7) + tile, F32),
        ],
        compiler_params=PARAMS,
    )(
        flat,
        cx,
        cy,
        from_south,
        from_north,
        *shifted,
        *edge_columns,
        corner_sw,
        corner_se,
        corner_nw,
        corner_ne,
        decay,
        source,
        span_target,
        onehot,
    )
    received = lax.all_to_all(
        placed.reshape(wide, rows, cols), "wide", split_axis=0, concat_axis=0, tiled=True
    )
    span_diag, state = pl.pallas_call(
        finish_kernel,
        out_shape=(array(rows, cols), array(fields * pairs, *tile)),
        in_specs=[VMEM] * 2,
        out_specs=[HBM] * 2,
        scratch_shapes=[pltpu.VMEM((rows, cols), F32), pltpu.SemaphoreType.DMA((2,))],
        compiler_params=PARAMS,
    )(received, state)
    return state.reshape(fields, levels, rows, cols), span_diag


def solution(mesh):
    return jax.shard_map(
        body,
        mesh=mesh,
        in_specs=(
            P(None, None, "wide", "narrow"),
            P(None, "wide", "narrow"),
            P(None, "wide", "narrow"),
            P(),
            P(),
            P("wide", "narrow"),
            P("wide", "narrow"),
        ),
        out_specs=(P(None, None, "wide", "narrow"), P("wide", "narrow")),
        check_vma=False,
    )
```

```python
import functools
import math

import jax
import jax.numpy as jnp
from jax import lax
from jax.experimental import pallas as pl
from jax.experimental.pallas import tpu as pltpu
from jax.sharding import PartitionSpec as P

VMEM = pl.BlockSpec(memory_space=pltpu.VMEM)
HBM = pl.BlockSpec(memory_space=pltpu.HBM)
SMEM = pl.BlockSpec(memory_space=pltpu.SMEM)
F32 = jnp.float32
PARAMS = pltpu.CompilerParams(vmem_limit_bytes=12 * 1024 * 1024)


def sub_roll(value, shift):
    shift = shift % value.shape[0]
    return value if shift == 0 else pltpu.roll(value, shift, 0)


def lane_roll(value, shift):
    shift = shift % value.shape[1]
    return value if shift == 0 else pltpu.roll(value, shift, 1)


def iotas(shape):
    return lax.broadcasted_iota(jnp.int32, shape, 0), lax.broadcasted_iota(jnp.int32, shape, 1)


def pack_rows_kernel(
    levels, split, tracers_in, cx_in, cy_in, tracers, cx, cy, north, south, semaphores
):
    copies = [
        pltpu.make_async_copy(source, into, semaphores.at[i])
        for i, (source, into) in enumerate(((tracers_in, tracers), (cx_in, cx), (cy_in, cy)))
    ]
    for copy in copies:
        copy.start()
    for copy in copies:
        copy.wait()
    pairs = levels // 2
    half = pairs // 2
    tile = tracers.shape[1:]
    rows = tile[0] // 2
    local = iotas(tile)[0] % rows
    upper = local >= rows // 2

    def one_row(vectors, row, step):
        packed = []
        for start in range(0, pairs, rows):
            total = vectors[start]
            for t in range(1, rows):
                total = jnp.where(
                    local == row + step * t, sub_roll(vectors[start + t], step * t), total
                )
            packed.append(total)
        return packed

    fields = tracers.shape[0] // pairs
    for f in range(fields):
        for k in range(half):
            one, two = tracers[f * pairs + 2 * k], tracers[f * pairs + 2 * k + 1]
            south[f * half + k] = jnp.where(upper, sub_roll(two, -2), one)
            if f < split:
                north[f * half + k] = jnp.where(upper, one, sub_roll(two, 2))
    vectors_x = [cx[k] for k in range(pairs)]
    vectors_y = [cy[k] for k in range(pairs)]
    base = split * half
    for k in range(half):
        north[base + k] = jnp.where(upper, vectors_y[2 * k], sub_roll(vectors_y[2 * k + 1], 2))
    for k, value in enumerate(one_row(vectors_x, rows - 1, -1)):
        north[base + half + k] = value
    base = fields * half
    south_rows = one_row(vectors_x, 0, 1) + one_row(vectors_y, 0, 1)
    for k, value in enumerate(south_rows):
        south[base + k] = value


def pack_edges_kernel(levels, tracers, cx, cy, edge, corner):
    pairs = levels // 2
    half = pairs // 2
    fields = tracers.shape[0] // pairs
    tile = tracers.shape[1:]
    rows = tile[0] // 2
    lanes = tile[1]
    group = lanes // levels
    sub, lane = iotas(tile)
    upper = sub % rows >= rows // 2
    odd_sub = sub % 2 == 1
    corners = [jnp.zeros(tile, F32)]

    def pack_edge(vectors, slot):
        total = lane_roll(vectors[0], 2)
        for k in range(1, pairs):
            total = jnp.where(
                lane // (2 * group) == k, lane_roll(vectors[k], 2 + 2 * group * k), total
            )
        total = jnp.where(
            lane % (2 * group) < group, total, sub_roll(lane_roll(total, group), rows)
        )
        edge[slot] = jnp.where(lane % group < group // 2, total, lane_roll(total, group // 2))
        for k in range(half):
            one, two = vectors[2 * k], vectors[2 * k + 1]
            place = slot * half + k
            north = jnp.where(upper, one, sub_roll(two, 2))
            south = jnp.where(upper, sub_roll(two, -2), one)
            value = lane_roll(jnp.where(odd_sub, north, south), 2 * place + 1)
            corners[0] = jnp.where(lane // 2 == place, value, corners[0])

    for f in range(fields):
        pack_edge([tracers[f * pairs + k] for k in range(pairs)], f)
    pack_edge([cx[k] for k in range(pairs)], fields)
    pack_edge([cy[k] for k in range(pairs)], fields + 1)
    corner[...] = corners[0]


def pack_late_kernel(levels, split, tracers, _, north):
    pairs = levels // 2
    half = pairs // 2
    rows = tracers.shape[1] // 2
    upper = iotas(tracers.shape[1:])[0] % rows >= rows // 2
    for f in range(split, tracers.shape[0] // pairs):
        for k in range(half):
            one, two = tracers[f * pairs + 2 * k], tracers[f * pairs + 2 * k + 1]
            north[(f - split) * half + k] = jnp.where(upper, one, sub_roll(two, 2))


def cosine_sums(values):
    count = len(values)
    if count == 1:
        return values
    half = count // 2
    plus = [values[n] + values[count - 1 - n] for n in range(half)]
    minus = [
        (values[n] - values[count - 1 - n])
        * (0.5 / math.cos(math.pi * (2 * n + 1) / (2 * count)))
        for n in range(half)
    ]
    even = cosine_sums(plus)
    odd = cosine_sums(minus)
    result = []
    for k in range(half):
        result.append(even[k])
        result.append(odd[k] + odd[k + 1] if k + 1 < half else odd[k])
    return result


def cosine_series(values):
    count = len(values)
    if count == 1:
        return values
    half = count // 2
    odd_in = [values[2 * k + 1] + values[2 * k - 1] if k else values[1] for k in range(half)]
    even = cosine_series(values[0::2])
    odd = cosine_series(odd_in)
    odd = [
        odd[n] * (0.5 / math.cos(math.pi * (2 * n + 1) / (2 * count))) for n in range(half)
    ]
    return [even[n] + odd[n] for n in range(half)] + [
        even[n] - odd[n] for n in range(half - 1, -1, -1)
    ]


def prep_kernel(coeffs, profile, klass, target, _, decay, source, onehot):
    levels, pairs = decay.shape[:2]
    fields = profile.shape[0]
    tile = decay.shape[2:]
    rows, lanes = klass.shape
    sub, lane = iotas(tile)
    low = sub < rows
    kind = jnp.concatenate([klass[...], klass[...]], axis=0)
    is_two = kind == 2
    is_one = kind == 1

    def by_class(which, f):
        return jnp.where(
            is_two,
            coeffs[which, 2, f] * 0.25,
            jnp.where(is_one, coeffs[which, 1, f] * 0.5, coeffs[which, 0, f]),
        )

    for p in range(pairs):
        f1 = 2 * p
        f2 = min(2 * p + 1, fields - 1)
        diffusion = jnp.where(low, by_class(0, f1), by_class(0, f2))
        relax = jnp.where(low, by_class(1, f1), by_class(1, f2))
        waves = cosine_sums([jnp.where(low, profile[f1, l], profile[f2, l]) for l in range(levels)])
        for m in range(levels):
            rate = relax + diffusion * (2.0 - 2.0 * math.cos(math.pi * m / levels))
            once = 1.0 / (1.0 + rate)
            square = once * once
            twice = once + square
            steps = jnp.where(is_two, twice + twice * square, jnp.where(is_one, twice, once))
            steps = steps * ((1.0 if m == 0 else 2.0) / levels)
            decay[m, p] = steps * rate
            source[m, p] = steps * relax * waves[m]
    low_part = target[...] & (lanes - 1)
    slot, _ = iotas((lanes, lanes))
    for r in range(rows):
        hit = jnp.where(slot == low_part[r : r + 1], 1.0, 0.0)
        onehot[r * lanes : (r + 1) * lanes, :] = jnp.transpose(hit).astype(jnp.bfloat16)


def combine(coefs, center, east, west, north, south):
    return (
        coefs[0] * center
        + (coefs[1] * east + coefs[2] * west)
        + (coefs[3] * north + coefs[4] * south)
    )


def coefficients(here_x, west_x, here_y, south_y):
    return (
        1.0
        - jnp.maximum(here_x, 0.0)
        + jnp.minimum(west_x, 0.0)
        - jnp.maximum(here_y, 0.0)
        + jnp.minimum(south_y, 0.0),
        jnp.maximum(-here_x, 0.0),
        jnp.maximum(west_x, 0.0),
        jnp.maximum(-here_y, 0.0),
        jnp.maximum(south_y, 0.0),
    )


def side_by_side(value, place):
    return jnp.where(place == 3, lane_roll(value, -2), value)


def beside(edge, edge_west, edge_east, slot, place):
    from_east = (place == 2) | (place == 3)
    from_west = (place == 4) | (place == 5)
    return jnp.where(
        from_east, edge_east[slot], jnp.where(from_west, edge_west[slot], edge[slot])
    )


def spread(value, levels):
    lanes = value.shape[1]
    rows = value.shape[0] // 2
    group = lanes // levels
    sub, lane = iotas(value.shape)
    value = side_by_side(value, lane % group)
    value = jnp.where(sub < rows, value, sub_roll(lane_roll(value, -group), rows))
    return [lane_roll(value, -(2 * group * k + 3)) for k in range(levels // 2)]


def shift_kernel(levels, tracers, edge, edge_west, edge_east, east, west):
    pairs = levels // 2
    tile = tracers.shape[1:]
    lanes = tile[1]
    lane = iotas(tile)[1]
    place = lane % (lanes // levels)
    for f in range(tracers.shape[0] // pairs):
        for k, sides in enumerate(spread(beside(edge, edge_west, edge_east, f, place), levels)):
            own = tracers[f * pairs + k]
            east[f * pairs + k] = jnp.where(lane == lanes - 1, sides, lane_roll(own, -1))
            west[f * pairs + k] = jnp.where(lane == 0, sides, lane_roll(own, 1))


def next_kernel(levels, cx, edge, edge_west, edge_east, next_sides, west_x, sides_y):
    pairs = levels // 2
    fields = next_sides.shape[0] // pairs
    tile = cx.shape[1:]
    rows = tile[0] // 2
    sub, lane = iotas(tile)
    place = lane % (tile[1] // levels)

    def own_rows(slot):
        value = beside(edge, edge_west, edge_east, slot, place)
        return jnp.where(sub < rows, value, 0.0)

    edge_x = own_rows(fields)
    edge_y = own_rows(fields + 1)
    coefs = coefficients(edge_x, lane_roll(edge_x, 1), edge_y, sub_roll(edge_y, 1))
    for k, sides in enumerate(spread(edge_x, levels)):
        west_x[k] = jnp.where(lane == 0, sides, lane_roll(cx[k], 1))
    for k, sides in enumerate(spread(edge_y, levels)):
        sides_y[k] = sides
    for f in range(fields):
        raw = own_rows(f)
        moved = combine(
            coefs,
            raw,
            lane_roll(raw, -1),
            lane_roll(raw, 1),
            sub_roll(raw, -1),
            sub_roll(raw, 1),
        )
        for k, sides in enumerate(spread(moved, levels)):
            next_sides[f * pairs + k] = sides


def courant_kernel(base, from_south, south_x, south_y):
    pairs = south_x.shape[0]
    rows = south_x.shape[1] // 2
    for k in range(pairs):
        value = from_south[base + pairs // 2 + k // rows]
        south_x[k] = sub_roll(value, rows + k % rows)
        south_y[k] = sub_roll(from_south[base + k // 2], rows if k % 2 == 0 else 2)


def corner(dense, place):
    return pltpu.roll(dense, dense.shape[1] - 2 * place - 1, 1)


def to_halo(value, k):
    rows = value.shape[0] // 2
    if k % 2 == 0:
        return sub_roll(value, rows)
    local = iotas(value.shape)[0] % rows
    return jnp.where(local == 0, sub_roll(value, -2), sub_roll(value, 2))


def to_ends(value, k):
    rows = value.shape[0] // 2
    local = iotas(value.shape)[0] % rows
    down, up = sub_roll(value, 1 - rows), sub_roll(value, rows - 1)
    return jnp.where(local == 0, down, up) if k % 2 == 0 else jnp.where(local == 0, up, down)


def set_coefficients(
    fields,
    levels,
    cx,
    cy,
    south_x,
    south_y,
    from_north,
    west_x,
    sides_y,
    corner_sw,
    corner_se,
    corner_nw,
    corner_ne,
    full_coefs,
    half_coefs,
    dense_out,
):
    pairs = levels // 2
    half = pairs // 2
    tile = cx.shape[1:]
    rows = tile[0] // 2
    lanes = tile[1]
    sub, lane = iotas(tile)
    local = sub % rows
    low = sub < rows
    lower = local < rows // 2
    odd_sub = sub % 2 == 1
    first_lane = lane == 0

    even_lane = lane % 2 == 0
    dense = jnp.where(
        odd_sub,
        jnp.where(even_lane, lane_roll(corner_se[...], -1), lane_roll(corner_sw[...], 1)),
        jnp.where(even_lane, lane_roll(corner_ne[...], -1), lane_roll(corner_nw[...], 1)),
    )
    dense_out[...] = dense

    base = fields * half
    count = pairs // rows
    for k in range(pairs):
        quad, t = k // rows, k % rows
        row_north = sub_roll(from_north[base + quad], rows - t)
        halo_x = jnp.where(local == 0, row_north, south_x[k])
        north_y = sub_roll(from_north[base + count + quad], rows - t)
        halo_y = jnp.where(lower, north_y, south_y[k])
        own_x = cx[k]
        own_y = cy[k]
        own_west = west_x[k]
        halo_west = jnp.where(
            first_lane, to_halo(corner(dense, fields * half + k // 2), k), lane_roll(halo_x, 1)
        )
        both = []
        for odd in range(2):
            here_x = jnp.where(low, halo_x, own_x) if odd else jnp.where(low, own_x, halo_x)
            here_y = jnp.where(low, halo_y, own_y) if odd else jnp.where(low, own_y, halo_y)
            west_face = (
                jnp.where(low, halo_west, own_west) if odd else jnp.where(low, own_west, halo_west)
            )
            coefs = coefficients(here_x, west_face, here_y, sub_roll(here_y, 1))
            for c in range(5):
                full_coefs[2 * k + odd, c] = coefs[c]
            both.append(coefs)
        for c in range(5):
            half_coefs[k, c] = jnp.where(low, both[0][c], both[1][c])
        south_face = to_ends(corner(dense, (fields + 1) * half + k // 2), k)
        half_coefs[k, 5] = jnp.where(local == 0, jnp.minimum(south_face, 0.0), 0.0)
        half_coefs[k, 6] = jnp.where(
            local == 0,
            jnp.maximum(south_face, 0.0),
            jnp.where(local == rows - 1, jnp.maximum(-sides_y[k], 0.0), 0.0),
        )


def transport_and_solve(
    fields,
    levels,
    begin,
    end,
    tracers,
    from_south,
    from_north,
    east,
    west,
    next_sides,
    decay,
    source,
    full_coefs,
    half_coefs,
    dense_in,
    state,
):
    pairs = levels // 2
    half = pairs // 2
    tile = tracers.shape[1:]
    rows = tile[0] // 2
    lanes = tile[1]
    sub, lane = iotas(tile)
    local = sub % rows
    low = sub < rows
    lower = local < rows // 2
    odd_sub = sub % 2 == 1
    first_lane = lane == 0
    last_lane = lane == lanes - 1
    north_even = (sub < rows - 1) | (sub == 2 * rows - 1)
    south_even = (sub >= 1) & (sub <= rows)
    north_part = (sub >= 1) & (sub <= rows)
    south_part = (sub < rows - 1) | (sub == 2 * rows - 1)
    dense = dense_in[...]

    def halos(f, k):
        message_south = from_south[(f - begin) * half + k]
        message_north = from_north[f * half + k]
        center = jnp.where(odd_sub, message_south, message_north)
        sides = corner(dense, f * half + k)
        shifted = (
            jnp.where(last_lane, sides, lane_roll(center, -1)),
            jnp.where(first_lane, sides, lane_roll(center, 1)),
        )
        first = sub_roll(jnp.where(lower, message_north, message_south), rows)
        second = jnp.where(lower, sub_roll(message_north, -2), sub_roll(message_south, 2))
        return tuple(
            (here, *(to_halo(value, i) for value in shifted), to_ends(sides, i))
            for i, here in enumerate((first, second))
        )

    def advect(f, k, halo, first_coefs, second_coefs):
        slot = f * pairs + k
        own = (tracers[slot], east[slot], west[slot])
        own_north, own_south = sub_roll(own[0], -1), sub_roll(own[0], 1)
        halo_north, halo_south = sub_roll(halo[0], -1), sub_roll(halo[0], 1)
        even = combine(
            first_coefs[0],
            *(jnp.where(low, mine, other) for mine, other in zip(own, halo[:3])),
            jnp.where(north_even, own_north, halo_north),
            jnp.where(south_even, own_south, halo_south),
        )
        odd = combine(
            first_coefs[1],
            *(jnp.where(low, other, mine) for mine, other in zip(own, halo[:3])),
            jnp.where(north_even, halo_north, own_north),
            jnp.where(south_even, halo_south, own_south),
        )
        center = jnp.where(low, even, odd)
        sides = (
            next_sides[slot]
            + second_coefs[5] * jnp.where(first_lane, own[2], own[1])
            + second_coefs[6] * halo[3]
        )
        return combine(
            second_coefs,
            center,
            jnp.where(last_lane, sides, lane_roll(center, -1)),
            jnp.where(first_lane, sides, lane_roll(center, 1)),
            sub_roll(jnp.where(north_part, even, odd), -1),
            sub_roll(jnp.where(south_part, even, odd), 1),
        )

    def transport(p):
        f1 = 2 * p
        f2 = jnp.minimum(f1 + 1, fields - 1)
        columns = []
        for k in range(half):
            halo_one, halo_two = halos(f1, k), halos(f2, k)
            for i in range(2):
                j = 2 * k + i
                first_coefs = [[full_coefs[2 * j + odd, c] for c in range(5)] for odd in range(2)]
                second_coefs = [half_coefs[j, c] for c in range(7)]
                one = advect(f1, j, halo_one[i], first_coefs, second_coefs)
                two = advect(f2, j, halo_two[i], first_coefs, second_coefs)
                columns.append(jnp.where(low, one, sub_roll(two, rows)))
                columns.append(jnp.where(low, sub_roll(one, rows), two))
        return tuple(columns)

    def solve(p, columns):
        f1 = 2 * p
        f2 = jnp.minimum(f1 + 1, fields - 1)
        waves = cosine_sums(columns)
        change = cosine_series([source[m, p] - decay[m, p] * waves[m] for m in range(levels)])
        square = change[0] * change[0]
        for l in range(1, levels):
            square = square + change[l] * change[l]
        for k in range(pairs):
            even, odd = (columns[l] + change[l] for l in (2 * k, 2 * k + 1))
            state[(f1 - begin) * pairs + k] = jnp.where(low, even, sub_roll(odd, rows))
            state[(f2 - begin) * pairs + k] = jnp.where(low, sub_roll(even, rows), odd)
        return jnp.where(low | (f1 + 1 < fields), square, 0.0)

    def pair_step(p, carried):
        total, columns = carried
        following = transport(p)
        return total + solve(p - 1, columns), following

    first_pair, last_pair = begin // 2, (end - 1) // 2
    total, columns = lax.fori_loop(
        first_pair + 1, last_pair + 1, pair_step, (jnp.zeros(tile, F32), transport(first_pair))
    )
    return total + solve(last_pair, columns)


def first_kernel(
    fields,
    levels,
    split,
    tracers,
    cx,
    cy,
    south_x,
    south_y,
    from_south,
    from_north,
    east,
    west,
    next_sides,
    west_x,
    sides_y,
    corner_sw,
    corner_se,
    corner_nw,
    corner_ne,
    decay,
    source,
    state,
    heat,
    full_coefs,
    half_coefs,
    dense,
):
    set_coefficients(
        fields,
        levels,
        cx,
        cy,
        south_x,
        south_y,
        from_north,
        west_x,
        sides_y,
        corner_sw,
        corner_se,
        corner_nw,
        corner_ne,
        full_coefs,
        half_coefs,
        dense,
    )
    heat[...] = transport_and_solve(
        fields,
        levels,
        0,
        split,
        tracers,
        from_south,
        from_north,
        east,
        west,
        next_sides,
        decay,
        source,
        full_coefs,
        half_coefs,
        dense,
        state,
    )


def second_kernel(fields, levels, split, *refs):
    inputs, (heat_first, target, onehot), (state, placed) = refs[:11], refs[11:14], refs[14:]
    rows, lanes = target.shape
    total = heat_first[...] + transport_and_solve(fields, levels, split, fields, *inputs, state)

    heat = (total + sub_roll(total, rows)) * (1.0 / (fields * levels))
    first = heat.astype(jnp.bfloat16).astype(F32)
    rest = heat - first
    second = rest.astype(jnp.bfloat16).astype(F32)
    third = rest - second
    spans = placed.shape[0]
    slot_row, _ = iotas((spans, lanes))
    high = lax.shift_right_logical(target[...], lanes.bit_length() - 1)
    hits = [slot_row == high[r : r + 1] for r in range(rows)]
    left = jnp.concatenate(
        [
            jnp.concatenate(
                [
                    jnp.where(hits[r], part[r : r + 1], 0.0).astype(jnp.bfloat16)
                    for r in range(rows)
                ],
                axis=1,
            )
            for part in (first, second, third)
        ],
        axis=0,
    )
    result = jnp.dot(left, onehot[...], preferred_element_type=F32)
    placed[...] = result[:spans] + result[spans : 2 * spans] + result[2 * spans :]


def finish_kernel(parts, state_first, state_second, total_out, state_out, total, semaphores):
    split = state_first.shape[0]
    copies = [
        pltpu.make_async_copy(state_first, state_out.at[pl.ds(0, split)], semaphores.at[0]),
        pltpu.make_async_copy(
            state_second, state_out.at[pl.ds(split, state_second.shape[0])], semaphores.at[1]
        ),
        pltpu.make_async_copy(total, total_out, semaphores.at[2]),
    ]
    copies[0].start()
    copies[1].start()
    value = parts[0]
    for i in range(1, parts.shape[0]):
        value = value + parts[i]
    total[...] = value
    copies[2].start()
    for copy in copies:
        copy.wait()


def body(tracers, courant_x, courant_y, physics_ref, class_coeffs, span_target, cloud_class):
    fields, levels, rows, cols = tracers.shape
    wide = lax.axis_size("wide")
    narrow = lax.axis_size("narrow")
    pairs = levels // 2
    half = pairs // 2
    tile = (2 * rows, cols)
    field_pairs = (fields + 1) // 2
    flat = tracers.reshape(fields * pairs, *tile)
    cx = courant_x.reshape(pairs, *tile)
    cy = courant_y.reshape(pairs, *tile)
    quads = pairs // rows

    def array(*shape, dtype=F32):
        return jax.ShapeDtypeStruct(shape, dtype)

    split = 4 * ((fields + 6) // 7)
    flat, cx, cy, north, south = pl.pallas_call(
        functools.partial(pack_rows_kernel, levels, split),
        out_shape=(
            array(fields * pairs, *tile),
            array(pairs, *tile),
            array(pairs, *tile),
            array(split * half + half + quads, *tile),
            array(fields * half + 2 * quads, *tile),
        ),
        in_specs=[HBM] * 3,
        out_specs=[VMEM] * 5,
        scratch_shapes=[pltpu.SemaphoreType.DMA((3,))],
        compiler_params=PARAMS,
    )(*(pltpu.with_memory_space_constraint(x, pltpu.HBM) for x in (flat, cx, cy)))
    edge, corner = pl.pallas_call(
        functools.partial(pack_edges_kernel, levels),
        out_shape=(array(fields + 2, *tile), array(*tile)),
        in_specs=[VMEM] * 3,
        out_specs=[VMEM] * 2,
        compiler_params=PARAMS,
    )(flat, cx, cy)

    def send(value, up, right):
        pairs_ = []
        for w in range(wide):
            for n in range(narrow):
                to = ((w + up) % wide) * narrow + (n + right) % narrow
                pairs_.append((w * narrow + n, to))
        return lax.ppermute(value, ("wide", "narrow"), pairs_)

    def to_both_sides(value, up):
        from_west = send(value, up, 1)
        from_east = from_west if narrow == 2 else send(value, up, -1)
        return from_west, from_east

    from_south = send(north, 1, 0)
    from_north = send(south, -1, 0)
    edge_west, edge_east = to_both_sides(edge, 0)
    corner_sw, corner_se = to_both_sides(corner, 1)
    corner_nw, corner_ne = to_both_sides(corner, -1)

    north_late = pl.pallas_call(
        functools.partial(pack_late_kernel, levels, split),
        out_shape=array((fields - split) * half, *tile),
        in_specs=[VMEM] * 2,
        out_specs=VMEM,
        compiler_params=PARAMS,
    )(flat, edge_west)
    from_south_late = send(north_late, 1, 0)

    decay, source, onehot = pl.pallas_call(
        prep_kernel,
        out_shape=(array(levels, field_pairs, *tile),) * 2
        + (array(rows * cols, cols, dtype=jnp.bfloat16),),
        in_specs=[SMEM, SMEM, VMEM, VMEM, VMEM],
        out_specs=[VMEM] * 3,
        cost_estimate=pl.CostEstimate(flops=4000000, bytes_accessed=2000000, transcendentals=0),
        compiler_params=PARAMS,
    )(class_coeffs, physics_ref, cloud_class, span_target, north_late)

    east, west = pl.pallas_call(
        functools.partial(shift_kernel, levels),
        out_shape=(array(fields * pairs, *tile),) * 2,
        in_specs=[VMEM] * 4,
        out_specs=[VMEM] * 2,
        compiler_params=PARAMS,
    )(flat, edge, edge_west, edge_east)
    next_sides, west_x, sides_y = pl.pallas_call(
        functools.partial(next_kernel, levels),
        out_shape=(array(fields * pairs, *tile),) + (array(pairs, *tile),) * 2,
        in_specs=[VMEM] * 4,
        out_specs=[VMEM] * 3,
        compiler_params=PARAMS,
    )(cx, edge, edge_west, edge_east)
    south_x, south_y = pl.pallas_call(
        functools.partial(courant_kernel, split * half),
        out_shape=(array(pairs, *tile),) * 2,
        in_specs=[VMEM],
        out_specs=[VMEM] * 2,
        cost_estimate=pl.CostEstimate(flops=1200000000, bytes_accessed=1000000, transcendentals=0),
        compiler_params=PARAMS,
    )(from_south)
    state_first, heat_first, *shared = pl.pallas_call(
        functools.partial(first_kernel, fields, levels, split),
        out_shape=(
            array(split * pairs, *tile),
            array(*tile),
            array(levels, 5, *tile),
            array(pairs, 7, *tile),
            array(*tile),
        ),
        in_specs=[VMEM] * 18,
        out_specs=[VMEM] * 5,
        cost_estimate=pl.CostEstimate(flops=1000000000, bytes_accessed=2000000, transcendentals=0),
        compiler_params=PARAMS,
    )(
        flat,
        cx,
        cy,
        south_x,
        south_y,
        from_south,
        from_north,
        east,
        west,
        next_sides,
        west_x,
        sides_y,
        corner_sw,
        corner_se,
        corner_nw,
        corner_ne,
        decay,
        source,
    )
    state_second, placed = pl.pallas_call(
        functools.partial(second_kernel, fields, levels, split),
        out_shape=(array((fields - split) * pairs, *tile), array(wide * rows, cols)),
        in_specs=[VMEM] * 14,
        out_specs=[VMEM] * 2,
        compiler_params=PARAMS,
    )(
        flat,
        from_south_late,
        from_north,
        east,
        west,
        next_sides,
        decay,
        source,
        *shared,
        heat_first,
        span_target,
        onehot,
    )
    received = lax.all_to_all(
        placed.reshape(wide, rows, cols), "wide", split_axis=0, concat_axis=0, tiled=True
    )
    span_diag, state = pl.pallas_call(
        finish_kernel,
        out_shape=(array(rows, cols), array(fields * pairs, *tile)),
        in_specs=[VMEM] * 3,
        out_specs=[HBM] * 2,
        scratch_shapes=[pltpu.VMEM((rows, cols), F32), pltpu.SemaphoreType.DMA((3,))],
        compiler_params=PARAMS,
    )(received, state_first, state_second)
    return state.reshape(fields, levels, rows, cols), span_diag


def solution(mesh):
    return jax.shard_map(
        body,
        mesh=mesh,
        in_specs=(
            P(None, None, "wide", "narrow"),
            P(None, "wide", "narrow"),
            P(None, "wide", "narrow"),
            P(),
            P(),
            P("wide", "narrow"),
            P("wide", "narrow"),
        ),
        out_specs=(P(None, None, "wide", "narrow"), P("wide", "narrow")),
        check_vma=False,
    )
```

```python
import functools
import math

import jax
import jax.numpy as jnp
from jax import lax
from jax.experimental import pallas as pl
from jax.experimental.pallas import tpu as pltpu
from jax.sharding import PartitionSpec as P

VMEM = pl.BlockSpec(memory_space=pltpu.VMEM)
HBM = pl.BlockSpec(memory_space=pltpu.HBM)
SMEM = pl.BlockSpec(memory_space=pltpu.SMEM)
F32 = jnp.float32
PARAMS = pltpu.CompilerParams(vmem_limit_bytes=12 * 1024 * 1024)


def sub_roll(value, shift):
    shift = shift % value.shape[0]
    return value if shift == 0 else pltpu.roll(value, shift, 0)


def lane_roll(value, shift):
    shift = shift % value.shape[1]
    return value if shift == 0 else pltpu.roll(value, shift, 1)


def iotas(shape):
    return lax.broadcasted_iota(jnp.int32, shape, 0), lax.broadcasted_iota(jnp.int32, shape, 1)


def pack_rows(tracers, f, pairs, north, south, slot):
    local = iotas(tracers.shape[1:])[0] % (tracers.shape[1] // 2)
    lower = local < tracers.shape[1] // 4
    for k in range(pairs // 2):
        first, second = tracers[f * pairs + 2 * k], tracers[f * pairs + 2 * k + 1]
        north[slot + k] = jnp.where(lower, sub_roll(second, 2), first)
        south[slot + k] = jnp.where(lower, first, sub_roll(second, -2))


def pack_rows_kernel(
    levels, tracers_in, cx_in, cy_in, tracers, cx, cy, north, south, semaphores
):
    copies = [
        pltpu.make_async_copy(source, into, semaphores.at[i])
        for i, (source, into) in enumerate(((tracers_in, tracers), (cx_in, cx), (cy_in, cy)))
    ]
    for copy in copies:
        copy.start()
    for copy in copies:
        copy.wait()
    pairs = levels // 2
    half = pairs // 2
    tile = tracers.shape[1:]
    rows = tile[0] // 2
    local = iotas(tile)[0] % rows
    upper = local >= rows // 2

    def one_row(vectors, row, step):
        packed = []
        for start in range(0, pairs, rows):
            total = vectors[start]
            for t in range(1, rows):
                total = jnp.where(
                    local == row + step * t, sub_roll(vectors[start + t], step * t), total
                )
            packed.append(total)
        return packed

    fields = tracers.shape[0] // pairs
    for f in range(fields):
        pack_rows(tracers, f, pairs, north, south, f * half)
    vectors_x = [cx[k] for k in range(pairs)]
    vectors_y = [cy[k] for k in range(pairs)]
    base = fields * half
    for k in range(half):
        north[base + k] = jnp.where(upper, vectors_y[2 * k], sub_roll(vectors_y[2 * k + 1], 2))
    for k, value in enumerate(one_row(vectors_x, rows - 1, -1)):
        north[base + half + k] = value
    south_rows = one_row(vectors_x, 0, 1) + one_row(vectors_y, 0, 1)
    for k, value in enumerate(south_rows):
        south[base + k] = value


def pack_edges_kernel(levels, tracers, cx, cy, edge, corner):
    pairs = levels // 2
    half = pairs // 2
    fields = tracers.shape[0] // pairs
    tile = tracers.shape[1:]
    rows = tile[0] // 2
    lanes = tile[1]
    group = lanes // levels
    sub, lane = iotas(tile)
    upper = sub % rows >= rows // 2
    odd_sub = sub % 2 == 1
    corners = [jnp.zeros(tile, F32)]

    def pack_edge(vectors, slot):
        total = lane_roll(vectors[0], 2)
        for k in range(1, pairs):
            total = jnp.where(
                lane // (2 * group) == k, lane_roll(vectors[k], 2 + 2 * group * k), total
            )
        total = jnp.where(
            lane % (2 * group) < group, total, sub_roll(lane_roll(total, group), rows)
        )
        edge[slot] = jnp.where(lane % group < group // 2, total, lane_roll(total, group // 2))
        for k in range(half):
            one, two = vectors[2 * k], vectors[2 * k + 1]
            place = slot * half + k
            north = jnp.where(upper, one, sub_roll(two, 2))
            south = jnp.where(upper, sub_roll(two, -2), one)
            value = lane_roll(jnp.where(odd_sub, north, south), 2 * place + 1)
            corners[0] = jnp.where(lane // 2 == place, value, corners[0])

    for f in range(fields):
        pack_edge([tracers[f * pairs + k] for k in range(pairs)], f)
    pack_edge([cx[k] for k in range(pairs)], fields)
    pack_edge([cy[k] for k in range(pairs)], fields + 1)
    corner[...] = corners[0]


def cosine_sums(values):
    count = len(values)
    if count == 1:
        return values
    half = count // 2
    plus = [values[n] + values[count - 1 - n] for n in range(half)]
    minus = [
        (values[n] - values[count - 1 - n])
        * (0.5 / math.cos(math.pi * (2 * n + 1) / (2 * count)))
        for n in range(half)
    ]
    even = cosine_sums(plus)
    odd = cosine_sums(minus)
    result = []
    for k in range(half):
        result.append(even[k])
        result.append(odd[k] + odd[k + 1] if k + 1 < half else odd[k])
    return result


def cosine_series(values):
    count = len(values)
    if count == 1:
        return values
    half = count // 2
    odd_in = [values[2 * k + 1] + values[2 * k - 1] if k else values[1] for k in range(half)]
    even = cosine_series(values[0::2])
    odd = cosine_series(odd_in)
    odd = [
        odd[n] * (0.5 / math.cos(math.pi * (2 * n + 1) / (2 * count))) for n in range(half)
    ]
    return [even[n] + odd[n] for n in range(half)] + [
        even[n] - odd[n] for n in range(half - 1, -1, -1)
    ]


def prep_kernel(coeffs, profile, klass, target, decay, source, onehot):
    levels, pairs = decay.shape[:2]
    fields = profile.shape[0]
    tile = decay.shape[2:]
    rows, lanes = klass.shape
    sub, lane = iotas(tile)
    low = sub < rows
    kind = jnp.concatenate([klass[...], klass[...]], axis=0)
    is_two = kind == 2
    is_one = kind == 1

    def by_class(which, f):
        return jnp.where(
            is_two,
            coeffs[which, 2, f] * 0.25,
            jnp.where(is_one, coeffs[which, 1, f] * 0.5, coeffs[which, 0, f]),
        )

    for p in range(pairs):
        f1 = 2 * p
        f2 = min(2 * p + 1, fields - 1)
        diffusion = jnp.where(low, by_class(0, f1), by_class(0, f2))
        relax = jnp.where(low, by_class(1, f1), by_class(1, f2))
        waves = cosine_sums([jnp.where(low, profile[f1, l], profile[f2, l]) for l in range(levels)])
        for m in range(levels):
            rate = relax + diffusion * (2.0 - 2.0 * math.cos(math.pi * m / levels))
            once = 1.0 / (1.0 + rate)
            square = once * once
            twice = once + square
            steps = jnp.where(is_two, twice + twice * square, jnp.where(is_one, twice, once))
            steps = steps * ((1.0 if m == 0 else 2.0) / levels)
            decay[m, p] = steps * rate
            source[m, p] = steps * relax * waves[m]
    low_part = target[...] & (lanes - 1)
    slot, _ = iotas((lanes, lanes))
    for r in range(rows):
        hit = jnp.where(slot == low_part[r : r + 1], 1.0, 0.0)
        onehot[r * lanes : (r + 1) * lanes, :] = jnp.transpose(hit).astype(jnp.bfloat16)


def combine(coefs, center, east, west, north, south):
    return (
        coefs[0] * center
        + (coefs[1] * east + coefs[2] * west)
        + (coefs[3] * north + coefs[4] * south)
    )


def coefficients(here_x, west_x, here_y, south_y):
    return (
        1.0
        - jnp.maximum(here_x, 0.0)
        + jnp.minimum(west_x, 0.0)
        - jnp.maximum(here_y, 0.0)
        + jnp.minimum(south_y, 0.0),
        jnp.maximum(-here_x, 0.0),
        jnp.maximum(west_x, 0.0),
        jnp.maximum(-here_y, 0.0),
        jnp.maximum(south_y, 0.0),
    )


def side_by_side(value, place):
    return jnp.where(place == 3, lane_roll(value, -2), value)


def beside(edge, edge_west, edge_east, slot, place):
    from_east = (place == 2) | (place == 3)
    from_west = (place == 4) | (place == 5)
    return jnp.where(
        from_east, edge_east[slot], jnp.where(from_west, edge_west[slot], edge[slot])
    )


def spread(value, levels):
    lanes = value.shape[1]
    rows = value.shape[0] // 2
    group = lanes // levels
    sub, lane = iotas(value.shape)
    value = side_by_side(value, lane % group)
    value = jnp.where(sub < rows, value, sub_roll(lane_roll(value, -group), rows))
    return [lane_roll(value, -(2 * group * k + 3)) for k in range(levels // 2)]


def shift_kernel(levels, tracers, edge, edge_west, edge_east, east, west):
    pairs = levels // 2
    tile = tracers.shape[1:]
    lanes = tile[1]
    lane = iotas(tile)[1]
    place = lane % (lanes // levels)
    for f in range(tracers.shape[0] // pairs):
        for k, sides in enumerate(spread(beside(edge, edge_west, edge_east, f, place), levels)):
            own = tracers[f * pairs + k]
            east[f * pairs + k] = jnp.where(lane == lanes - 1, sides, lane_roll(own, -1))
            west[f * pairs + k] = jnp.where(lane == 0, sides, lane_roll(own, 1))


def next_kernel(levels, cx, edge, edge_west, edge_east, next_sides, west_x, sides_y):
    pairs = levels // 2
    fields = next_sides.shape[0] // pairs
    tile = cx.shape[1:]
    rows = tile[0] // 2
    sub, lane = iotas(tile)
    place = lane % (tile[1] // levels)

    def own_rows(slot):
        value = beside(edge, edge_west, edge_east, slot, place)
        return jnp.where(sub < rows, value, 0.0)

    edge_x = own_rows(fields)
    edge_y = own_rows(fields + 1)
    coefs = coefficients(edge_x, lane_roll(edge_x, 1), edge_y, sub_roll(edge_y, 1))
    for k, sides in enumerate(spread(edge_x, levels)):
        west_x[k] = jnp.where(lane == 0, sides, lane_roll(cx[k], 1))
    for k, sides in enumerate(spread(edge_y, levels)):
        sides_y[k] = sides
    for f in range(fields):
        raw = own_rows(f)
        moved = combine(
            coefs,
            raw,
            lane_roll(raw, -1),
            lane_roll(raw, 1),
            sub_roll(raw, -1),
            sub_roll(raw, 1),
        )
        for k, sides in enumerate(spread(moved, levels)):
            next_sides[f * pairs + k] = sides


def transport_and_solve(
    fields,
    levels,
    tracers,
    cx,
    cy,
    from_south,
    from_north,
    east,
    west,
    next_sides,
    west_x,
    sides_y,
    corner_sw,
    corner_se,
    corner_nw,
    corner_ne,
    decay,
    source,
    state,
    own_coefs,
    halo_coefs,
):
    pairs = levels // 2
    half = pairs // 2
    tile = tracers.shape[1:]
    rows = tile[0] // 2
    lanes = tile[1]
    group = lanes // levels
    sub, lane = iotas(tile)
    local = sub % rows
    low = sub < rows
    first_lane = lane == 0
    last_lane = lane == lanes - 1
    odd_sub = sub % 2 == 1
    bottom = local == 0
    top = local == rows - 1
    in_first = bottom | top

    even_lane = lane % 2 == 0
    dense = jnp.where(
        odd_sub,
        jnp.where(even_lane, lane_roll(corner_se[...], -1), lane_roll(corner_sw[...], 1)),
        jnp.where(even_lane, lane_roll(corner_ne[...], -1), lane_roll(corner_nw[...], 1)),
    )

    def corner(slot, k):
        return pltpu.roll(dense, lanes - 2 * (slot * half + k) - 1, 1)


    def turned(value):
        up, down = sub_roll(value, rows - 1), sub_roll(value, 1 - rows)
        return ((up, down), (down, up))

    def inner_rows(first, second):
        (first_up, first_down), _ = turned(first)
        (second_up, second_down), _ = turned(second)
        return (
            jnp.where(in_first, first_up, second_down),
            jnp.where(in_first, first_down, second_up),
        )

    base = fields * half
    count = pairs // rows
    for k in range(half):
        quad, t = 2 * k // rows, 2 * k % rows
        packed_south = from_south[base + half + quad]
        packed_north = from_north[base + quad]
        packed_north_y = from_north[base + count + quad]
        message_y = from_south[base + k]
        south_x = jnp.where(in_first, sub_roll(packed_south, t), sub_roll(packed_south, 3 + t))
        north_x = jnp.where(in_first, sub_roll(packed_north, -t), sub_roll(packed_north, 5 - t))
        north_y = jnp.where(
            in_first, sub_roll(packed_north_y, -t), sub_roll(packed_north_y, 5 - t)
        )
        halo_x = jnp.where(odd_sub, south_x, north_x)
        halo_y = jnp.where(odd_sub, message_y, north_y)
        halo_west = jnp.where(first_lane, corner(fields, k), lane_roll(halo_x, 1))
        _, inner_top = inner_rows(cy[2 * k], cy[2 * k + 1])
        halo_south = jnp.where(odd_sub, sub_roll(message_y, 1), inner_top)
        for c, value in enumerate(coefficients(halo_x, halo_west, halo_y, halo_south)):
            halo_coefs[k, c] = value
        places = turned(message_y)
        edge_places = turned(corner(fields + 1, k))
        for i in range(2):
            j = 2 * k + i
            south_y = jnp.where(bottom, places[i][1], sub_roll(cy[j], 1))
            for c, value in enumerate(coefficients(cx[j], west_x[j], cy[j], south_y)):
                own_coefs[j, c] = value
            south_face = edge_places[i][1]
            own_coefs[j, 5] = jnp.where(bottom, jnp.minimum(south_face, 0.0), 0.0)
            own_coefs[j, 6] = jnp.where(
                bottom,
                jnp.maximum(south_face, 0.0),
                jnp.where(top, jnp.maximum(-sides_y[j], 0.0), 0.0),
            )

    def advect(f, k, own_set, halo_set):
        message_south = from_south[f * half + k]
        message_north = from_north[f * half + k]
        slots = (f * pairs + 2 * k, f * pairs + 2 * k + 1)
        own = [tracers[slot] for slot in slots]
        own_east = [east[slot] for slot in slots]
        own_west = [west[slot] for slot in slots]
        sides = corner(f, k)
        halo = jnp.where(odd_sub, message_south, message_north)
        inner_bottom, inner_top = inner_rows(*own)
        next_halo = combine(
            halo_set,
            halo,
            jnp.where(last_lane, sides, lane_roll(halo, -1)),
            jnp.where(first_lane, sides, lane_roll(halo, 1)),
            jnp.where(odd_sub, inner_bottom, sub_roll(message_north, -1)),
            jnp.where(odd_sub, sub_roll(message_south, 1), inner_top),
        )
        places, next_places, side_places = turned(halo), turned(next_halo), turned(sides)
        results = []
        for i in range(2):
            north, south = places[i]
            once = combine(
                own_set[i],
                own[i],
                own_east[i],
                own_west[i],
                jnp.where(top, north, sub_roll(own[i], -1)),
                jnp.where(bottom, south, sub_roll(own[i], 1)),
            )
            side_north, side_south = side_places[i]
            next_column = (
                next_sides[slots[i]]
                + own_set[i][5] * jnp.where(first_lane, own_west[i], own_east[i])
                + own_set[i][6] * jnp.where(bottom, side_south, side_north)
            )
            north, south = next_places[i]
            results.append(
                combine(
                    own_set[i],
                    once,
                    jnp.where(last_lane, next_column, lane_roll(once, -1)),
                    jnp.where(first_lane, next_column, lane_roll(once, 1)),
                    jnp.where(top, north, sub_roll(once, -1)),
                    jnp.where(bottom, south, sub_roll(once, 1)),
                )
            )
        return results

    def transport(p):
        f1 = 2 * p
        f2 = jnp.minimum(f1 + 1, fields - 1)
        columns = []
        for k in range(half):
            own_set = [[own_coefs[2 * k + i, c] for c in range(7)] for i in range(2)]
            halo_set = [halo_coefs[k, c] for c in range(5)]
            for one, two in zip(
                advect(f1, k, own_set, halo_set), advect(f2, k, own_set, halo_set)
            ):
                columns.append(jnp.where(low, one, sub_roll(two, rows)))
                columns.append(jnp.where(low, sub_roll(one, rows), two))
        return tuple(columns)

    def solve(p, columns):
        f1 = 2 * p
        f2 = jnp.minimum(f1 + 1, fields - 1)
        waves = cosine_sums(columns)
        change = cosine_series([source[m, p] - decay[m, p] * waves[m] for m in range(levels)])
        square = change[0] * change[0]
        for l in range(1, levels):
            square = square + change[l] * change[l]
        for k in range(pairs):
            even, odd = (columns[l] + change[l] for l in (2 * k, 2 * k + 1))
            state[f1 * pairs + k] = jnp.where(low, even, sub_roll(odd, rows))
            state[f2 * pairs + k] = jnp.where(low, sub_roll(even, rows), odd)
        return jnp.where(low | (f1 + 1 < fields), square, 0.0)

    def pair_step(p, carried):
        total, columns = carried
        following = transport(p)
        return total + solve(p - 1, columns), following

    field_pairs = (fields + 1) // 2
    total, columns = lax.fori_loop(
        1, field_pairs, pair_step, (jnp.zeros(tile, F32), transport(0))
    )
    return total + solve(field_pairs - 1, columns)


def main_kernel(fields, levels, *refs):
    inputs, (target, onehot), (state, placed), coefs = refs[:16], refs[16:18], refs[18:20], refs[20:]
    rows, lanes = target.shape
    total = transport_and_solve(fields, levels, *inputs, state, *coefs)

    heat = (total + sub_roll(total, rows)) * (1.0 / (fields * levels))
    first = heat.astype(jnp.bfloat16).astype(F32)
    rest = heat - first
    second = rest.astype(jnp.bfloat16).astype(F32)
    third = rest - second
    spans = placed.shape[0]
    slot_row, _ = iotas((spans, lanes))
    high = lax.shift_right_logical(target[...], lanes.bit_length() - 1)
    hits = [slot_row == high[r : r + 1] for r in range(rows)]
    left = jnp.concatenate(
        [
            jnp.concatenate(
                [
                    jnp.where(hits[r], part[r : r + 1], 0.0).astype(jnp.bfloat16)
                    for r in range(rows)
                ],
                axis=1,
            )
            for part in (first, second, third)
        ],
        axis=0,
    )
    result = jnp.dot(left, onehot[...], preferred_element_type=F32)
    placed[...] = result[:spans] + result[spans : 2 * spans] + result[2 * spans :]


def finish_kernel(parts, state, total_out, state_out, total, semaphores):
    copy_state = pltpu.make_async_copy(state, state_out, semaphores.at[0])
    copy_state.start()
    value = parts[0]
    for i in range(1, parts.shape[0]):
        value = value + parts[i]
    total[...] = value
    copy_total = pltpu.make_async_copy(total, total_out, semaphores.at[1])
    copy_total.start()
    copy_state.wait()
    copy_total.wait()


def body(tracers, courant_x, courant_y, physics_ref, class_coeffs, span_target, cloud_class):
    fields, levels, rows, cols = tracers.shape
    wide = lax.axis_size("wide")
    narrow = lax.axis_size("narrow")
    pairs = levels // 2
    half = pairs // 2
    tile = (2 * rows, cols)
    field_pairs = (fields + 1) // 2
    flat = tracers.reshape(fields * pairs, *tile)
    cx = courant_x.reshape(pairs, *tile)
    cy = courant_y.reshape(pairs, *tile)
    quads = pairs // rows

    def array(*shape, dtype=F32):
        return jax.ShapeDtypeStruct(shape, dtype)

    flat, cx, cy, north, south = pl.pallas_call(
        functools.partial(pack_rows_kernel, levels),
        out_shape=(
            array(fields * pairs, *tile),
            array(pairs, *tile),
            array(pairs, *tile),
            array(fields * half + half + quads, *tile),
            array(fields * half + 2 * quads, *tile),
        ),
        in_specs=[HBM] * 3,
        out_specs=[VMEM] * 5,
        scratch_shapes=[pltpu.SemaphoreType.DMA((3,))],
        compiler_params=PARAMS,
    )(*(pltpu.with_memory_space_constraint(x, pltpu.HBM) for x in (flat, cx, cy)))
    edge, corner = pl.pallas_call(
        functools.partial(pack_edges_kernel, levels),
        out_shape=(array(fields + 2, *tile), array(*tile)),
        in_specs=[VMEM] * 3,
        out_specs=[VMEM] * 2,
        compiler_params=PARAMS,
    )(flat, cx, cy)

    def send(value, up, right):
        pairs_ = []
        for w in range(wide):
            for n in range(narrow):
                to = ((w + up) % wide) * narrow + (n + right) % narrow
                pairs_.append((w * narrow + n, to))
        return lax.ppermute(value, ("wide", "narrow"), pairs_)

    def to_both_sides(value, up):
        from_west = send(value, up, 1)
        from_east = from_west if narrow == 2 else send(value, up, -1)
        return from_west, from_east

    from_south = send(north, 1, 0)
    from_north = send(south, -1, 0)
    edge_west, edge_east = to_both_sides(edge, 0)
    corner_sw, corner_se = to_both_sides(corner, 1)
    corner_nw, corner_ne = to_both_sides(corner, -1)

    decay, source, onehot = pl.pallas_call(
        prep_kernel,
        out_shape=(array(levels, field_pairs, *tile),) * 2
        + (array(rows * cols, cols, dtype=jnp.bfloat16),),
        in_specs=[SMEM, SMEM, VMEM, VMEM],
        out_specs=[VMEM] * 3,
        cost_estimate=pl.CostEstimate(flops=4000000, bytes_accessed=2000000, transcendentals=0),
        compiler_params=PARAMS,
    )(class_coeffs, physics_ref, cloud_class, span_target)

    shifted = pl.pallas_call(
        functools.partial(shift_kernel, levels),
        out_shape=(array(fields * pairs, *tile),) * 2,
        in_specs=[VMEM] * 4,
        out_specs=[VMEM] * 2,
        compiler_params=PARAMS,
    )(flat, edge, edge_west, edge_east)
    edge_columns = pl.pallas_call(
        functools.partial(next_kernel, levels),
        out_shape=(array(fields * pairs, *tile),) + (array(pairs, *tile),) * 2,
        in_specs=[VMEM] * 4,
        out_specs=[VMEM] * 3,
        compiler_params=PARAMS,
    )(cx, edge, edge_west, edge_east)
    state, placed = pl.pallas_call(
        functools.partial(main_kernel, fields, levels),
        out_shape=(array(fields * pairs, *tile), array(wide * rows, cols)),
        in_specs=[VMEM] * 18,
        out_specs=[VMEM] * 2,
        scratch_shapes=[
            pltpu.VMEM((pairs, 7) + tile, F32),
            pltpu.VMEM((half, 5) + tile, F32),
        ],
        compiler_params=PARAMS,
    )(
        flat,
        cx,
        cy,
        from_south,
        from_north,
        *shifted,
        *edge_columns,
        corner_sw,
        corner_se,
        corner_nw,
        corner_ne,
        decay,
        source,
        span_target,
        onehot,
    )
    received = lax.all_to_all(
        placed.reshape(wide, rows, cols), "wide", split_axis=0, concat_axis=0, tiled=True
    )
    span_diag, state = pl.pallas_call(
        finish_kernel,
        out_shape=(array(rows, cols), array(fields * pairs, *tile)),
        in_specs=[VMEM] * 2,
        out_specs=[HBM] * 2,
        scratch_shapes=[pltpu.VMEM((rows, cols), F32), pltpu.SemaphoreType.DMA((2,))],
        compiler_params=PARAMS,
    )(received, state)
    return state.reshape(fields, levels, rows, cols), span_diag


def solution(mesh):
    return jax.shard_map(
        body,
        mesh=mesh,
        in_specs=(
            P(None, None, "wide", "narrow"),
            P(None, "wide", "narrow"),
            P(None, "wide", "narrow"),
            P(),
            P(),
            P("wide", "narrow"),
            P("wide", "narrow"),
        ),
        out_specs=(P(None, None, "wide", "narrow"), P("wide", "narrow")),
        check_vma=False,
    )
```

```python
import functools
import math

import jax
import jax.numpy as jnp
from jax import lax
from jax.experimental import pallas as pl
from jax.experimental.pallas import tpu as pltpu
from jax.sharding import PartitionSpec as P

VMEM = pl.BlockSpec(memory_space=pltpu.VMEM)
HBM = pl.BlockSpec(memory_space=pltpu.HBM)
SMEM = pl.BlockSpec(memory_space=pltpu.SMEM)
F32 = jnp.float32
PARAMS = pltpu.CompilerParams(vmem_limit_bytes=12 * 1024 * 1024)


def sub_roll(value, shift):
    shift = shift % value.shape[0]
    return value if shift == 0 else pltpu.roll(value, shift, 0)


def lane_roll(value, shift):
    shift = shift % value.shape[1]
    return value if shift == 0 else pltpu.roll(value, shift, 1)


def iotas(shape):
    return lax.broadcasted_iota(jnp.int32, shape, 0), lax.broadcasted_iota(jnp.int32, shape, 1)


def one_row(vectors, row, step):
    rows = vectors[0].shape[0] // 2
    local = iotas(vectors[0].shape)[0] % rows
    packed = []
    for start in range(0, len(vectors), rows):
        total = vectors[start]
        for t in range(1, rows):
            total = jnp.where(
                local == row + step * t, sub_roll(vectors[start + t], step * t), total
            )
        packed.append(total)
    return packed


def pack_north_kernel(levels, tracers_in, cx_in, cy_in, tracers, cx, cy, north, semaphores):
    copies = [
        pltpu.make_async_copy(source, into, semaphores.at[i])
        for i, (source, into) in enumerate(((tracers_in, tracers), (cx_in, cx), (cy_in, cy)))
    ]
    for copy in copies:
        copy.start()
    for copy in copies:
        copy.wait()
    pairs = levels // 2
    half = pairs // 2
    tile = tracers.shape[1:]
    rows = tile[0] // 2
    upper = iotas(tile)[0] % rows >= rows // 2
    fields = tracers.shape[0] // pairs
    for f in range(fields):
        for k in range(half):
            one, two = tracers[f * pairs + 2 * k], tracers[f * pairs + 2 * k + 1]
            north[f * half + k] = jnp.where(upper, one, sub_roll(two, 2))
    base = fields * half
    for k in range(half):
        north[base + k] = jnp.where(upper, cy[2 * k], sub_roll(cy[2 * k + 1], 2))
    for k, value in enumerate(one_row([cx[k] for k in range(pairs)], rows - 1, -1)):
        north[base + half + k] = value


def pack_edges_kernel(levels, tracers, cx, cy, edge, corner, south_rows):
    pairs = levels // 2
    half = pairs // 2
    fields = tracers.shape[0] // pairs
    tile = tracers.shape[1:]
    rows = tile[0] // 2
    lanes = tile[1]
    group = lanes // levels
    sub, lane = iotas(tile)
    upper = sub % rows >= rows // 2
    odd_sub = sub % 2 == 1
    corners = [jnp.zeros(tile, F32)]

    def pack_edge(vectors, slot):
        total = lane_roll(vectors[0], 2)
        for k in range(1, pairs):
            total = jnp.where(
                lane // (2 * group) == k, lane_roll(vectors[k], 2 + 2 * group * k), total
            )
        total = jnp.where(
            lane % (2 * group) < group, total, sub_roll(lane_roll(total, group), rows)
        )
        edge[slot] = jnp.where(lane % group < group // 2, total, lane_roll(total, group // 2))
        for k in range(half):
            one, two = vectors[2 * k], vectors[2 * k + 1]
            place = slot * half + k
            north = jnp.where(upper, one, sub_roll(two, 2))
            south = jnp.where(upper, sub_roll(two, -2), one)
            if slot < fields:
                south_rows[place] = south
            value = lane_roll(jnp.where(odd_sub, north, south), 2 * place + 1)
            corners[0] = jnp.where(lane // 2 == place, value, corners[0])

    for f in range(fields):
        pack_edge([tracers[f * pairs + k] for k in range(pairs)], f)
    pack_edge([cx[k] for k in range(pairs)], fields)
    pack_edge([cy[k] for k in range(pairs)], fields + 1)
    corner[...] = corners[0]
    courant = one_row([cx[k] for k in range(pairs)], 0, 1)
    courant += one_row([cy[k] for k in range(pairs)], 0, 1)
    for k, value in enumerate(courant):
        south_rows[fields * half + k] = value


def cosine_sums(values):
    count = len(values)
    if count == 1:
        return values
    half = count // 2
    plus = [values[n] + values[count - 1 - n] for n in range(half)]
    minus = [
        (values[n] - values[count - 1 - n])
        * (0.5 / math.cos(math.pi * (2 * n + 1) / (2 * count)))
        for n in range(half)
    ]
    even = cosine_sums(plus)
    odd = cosine_sums(minus)
    result = []
    for k in range(half):
        result.append(even[k])
        result.append(odd[k] + odd[k + 1] if k + 1 < half else odd[k])
    return result


def cosine_series(values):
    count = len(values)
    if count == 1:
        return values
    half = count // 2
    odd_in = [values[2 * k + 1] + values[2 * k - 1] if k else values[1] for k in range(half)]
    even = cosine_series(values[0::2])
    odd = cosine_series(odd_in)
    odd = [
        odd[n] * (0.5 / math.cos(math.pi * (2 * n + 1) / (2 * count))) for n in range(half)
    ]
    return [even[n] + odd[n] for n in range(half)] + [
        even[n] - odd[n] for n in range(half - 1, -1, -1)
    ]


def prep_kernel(coeffs, profile, klass, target, decay, source, onehot):
    levels, pairs = decay.shape[:2]
    fields = profile.shape[0]
    tile = decay.shape[2:]
    rows, lanes = klass.shape
    sub, lane = iotas(tile)
    low = sub < rows
    kind = jnp.concatenate([klass[...], klass[...]], axis=0)
    is_two = kind == 2
    is_one = kind == 1

    def by_class(which, f):
        return jnp.where(
            is_two,
            coeffs[which, 2, f] * 0.25,
            jnp.where(is_one, coeffs[which, 1, f] * 0.5, coeffs[which, 0, f]),
        )

    for p in range(pairs):
        f1 = 2 * p
        f2 = min(2 * p + 1, fields - 1)
        diffusion = jnp.where(low, by_class(0, f1), by_class(0, f2))
        relax = jnp.where(low, by_class(1, f1), by_class(1, f2))
        waves = cosine_sums([jnp.where(low, profile[f1, l], profile[f2, l]) for l in range(levels)])
        for m in range(levels):
            rate = relax + diffusion * (2.0 - 2.0 * math.cos(math.pi * m / levels))
            once = 1.0 / (1.0 + rate)
            square = once * once
            twice = once + square
            steps = jnp.where(is_two, twice + twice * square, jnp.where(is_one, twice, once))
            steps = steps * ((1.0 if m == 0 else 2.0) / levels)
            decay[m, p] = steps * rate
            source[m, p] = steps * relax * waves[m]
    low_part = target[...] & (lanes - 1)
    slot, _ = iotas((lanes, lanes))
    for r in range(rows):
        hit = jnp.where(slot == low_part[r : r + 1], 1.0, 0.0)
        onehot[r * lanes : (r + 1) * lanes, :] = jnp.transpose(hit).astype(jnp.bfloat16)


def combine(coefs, center, east, west, north, south):
    return (
        coefs[0] * center
        + (coefs[1] * east + coefs[2] * west)
        + (coefs[3] * north + coefs[4] * south)
    )


def coefficients(here_x, west_x, here_y, south_y):
    return (
        1.0
        - jnp.maximum(here_x, 0.0)
        + jnp.minimum(west_x, 0.0)
        - jnp.maximum(here_y, 0.0)
        + jnp.minimum(south_y, 0.0),
        jnp.maximum(-here_x, 0.0),
        jnp.maximum(west_x, 0.0),
        jnp.maximum(-here_y, 0.0),
        jnp.maximum(south_y, 0.0),
    )


def side_by_side(value, place):
    return jnp.where(place == 3, lane_roll(value, -2), value)


def beside(edge, edge_west, edge_east, slot, place):
    from_east = (place == 2) | (place == 3)
    from_west = (place == 4) | (place == 5)
    return jnp.where(
        from_east, edge_east[slot], jnp.where(from_west, edge_west[slot], edge[slot])
    )


def spread(value, levels):
    lanes = value.shape[1]
    rows = value.shape[0] // 2
    group = lanes // levels
    sub, lane = iotas(value.shape)
    value = side_by_side(value, lane % group)
    value = jnp.where(sub < rows, value, sub_roll(lane_roll(value, -group), rows))
    return [lane_roll(value, -(2 * group * k + 3)) for k in range(levels // 2)]


def shift_kernel(levels, tracers, edge, edge_west, edge_east, east, west):
    pairs = levels // 2
    tile = tracers.shape[1:]
    lanes = tile[1]
    lane = iotas(tile)[1]
    place = lane % (lanes // levels)
    for f in range(tracers.shape[0] // pairs):
        for k, sides in enumerate(spread(beside(edge, edge_west, edge_east, f, place), levels)):
            own = tracers[f * pairs + k]
            east[f * pairs + k] = jnp.where(lane == lanes - 1, sides, lane_roll(own, -1))
            west[f * pairs + k] = jnp.where(lane == 0, sides, lane_roll(own, 1))


def next_kernel(levels, cx, edge, edge_west, edge_east, next_sides, west_x, sides_y):
    pairs = levels // 2
    fields = next_sides.shape[0] // pairs
    tile = cx.shape[1:]
    rows = tile[0] // 2
    sub, lane = iotas(tile)
    place = lane % (tile[1] // levels)

    def own_rows(slot):
        value = beside(edge, edge_west, edge_east, slot, place)
        return jnp.where(sub < rows, value, 0.0)

    edge_x = own_rows(fields)
    edge_y = own_rows(fields + 1)
    coefs = coefficients(edge_x, lane_roll(edge_x, 1), edge_y, sub_roll(edge_y, 1))
    for k, sides in enumerate(spread(edge_x, levels)):
        west_x[k] = jnp.where(lane == 0, sides, lane_roll(cx[k], 1))
    for k, sides in enumerate(spread(edge_y, levels)):
        sides_y[k] = sides
    for f in range(fields):
        raw = own_rows(f)
        moved = combine(
            coefs,
            raw,
            lane_roll(raw, -1),
            lane_roll(raw, 1),
            sub_roll(raw, -1),
            sub_roll(raw, 1),
        )
        for k, sides in enumerate(spread(moved, levels)):
            next_sides[f * pairs + k] = sides


def transport_and_solve(
    fields,
    levels,
    tracers,
    cx,
    cy,
    from_south,
    from_north,
    east,
    west,
    next_sides,
    west_x,
    sides_y,
    corner_sw,
    corner_se,
    corner_nw,
    corner_ne,
    decay,
    source,
    state,
    own_coefs,
    halo_coefs,
):
    pairs = levels // 2
    half = pairs // 2
    tile = tracers.shape[1:]
    rows = tile[0] // 2
    lanes = tile[1]
    group = lanes // levels
    sub, lane = iotas(tile)
    local = sub % rows
    low = sub < rows
    first_lane = lane == 0
    last_lane = lane == lanes - 1
    odd_sub = sub % 2 == 1
    bottom = local == 0
    top = local == rows - 1
    in_first = bottom | top

    even_lane = lane % 2 == 0
    dense = jnp.where(
        odd_sub,
        jnp.where(even_lane, lane_roll(corner_se[...], -1), lane_roll(corner_sw[...], 1)),
        jnp.where(even_lane, lane_roll(corner_ne[...], -1), lane_roll(corner_nw[...], 1)),
    )

    def corner(slot, k):
        return pltpu.roll(dense, lanes - 2 * (slot * half + k) - 1, 1)


    def turned(value):
        up, down = sub_roll(value, rows - 1), sub_roll(value, 1 - rows)
        return ((up, down), (down, up))

    def inner_rows(first, second):
        (first_up, first_down), _ = turned(first)
        (second_up, second_down), _ = turned(second)
        return (
            jnp.where(in_first, first_up, second_down),
            jnp.where(in_first, first_down, second_up),
        )

    base = fields * half
    count = pairs // rows
    for k in range(half):
        quad, t = 2 * k // rows, 2 * k % rows
        packed_south = from_south[base + half + quad]
        packed_north = from_north[base + quad]
        packed_north_y = from_north[base + count + quad]
        message_y = from_south[base + k]
        south_x = jnp.where(in_first, sub_roll(packed_south, t), sub_roll(packed_south, 3 + t))
        north_x = jnp.where(in_first, sub_roll(packed_north, -t), sub_roll(packed_north, 5 - t))
        north_y = jnp.where(
            in_first, sub_roll(packed_north_y, -t), sub_roll(packed_north_y, 5 - t)
        )
        halo_x = jnp.where(odd_sub, south_x, north_x)
        halo_y = jnp.where(odd_sub, message_y, north_y)
        halo_west = jnp.where(first_lane, corner(fields, k), lane_roll(halo_x, 1))
        _, inner_top = inner_rows(cy[2 * k], cy[2 * k + 1])
        halo_south = jnp.where(odd_sub, sub_roll(message_y, 1), inner_top)
        for c, value in enumerate(coefficients(halo_x, halo_west, halo_y, halo_south)):
            halo_coefs[k, c] = value
        places = turned(message_y)
        edge_places = turned(corner(fields + 1, k))
        for i in range(2):
            j = 2 * k + i
            south_y = jnp.where(bottom, places[i][1], sub_roll(cy[j], 1))
            for c, value in enumerate(coefficients(cx[j], west_x[j], cy[j], south_y)):
                own_coefs[j, c] = value
            south_face = edge_places[i][1]
            own_coefs[j, 5] = jnp.where(bottom, jnp.minimum(south_face, 0.0), 0.0)
            own_coefs[j, 6] = jnp.where(
                bottom,
                jnp.maximum(south_face, 0.0),
                jnp.where(top, jnp.maximum(-sides_y[j], 0.0), 0.0),
            )

    def advect(f, k, own_set, halo_set):
        message_south = from_south[f * half + k]
        message_north = from_north[f * half + k]
        slots = (f * pairs + 2 * k, f * pairs + 2 * k + 1)
        own = [tracers[slot] for slot in slots]
        own_east = [east[slot] for slot in slots]
        own_west = [west[slot] for slot in slots]
        sides = corner(f, k)
        halo = jnp.where(odd_sub, message_south, message_north)
        inner_bottom, inner_top = inner_rows(*own)
        next_halo = combine(
            halo_set,
            halo,
            jnp.where(last_lane, sides, lane_roll(halo, -1)),
            jnp.where(first_lane, sides, lane_roll(halo, 1)),
            jnp.where(odd_sub, inner_bottom, sub_roll(message_north, -1)),
            jnp.where(odd_sub, sub_roll(message_south, 1), inner_top),
        )
        places, next_places, side_places = turned(halo), turned(next_halo), turned(sides)
        results = []
        for i in range(2):
            north, south = places[i]
            once = combine(
                own_set[i],
                own[i],
                own_east[i],
                own_west[i],
                jnp.where(top, north, sub_roll(own[i], -1)),
                jnp.where(bottom, south, sub_roll(own[i], 1)),
            )
            side_north, side_south = side_places[i]
            next_column = (
                next_sides[slots[i]]
                + own_set[i][5] * jnp.where(first_lane, own_west[i], own_east[i])
                + own_set[i][6] * jnp.where(bottom, side_south, side_north)
            )
            north, south = next_places[i]
            results.append(
                combine(
                    own_set[i],
                    once,
                    jnp.where(last_lane, next_column, lane_roll(once, -1)),
                    jnp.where(first_lane, next_column, lane_roll(once, 1)),
                    jnp.where(top, north, sub_roll(once, -1)),
                    jnp.where(bottom, south, sub_roll(once, 1)),
                )
            )
        return results

    def transport(p):
        f1 = 2 * p
        f2 = jnp.minimum(f1 + 1, fields - 1)
        columns = []
        for k in range(half):
            own_set = [[own_coefs[2 * k + i, c] for c in range(7)] for i in range(2)]
            halo_set = [halo_coefs[k, c] for c in range(5)]
            for one, two in zip(
                advect(f1, k, own_set, halo_set), advect(f2, k, own_set, halo_set)
            ):
                columns.append(jnp.where(low, one, sub_roll(two, rows)))
                columns.append(jnp.where(low, sub_roll(one, rows), two))
        return tuple(columns)

    def solve(p, columns):
        f1 = 2 * p
        f2 = jnp.minimum(f1 + 1, fields - 1)
        waves = cosine_sums(columns)
        change = cosine_series([source[m, p] - decay[m, p] * waves[m] for m in range(levels)])
        square = change[0] * change[0]
        for l in range(1, levels):
            square = square + change[l] * change[l]
        for k in range(pairs):
            even, odd = (columns[l] + change[l] for l in (2 * k, 2 * k + 1))
            state[f1 * pairs + k] = jnp.where(low, even, sub_roll(odd, rows))
            state[f2 * pairs + k] = jnp.where(low, sub_roll(even, rows), odd)
        return jnp.where(low | (f1 + 1 < fields), square, 0.0)

    def pair_step(p, carried):
        total, columns = carried
        following = transport(p)
        return total + solve(p - 1, columns), following

    field_pairs = (fields + 1) // 2
    total, columns = lax.fori_loop(
        1, field_pairs, pair_step, (jnp.zeros(tile, F32), transport(0))
    )
    return total + solve(field_pairs - 1, columns)


def main_kernel(fields, levels, *refs):
    inputs, (target, onehot), (state, placed), coefs = refs[:16], refs[16:18], refs[18:20], refs[20:]
    rows, lanes = target.shape
    total = transport_and_solve(fields, levels, *inputs, state, *coefs)

    heat = (total + sub_roll(total, rows)) * (1.0 / (fields * levels))
    first = heat.astype(jnp.bfloat16).astype(F32)
    rest = heat - first
    second = rest.astype(jnp.bfloat16).astype(F32)
    third = rest - second
    spans = placed.shape[0]
    slot_row, _ = iotas((spans, lanes))
    high = lax.shift_right_logical(target[...], lanes.bit_length() - 1)
    hits = [slot_row == high[r : r + 1] for r in range(rows)]
    left = jnp.concatenate(
        [
            jnp.concatenate(
                [
                    jnp.where(hits[r], part[r : r + 1], 0.0).astype(jnp.bfloat16)
                    for r in range(rows)
                ],
                axis=1,
            )
            for part in (first, second, third)
        ],
        axis=0,
    )
    result = jnp.dot(left, onehot[...], preferred_element_type=F32)
    placed[...] = result[:spans] + result[spans : 2 * spans] + result[2 * spans :]


def finish_kernel(parts, state, total_out, state_out, total, semaphores):
    copy_state = pltpu.make_async_copy(state, state_out, semaphores.at[0])
    copy_state.start()
    value = parts[0]
    for i in range(1, parts.shape[0]):
        value = value + parts[i]
    total[...] = value
    copy_total = pltpu.make_async_copy(total, total_out, semaphores.at[1])
    copy_total.start()
    copy_state.wait()
    copy_total.wait()


def body(tracers, courant_x, courant_y, physics_ref, class_coeffs, span_target, cloud_class):
    fields, levels, rows, cols = tracers.shape
    wide = lax.axis_size("wide")
    narrow = lax.axis_size("narrow")
    pairs = levels // 2
    half = pairs // 2
    tile = (2 * rows, cols)
    field_pairs = (fields + 1) // 2
    flat = tracers.reshape(fields * pairs, *tile)
    cx = courant_x.reshape(pairs, *tile)
    cy = courant_y.reshape(pairs, *tile)
    quads = pairs // rows

    def array(*shape, dtype=F32):
        return jax.ShapeDtypeStruct(shape, dtype)

    flat, cx, cy, north = pl.pallas_call(
        functools.partial(pack_north_kernel, levels),
        out_shape=(
            array(fields * pairs, *tile),
            array(pairs, *tile),
            array(pairs, *tile),
            array(fields * half + half + quads, *tile),
        ),
        in_specs=[HBM] * 3,
        out_specs=[VMEM] * 4,
        scratch_shapes=[pltpu.SemaphoreType.DMA((3,))],
        compiler_params=PARAMS,
    )(*(pltpu.with_memory_space_constraint(x, pltpu.HBM) for x in (flat, cx, cy)))
    edge, corner, south = pl.pallas_call(
        functools.partial(pack_edges_kernel, levels),
        out_shape=(
            array(fields + 2, *tile),
            array(*tile),
            array(fields * half + 2 * quads, *tile),
        ),
        in_specs=[VMEM] * 3,
        out_specs=[VMEM] * 3,
        compiler_params=PARAMS,
    )(flat, cx, cy)

    def send(value, up, right):
        pairs_ = []
        for w in range(wide):
            for n in range(narrow):
                to = ((w + up) % wide) * narrow + (n + right) % narrow
                pairs_.append((w * narrow + n, to))
        return lax.ppermute(value, ("wide", "narrow"), pairs_)

    def to_both_sides(value, up):
        from_west = send(value, up, 1)
        from_east = from_west if narrow == 2 else send(value, up, -1)
        return from_west, from_east

    from_south = send(north, 1, 0)
    from_north = send(south, -1, 0)
    edge_west, edge_east = to_both_sides(edge, 0)
    corner_sw, corner_se = to_both_sides(corner, 1)
    corner_nw, corner_ne = to_both_sides(corner, -1)

    decay, source, onehot = pl.pallas_call(
        prep_kernel,
        out_shape=(array(levels, field_pairs, *tile),) * 2
        + (array(rows * cols, cols, dtype=jnp.bfloat16),),
        in_specs=[SMEM, SMEM, VMEM, VMEM],
        out_specs=[VMEM] * 3,
        cost_estimate=pl.CostEstimate(flops=4000000, bytes_accessed=2000000, transcendentals=0),
        compiler_params=PARAMS,
    )(class_coeffs, physics_ref, cloud_class, span_target)

    shifted = pl.pallas_call(
        functools.partial(shift_kernel, levels),
        out_shape=(array(fields * pairs, *tile),) * 2,
        in_specs=[VMEM] * 4,
        out_specs=[VMEM] * 2,
        compiler_params=PARAMS,
    )(flat, edge, edge_west, edge_east)
    edge_columns = pl.pallas_call(
        functools.partial(next_kernel, levels),
        out_shape=(array(fields * pairs, *tile),) + (array(pairs, *tile),) * 2,
        in_specs=[VMEM] * 4,
        out_specs=[VMEM] * 3,
        compiler_params=PARAMS,
    )(cx, edge, edge_west, edge_east)
    state, placed = pl.pallas_call(
        functools.partial(main_kernel, fields, levels),
        out_shape=(array(fields * pairs, *tile), array(wide * rows, cols)),
        in_specs=[VMEM] * 18,
        out_specs=[VMEM] * 2,
        scratch_shapes=[
            pltpu.VMEM((pairs, 7) + tile, F32),
            pltpu.VMEM((half, 5) + tile, F32),
        ],
        compiler_params=PARAMS,
    )(
        flat,
        cx,
        cy,
        from_south,
        from_north,
        *shifted,
        *edge_columns,
        corner_sw,
        corner_se,
        corner_nw,
        corner_ne,
        decay,
        source,
        span_target,
        onehot,
    )
    received = lax.all_to_all(
        placed.reshape(wide, rows, cols), "wide", split_axis=0, concat_axis=0, tiled=True
    )
    span_diag, state = pl.pallas_call(
        finish_kernel,
        out_shape=(array(rows, cols), array(fields * pairs, *tile)),
        in_specs=[VMEM] * 2,
        out_specs=[HBM] * 2,
        scratch_shapes=[pltpu.VMEM((rows, cols), F32), pltpu.SemaphoreType.DMA((2,))],
        compiler_params=PARAMS,
    )(received, state)
    return state.reshape(fields, levels, rows, cols), span_diag


def solution(mesh):
    return jax.shard_map(
        body,
        mesh=mesh,
        in_specs=(
            P(None, None, "wide", "narrow"),
            P(None, "wide", "narrow"),
            P(None, "wide", "narrow"),
            P(),
            P(),
            P("wide", "narrow"),
            P("wide", "narrow"),
        ),
        out_specs=(P(None, None, "wide", "narrow"), P("wide", "narrow")),
        check_vma=False,
    )
```

```python
import functools
import math

import jax
import jax.numpy as jnp
from jax import lax
from jax.experimental import pallas as pl
from jax.experimental.pallas import tpu as pltpu
from jax.sharding import PartitionSpec as P

VMEM = pl.BlockSpec(memory_space=pltpu.VMEM)
HBM = pl.BlockSpec(memory_space=pltpu.HBM)
SMEM = pl.BlockSpec(memory_space=pltpu.SMEM)
F32 = jnp.float32
PARAMS = pltpu.CompilerParams(vmem_limit_bytes=12 * 1024 * 1024)


def sub_roll(value, shift):
    shift = shift % value.shape[0]
    return value if shift == 0 else pltpu.roll(value, shift, 0)


def lane_roll(value, shift):
    shift = shift % value.shape[1]
    return value if shift == 0 else pltpu.roll(value, shift, 1)


def iotas(shape):
    return lax.broadcasted_iota(jnp.int32, shape, 0), lax.broadcasted_iota(jnp.int32, shape, 1)


def one_row(vectors, row, step):
    rows = vectors[0].shape[0] // 2
    local = iotas(vectors[0].shape)[0] % rows
    packed = []
    for start in range(0, len(vectors), rows):
        total = vectors[start]
        for t in range(1, rows):
            total = jnp.where(
                local == row + step * t, sub_roll(vectors[start + t], step * t), total
            )
        packed.append(total)
    return packed


def inner_flux(value, courant):
    return jnp.maximum(courant, 0.0) * value + jnp.minimum(courant, 0.0) * sub_roll(value, -1)


def northward_rows(value, courant):
    local = iotas(value.shape)[0] % (value.shape[0] // 2)
    return jnp.where(local == 2, inner_flux(value, courant), value)


def southward_rows(value, courant):
    local = iotas(value.shape)[0] % (value.shape[0] // 2)
    return jnp.where(local == 1, sub_roll(-inner_flux(value, courant), 1), value)


def pack_north_kernel(levels, tracers_in, cx_in, cy_in, tracers, cx, cy, north, semaphores):
    copies = [
        pltpu.make_async_copy(source, into, semaphores.at[i])
        for i, (source, into) in enumerate(((tracers_in, tracers), (cx_in, cx), (cy_in, cy)))
    ]
    for copy in copies:
        copy.start()
    for copy in copies:
        copy.wait()
    pairs = levels // 2
    half = pairs // 2
    tile = tracers.shape[1:]
    rows = tile[0] // 2
    upper = iotas(tile)[0] % rows >= rows // 2
    fields = tracers.shape[0] // pairs
    for f in range(fields):
        for k in range(half):
            one, two = (
                northward_rows(tracers[f * pairs + j], cy[j]) for j in (2 * k, 2 * k + 1)
            )
            north[f * half + k] = jnp.where(upper, one, sub_roll(two, 2))
    courant = one_row([cx[k] for k in range(pairs)], rows - 1, -1)
    courant += one_row([cy[k] for k in range(pairs)], rows - 1, -1)
    for k, value in enumerate(courant):
        north[fields * half + k] = value


def pack_edges_kernel(levels, tracers, cx, cy, edge, corner, south_rows):
    pairs = levels // 2
    half = pairs // 2
    fields = tracers.shape[0] // pairs
    tile = tracers.shape[1:]
    rows = tile[0] // 2
    lanes = tile[1]
    group = lanes // levels
    sub, lane = iotas(tile)
    upper = sub % rows >= rows // 2
    odd_sub = sub % 2 == 1
    corners = [jnp.zeros(tile, F32)]

    def pack_edge(vectors, slot):
        total = lane_roll(vectors[0], 2)
        for k in range(1, pairs):
            total = jnp.where(
                lane // (2 * group) == k, lane_roll(vectors[k], 2 + 2 * group * k), total
            )
        total = jnp.where(
            lane % (2 * group) < group, total, sub_roll(lane_roll(total, group), rows)
        )
        edge[slot] = jnp.where(lane % group < group // 2, total, lane_roll(total, group // 2))
        for k in range(half):
            one, two = vectors[2 * k], vectors[2 * k + 1]
            place = slot * half + k
            north = jnp.where(upper, one, sub_roll(two, 2))
            south = jnp.where(upper, sub_roll(two, -2), one)
            if slot < fields:
                first = southward_rows(one, cy[2 * k])
                second = southward_rows(two, cy[2 * k + 1])
                south_rows[place] = jnp.where(upper, sub_roll(second, -2), first)
            value = lane_roll(jnp.where(odd_sub, north, south), 2 * place + 1)
            corners[0] = jnp.where(lane // 2 == place, value, corners[0])

    for f in range(fields):
        pack_edge([tracers[f * pairs + k] for k in range(pairs)], f)
    pack_edge([cx[k] for k in range(pairs)], fields)
    pack_edge([cy[k] for k in range(pairs)], fields + 1)
    corner[...] = corners[0]
    for k, value in enumerate(one_row([cx[k] for k in range(pairs)], 0, 1)):
        south_rows[fields * half + k] = value


def cosine_sums(values):
    count = len(values)
    if count == 1:
        return values
    half = count // 2
    plus = [values[n] + values[count - 1 - n] for n in range(half)]
    minus = [
        (values[n] - values[count - 1 - n])
        * (0.5 / math.cos(math.pi * (2 * n + 1) / (2 * count)))
        for n in range(half)
    ]
    even = cosine_sums(plus)
    odd = cosine_sums(minus)
    result = []
    for k in range(half):
        result.append(even[k])
        result.append(odd[k] + odd[k + 1] if k + 1 < half else odd[k])
    return result


def cosine_series(values):
    count = len(values)
    if count == 1:
        return values
    half = count // 2
    odd_in = [values[2 * k + 1] + values[2 * k - 1] if k else values[1] for k in range(half)]
    even = cosine_series(values[0::2])
    odd = cosine_series(odd_in)
    odd = [
        odd[n] * (0.5 / math.cos(math.pi * (2 * n + 1) / (2 * count))) for n in range(half)
    ]
    return [even[n] + odd[n] for n in range(half)] + [
        even[n] - odd[n] for n in range(half - 1, -1, -1)
    ]


def prep_kernel(coeffs, profile, klass, target, decay, source, onehot):
    levels, pairs = decay.shape[:2]
    fields = profile.shape[0]
    tile = decay.shape[2:]
    rows, lanes = klass.shape
    sub, lane = iotas(tile)
    low = sub < rows
    kind = jnp.concatenate([klass[...], klass[...]], axis=0)
    is_two = kind == 2
    is_one = kind == 1

    def by_class(which, f):
        return jnp.where(
            is_two,
            coeffs[which, 2, f] * 0.25,
            jnp.where(is_one, coeffs[which, 1, f] * 0.5, coeffs[which, 0, f]),
        )

    for p in range(pairs):
        f1 = 2 * p
        f2 = min(2 * p + 1, fields - 1)
        diffusion = jnp.where(low, by_class(0, f1), by_class(0, f2))
        relax = jnp.where(low, by_class(1, f1), by_class(1, f2))
        waves = cosine_sums([jnp.where(low, profile[f1, l], profile[f2, l]) for l in range(levels)])
        for m in range(levels):
            rate = relax + diffusion * (2.0 - 2.0 * math.cos(math.pi * m / levels))
            once = 1.0 / (1.0 + rate)
            square = once * once
            twice = once + square
            steps = jnp.where(is_two, twice + twice * square, jnp.where(is_one, twice, once))
            steps = steps * ((1.0 if m == 0 else 2.0) / levels)
            decay[m, p] = steps * rate
            source[m, p] = steps * relax * waves[m]
    low_part = target[...] & (lanes - 1)
    slot, _ = iotas((lanes, lanes))
    for r in range(rows):
        hit = jnp.where(slot == low_part[r : r + 1], 1.0, 0.0)
        onehot[r * lanes : (r + 1) * lanes, :] = jnp.transpose(hit).astype(jnp.bfloat16)


def combine(coefs, center, east, west, north, south):
    return (
        coefs[0] * center
        + (coefs[1] * east + coefs[2] * west)
        + (coefs[3] * north + coefs[4] * south)
    )


def coefficients(here_x, west_x, here_y, south_y):
    return (
        1.0
        - jnp.maximum(here_x, 0.0)
        + jnp.minimum(west_x, 0.0)
        - jnp.maximum(here_y, 0.0)
        + jnp.minimum(south_y, 0.0),
        jnp.maximum(-here_x, 0.0),
        jnp.maximum(west_x, 0.0),
        jnp.maximum(-here_y, 0.0),
        jnp.maximum(south_y, 0.0),
    )


def side_by_side(value, place):
    return jnp.where(place == 3, lane_roll(value, -2), value)


def beside(edge, edge_west, edge_east, slot, place):
    from_east = (place == 2) | (place == 3)
    from_west = (place == 4) | (place == 5)
    return jnp.where(
        from_east, edge_east[slot], jnp.where(from_west, edge_west[slot], edge[slot])
    )


def spread(value, levels):
    lanes = value.shape[1]
    rows = value.shape[0] // 2
    group = lanes // levels
    sub, lane = iotas(value.shape)
    value = side_by_side(value, lane % group)
    value = jnp.where(sub < rows, value, sub_roll(lane_roll(value, -group), rows))
    return [lane_roll(value, -(2 * group * k + 3)) for k in range(levels // 2)]


def shift_kernel(levels, tracers, edge, edge_west, edge_east, east, west):
    pairs = levels // 2
    tile = tracers.shape[1:]
    lanes = tile[1]
    lane = iotas(tile)[1]
    place = lane % (lanes // levels)
    for f in range(tracers.shape[0] // pairs):
        for k, sides in enumerate(spread(beside(edge, edge_west, edge_east, f, place), levels)):
            own = tracers[f * pairs + k]
            east[f * pairs + k] = jnp.where(lane == lanes - 1, sides, lane_roll(own, -1))
            west[f * pairs + k] = jnp.where(lane == 0, sides, lane_roll(own, 1))


def next_kernel(levels, cx, edge, edge_west, edge_east, next_sides, west_x, sides_y):
    pairs = levels // 2
    fields = next_sides.shape[0] // pairs
    tile = cx.shape[1:]
    rows = tile[0] // 2
    sub, lane = iotas(tile)
    place = lane % (tile[1] // levels)

    def own_rows(slot):
        value = beside(edge, edge_west, edge_east, slot, place)
        return jnp.where(sub < rows, value, 0.0)

    edge_x = own_rows(fields)
    edge_y = own_rows(fields + 1)
    coefs = coefficients(edge_x, lane_roll(edge_x, 1), edge_y, sub_roll(edge_y, 1))
    for k, sides in enumerate(spread(edge_x, levels)):
        west_x[k] = jnp.where(lane == 0, sides, lane_roll(cx[k], 1))
    for k, sides in enumerate(spread(edge_y, levels)):
        sides_y[k] = sides
    for f in range(fields):
        raw = own_rows(f)
        moved = combine(
            coefs,
            raw,
            lane_roll(raw, -1),
            lane_roll(raw, 1),
            sub_roll(raw, -1),
            sub_roll(raw, 1),
        )
        for k, sides in enumerate(spread(moved, levels)):
            next_sides[f * pairs + k] = sides


def transport_and_solve(
    fields,
    levels,
    tracers,
    cx,
    cy,
    from_south,
    from_north,
    east,
    west,
    next_sides,
    west_x,
    sides_y,
    corner_sw,
    corner_se,
    corner_nw,
    corner_ne,
    decay,
    source,
    state,
    own_coefs,
    halo_coefs,
):
    pairs = levels // 2
    half = pairs // 2
    tile = tracers.shape[1:]
    rows = tile[0] // 2
    lanes = tile[1]
    group = lanes // levels
    sub, lane = iotas(tile)
    local = sub % rows
    low = sub < rows
    first_lane = lane == 0
    last_lane = lane == lanes - 1
    odd_sub = sub % 2 == 1
    bottom = local == 0
    top = local == rows - 1
    in_first = bottom | top

    even_lane = lane % 2 == 0
    dense = jnp.where(
        odd_sub,
        jnp.where(even_lane, lane_roll(corner_se[...], -1), lane_roll(corner_sw[...], 1)),
        jnp.where(even_lane, lane_roll(corner_ne[...], -1), lane_roll(corner_nw[...], 1)),
    )

    def corner(slot, k):
        return pltpu.roll(dense, lanes - 2 * (slot * half + k) - 1, 1)


    def turned(value):
        up, down = sub_roll(value, rows - 1), sub_roll(value, 1 - rows)
        return ((up, down), (down, up))

    def inner_rows(first, second):
        (first_up, first_down), _ = turned(first)
        (second_up, second_down), _ = turned(second)
        return (
            jnp.where(in_first, first_up, second_down),
            jnp.where(in_first, first_down, second_up),
        )

    base = fields * half
    count = pairs // rows
    for k in range(half):
        quad, t = 2 * k // rows, 2 * k % rows
        packed_south = from_south[base + quad]
        packed_south_y = from_south[base + count + quad]
        packed_north = from_north[base + quad]
        south_x = jnp.where(in_first, sub_roll(packed_south, t), sub_roll(packed_south, 3 + t))
        south_y = jnp.where(
            in_first, sub_roll(packed_south_y, t), sub_roll(packed_south_y, 3 + t)
        )
        north_x = jnp.where(in_first, sub_roll(packed_north, -t), sub_roll(packed_north, 5 - t))
        halo_x = jnp.where(odd_sub, south_x, north_x)
        halo_west = jnp.where(first_lane, corner(fields, k), lane_roll(halo_x, 1))
        _, inner_top = inner_rows(cy[2 * k], cy[2 * k + 1])
        face = jnp.where(odd_sub, -south_y, inner_top)
        halo_coefs[k, 0] = (
            1.0
            - jnp.maximum(halo_x, 0.0)
            + jnp.minimum(halo_west, 0.0)
            + jnp.minimum(face, 0.0)
        )
        halo_coefs[k, 1] = jnp.maximum(-halo_x, 0.0)
        halo_coefs[k, 2] = jnp.maximum(halo_west, 0.0)
        halo_coefs[k, 3] = jnp.maximum(face, 0.0)
        places = turned(south_y)
        edge_places = turned(corner(fields + 1, k))
        for i in range(2):
            j = 2 * k + i
            below = jnp.where(bottom, places[i][1], sub_roll(cy[j], 1))
            for c, value in enumerate(coefficients(cx[j], west_x[j], cy[j], below)):
                own_coefs[j, c] = value
            south_face = edge_places[i][1]
            own_coefs[j, 5] = jnp.where(bottom, jnp.minimum(south_face, 0.0), 0.0)
            own_coefs[j, 6] = jnp.where(
                bottom,
                jnp.maximum(south_face, 0.0),
                jnp.where(top, jnp.maximum(-sides_y[j], 0.0), 0.0),
            )

    def advect(f, k, own_set, halo_set):
        message_south = from_south[f * half + k]
        message_north = from_north[f * half + k]
        slots = (f * pairs + 2 * k, f * pairs + 2 * k + 1)
        own = [tracers[slot] for slot in slots]
        own_east = [east[slot] for slot in slots]
        own_west = [west[slot] for slot in slots]
        sides = corner(f, k)
        halo = jnp.where(odd_sub, message_south, message_north)
        inner_bottom, inner_top = inner_rows(*own)
        flux = jnp.where(odd_sub, sub_roll(message_south, 1), sub_roll(message_north, -1))
        next_halo = (
            halo_set[0] * halo
            + (
                halo_set[1] * jnp.where(last_lane, sides, lane_roll(halo, -1))
                + halo_set[2] * jnp.where(first_lane, sides, lane_roll(halo, 1))
            )
            + (halo_set[3] * jnp.where(odd_sub, inner_bottom, inner_top) + flux)
        )
        places, next_places, side_places = turned(halo), turned(next_halo), turned(sides)
        results = []
        for i in range(2):
            north, south = places[i]
            once = combine(
                own_set[i],
                own[i],
                own_east[i],
                own_west[i],
                jnp.where(top, north, sub_roll(own[i], -1)),
                jnp.where(bottom, south, sub_roll(own[i], 1)),
            )
            side_north, side_south = side_places[i]
            next_column = (
                next_sides[slots[i]]
                + own_set[i][5] * jnp.where(first_lane, own_west[i], own_east[i])
                + own_set[i][6] * jnp.where(bottom, side_south, side_north)
            )
            north, south = next_places[i]
            results.append(
                combine(
                    own_set[i],
                    once,
                    jnp.where(last_lane, next_column, lane_roll(once, -1)),
                    jnp.where(first_lane, next_column, lane_roll(once, 1)),
                    jnp.where(top, north, sub_roll(once, -1)),
                    jnp.where(bottom, south, sub_roll(once, 1)),
                )
            )
        return results

    def transport(p):
        f1 = 2 * p
        f2 = jnp.minimum(f1 + 1, fields - 1)
        columns = []
        for k in range(half):
            own_set = [[own_coefs[2 * k + i, c] for c in range(7)] for i in range(2)]
            halo_set = [halo_coefs[k, c] for c in range(4)]
            for one, two in zip(
                advect(f1, k, own_set, halo_set), advect(f2, k, own_set, halo_set)
            ):
                columns.append(jnp.where(low, one, sub_roll(two, rows)))
                columns.append(jnp.where(low, sub_roll(one, rows), two))
        return tuple(columns)

    def solve(p, columns):
        f1 = 2 * p
        f2 = jnp.minimum(f1 + 1, fields - 1)
        waves = cosine_sums(columns)
        change = cosine_series([source[m, p] - decay[m, p] * waves[m] for m in range(levels)])
        square = change[0] * change[0]
        for l in range(1, levels):
            square = square + change[l] * change[l]
        for k in range(pairs):
            even, odd = (columns[l] + change[l] for l in (2 * k, 2 * k + 1))
            state[f1 * pairs + k] = jnp.where(low, even, sub_roll(odd, rows))
            state[f2 * pairs + k] = jnp.where(low, sub_roll(even, rows), odd)
        return jnp.where(low | (f1 + 1 < fields), square, 0.0)

    def pair_step(p, carried):
        total, columns = carried
        following = transport(p)
        return total + solve(p - 1, columns), following

    field_pairs = (fields + 1) // 2
    total, columns = lax.fori_loop(
        1, field_pairs, pair_step, (jnp.zeros(tile, F32), transport(0))
    )
    return total + solve(field_pairs - 1, columns)


def main_kernel(fields, levels, *refs):
    inputs, (target, onehot), (state, placed), coefs = refs[:16], refs[16:18], refs[18:20], refs[20:]
    rows, lanes = target.shape
    total = transport_and_solve(fields, levels, *inputs, state, *coefs)

    heat = (total + sub_roll(total, rows)) * (1.0 / (fields * levels))
    first = heat.astype(jnp.bfloat16).astype(F32)
    rest = heat - first
    second = rest.astype(jnp.bfloat16).astype(F32)
    third = rest - second
    spans = placed.shape[0]
    slot_row, _ = iotas((spans, lanes))
    high = lax.shift_right_logical(target[...], lanes.bit_length() - 1)
    hits = [slot_row == high[r : r + 1] for r in range(rows)]
    left = jnp.concatenate(
        [
            jnp.concatenate(
                [
                    jnp.where(hits[r], part[r : r + 1], 0.0).astype(jnp.bfloat16)
                    for r in range(rows)
                ],
                axis=1,
            )
            for part in (first, second, third)
        ],
        axis=0,
    )
    result = jnp.dot(left, onehot[...], preferred_element_type=F32)
    placed[...] = result[:spans] + result[spans : 2 * spans] + result[2 * spans :]


def finish_kernel(parts, state, total_out, state_out, total, semaphores):
    copy_state = pltpu.make_async_copy(state, state_out, semaphores.at[0])
    copy_state.start()
    value = parts[0]
    for i in range(1, parts.shape[0]):
        value = value + parts[i]
    total[...] = value
    copy_total = pltpu.make_async_copy(total, total_out, semaphores.at[1])
    copy_total.start()
    copy_state.wait()
    copy_total.wait()


def body(tracers, courant_x, courant_y, physics_ref, class_coeffs, span_target, cloud_class):
    fields, levels, rows, cols = tracers.shape
    wide = lax.axis_size("wide")
    narrow = lax.axis_size("narrow")
    pairs = levels // 2
    half = pairs // 2
    tile = (2 * rows, cols)
    field_pairs = (fields + 1) // 2
    flat = tracers.reshape(fields * pairs, *tile)
    cx = courant_x.reshape(pairs, *tile)
    cy = courant_y.reshape(pairs, *tile)
    quads = pairs // rows

    def array(*shape, dtype=F32):
        return jax.ShapeDtypeStruct(shape, dtype)

    flat, cx, cy, north = pl.pallas_call(
        functools.partial(pack_north_kernel, levels),
        out_shape=(
            array(fields * pairs, *tile),
            array(pairs, *tile),
            array(pairs, *tile),
            array(fields * half + 2 * quads, *tile),
        ),
        in_specs=[HBM] * 3,
        out_specs=[VMEM] * 4,
        scratch_shapes=[pltpu.SemaphoreType.DMA((3,))],
        compiler_params=PARAMS,
    )(*(pltpu.with_memory_space_constraint(x, pltpu.HBM) for x in (flat, cx, cy)))
    edge, corner, south = pl.pallas_call(
        functools.partial(pack_edges_kernel, levels),
        out_shape=(
            array(fields + 2, *tile),
            array(*tile),
            array(fields * half + quads, *tile),
        ),
        in_specs=[VMEM] * 3,
        out_specs=[VMEM] * 3,
        compiler_params=PARAMS,
    )(flat, cx, cy)

    def send(value, up, right):
        pairs_ = []
        for w in range(wide):
            for n in range(narrow):
                to = ((w + up) % wide) * narrow + (n + right) % narrow
                pairs_.append((w * narrow + n, to))
        return lax.ppermute(value, ("wide", "narrow"), pairs_)

    def to_both_sides(value, up):
        from_west = send(value, up, 1)
        from_east = from_west if narrow == 2 else send(value, up, -1)
        return from_west, from_east

    from_south = send(north, 1, 0)
    from_north = send(south, -1, 0)
    edge_west, edge_east = to_both_sides(edge, 0)
    corner_sw, corner_se = to_both_sides(corner, 1)
    corner_nw, corner_ne = to_both_sides(corner, -1)

    decay, source, onehot = pl.pallas_call(
        prep_kernel,
        out_shape=(array(levels, field_pairs, *tile),) * 2
        + (array(rows * cols, cols, dtype=jnp.bfloat16),),
        in_specs=[SMEM, SMEM, VMEM, VMEM],
        out_specs=[VMEM] * 3,
        cost_estimate=pl.CostEstimate(flops=4000000, bytes_accessed=2000000, transcendentals=0),
        compiler_params=PARAMS,
    )(class_coeffs, physics_ref, cloud_class, span_target)

    shifted = pl.pallas_call(
        functools.partial(shift_kernel, levels),
        out_shape=(array(fields * pairs, *tile),) * 2,
        in_specs=[VMEM] * 4,
        out_specs=[VMEM] * 2,
        compiler_params=PARAMS,
    )(flat, edge, edge_west, edge_east)
    edge_columns = pl.pallas_call(
        functools.partial(next_kernel, levels),
        out_shape=(array(fields * pairs, *tile),) + (array(pairs, *tile),) * 2,
        in_specs=[VMEM] * 4,
        out_specs=[VMEM] * 3,
        compiler_params=PARAMS,
    )(cx, edge, edge_west, edge_east)
    state, placed = pl.pallas_call(
        functools.partial(main_kernel, fields, levels),
        out_shape=(array(fields * pairs, *tile), array(wide * rows, cols)),
        in_specs=[VMEM] * 18,
        out_specs=[VMEM] * 2,
        scratch_shapes=[
            pltpu.VMEM((pairs, 7) + tile, F32),
            pltpu.VMEM((half, 4) + tile, F32),
        ],
        compiler_params=PARAMS,
    )(
        flat,
        cx,
        cy,
        from_south,
        from_north,
        *shifted,
        *edge_columns,
        corner_sw,
        corner_se,
        corner_nw,
        corner_ne,
        decay,
        source,
        span_target,
        onehot,
    )
    received = lax.all_to_all(
        placed.reshape(wide, rows, cols), "wide", split_axis=0, concat_axis=0, tiled=True
    )
    span_diag, state = pl.pallas_call(
        finish_kernel,
        out_shape=(array(rows, cols), array(fields * pairs, *tile)),
        in_specs=[VMEM] * 2,
        out_specs=[HBM] * 2,
        scratch_shapes=[pltpu.VMEM((rows, cols), F32), pltpu.SemaphoreType.DMA((2,))],
        compiler_params=PARAMS,
    )(received, state)
    return state.reshape(fields, levels, rows, cols), span_diag


def solution(mesh):
    return jax.shard_map(
        body,
        mesh=mesh,
        in_specs=(
            P(None, None, "wide", "narrow"),
            P(None, "wide", "narrow"),
            P(None, "wide", "narrow"),
            P(),
            P(),
            P("wide", "narrow"),
            P("wide", "narrow"),
        ),
        out_specs=(P(None, None, "wide", "narrow"), P("wide", "narrow")),
        check_vma=False,
    )
```

```python
import functools
import math

import jax
import jax.numpy as jnp
from jax import lax
from jax.experimental import pallas as pl
from jax.experimental.pallas import tpu as pltpu
from jax.sharding import PartitionSpec as P

VMEM = pl.BlockSpec(memory_space=pltpu.VMEM)
HBM = pl.BlockSpec(memory_space=pltpu.HBM)
SMEM = pl.BlockSpec(memory_space=pltpu.SMEM)
F32 = jnp.float32
PARAMS = pltpu.CompilerParams(vmem_limit_bytes=12 * 1024 * 1024)


def sub_roll(value, shift):
    shift = shift % value.shape[0]
    return value if shift == 0 else pltpu.roll(value, shift, 0)


def lane_roll(value, shift):
    shift = shift % value.shape[1]
    return value if shift == 0 else pltpu.roll(value, shift, 1)


def iotas(shape):
    return lax.broadcasted_iota(jnp.int32, shape, 0), lax.broadcasted_iota(jnp.int32, shape, 1)


def one_row(vectors, row, step):
    rows = vectors[0].shape[0] // 2
    local = iotas(vectors[0].shape)[0] % rows
    packed = []
    for start in range(0, len(vectors), rows):
        total = vectors[start]
        for t in range(1, rows):
            total = jnp.where(
                local == row + step * t, sub_roll(vectors[start + t], step * t), total
            )
        packed.append(total)
    return packed


def inner_flux(value, courant):
    return jnp.maximum(courant, 0.0) * value + jnp.minimum(courant, 0.0) * sub_roll(value, -1)


def northward_rows(value, courant):
    local = iotas(value.shape)[0] % (value.shape[0] // 2)
    return jnp.where(local == 2, inner_flux(value, courant), value)


def southward_rows(value, courant):
    local = iotas(value.shape)[0] % (value.shape[0] // 2)
    return jnp.where(local == 1, sub_roll(-inner_flux(value, courant), 1), value)


def pack_north_kernel(levels, tracers_in, cx_in, cy_in, tracers, cx, cy, north, semaphores):
    copies = [
        pltpu.make_async_copy(source, into, semaphores.at[i])
        for i, (source, into) in enumerate(((tracers_in, tracers), (cx_in, cx), (cy_in, cy)))
    ]
    for copy in copies:
        copy.start()
    for copy in copies:
        copy.wait()
    pairs = levels // 2
    half = pairs // 2
    tile = tracers.shape[1:]
    rows = tile[0] // 2
    upper = iotas(tile)[0] % rows >= rows // 2
    fields = tracers.shape[0] // pairs
    for f in range(fields):
        for k in range(half):
            one, two = (
                northward_rows(tracers[f * pairs + j], cy[j]) for j in (2 * k, 2 * k + 1)
            )
            north[f * half + k] = jnp.where(upper, one, sub_roll(two, 2))
    courant = one_row([cx[k] for k in range(pairs)], rows - 1, -1)
    courant += one_row([cy[k] for k in range(pairs)], rows - 1, -1)
    for k, value in enumerate(courant):
        north[fields * half + k] = value


def pack_edges_kernel(levels, tracers, cx, cy, edge, corner, south_rows):
    pairs = levels // 2
    half = pairs // 2
    fields = tracers.shape[0] // pairs
    tile = tracers.shape[1:]
    rows = tile[0] // 2
    lanes = tile[1]
    group = lanes // levels
    sub, lane = iotas(tile)
    upper = sub % rows >= rows // 2
    odd_sub = sub % 2 == 1
    corners = [jnp.zeros(tile, F32)]

    def pack_edge(vectors, slot):
        total = lane_roll(vectors[0], 2)
        for k in range(1, pairs):
            total = jnp.where(
                lane // (2 * group) == k, lane_roll(vectors[k], 2 + 2 * group * k), total
            )
        total = jnp.where(
            lane % (2 * group) < group, total, sub_roll(lane_roll(total, group), rows)
        )
        edge[slot] = jnp.where(lane % group < group // 2, total, lane_roll(total, group // 2))
        for k in range(half):
            one, two = vectors[2 * k], vectors[2 * k + 1]
            place = slot * half + k
            north = jnp.where(upper, one, sub_roll(two, 2))
            south = jnp.where(upper, sub_roll(two, -2), one)
            if slot < fields:
                first = southward_rows(one, cy[2 * k])
                second = southward_rows(two, cy[2 * k + 1])
                south_rows[place] = jnp.where(upper, sub_roll(second, -2), first)
            value = lane_roll(jnp.where(odd_sub, north, south), 2 * place + 1)
            corners[0] = jnp.where(lane // 2 == place, value, corners[0])

    for f in range(fields):
        pack_edge([tracers[f * pairs + k] for k in range(pairs)], f)
    pack_edge([cx[k] for k in range(pairs)], fields)
    pack_edge([cy[k] for k in range(pairs)], fields + 1)
    corner[...] = corners[0]
    for k, value in enumerate(one_row([cx[k] for k in range(pairs)], 0, 1)):
        south_rows[fields * half + k] = value


def cosine_sums(values):
    count = len(values)
    if count == 1:
        return values
    half = count // 2
    plus = [values[n] + values[count - 1 - n] for n in range(half)]
    minus = [
        (values[n] - values[count - 1 - n])
        * (0.5 / math.cos(math.pi * (2 * n + 1) / (2 * count)))
        for n in range(half)
    ]
    even = cosine_sums(plus)
    odd = cosine_sums(minus)
    result = []
    for k in range(half):
        result.append(even[k])
        result.append(odd[k] + odd[k + 1] if k + 1 < half else odd[k])
    return result


def cosine_series(values):
    count = len(values)
    if count == 1:
        return values
    half = count // 2
    odd_in = [values[2 * k + 1] + values[2 * k - 1] if k else values[1] for k in range(half)]
    even = cosine_series(values[0::2])
    odd = cosine_series(odd_in)
    odd = [
        odd[n] * (0.5 / math.cos(math.pi * (2 * n + 1) / (2 * count))) for n in range(half)
    ]
    return [even[n] + odd[n] for n in range(half)] + [
        even[n] - odd[n] for n in range(half - 1, -1, -1)
    ]


def prep_kernel(coeffs, profile, klass, target, decay, source, onehot):
    levels, pairs = decay.shape[:2]
    fields = profile.shape[0]
    tile = decay.shape[2:]
    rows, lanes = klass.shape
    sub, lane = iotas(tile)
    low = sub < rows
    kind = jnp.concatenate([klass[...], klass[...]], axis=0)
    is_two = kind == 2
    is_one = kind == 1

    def by_class(which, f):
        return jnp.where(
            is_two,
            coeffs[which, 2, f] * 0.25,
            jnp.where(is_one, coeffs[which, 1, f] * 0.5, coeffs[which, 0, f]),
        )

    for p in range(pairs):
        f1 = 2 * p
        f2 = min(2 * p + 1, fields - 1)
        diffusion = jnp.where(low, by_class(0, f1), by_class(0, f2))
        relax = jnp.where(low, by_class(1, f1), by_class(1, f2))
        waves = cosine_sums([jnp.where(low, profile[f1, l], profile[f2, l]) for l in range(levels)])
        for m in range(levels):
            rate = relax + diffusion * (2.0 - 2.0 * math.cos(math.pi * m / levels))
            once = 1.0 / (1.0 + rate)
            square = once * once
            twice = once + square
            steps = jnp.where(is_two, twice + twice * square, jnp.where(is_one, twice, once))
            steps = steps * ((1.0 if m == 0 else 2.0) / levels)
            decay[m, p] = steps * rate
            source[m, p] = steps * relax * waves[m]
    low_part = target[...] & (lanes - 1)
    slot, _ = iotas((lanes, lanes))
    for r in range(rows):
        hit = jnp.where(slot == low_part[r : r + 1], 1.0, 0.0)
        onehot[r * lanes : (r + 1) * lanes, :] = jnp.transpose(hit).astype(jnp.bfloat16)


def combine(coefs, center, east, west, north, south):
    return (
        coefs[0] * center
        + (coefs[1] * east + coefs[2] * west)
        + (coefs[3] * north + coefs[4] * south)
    )


def coefficients(here_x, west_x, here_y, south_y):
    return (
        1.0
        - jnp.maximum(here_x, 0.0)
        + jnp.minimum(west_x, 0.0)
        - jnp.maximum(here_y, 0.0)
        + jnp.minimum(south_y, 0.0),
        jnp.maximum(-here_x, 0.0),
        jnp.maximum(west_x, 0.0),
        jnp.maximum(-here_y, 0.0),
        jnp.maximum(south_y, 0.0),
    )


def side_by_side(value, place):
    return jnp.where(place == 3, lane_roll(value, -2), value)


def beside(edge, edge_west, edge_east, slot, place):
    from_east = (place == 2) | (place == 3)
    from_west = (place == 4) | (place == 5)
    return jnp.where(
        from_east, edge_east[slot], jnp.where(from_west, edge_west[slot], edge[slot])
    )


def spread(value, levels):
    lanes = value.shape[1]
    rows = value.shape[0] // 2
    group = lanes // levels
    sub, lane = iotas(value.shape)
    value = side_by_side(value, lane % group)
    value = jnp.where(sub < rows, value, sub_roll(lane_roll(value, -group), rows))
    return [lane_roll(value, -(2 * group * k + 3)) for k in range(levels // 2)]


def shift_kernel(levels, tracers, edge, edge_west, edge_east, east, west):
    pairs = levels // 2
    tile = tracers.shape[1:]
    lanes = tile[1]
    lane = iotas(tile)[1]
    place = lane % (lanes // levels)
    for f in range(tracers.shape[0] // pairs):
        for k, sides in enumerate(spread(beside(edge, edge_west, edge_east, f, place), levels)):
            own = tracers[f * pairs + k]
            east[f * pairs + k] = jnp.where(lane == lanes - 1, sides, lane_roll(own, -1))
            west[f * pairs + k] = jnp.where(lane == 0, sides, lane_roll(own, 1))


def next_kernel(levels, cx, edge, edge_west, edge_east, next_sides, west_x, sides_y):
    pairs = levels // 2
    fields = next_sides.shape[0] // pairs
    tile = cx.shape[1:]
    rows = tile[0] // 2
    sub, lane = iotas(tile)
    place = lane % (tile[1] // levels)

    def own_rows(slot):
        value = beside(edge, edge_west, edge_east, slot, place)
        return jnp.where(sub < rows, value, 0.0)

    edge_x = own_rows(fields)
    edge_y = own_rows(fields + 1)
    coefs = coefficients(edge_x, lane_roll(edge_x, 1), edge_y, sub_roll(edge_y, 1))
    for k, sides in enumerate(spread(edge_x, levels)):
        west_x[k] = jnp.where(lane == 0, sides, lane_roll(cx[k], 1))
    for k, sides in enumerate(spread(edge_y, levels)):
        sides_y[k] = sides
    for f in range(fields):
        raw = own_rows(f)
        moved = combine(
            coefs,
            raw,
            lane_roll(raw, -1),
            lane_roll(raw, 1),
            sub_roll(raw, -1),
            sub_roll(raw, 1),
        )
        for k, sides in enumerate(spread(moved, levels)):
            next_sides[f * pairs + k] = sides


def turned(value):
    rows = value.shape[0] // 2
    up, down = sub_roll(value, rows - 1), sub_roll(value, 1 - rows)
    return ((up, down), (down, up))


def corner_kernel(
    levels, sides_y, corner_sw, corner_se, corner_nw, corner_ne, corners, shares
):
    half = levels // 4
    tile = corner_sw.shape
    rows = tile[0] // 2
    sub, lane = iotas(tile)
    local = sub % rows
    odd_sub = sub % 2 == 1
    bottom = local == 0
    top = local == rows - 1
    even_lane = lane % 2 == 0
    dense = jnp.where(
        odd_sub,
        jnp.where(even_lane, lane_roll(corner_se[...], -1), lane_roll(corner_sw[...], 1)),
        jnp.where(even_lane, lane_roll(corner_ne[...], -1), lane_roll(corner_nw[...], 1)),
    )
    count = corners.shape[0]
    for i in range(count):
        corners[i] = lane_roll(dense, -(2 * i + 1))
    for k in range(half):
        places = turned(lane_roll(dense, -(2 * (count + k) + 1)))
        for i in range(2):
            j = 2 * k + i
            south_face = places[i][1]
            shares[j, 0] = jnp.where(bottom, jnp.minimum(south_face, 0.0), 0.0)
            shares[j, 1] = jnp.where(
                bottom,
                jnp.maximum(south_face, 0.0),
                jnp.where(top, jnp.maximum(-sides_y[j], 0.0), 0.0),
            )


def transport_and_solve(
    fields,
    levels,
    tracers,
    cx,
    cy,
    from_south,
    from_north,
    east,
    west,
    next_sides,
    west_x,
    corners,
    shares,
    decay,
    source,
    state,
    own_coefs,
    halo_coefs,
):
    pairs = levels // 2
    half = pairs // 2
    tile = tracers.shape[1:]
    rows = tile[0] // 2
    lanes = tile[1]
    group = lanes // levels
    sub, lane = iotas(tile)
    local = sub % rows
    low = sub < rows
    first_lane = lane == 0
    last_lane = lane == lanes - 1
    odd_sub = sub % 2 == 1
    bottom = local == 0
    top = local == rows - 1
    in_first = bottom | top


    def inner_rows(first, second):
        (first_up, first_down), _ = turned(first)
        (second_up, second_down), _ = turned(second)
        return (
            jnp.where(in_first, first_up, second_down),
            jnp.where(in_first, first_down, second_up),
        )

    base = fields * half
    count = pairs // rows
    for k in range(half):
        quad, t = 2 * k // rows, 2 * k % rows
        packed_south = from_south[base + quad]
        packed_south_y = from_south[base + count + quad]
        packed_north = from_north[base + quad]
        south_x = jnp.where(in_first, sub_roll(packed_south, t), sub_roll(packed_south, 3 + t))
        south_y = jnp.where(
            in_first, sub_roll(packed_south_y, t), sub_roll(packed_south_y, 3 + t)
        )
        north_x = jnp.where(in_first, sub_roll(packed_north, -t), sub_roll(packed_north, 5 - t))
        halo_x = jnp.where(odd_sub, south_x, north_x)
        halo_west = jnp.where(
            first_lane, corners[fields * half + k], lane_roll(halo_x, 1)
        )
        _, inner_top = inner_rows(cy[2 * k], cy[2 * k + 1])
        face = jnp.where(odd_sub, -south_y, inner_top)
        halo_coefs[k, 0] = (
            1.0
            - jnp.maximum(halo_x, 0.0)
            + jnp.minimum(halo_west, 0.0)
            + jnp.minimum(face, 0.0)
        )
        halo_coefs[k, 1] = jnp.maximum(-halo_x, 0.0)
        halo_coefs[k, 2] = jnp.maximum(halo_west, 0.0)
        halo_coefs[k, 3] = jnp.maximum(face, 0.0)
        places = turned(south_y)
        for i in range(2):
            j = 2 * k + i
            below = jnp.where(bottom, places[i][1], sub_roll(cy[j], 1))
            for c, value in enumerate(coefficients(cx[j], west_x[j], cy[j], below)):
                own_coefs[j, c] = value

    def advect(f, k, own_set, halo_set):
        message_south = from_south[f * half + k]
        message_north = from_north[f * half + k]
        slots = (f * pairs + 2 * k, f * pairs + 2 * k + 1)
        own = [tracers[slot] for slot in slots]
        own_east = [east[slot] for slot in slots]
        own_west = [west[slot] for slot in slots]
        sides = corners[f * half + k]
        halo = jnp.where(odd_sub, message_south, message_north)
        inner_bottom, inner_top = inner_rows(*own)
        flux = jnp.where(odd_sub, sub_roll(message_south, 1), sub_roll(message_north, -1))
        next_halo = (
            halo_set[0] * halo
            + (
                halo_set[1] * jnp.where(last_lane, sides, lane_roll(halo, -1))
                + halo_set[2] * jnp.where(first_lane, sides, lane_roll(halo, 1))
            )
            + (halo_set[3] * jnp.where(odd_sub, inner_bottom, inner_top) + flux)
        )
        places, next_places, side_places = turned(halo), turned(next_halo), turned(sides)
        results = []
        for i in range(2):
            north, south = places[i]
            once = combine(
                own_set[i],
                own[i],
                own_east[i],
                own_west[i],
                jnp.where(top, north, sub_roll(own[i], -1)),
                jnp.where(bottom, south, sub_roll(own[i], 1)),
            )
            side_north, side_south = side_places[i]
            next_column = (
                next_sides[slots[i]]
                + own_set[i][5] * jnp.where(first_lane, own_west[i], own_east[i])
                + own_set[i][6] * jnp.where(bottom, side_south, side_north)
            )
            north, south = next_places[i]
            results.append(
                combine(
                    own_set[i],
                    once,
                    jnp.where(last_lane, next_column, lane_roll(once, -1)),
                    jnp.where(first_lane, next_column, lane_roll(once, 1)),
                    jnp.where(top, north, sub_roll(once, -1)),
                    jnp.where(bottom, south, sub_roll(once, 1)),
                )
            )
        return results

    def transport(p):
        f1 = 2 * p
        f2 = jnp.minimum(f1 + 1, fields - 1)
        columns = []
        for k in range(half):
            own_set = [
                [own_coefs[2 * k + i, c] for c in range(5)]
                + [shares[2 * k + i, c] for c in range(2)]
                for i in range(2)
            ]
            halo_set = [halo_coefs[k, c] for c in range(4)]
            for one, two in zip(
                advect(f1, k, own_set, halo_set), advect(f2, k, own_set, halo_set)
            ):
                columns.append(jnp.where(low, one, sub_roll(two, rows)))
                columns.append(jnp.where(low, sub_roll(one, rows), two))
        return tuple(columns)

    def solve(p, columns):
        f1 = 2 * p
        f2 = jnp.minimum(f1 + 1, fields - 1)
        waves = cosine_sums(columns)
        change = cosine_series([source[m, p] - decay[m, p] * waves[m] for m in range(levels)])
        square = change[0] * change[0]
        for l in range(1, levels):
            square = square + change[l] * change[l]
        for k in range(pairs):
            even, odd = (columns[l] + change[l] for l in (2 * k, 2 * k + 1))
            state[f1 * pairs + k] = jnp.where(low, even, sub_roll(odd, rows))
            state[f2 * pairs + k] = jnp.where(low, sub_roll(even, rows), odd)
        return jnp.where(low | (f1 + 1 < fields), square, 0.0)

    def pair_step(p, carried):
        total, columns = carried
        following = transport(p)
        return total + solve(p - 1, columns), following

    field_pairs = (fields + 1) // 2
    total, columns = lax.fori_loop(
        1, field_pairs, pair_step, (jnp.zeros(tile, F32), transport(0))
    )
    return total + solve(field_pairs - 1, columns)


def main_kernel(fields, levels, *refs):
    inputs, (target, onehot), (state, placed), coefs = refs[:13], refs[13:15], refs[15:17], refs[17:]
    rows, lanes = target.shape
    total = transport_and_solve(fields, levels, *inputs, state, *coefs)

    heat = (total + sub_roll(total, rows)) * (1.0 / (fields * levels))
    first = heat.astype(jnp.bfloat16).astype(F32)
    rest = heat - first
    second = rest.astype(jnp.bfloat16).astype(F32)
    third = rest - second
    spans = placed.shape[0]
    slot_row, _ = iotas((spans, lanes))
    high = lax.shift_right_logical(target[...], lanes.bit_length() - 1)
    hits = [slot_row == high[r : r + 1] for r in range(rows)]
    left = jnp.concatenate(
        [
            jnp.concatenate(
                [
                    jnp.where(hits[r], part[r : r + 1], 0.0).astype(jnp.bfloat16)
                    for r in range(rows)
                ],
                axis=1,
            )
            for part in (first, second, third)
        ],
        axis=0,
    )
    result = jnp.dot(left, onehot[...], preferred_element_type=F32)
    placed[...] = result[:spans] + result[spans : 2 * spans] + result[2 * spans :]


def finish_kernel(parts, state, total_out, state_out, total, semaphores):
    copy_state = pltpu.make_async_copy(state, state_out, semaphores.at[0])
    copy_state.start()
    value = parts[0]
    for i in range(1, parts.shape[0]):
        value = value + parts[i]
    total[...] = value
    copy_total = pltpu.make_async_copy(total, total_out, semaphores.at[1])
    copy_total.start()
    copy_state.wait()
    copy_total.wait()


def body(tracers, courant_x, courant_y, physics_ref, class_coeffs, span_target, cloud_class):
    fields, levels, rows, cols = tracers.shape
    wide = lax.axis_size("wide")
    narrow = lax.axis_size("narrow")
    pairs = levels // 2
    half = pairs // 2
    tile = (2 * rows, cols)
    field_pairs = (fields + 1) // 2
    flat = tracers.reshape(fields * pairs, *tile)
    cx = courant_x.reshape(pairs, *tile)
    cy = courant_y.reshape(pairs, *tile)
    quads = pairs // rows

    def array(*shape, dtype=F32):
        return jax.ShapeDtypeStruct(shape, dtype)

    flat, cx, cy, north = pl.pallas_call(
        functools.partial(pack_north_kernel, levels),
        out_shape=(
            array(fields * pairs, *tile),
            array(pairs, *tile),
            array(pairs, *tile),
            array(fields * half + 2 * quads, *tile),
        ),
        in_specs=[HBM] * 3,
        out_specs=[VMEM] * 4,
        scratch_shapes=[pltpu.SemaphoreType.DMA((3,))],
        compiler_params=PARAMS,
    )(*(pltpu.with_memory_space_constraint(x, pltpu.HBM) for x in (flat, cx, cy)))
    edge, corner, south = pl.pallas_call(
        functools.partial(pack_edges_kernel, levels),
        out_shape=(
            array(fields + 2, *tile),
            array(*tile),
            array(fields * half + quads, *tile),
        ),
        in_specs=[VMEM] * 3,
        out_specs=[VMEM] * 3,
        compiler_params=PARAMS,
    )(flat, cx, cy)

    def send(value, up, right):
        pairs_ = []
        for w in range(wide):
            for n in range(narrow):
                to = ((w + up) % wide) * narrow + (n + right) % narrow
                pairs_.append((w * narrow + n, to))
        return lax.ppermute(value, ("wide", "narrow"), pairs_)

    def to_both_sides(value, up):
        from_west = send(value, up, 1)
        from_east = from_west if narrow == 2 else send(value, up, -1)
        return from_west, from_east

    from_south = send(north, 1, 0)
    from_north = send(south, -1, 0)
    edge_west, edge_east = to_both_sides(edge, 0)
    corner_sw, corner_se = to_both_sides(corner, 1)
    corner_nw, corner_ne = to_both_sides(corner, -1)

    decay, source, onehot = pl.pallas_call(
        prep_kernel,
        out_shape=(array(levels, field_pairs, *tile),) * 2
        + (array(rows * cols, cols, dtype=jnp.bfloat16),),
        in_specs=[SMEM, SMEM, VMEM, VMEM],
        out_specs=[VMEM] * 3,
        cost_estimate=pl.CostEstimate(flops=4000000, bytes_accessed=2000000, transcendentals=0),
        compiler_params=PARAMS,
    )(class_coeffs, physics_ref, cloud_class, span_target)

    shifted = pl.pallas_call(
        functools.partial(shift_kernel, levels),
        out_shape=(array(fields * pairs, *tile),) * 2,
        in_specs=[VMEM] * 4,
        out_specs=[VMEM] * 2,
        compiler_params=PARAMS,
    )(flat, edge, edge_west, edge_east)
    next_sides, west_x, sides_y = pl.pallas_call(
        functools.partial(next_kernel, levels),
        out_shape=(array(fields * pairs, *tile),) + (array(pairs, *tile),) * 2,
        in_specs=[VMEM] * 4,
        out_specs=[VMEM] * 3,
        compiler_params=PARAMS,
    )(cx, edge, edge_west, edge_east)
    corners, shares = pl.pallas_call(
        functools.partial(corner_kernel, levels),
        out_shape=(array((fields + 1) * half, *tile), array(pairs, 2, *tile)),
        in_specs=[VMEM] * 5,
        out_specs=[VMEM] * 2,
        compiler_params=PARAMS,
    )(sides_y, corner_sw, corner_se, corner_nw, corner_ne)
    state, placed = pl.pallas_call(
        functools.partial(main_kernel, fields, levels),
        out_shape=(array(fields * pairs, *tile), array(wide * rows, cols)),
        in_specs=[VMEM] * 15,
        out_specs=[VMEM] * 2,
        scratch_shapes=[
            pltpu.VMEM((pairs, 5) + tile, F32),
            pltpu.VMEM((half, 4) + tile, F32),
        ],
        compiler_params=PARAMS,
    )(
        flat,
        cx,
        cy,
        from_south,
        from_north,
        *shifted,
        next_sides,
        west_x,
        corners,
        shares,
        decay,
        source,
        span_target,
        onehot,
    )
    received = lax.all_to_all(
        placed.reshape(wide, rows, cols), "wide", split_axis=0, concat_axis=0, tiled=True
    )
    span_diag, state = pl.pallas_call(
        finish_kernel,
        out_shape=(array(rows, cols), array(fields * pairs, *tile)),
        in_specs=[VMEM] * 2,
        out_specs=[HBM] * 2,
        scratch_shapes=[pltpu.VMEM((rows, cols), F32), pltpu.SemaphoreType.DMA((2,))],
        compiler_params=PARAMS,
    )(received, state)
    return state.reshape(fields, levels, rows, cols), span_diag


def solution(mesh):
    return jax.shard_map(
        body,
        mesh=mesh,
        in_specs=(
            P(None, None, "wide", "narrow"),
            P(None, "wide", "narrow"),
            P(None, "wide", "narrow"),
            P(),
            P(),
            P("wide", "narrow"),
            P("wide", "narrow"),
        ),
        out_specs=(P(None, None, "wide", "narrow"), P("wide", "narrow")),
        check_vma=False,
    )
```

```python
import functools
import math

import jax
import jax.numpy as jnp
from jax import lax
from jax.experimental import pallas as pl
from jax.experimental.pallas import tpu as pltpu
from jax.sharding import PartitionSpec as P

VMEM = pl.BlockSpec(memory_space=pltpu.VMEM)
HBM = pl.BlockSpec(memory_space=pltpu.HBM)
SMEM = pl.BlockSpec(memory_space=pltpu.SMEM)
F32 = jnp.float32
PARAMS = pltpu.CompilerParams(vmem_limit_bytes=12 * 1024 * 1024)


def sub_roll(value, shift):
    shift = shift % value.shape[0]
    return value if shift == 0 else pltpu.roll(value, shift, 0)


def lane_roll(value, shift):
    shift = shift % value.shape[1]
    return value if shift == 0 else pltpu.roll(value, shift, 1)


def iotas(shape):
    return lax.broadcasted_iota(jnp.int32, shape, 0), lax.broadcasted_iota(jnp.int32, shape, 1)


def one_row(vectors, row, step):
    rows = vectors[0].shape[0] // 2
    local = iotas(vectors[0].shape)[0] % rows
    packed = []
    for start in range(0, len(vectors), rows):
        total = vectors[start]
        for t in range(1, rows):
            total = jnp.where(
                local == row + step * t, sub_roll(vectors[start + t], step * t), total
            )
        packed.append(total)
    return packed


def inner_flux(value, courant):
    return jnp.maximum(courant, 0.0) * value + jnp.minimum(courant, 0.0) * sub_roll(value, -1)


def northward_rows(value, courant):
    local = iotas(value.shape)[0] % (value.shape[0] // 2)
    return jnp.where(local == 2, inner_flux(value, courant), value)


def southward_rows(value, courant):
    local = iotas(value.shape)[0] % (value.shape[0] // 2)
    return jnp.where(local == 1, sub_roll(-inner_flux(value, courant), 1), value)


def pack_north_kernel(levels, tracers_in, cx_in, cy_in, tracers, cx, cy, north, semaphores):
    pairs = levels // 2
    half = pairs // 2
    tile = tracers.shape[1:]
    rows = tile[0] // 2
    upper = iotas(tile)[0] % rows >= rows // 2
    fields = tracers.shape[0] // pairs
    groups = semaphores.shape[0] - 2
    bounds = [fields * g // groups for g in range(groups + 1)]
    courant_copies = [
        pltpu.make_async_copy(source, into, semaphores.at[groups + i])
        for i, (source, into) in enumerate(((cx_in, cx), (cy_in, cy)))
    ]
    copies = []
    for g in range(groups):
        part = pl.ds(bounds[g] * pairs, (bounds[g + 1] - bounds[g]) * pairs)
        copies.append(
            pltpu.make_async_copy(tracers_in.at[part], tracers.at[part], semaphores.at[g])
        )
    for copy in courant_copies + copies:
        copy.start()
    for copy in courant_copies:
        copy.wait()
    for g in range(groups):
        copies[g].wait()
        for f in range(bounds[g], bounds[g + 1]):
            for k in range(half):
                one, two = (
                    northward_rows(tracers[f * pairs + j], cy[j]) for j in (2 * k, 2 * k + 1)
                )
                north[f * half + k] = jnp.where(upper, one, sub_roll(two, 2))
    courant = one_row([cx[k] for k in range(pairs)], rows - 1, -1)
    courant += one_row([cy[k] for k in range(pairs)], rows - 1, -1)
    for k, value in enumerate(courant):
        north[fields * half + k] = value


def pack_edges_kernel(levels, tracers, cx, cy, edge, corner, south_rows):
    pairs = levels // 2
    half = pairs // 2
    fields = tracers.shape[0] // pairs
    tile = tracers.shape[1:]
    rows = tile[0] // 2
    lanes = tile[1]
    group = lanes // levels
    sub, lane = iotas(tile)
    upper = sub % rows >= rows // 2
    odd_sub = sub % 2 == 1
    corners = [jnp.zeros(tile, F32)]

    def pack_edge(vectors, slot):
        total = lane_roll(vectors[0], 2)
        for k in range(1, pairs):
            total = jnp.where(
                lane // (2 * group) == k, lane_roll(vectors[k], 2 + 2 * group * k), total
            )
        total = jnp.where(
            lane % (2 * group) < group, total, sub_roll(lane_roll(total, group), rows)
        )
        edge[slot] = jnp.where(lane % group < group // 2, total, lane_roll(total, group // 2))
        for k in range(half):
            one, two = vectors[2 * k], vectors[2 * k + 1]
            place = slot * half + k
            north = jnp.where(upper, one, sub_roll(two, 2))
            south = jnp.where(upper, sub_roll(two, -2), one)
            if slot < fields:
                first = southward_rows(one, cy[2 * k])
                second = southward_rows(two, cy[2 * k + 1])
                south_rows[place] = jnp.where(upper, sub_roll(second, -2), first)
            value = lane_roll(jnp.where(odd_sub, north, south), 2 * place + 1)
            corners[0] = jnp.where(lane // 2 == place, value, corners[0])

    for f in range(fields):
        pack_edge([tracers[f * pairs + k] for k in range(pairs)], f)
    pack_edge([cx[k] for k in range(pairs)], fields)
    pack_edge([cy[k] for k in range(pairs)], fields + 1)
    corner[...] = corners[0]
    for k, value in enumerate(one_row([cx[k] for k in range(pairs)], 0, 1)):
        south_rows[fields * half + k] = value


def cosine_sums(values):
    count = len(values)
    if count == 1:
        return values
    half = count // 2
    plus = [values[n] + values[count - 1 - n] for n in range(half)]
    minus = [
        (values[n] - values[count - 1 - n])
        * (0.5 / math.cos(math.pi * (2 * n + 1) / (2 * count)))
        for n in range(half)
    ]
    even = cosine_sums(plus)
    odd = cosine_sums(minus)
    result = []
    for k in range(half):
        result.append(even[k])
        result.append(odd[k] + odd[k + 1] if k + 1 < half else odd[k])
    return result


def cosine_series(values):
    count = len(values)
    if count == 1:
        return values
    half = count // 2
    odd_in = [values[2 * k + 1] + values[2 * k - 1] if k else values[1] for k in range(half)]
    even = cosine_series(values[0::2])
    odd = cosine_series(odd_in)
    odd = [
        odd[n] * (0.5 / math.cos(math.pi * (2 * n + 1) / (2 * count))) for n in range(half)
    ]
    return [even[n] + odd[n] for n in range(half)] + [
        even[n] - odd[n] for n in range(half - 1, -1, -1)
    ]


def prep_kernel(coeffs, profile, klass, target, decay, source, onehot):
    levels, pairs = decay.shape[:2]
    fields = profile.shape[0]
    tile = decay.shape[2:]
    rows, lanes = klass.shape
    sub, lane = iotas(tile)
    low = sub < rows
    kind = jnp.concatenate([klass[...], klass[...]], axis=0)
    is_two = kind == 2
    is_one = kind == 1

    def by_class(which, f):
        return jnp.where(
            is_two,
            coeffs[which, 2, f] * 0.25,
            jnp.where(is_one, coeffs[which, 1, f] * 0.5, coeffs[which, 0, f]),
        )

    for p in range(pairs):
        f1 = 2 * p
        f2 = min(2 * p + 1, fields - 1)
        diffusion = jnp.where(low, by_class(0, f1), by_class(0, f2))
        relax = jnp.where(low, by_class(1, f1), by_class(1, f2))
        waves = cosine_sums([jnp.where(low, profile[f1, l], profile[f2, l]) for l in range(levels)])
        for m in range(levels):
            rate = relax + diffusion * (2.0 - 2.0 * math.cos(math.pi * m / levels))
            once = 1.0 / (1.0 + rate)
            square = once * once
            twice = once + square
            steps = jnp.where(is_two, twice + twice * square, jnp.where(is_one, twice, once))
            steps = steps * ((1.0 if m == 0 else 2.0) / levels)
            decay[m, p] = steps * rate
            source[m, p] = steps * relax * waves[m]
    low_part = target[...] & (lanes - 1)
    slot, _ = iotas((lanes, lanes))
    for r in range(rows):
        hit = jnp.where(slot == low_part[r : r + 1], 1.0, 0.0)
        onehot[r * lanes : (r + 1) * lanes, :] = jnp.transpose(hit).astype(jnp.bfloat16)


def combine(coefs, center, east, west, north, south):
    return (
        coefs[0] * center
        + (coefs[1] * east + coefs[2] * west)
        + (coefs[3] * north + coefs[4] * south)
    )


def coefficients(here_x, west_x, here_y, south_y):
    return (
        1.0
        - jnp.maximum(here_x, 0.0)
        + jnp.minimum(west_x, 0.0)
        - jnp.maximum(here_y, 0.0)
        + jnp.minimum(south_y, 0.0),
        jnp.maximum(-here_x, 0.0),
        jnp.maximum(west_x, 0.0),
        jnp.maximum(-here_y, 0.0),
        jnp.maximum(south_y, 0.0),
    )


def side_by_side(value, place):
    return jnp.where(place == 3, lane_roll(value, -2), value)


def beside(edge, edge_west, edge_east, slot, place):
    from_east = (place == 2) | (place == 3)
    from_west = (place == 4) | (place == 5)
    return jnp.where(
        from_east, edge_east[slot], jnp.where(from_west, edge_west[slot], edge[slot])
    )


def spread(value, levels):
    lanes = value.shape[1]
    rows = value.shape[0] // 2
    group = lanes // levels
    sub, lane = iotas(value.shape)
    value = side_by_side(value, lane % group)
    value = jnp.where(sub < rows, value, sub_roll(lane_roll(value, -group), rows))
    return [lane_roll(value, -(2 * group * k + 3)) for k in range(levels // 2)]


def shift_kernel(levels, tracers, edge, edge_west, edge_east, east, west):
    pairs = levels // 2
    tile = tracers.shape[1:]
    lanes = tile[1]
    lane = iotas(tile)[1]
    place = lane % (lanes // levels)
    for f in range(tracers.shape[0] // pairs):
        for k, sides in enumerate(spread(beside(edge, edge_west, edge_east, f, place), levels)):
            own = tracers[f * pairs + k]
            east[f * pairs + k] = jnp.where(lane == lanes - 1, sides, lane_roll(own, -1))
            west[f * pairs + k] = jnp.where(lane == 0, sides, lane_roll(own, 1))


def next_kernel(levels, cx, edge, edge_west, edge_east, next_sides, west_x, sides_y):
    pairs = levels // 2
    fields = next_sides.shape[0] // pairs
    tile = cx.shape[1:]
    rows = tile[0] // 2
    sub, lane = iotas(tile)
    place = lane % (tile[1] // levels)

    def own_rows(slot):
        value = beside(edge, edge_west, edge_east, slot, place)
        return jnp.where(sub < rows, value, 0.0)

    edge_x = own_rows(fields)
    edge_y = own_rows(fields + 1)
    coefs = coefficients(edge_x, lane_roll(edge_x, 1), edge_y, sub_roll(edge_y, 1))
    for k, sides in enumerate(spread(edge_x, levels)):
        west_x[k] = jnp.where(lane == 0, sides, lane_roll(cx[k], 1))
    for k, sides in enumerate(spread(edge_y, levels)):
        sides_y[k] = sides
    for f in range(fields):
        raw = own_rows(f)
        moved = combine(
            coefs,
            raw,
            lane_roll(raw, -1),
            lane_roll(raw, 1),
            sub_roll(raw, -1),
            sub_roll(raw, 1),
        )
        for k, sides in enumerate(spread(moved, levels)):
            next_sides[f * pairs + k] = sides


def turned(value):
    rows = value.shape[0] // 2
    up, down = sub_roll(value, rows - 1), sub_roll(value, 1 - rows)
    return ((up, down), (down, up))


def corner_kernel(
    levels, sides_y, corner_sw, corner_se, corner_nw, corner_ne, corners, shares
):
    half = levels // 4
    tile = corner_sw.shape
    rows = tile[0] // 2
    sub, lane = iotas(tile)
    local = sub % rows
    odd_sub = sub % 2 == 1
    bottom = local == 0
    top = local == rows - 1
    even_lane = lane % 2 == 0
    dense = jnp.where(
        odd_sub,
        jnp.where(even_lane, lane_roll(corner_se[...], -1), lane_roll(corner_sw[...], 1)),
        jnp.where(even_lane, lane_roll(corner_ne[...], -1), lane_roll(corner_nw[...], 1)),
    )
    count = corners.shape[0]
    for i in range(count):
        corners[i] = lane_roll(dense, -(2 * i + 1))
    for k in range(half):
        places = turned(lane_roll(dense, -(2 * (count + k) + 1)))
        for i in range(2):
            j = 2 * k + i
            south_face = places[i][1]
            shares[j, 0] = jnp.where(bottom, jnp.minimum(south_face, 0.0), 0.0)
            shares[j, 1] = jnp.where(
                bottom,
                jnp.maximum(south_face, 0.0),
                jnp.where(top, jnp.maximum(-sides_y[j], 0.0), 0.0),
            )


def transport_and_solve(
    fields,
    levels,
    tracers,
    cx,
    cy,
    from_south,
    from_north,
    east,
    west,
    next_sides,
    west_x,
    corners,
    shares,
    decay,
    source,
    state,
    own_coefs,
    halo_coefs,
):
    pairs = levels // 2
    half = pairs // 2
    tile = tracers.shape[1:]
    rows = tile[0] // 2
    lanes = tile[1]
    group = lanes // levels
    sub, lane = iotas(tile)
    local = sub % rows
    low = sub < rows
    first_lane = lane == 0
    last_lane = lane == lanes - 1
    odd_sub = sub % 2 == 1
    bottom = local == 0
    top = local == rows - 1
    in_first = bottom | top


    def inner_rows(first, second):
        (first_up, first_down), _ = turned(first)
        (second_up, second_down), _ = turned(second)
        return (
            jnp.where(in_first, first_up, second_down),
            jnp.where(in_first, first_down, second_up),
        )

    base = fields * half
    count = pairs // rows
    for k in range(half):
        quad, t = 2 * k // rows, 2 * k % rows
        packed_south = from_south[base + quad]
        packed_south_y = from_south[base + count + quad]
        packed_north = from_north[base + quad]
        south_x = jnp.where(in_first, sub_roll(packed_south, t), sub_roll(packed_south, 3 + t))
        south_y = jnp.where(
            in_first, sub_roll(packed_south_y, t), sub_roll(packed_south_y, 3 + t)
        )
        north_x = jnp.where(in_first, sub_roll(packed_north, -t), sub_roll(packed_north, 5 - t))
        halo_x = jnp.where(odd_sub, south_x, north_x)
        halo_west = jnp.where(
            first_lane, corners[fields * half + k], lane_roll(halo_x, 1)
        )
        _, inner_top = inner_rows(cy[2 * k], cy[2 * k + 1])
        face = jnp.where(odd_sub, -south_y, inner_top)
        halo_coefs[k, 0] = (
            1.0
            - jnp.maximum(halo_x, 0.0)
            + jnp.minimum(halo_west, 0.0)
            + jnp.minimum(face, 0.0)
        )
        halo_coefs[k, 1] = jnp.maximum(-halo_x, 0.0)
        halo_coefs[k, 2] = jnp.maximum(halo_west, 0.0)
        halo_coefs[k, 3] = jnp.maximum(face, 0.0)
        places = turned(south_y)
        for i in range(2):
            j = 2 * k + i
            below = jnp.where(bottom, places[i][1], sub_roll(cy[j], 1))
            for c, value in enumerate(coefficients(cx[j], west_x[j], cy[j], below)):
                own_coefs[j, c] = value

    def advect(f, k, own_set, halo_set):
        message_south = from_south[f * half + k]
        message_north = from_north[f * half + k]
        slots = (f * pairs + 2 * k, f * pairs + 2 * k + 1)
        own = [tracers[slot] for slot in slots]
        own_east = [east[slot] for slot in slots]
        own_west = [west[slot] for slot in slots]
        sides = corners[f * half + k]
        halo = jnp.where(odd_sub, message_south, message_north)
        inner_bottom, inner_top = inner_rows(*own)
        flux = jnp.where(odd_sub, sub_roll(message_south, 1), sub_roll(message_north, -1))
        next_halo = (
            halo_set[0] * halo
            + (
                halo_set[1] * jnp.where(last_lane, sides, lane_roll(halo, -1))
                + halo_set[2] * jnp.where(first_lane, sides, lane_roll(halo, 1))
            )
            + (halo_set[3] * jnp.where(odd_sub, inner_bottom, inner_top) + flux)
        )
        places, next_places, side_places = turned(halo), turned(next_halo), turned(sides)
        results = []
        for i in range(2):
            north, south = places[i]
            once = combine(
                own_set[i],
                own[i],
                own_east[i],
                own_west[i],
                jnp.where(top, north, sub_roll(own[i], -1)),
                jnp.where(bottom, south, sub_roll(own[i], 1)),
            )
            side_north, side_south = side_places[i]
            next_column = (
                next_sides[slots[i]]
                + own_set[i][5] * jnp.where(first_lane, own_west[i], own_east[i])
                + own_set[i][6] * jnp.where(bottom, side_south, side_north)
            )
            north, south = next_places[i]
            results.append(
                combine(
                    own_set[i],
                    once,
                    jnp.where(last_lane, next_column, lane_roll(once, -1)),
                    jnp.where(first_lane, next_column, lane_roll(once, 1)),
                    jnp.where(top, north, sub_roll(once, -1)),
                    jnp.where(bottom, south, sub_roll(once, 1)),
                )
            )
        return results

    def transport(p):
        f1 = 2 * p
        f2 = jnp.minimum(f1 + 1, fields - 1)
        columns = []
        for k in range(half):
            own_set = [
                [own_coefs[2 * k + i, c] for c in range(5)]
                + [shares[2 * k + i, c] for c in range(2)]
                for i in range(2)
            ]
            halo_set = [halo_coefs[k, c] for c in range(4)]
            for one, two in zip(
                advect(f1, k, own_set, halo_set), advect(f2, k, own_set, halo_set)
            ):
                columns.append(jnp.where(low, one, sub_roll(two, rows)))
                columns.append(jnp.where(low, sub_roll(one, rows), two))
        return tuple(columns)

    def solve(p, columns):
        f1 = 2 * p
        f2 = jnp.minimum(f1 + 1, fields - 1)
        waves = cosine_sums(columns)
        change = cosine_series([source[m, p] - decay[m, p] * waves[m] for m in range(levels)])
        square = change[0] * change[0]
        for l in range(1, levels):
            square = square + change[l] * change[l]
        for k in range(pairs):
            even, odd = (columns[l] + change[l] for l in (2 * k, 2 * k + 1))
            state[f1 * pairs + k] = jnp.where(low, even, sub_roll(odd, rows))
            state[f2 * pairs + k] = jnp.where(low, sub_roll(even, rows), odd)
        return jnp.where(low | (f1 + 1 < fields), square, 0.0)

    def pair_step(p, carried):
        total, columns = carried
        following = transport(p)
        return total + solve(p - 1, columns), following

    field_pairs = (fields + 1) // 2
    total, columns = lax.fori_loop(
        1, field_pairs, pair_step, (jnp.zeros(tile, F32), transport(0))
    )
    return total + solve(field_pairs - 1, columns)


def main_kernel(fields, levels, *refs):
    inputs, (target, onehot), (state, placed), coefs = refs[:13], refs[13:15], refs[15:17], refs[17:]
    rows, lanes = target.shape
    total = transport_and_solve(fields, levels, *inputs, state, *coefs)

    heat = (total + sub_roll(total, rows)) * (1.0 / (fields * levels))
    first = heat.astype(jnp.bfloat16).astype(F32)
    rest = heat - first
    second = rest.astype(jnp.bfloat16).astype(F32)
    third = rest - second
    spans = placed.shape[0]
    slot_row, _ = iotas((spans, lanes))
    high = lax.shift_right_logical(target[...], lanes.bit_length() - 1)
    hits = [slot_row == high[r : r + 1] for r in range(rows)]
    left = jnp.concatenate(
        [
            jnp.concatenate(
                [
                    jnp.where(hits[r], part[r : r + 1], 0.0).astype(jnp.bfloat16)
                    for r in range(rows)
                ],
                axis=1,
            )
            for part in (first, second, third)
        ],
        axis=0,
    )
    result = jnp.dot(left, onehot[...], preferred_element_type=F32)
    placed[...] = result[:spans] + result[spans : 2 * spans] + result[2 * spans :]


def finish_kernel(parts, state, total_out, state_out, total, semaphores):
    copy_state = pltpu.make_async_copy(state, state_out, semaphores.at[0])
    copy_state.start()
    value = parts[0]
    for i in range(1, parts.shape[0]):
        value = value + parts[i]
    total[...] = value
    copy_total = pltpu.make_async_copy(total, total_out, semaphores.at[1])
    copy_total.start()
    copy_state.wait()
    copy_total.wait()


def body(tracers, courant_x, courant_y, physics_ref, class_coeffs, span_target, cloud_class):
    fields, levels, rows, cols = tracers.shape
    wide = lax.axis_size("wide")
    narrow = lax.axis_size("narrow")
    pairs = levels // 2
    half = pairs // 2
    tile = (2 * rows, cols)
    field_pairs = (fields + 1) // 2
    flat = tracers.reshape(fields * pairs, *tile)
    cx = courant_x.reshape(pairs, *tile)
    cy = courant_y.reshape(pairs, *tile)
    quads = pairs // rows

    def array(*shape, dtype=F32):
        return jax.ShapeDtypeStruct(shape, dtype)

    flat, cx, cy, north = pl.pallas_call(
        functools.partial(pack_north_kernel, levels),
        out_shape=(
            array(fields * pairs, *tile),
            array(pairs, *tile),
            array(pairs, *tile),
            array(fields * half + 2 * quads, *tile),
        ),
        in_specs=[HBM] * 3,
        out_specs=[VMEM] * 4,
        scratch_shapes=[pltpu.SemaphoreType.DMA((6,))],
        compiler_params=PARAMS,
    )(*(pltpu.with_memory_space_constraint(x, pltpu.HBM) for x in (flat, cx, cy)))
    edge, corner, south = pl.pallas_call(
        functools.partial(pack_edges_kernel, levels),
        out_shape=(
            array(fields + 2, *tile),
            array(*tile),
            array(fields * half + quads, *tile),
        ),
        in_specs=[VMEM] * 3,
        out_specs=[VMEM] * 3,
        compiler_params=PARAMS,
    )(flat, cx, cy)

    def send(value, up, right):
        pairs_ = []
        for w in range(wide):
            for n in range(narrow):
                to = ((w + up) % wide) * narrow + (n + right) % narrow
                pairs_.append((w * narrow + n, to))
        return lax.ppermute(value, ("wide", "narrow"), pairs_)

    def to_both_sides(value, up):
        from_west = send(value, up, 1)
        from_east = from_west if narrow == 2 else send(value, up, -1)
        return from_west, from_east

    from_south = send(north, 1, 0)
    from_north = send(south, -1, 0)
    edge_west, edge_east = to_both_sides(edge, 0)
    corner_sw, corner_se = to_both_sides(corner, 1)
    corner_nw, corner_ne = to_both_sides(corner, -1)

    decay, source, onehot = pl.pallas_call(
        prep_kernel,
        out_shape=(array(levels, field_pairs, *tile),) * 2
        + (array(rows * cols, cols, dtype=jnp.bfloat16),),
        in_specs=[SMEM, SMEM, VMEM, VMEM],
        out_specs=[VMEM] * 3,
        cost_estimate=pl.CostEstimate(flops=4000000, bytes_accessed=2000000, transcendentals=0),
        compiler_params=PARAMS,
    )(class_coeffs, physics_ref, cloud_class, span_target)

    shifted = pl.pallas_call(
        functools.partial(shift_kernel, levels),
        out_shape=(array(fields * pairs, *tile),) * 2,
        in_specs=[VMEM] * 4,
        out_specs=[VMEM] * 2,
        compiler_params=PARAMS,
    )(flat, edge, edge_west, edge_east)
    next_sides, west_x, sides_y = pl.pallas_call(
        functools.partial(next_kernel, levels),
        out_shape=(array(fields * pairs, *tile),) + (array(pairs, *tile),) * 2,
        in_specs=[VMEM] * 4,
        out_specs=[VMEM] * 3,
        compiler_params=PARAMS,
    )(cx, edge, edge_west, edge_east)
    corners, shares = pl.pallas_call(
        functools.partial(corner_kernel, levels),
        out_shape=(array((fields + 1) * half, *tile), array(pairs, 2, *tile)),
        in_specs=[VMEM] * 5,
        out_specs=[VMEM] * 2,
        compiler_params=PARAMS,
    )(sides_y, corner_sw, corner_se, corner_nw, corner_ne)
    state, placed = pl.pallas_call(
        functools.partial(main_kernel, fields, levels),
        out_shape=(array(fields * pairs, *tile), array(wide * rows, cols)),
        in_specs=[VMEM] * 15,
        out_specs=[VMEM] * 2,
        scratch_shapes=[
            pltpu.VMEM((pairs, 5) + tile, F32),
            pltpu.VMEM((half, 4) + tile, F32),
        ],
        compiler_params=PARAMS,
    )(
        flat,
        cx,
        cy,
        from_south,
        from_north,
        *shifted,
        next_sides,
        west_x,
        corners,
        shares,
        decay,
        source,
        span_target,
        onehot,
    )
    received = lax.all_to_all(
        placed.reshape(wide, rows, cols), "wide", split_axis=0, concat_axis=0, tiled=True
    )
    span_diag, state = pl.pallas_call(
        finish_kernel,
        out_shape=(array(rows, cols), array(fields * pairs, *tile)),
        in_specs=[VMEM] * 2,
        out_specs=[HBM] * 2,
        scratch_shapes=[pltpu.VMEM((rows, cols), F32), pltpu.SemaphoreType.DMA((2,))],
        compiler_params=PARAMS,
    )(received, state)
    return state.reshape(fields, levels, rows, cols), span_diag


def solution(mesh):
    return jax.shard_map(
        body,
        mesh=mesh,
        in_specs=(
            P(None, None, "wide", "narrow"),
            P(None, "wide", "narrow"),
            P(None, "wide", "narrow"),
            P(),
            P(),
            P("wide", "narrow"),
            P("wide", "narrow"),
        ),
        out_specs=(P(None, None, "wide", "narrow"), P("wide", "narrow")),
        check_vma=False,
    )
```

```python
import functools
import math

import jax
import jax.numpy as jnp
from jax import lax
from jax.experimental import pallas as pl
from jax.experimental.pallas import tpu as pltpu
from jax.sharding import PartitionSpec as P

VMEM = pl.BlockSpec(memory_space=pltpu.VMEM)
HBM = pl.BlockSpec(memory_space=pltpu.HBM)
SMEM = pl.BlockSpec(memory_space=pltpu.SMEM)
F32 = jnp.float32
PARAMS = pltpu.CompilerParams(vmem_limit_bytes=12 * 1024 * 1024)


def sub_roll(value, shift):
    shift = shift % value.shape[0]
    return value if shift == 0 else pltpu.roll(value, shift, 0)


def lane_roll(value, shift):
    shift = shift % value.shape[1]
    return value if shift == 0 else pltpu.roll(value, shift, 1)


def iotas(shape):
    return lax.broadcasted_iota(jnp.int32, shape, 0), lax.broadcasted_iota(jnp.int32, shape, 1)


def one_row(vectors, row, step):
    rows = vectors[0].shape[0] // 2
    local = iotas(vectors[0].shape)[0] % rows
    packed = []
    for start in range(0, len(vectors), rows):
        total = vectors[start]
        for t in range(1, rows):
            total = jnp.where(
                local == row + step * t, sub_roll(vectors[start + t], step * t), total
            )
        packed.append(total)
    return packed


def inner_flux(value, courant):
    return jnp.maximum(courant, 0.0) * value + jnp.minimum(courant, 0.0) * sub_roll(value, -1)


def northward_rows(value, courant):
    local = iotas(value.shape)[0] % (value.shape[0] // 2)
    return jnp.where(local == 2, inner_flux(value, courant), value)


def southward_rows(value, courant):
    local = iotas(value.shape)[0] % (value.shape[0] // 2)
    return jnp.where(local == 1, sub_roll(-inner_flux(value, courant), 1), value)


def pack_north_kernel(levels, tracers_in, cx_in, cy_in, tracers, cx, cy, north, semaphores):
    copies = [
        pltpu.make_async_copy(source, into, semaphores.at[i])
        for i, (source, into) in enumerate(((tracers_in, tracers), (cx_in, cx), (cy_in, cy)))
    ]
    for copy in copies:
        copy.start()
    for copy in copies:
        copy.wait()
    pairs = levels // 2
    half = pairs // 2
    tile = tracers.shape[1:]
    rows = tile[0] // 2
    upper = iotas(tile)[0] % rows >= rows // 2
    fields = tracers.shape[0] // pairs
    for f in range(fields):
        for k in range(half):
            one, two = (
                northward_rows(tracers[f * pairs + j], cy[j]) for j in (2 * k, 2 * k + 1)
            )
            north[f * half + k] = jnp.where(upper, one, sub_roll(two, 2))
    courant = one_row([cx[k] for k in range(pairs)], rows - 1, -1)
    courant += one_row([cy[k] for k in range(pairs)], rows - 1, -1)
    for k, value in enumerate(courant):
        north[fields * half + k] = value


def pack_edges_kernel(levels, tracers, cx, cy, edge, corner, south_rows):
    pairs = levels // 2
    half = pairs // 2
    fields = tracers.shape[0] // pairs
    tile = tracers.shape[1:]
    rows = tile[0] // 2
    lanes = tile[1]
    group = lanes // levels
    sub, lane = iotas(tile)
    upper = sub % rows >= rows // 2
    odd_sub = sub % 2 == 1
    corners = [jnp.zeros(tile, F32)]

    def pack_edge(vectors, slot):
        total = lane_roll(vectors[0], 2)
        for k in range(1, pairs):
            total = jnp.where(
                lane // (2 * group) == k, lane_roll(vectors[k], 2 + 2 * group * k), total
            )
        total = jnp.where(
            lane % (2 * group) < group, total, sub_roll(lane_roll(total, group), rows)
        )
        edge[slot] = jnp.where(lane % group < group // 2, total, lane_roll(total, group // 2))
        for k in range(half):
            one, two = vectors[2 * k], vectors[2 * k + 1]
            place = slot * half + k
            north = jnp.where(upper, one, sub_roll(two, 2))
            south = jnp.where(upper, sub_roll(two, -2), one)
            if slot < fields:
                first = southward_rows(one, cy[2 * k])
                second = southward_rows(two, cy[2 * k + 1])
                south_rows[place] = jnp.where(upper, sub_roll(second, -2), first)
            value = lane_roll(jnp.where(odd_sub, north, south), 2 * place + 1)
            corners[0] = jnp.where(lane // 2 == place, value, corners[0])

    for f in range(fields):
        pack_edge([tracers[f * pairs + k] for k in range(pairs)], f)
    pack_edge([cx[k] for k in range(pairs)], fields)
    pack_edge([cy[k] for k in range(pairs)], fields + 1)
    corner[...] = corners[0]
    for k, value in enumerate(one_row([cx[k] for k in range(pairs)], 0, 1)):
        south_rows[fields * half + k] = value


def cosine_sums(values):
    count = len(values)
    if count == 1:
        return values
    half = count // 2
    plus = [values[n] + values[count - 1 - n] for n in range(half)]
    minus = [
        (values[n] - values[count - 1 - n])
        * (0.5 / math.cos(math.pi * (2 * n + 1) / (2 * count)))
        for n in range(half)
    ]
    even = cosine_sums(plus)
    odd = cosine_sums(minus)
    result = []
    for k in range(half):
        result.append(even[k])
        result.append(odd[k] + odd[k + 1] if k + 1 < half else odd[k])
    return result


def cosine_series(values):
    count = len(values)
    if count == 1:
        return values
    half = count // 2
    odd_in = [values[2 * k + 1] + values[2 * k - 1] if k else values[1] for k in range(half)]
    even = cosine_series(values[0::2])
    odd = cosine_series(odd_in)
    odd = [
        odd[n] * (0.5 / math.cos(math.pi * (2 * n + 1) / (2 * count))) for n in range(half)
    ]
    return [even[n] + odd[n] for n in range(half)] + [
        even[n] - odd[n] for n in range(half - 1, -1, -1)
    ]


def prep_kernel(coeffs, profile, klass, target, decay, source, onehot):
    levels, pairs = decay.shape[:2]
    fields = profile.shape[0]
    tile = decay.shape[2:]
    rows, lanes = klass.shape
    sub, lane = iotas(tile)
    low = sub < rows
    kind = jnp.concatenate([klass[...], klass[...]], axis=0)
    is_two = kind == 2
    is_one = kind == 1

    def by_class(which, f):
        return jnp.where(
            is_two,
            coeffs[which, 2, f] * 0.25,
            jnp.where(is_one, coeffs[which, 1, f] * 0.5, coeffs[which, 0, f]),
        )

    for p in range(pairs):
        f1 = 2 * p
        f2 = min(2 * p + 1, fields - 1)
        diffusion = jnp.where(low, by_class(0, f1), by_class(0, f2))
        relax = jnp.where(low, by_class(1, f1), by_class(1, f2))
        waves = cosine_sums([jnp.where(low, profile[f1, l], profile[f2, l]) for l in range(levels)])
        for m in range(levels):
            rate = relax + diffusion * (2.0 - 2.0 * math.cos(math.pi * m / levels))
            once = 1.0 / (1.0 + rate)
            square = once * once
            twice = once + square
            steps = jnp.where(is_two, twice + twice * square, jnp.where(is_one, twice, once))
            steps = steps * ((1.0 if m == 0 else 2.0) / levels)
            decay[m, p] = steps * rate
            source[m, p] = steps * relax * waves[m]
    low_part = target[...] & (lanes - 1)
    slot, _ = iotas((lanes, lanes))
    for r in range(rows):
        hit = jnp.where(slot == low_part[r : r + 1], 1.0, 0.0)
        onehot[r * lanes : (r + 1) * lanes, :] = jnp.transpose(hit).astype(jnp.bfloat16)


def combine(coefs, center, east, west, north, south):
    return (
        coefs[0] * center
        + (coefs[1] * east + coefs[2] * west)
        + (coefs[3] * north + coefs[4] * south)
    )


def coefficients(here_x, west_x, here_y, south_y):
    return (
        1.0
        - jnp.maximum(here_x, 0.0)
        + jnp.minimum(west_x, 0.0)
        - jnp.maximum(here_y, 0.0)
        + jnp.minimum(south_y, 0.0),
        jnp.maximum(-here_x, 0.0),
        jnp.maximum(west_x, 0.0),
        jnp.maximum(-here_y, 0.0),
        jnp.maximum(south_y, 0.0),
    )


def side_by_side(value, place):
    return jnp.where(place == 3, lane_roll(value, -2), value)


def beside(edge, edge_west, edge_east, slot, place):
    from_east = (place == 2) | (place == 3)
    from_west = (place == 4) | (place == 5)
    return jnp.where(
        from_east, edge_east[slot], jnp.where(from_west, edge_west[slot], edge[slot])
    )


def spread(value, levels):
    lanes = value.shape[1]
    rows = value.shape[0] // 2
    group = lanes // levels
    sub, lane = iotas(value.shape)
    value = side_by_side(value, lane % group)
    value = jnp.where(sub < rows, value, sub_roll(lane_roll(value, -group), rows))
    return [lane_roll(value, -(2 * group * k + 3)) for k in range(levels // 2)]


def shift_kernel(levels, tracers, edge, edge_west, edge_east, east, west):
    pairs = levels // 2
    tile = tracers.shape[1:]
    lanes = tile[1]
    lane = iotas(tile)[1]
    place = lane % (lanes // levels)
    for f in range(tracers.shape[0] // pairs):
        for k, sides in enumerate(spread(beside(edge, edge_west, edge_east, f, place), levels)):
            own = tracers[f * pairs + k]
            east[f * pairs + k] = jnp.where(lane == lanes - 1, sides, lane_roll(own, -1))
            west[f * pairs + k] = jnp.where(lane == 0, sides, lane_roll(own, 1))


def next_kernel(levels, cx, edge, edge_west, edge_east, next_sides, west_x, sides_y):
    pairs = levels // 2
    fields = next_sides.shape[0] // pairs
    tile = cx.shape[1:]
    rows = tile[0] // 2
    sub, lane = iotas(tile)
    place = lane % (tile[1] // levels)

    def own_rows(slot):
        value = beside(edge, edge_west, edge_east, slot, place)
        return jnp.where(sub < rows, value, 0.0)

    edge_x = own_rows(fields)
    edge_y = own_rows(fields + 1)
    coefs = coefficients(edge_x, lane_roll(edge_x, 1), edge_y, sub_roll(edge_y, 1))
    for k, sides in enumerate(spread(edge_x, levels)):
        west_x[k] = jnp.where(lane == 0, sides, lane_roll(cx[k], 1))
    for k, sides in enumerate(spread(edge_y, levels)):
        sides_y[k] = sides
    for f in range(fields):
        raw = own_rows(f)
        moved = combine(
            coefs,
            raw,
            lane_roll(raw, -1),
            lane_roll(raw, 1),
            sub_roll(raw, -1),
            sub_roll(raw, 1),
        )
        for k, sides in enumerate(spread(moved, levels)):
            next_sides[f * pairs + k] = sides


def turned(value):
    rows = value.shape[0] // 2
    up, down = sub_roll(value, rows - 1), sub_roll(value, 1 - rows)
    return ((up, down), (down, up))


def corner_kernel(
    levels, sides_y, corner_sw, corner_se, corner_nw, corner_ne, corners, shares
):
    half = levels // 4
    tile = corner_sw.shape
    rows = tile[0] // 2
    sub, lane = iotas(tile)
    local = sub % rows
    odd_sub = sub % 2 == 1
    bottom = local == 0
    top = local == rows - 1
    even_lane = lane % 2 == 0
    dense = jnp.where(
        odd_sub,
        jnp.where(even_lane, lane_roll(corner_se[...], -1), lane_roll(corner_sw[...], 1)),
        jnp.where(even_lane, lane_roll(corner_ne[...], -1), lane_roll(corner_nw[...], 1)),
    )
    count = corners.shape[0]
    for i in range(count):
        corners[i] = lane_roll(dense, -(2 * i + 1))
    for k in range(half):
        places = turned(lane_roll(dense, -(2 * (count + k) + 1)))
        for i in range(2):
            j = 2 * k + i
            south_face = places[i][1]
            shares[j, 0] = jnp.where(bottom, jnp.minimum(south_face, 0.0), 0.0)
            shares[j, 1] = jnp.where(
                bottom,
                jnp.maximum(south_face, 0.0),
                jnp.where(top, jnp.maximum(-sides_y[j], 0.0), 0.0),
            )


def transport_and_solve(
    fields,
    levels,
    tracers,
    cx,
    cy,
    from_south,
    from_north,
    east,
    west,
    next_sides,
    west_x,
    corners,
    shares,
    decay,
    source,
    state,
    own_coefs,
    halo_coefs,
):
    pairs = levels // 2
    half = pairs // 2
    tile = tracers.shape[1:]
    rows = tile[0] // 2
    lanes = tile[1]
    group = lanes // levels
    sub, lane = iotas(tile)
    local = sub % rows
    low = sub < rows
    first_lane = lane == 0
    last_lane = lane == lanes - 1
    odd_sub = sub % 2 == 1
    bottom = local == 0
    top = local == rows - 1
    in_first = bottom | top


    def inner_rows(first, second):
        (first_up, first_down), _ = turned(first)
        (second_up, second_down), _ = turned(second)
        return (
            jnp.where(in_first, first_up, second_down),
            jnp.where(in_first, first_down, second_up),
        )

    base = fields * half
    count = pairs // rows
    for k in range(half):
        quad, t = 2 * k // rows, 2 * k % rows
        packed_south = from_south[base + quad]
        packed_south_y = from_south[base + count + quad]
        packed_north = from_north[base + quad]
        south_x = jnp.where(in_first, sub_roll(packed_south, t), sub_roll(packed_south, 3 + t))
        south_y = jnp.where(
            in_first, sub_roll(packed_south_y, t), sub_roll(packed_south_y, 3 + t)
        )
        north_x = jnp.where(in_first, sub_roll(packed_north, -t), sub_roll(packed_north, 5 - t))
        halo_x = jnp.where(odd_sub, south_x, north_x)
        halo_west = jnp.where(
            first_lane, corners[fields * half + k], lane_roll(halo_x, 1)
        )
        _, inner_top = inner_rows(cy[2 * k], cy[2 * k + 1])
        face = jnp.where(odd_sub, -south_y, inner_top)
        halo_coefs[k, 0] = (
            1.0
            - jnp.maximum(halo_x, 0.0)
            + jnp.minimum(halo_west, 0.0)
            + jnp.minimum(face, 0.0)
        )
        halo_coefs[k, 1] = jnp.maximum(-halo_x, 0.0)
        halo_coefs[k, 2] = jnp.maximum(halo_west, 0.0)
        halo_coefs[k, 3] = jnp.maximum(face, 0.0)
        places = turned(south_y)
        for i in range(2):
            j = 2 * k + i
            below = jnp.where(bottom, places[i][1], sub_roll(cy[j], 1))
            for c, value in enumerate(coefficients(cx[j], west_x[j], cy[j], below)):
                own_coefs[j, c] = value

    def advect(f, k, own_set, halo_set):
        message_south = from_south[f * half + k]
        message_north = from_north[f * half + k]
        slots = (f * pairs + 2 * k, f * pairs + 2 * k + 1)
        own = [tracers[slot] for slot in slots]
        own_east = [east[slot] for slot in slots]
        own_west = [west[slot] for slot in slots]
        sides = corners[f * half + k]
        halo = jnp.where(odd_sub, message_south, message_north)
        inner_bottom, inner_top = inner_rows(*own)
        flux = jnp.where(odd_sub, sub_roll(message_south, 1), sub_roll(message_north, -1))
        next_halo = (
            halo_set[0] * halo
            + (
                halo_set[1] * jnp.where(last_lane, sides, lane_roll(halo, -1))
                + halo_set[2] * jnp.where(first_lane, sides, lane_roll(halo, 1))
            )
            + (halo_set[3] * jnp.where(odd_sub, inner_bottom, inner_top) + flux)
        )
        places, next_places, side_places = turned(halo), turned(next_halo), turned(sides)
        results = []
        for i in range(2):
            north, south = places[i]
            once = combine(
                own_set[i],
                own[i],
                own_east[i],
                own_west[i],
                jnp.where(top, north, sub_roll(own[i], -1)),
                jnp.where(bottom, south, sub_roll(own[i], 1)),
            )
            side_north, side_south = side_places[i]
            next_column = (
                next_sides[slots[i]]
                + own_set[i][5] * jnp.where(first_lane, own_west[i], own_east[i])
                + own_set[i][6] * jnp.where(bottom, side_south, side_north)
            )
            north, south = next_places[i]
            results.append(
                combine(
                    own_set[i],
                    once,
                    jnp.where(last_lane, next_column, lane_roll(once, -1)),
                    jnp.where(first_lane, next_column, lane_roll(once, 1)),
                    jnp.where(top, north, sub_roll(once, -1)),
                    jnp.where(bottom, south, sub_roll(once, 1)),
                )
            )
        return results

    def transport(p):
        f1 = 2 * p
        f2 = jnp.minimum(f1 + 1, fields - 1)
        columns = []
        for k in range(half):
            own_set = [
                [own_coefs[2 * k + i, c] for c in range(5)]
                + [shares[2 * k + i, c] for c in range(2)]
                for i in range(2)
            ]
            halo_set = [halo_coefs[k, c] for c in range(4)]
            for one, two in zip(
                advect(f1, k, own_set, halo_set), advect(f2, k, own_set, halo_set)
            ):
                columns.append(jnp.where(low, one, sub_roll(two, rows)))
                columns.append(jnp.where(low, sub_roll(one, rows), two))
        return tuple(columns)

    def solve(p, columns):
        f1 = 2 * p
        f2 = jnp.minimum(f1 + 1, fields - 1)
        waves = cosine_sums(columns)
        change = cosine_series([source[m, p] - decay[m, p] * waves[m] for m in range(levels)])
        square = change[0] * change[0]
        for l in range(1, levels):
            square = square + change[l] * change[l]
        for k in range(pairs):
            even, odd = (columns[l] + change[l] for l in (2 * k, 2 * k + 1))
            state[f1 * pairs + k] = jnp.where(low, even, sub_roll(odd, rows))
            state[f2 * pairs + k] = jnp.where(low, sub_roll(even, rows), odd)
        return jnp.where(low | (f1 + 1 < fields), square, 0.0)

    def pair_step(p, carried):
        total, columns = carried
        following = transport(p)
        return total + solve(p - 1, columns), following

    field_pairs = (fields + 1) // 2
    total, columns = lax.fori_loop(
        1, field_pairs, pair_step, (jnp.zeros(tile, F32), transport(0))
    )
    return total + solve(field_pairs - 1, columns)


def main_kernel(fields, levels, *refs):
    inputs, (target, onehot), (state, placed), coefs = refs[:13], refs[13:15], refs[15:17], refs[17:]
    rows, lanes = target.shape
    total = transport_and_solve(fields, levels, *inputs, state, *coefs)

    heat = (total + sub_roll(total, rows)) * (1.0 / (fields * levels))
    first = heat.astype(jnp.bfloat16).astype(F32)
    rest = heat - first
    second = rest.astype(jnp.bfloat16).astype(F32)
    third = rest - second
    spans = placed.shape[0]
    slot_row, _ = iotas((spans, lanes))
    high = lax.shift_right_logical(target[...], lanes.bit_length() - 1)
    hits = [slot_row == high[r : r + 1] for r in range(rows)]
    left = jnp.concatenate(
        [
            jnp.concatenate(
                [
                    jnp.where(hits[r], part[r : r + 1], 0.0).astype(jnp.bfloat16)
                    for r in range(rows)
                ],
                axis=1,
            )
            for part in (first, second, third)
        ],
        axis=0,
    )
    result = jnp.dot(left, onehot[...], preferred_element_type=F32)
    placed[...] = result[:spans] + result[spans : 2 * spans] + result[2 * spans :]


def write_kernel(state, state_out, semaphore):
    copy = pltpu.make_async_copy(state, state_out, semaphore)
    copy.start()
    copy.wait()


def finish_kernel(parts, total):
    value = parts[0]
    for i in range(1, parts.shape[0]):
        value = value + parts[i]
    total[...] = value


def body(tracers, courant_x, courant_y, physics_ref, class_coeffs, span_target, cloud_class):
    fields, levels, rows, cols = tracers.shape
    wide = lax.axis_size("wide")
    narrow = lax.axis_size("narrow")
    pairs = levels // 2
    half = pairs // 2
    tile = (2 * rows, cols)
    field_pairs = (fields + 1) // 2
    flat = tracers.reshape(fields * pairs, *tile)
    cx = courant_x.reshape(pairs, *tile)
    cy = courant_y.reshape(pairs, *tile)
    quads = pairs // rows

    def array(*shape, dtype=F32):
        return jax.ShapeDtypeStruct(shape, dtype)

    flat, cx, cy, north = pl.pallas_call(
        functools.partial(pack_north_kernel, levels),
        out_shape=(
            array(fields * pairs, *tile),
            array(pairs, *tile),
            array(pairs, *tile),
            array(fields * half + 2 * quads, *tile),
        ),
        in_specs=[HBM] * 3,
        out_specs=[VMEM] * 4,
        scratch_shapes=[pltpu.SemaphoreType.DMA((3,))],
        compiler_params=PARAMS,
    )(*(pltpu.with_memory_space_constraint(x, pltpu.HBM) for x in (flat, cx, cy)))
    edge, corner, south = pl.pallas_call(
        functools.partial(pack_edges_kernel, levels),
        out_shape=(
            array(fields + 2, *tile),
            array(*tile),
            array(fields * half + quads, *tile),
        ),
        in_specs=[VMEM] * 3,
        out_specs=[VMEM] * 3,
        compiler_params=PARAMS,
    )(flat, cx, cy)

    def send(value, up, right):
        pairs_ = []
        for w in range(wide):
            for n in range(narrow):
                to = ((w + up) % wide) * narrow + (n + right) % narrow
                pairs_.append((w * narrow + n, to))
        return lax.ppermute(value, ("wide", "narrow"), pairs_)

    def to_both_sides(value, up):
        from_west = send(value, up, 1)
        from_east = from_west if narrow == 2 else send(value, up, -1)
        return from_west, from_east

    from_south = send(north, 1, 0)
    from_north = send(south, -1, 0)
    edge_west, edge_east = to_both_sides(edge, 0)
    corner_sw, corner_se = to_both_sides(corner, 1)
    corner_nw, corner_ne = to_both_sides(corner, -1)

    decay, source, onehot = pl.pallas_call(
        prep_kernel,
        out_shape=(array(levels, field_pairs, *tile),) * 2
        + (array(rows * cols, cols, dtype=jnp.bfloat16),),
        in_specs=[SMEM, SMEM, VMEM, VMEM],
        out_specs=[VMEM] * 3,
        cost_estimate=pl.CostEstimate(flops=4000000, bytes_accessed=2000000, transcendentals=0),
        compiler_params=PARAMS,
    )(class_coeffs, physics_ref, cloud_class, span_target)

    shifted = pl.pallas_call(
        functools.partial(shift_kernel, levels),
        out_shape=(array(fields * pairs, *tile),) * 2,
        in_specs=[VMEM] * 4,
        out_specs=[VMEM] * 2,
        compiler_params=PARAMS,
    )(flat, edge, edge_west, edge_east)
    next_sides, west_x, sides_y = pl.pallas_call(
        functools.partial(next_kernel, levels),
        out_shape=(array(fields * pairs, *tile),) + (array(pairs, *tile),) * 2,
        in_specs=[VMEM] * 4,
        out_specs=[VMEM] * 3,
        compiler_params=PARAMS,
    )(cx, edge, edge_west, edge_east)
    corners, shares = pl.pallas_call(
        functools.partial(corner_kernel, levels),
        out_shape=(array((fields + 1) * half, *tile), array(pairs, 2, *tile)),
        in_specs=[VMEM] * 5,
        out_specs=[VMEM] * 2,
        compiler_params=PARAMS,
    )(sides_y, corner_sw, corner_se, corner_nw, corner_ne)
    state, placed = pl.pallas_call(
        functools.partial(main_kernel, fields, levels),
        out_shape=(array(fields * pairs, *tile), array(wide * rows, cols)),
        in_specs=[VMEM] * 15,
        out_specs=[VMEM] * 2,
        scratch_shapes=[
            pltpu.VMEM((pairs, 5) + tile, F32),
            pltpu.VMEM((half, 4) + tile, F32),
        ],
        compiler_params=PARAMS,
    )(
        flat,
        cx,
        cy,
        from_south,
        from_north,
        *shifted,
        next_sides,
        west_x,
        corners,
        shares,
        decay,
        source,
        span_target,
        onehot,
    )
    received = lax.all_to_all(
        placed.reshape(wide, rows, cols), "wide", split_axis=0, concat_axis=0, tiled=True
    )
    state = pl.pallas_call(
        write_kernel,
        out_shape=array(fields * pairs, *tile),
        in_specs=[VMEM],
        out_specs=HBM,
        scratch_shapes=[pltpu.SemaphoreType.DMA],
        cost_estimate=pl.CostEstimate(flops=0, bytes_accessed=40000000, transcendentals=0),
        compiler_params=PARAMS,
    )(state)
    span_diag = pl.pallas_call(
        finish_kernel,
        out_shape=array(rows, cols),
        in_specs=[VMEM],
        out_specs=VMEM,
        compiler_params=PARAMS,
    )(received)
    return state.reshape(fields, levels, rows, cols), span_diag


def solution(mesh):
    return jax.shard_map(
        body,
        mesh=mesh,
        in_specs=(
            P(None, None, "wide", "narrow"),
            P(None, "wide", "narrow"),
            P(None, "wide", "narrow"),
            P(),
            P(),
            P("wide", "narrow"),
            P("wide", "narrow"),
        ),
        out_specs=(P(None, None, "wide", "narrow"), P("wide", "narrow")),
        check_vma=False,
    )
```

```python
import functools
import math

import jax
import jax.numpy as jnp
from jax import lax
from jax.experimental import pallas as pl
from jax.experimental.pallas import tpu as pltpu
from jax.sharding import PartitionSpec as P

VMEM = pl.BlockSpec(memory_space=pltpu.VMEM)
HBM = pl.BlockSpec(memory_space=pltpu.HBM)
SMEM = pl.BlockSpec(memory_space=pltpu.SMEM)
F32 = jnp.float32
PARAMS = pltpu.CompilerParams(vmem_limit_bytes=12 * 1024 * 1024)


def sub_roll(value, shift):
    shift = shift % value.shape[0]
    return value if shift == 0 else pltpu.roll(value, shift, 0)


def lane_roll(value, shift):
    shift = shift % value.shape[1]
    return value if shift == 0 else pltpu.roll(value, shift, 1)


def iotas(shape):
    return lax.broadcasted_iota(jnp.int32, shape, 0), lax.broadcasted_iota(jnp.int32, shape, 1)


def one_row(vectors, row, step):
    rows = vectors[0].shape[0] // 2
    local = iotas(vectors[0].shape)[0] % rows
    packed = []
    for start in range(0, len(vectors), rows):
        total = vectors[start]
        for t in range(1, rows):
            total = jnp.where(
                local == row + step * t, sub_roll(vectors[start + t], step * t), total
            )
        packed.append(total)
    return packed


def inner_flux(value, courant):
    return jnp.maximum(courant, 0.0) * value + jnp.minimum(courant, 0.0) * sub_roll(value, -1)


def northward_rows(value, courant):
    local = iotas(value.shape)[0] % (value.shape[0] // 2)
    return jnp.where(local == 2, inner_flux(value, courant), value)


def southward_rows(value, courant):
    local = iotas(value.shape)[0] % (value.shape[0] // 2)
    return jnp.where(local == 1, sub_roll(-inner_flux(value, courant), 1), value)


def pack_north_kernel(levels, tracers_in, cx_in, cy_in, tracers, cx, cy, north, semaphores):
    copies = [
        pltpu.make_async_copy(source, into, semaphores.at[i])
        for i, (source, into) in enumerate(((tracers_in, tracers), (cx_in, cx), (cy_in, cy)))
    ]
    for copy in copies:
        copy.start()
    for copy in copies:
        copy.wait()
    pairs = levels // 2
    half = pairs // 2
    tile = tracers.shape[1:]
    rows = tile[0] // 2
    upper = iotas(tile)[0] % rows >= rows // 2
    fields = tracers.shape[0] // pairs
    for f in range(fields):
        for k in range(half):
            one, two = (
                northward_rows(tracers[f * pairs + j], cy[j]) for j in (2 * k, 2 * k + 1)
            )
            north[f * half + k] = jnp.where(upper, one, sub_roll(two, 2))
    courant = one_row([cx[k] for k in range(pairs)], rows - 1, -1)
    courant += one_row([cy[k] for k in range(pairs)], rows - 1, -1)
    for k, value in enumerate(courant):
        north[fields * half + k] = value


def pack_edges_kernel(levels, tracers, cx, cy, edge, corner, south_rows):
    pairs = levels // 2
    half = pairs // 2
    fields = tracers.shape[0] // pairs
    tile = tracers.shape[1:]
    rows = tile[0] // 2
    lanes = tile[1]
    group = lanes // levels
    sub, lane = iotas(tile)
    upper = sub % rows >= rows // 2
    odd_sub = sub % 2 == 1
    corners = [jnp.zeros(tile, F32)]

    def pack_edge(vectors, slot):
        total = lane_roll(vectors[0], 2)
        for k in range(1, pairs):
            total = jnp.where(
                lane // (2 * group) == k, lane_roll(vectors[k], 2 + 2 * group * k), total
            )
        total = jnp.where(
            lane % (2 * group) < group, total, sub_roll(lane_roll(total, group), rows)
        )
        edge[slot] = jnp.where(lane % group < group // 2, total, lane_roll(total, group // 2))
        for k in range(half):
            one, two = vectors[2 * k], vectors[2 * k + 1]
            place = slot * half + k
            north = jnp.where(upper, one, sub_roll(two, 2))
            south = jnp.where(upper, sub_roll(two, -2), one)
            if slot < fields:
                first = southward_rows(one, cy[2 * k])
                second = southward_rows(two, cy[2 * k + 1])
                south_rows[place] = jnp.where(upper, sub_roll(second, -2), first)
            value = lane_roll(jnp.where(odd_sub, north, south), 2 * place + 1)
            corners[0] = jnp.where(lane // 2 == place, value, corners[0])

    for f in range(fields):
        pack_edge([tracers[f * pairs + k] for k in range(pairs)], f)
    pack_edge([cx[k] for k in range(pairs)], fields)
    pack_edge([cy[k] for k in range(pairs)], fields + 1)
    corner[...] = corners[0]
    for k, value in enumerate(one_row([cx[k] for k in range(pairs)], 0, 1)):
        south_rows[fields * half + k] = value


def cosine_sums(values):
    count = len(values)
    if count == 1:
        return values
    half = count // 2
    plus = [values[n] + values[count - 1 - n] for n in range(half)]
    minus = [
        (values[n] - values[count - 1 - n])
        * (0.5 / math.cos(math.pi * (2 * n + 1) / (2 * count)))
        for n in range(half)
    ]
    even = cosine_sums(plus)
    odd = cosine_sums(minus)
    result = []
    for k in range(half):
        result.append(even[k])
        result.append(odd[k] + odd[k + 1] if k + 1 < half else odd[k])
    return result


def cosine_series(values):
    count = len(values)
    if count == 1:
        return values
    half = count // 2
    odd_in = [values[2 * k + 1] + values[2 * k - 1] if k else values[1] for k in range(half)]
    even = cosine_series(values[0::2])
    odd = cosine_series(odd_in)
    odd = [
        odd[n] * (0.5 / math.cos(math.pi * (2 * n + 1) / (2 * count))) for n in range(half)
    ]
    return [even[n] + odd[n] for n in range(half)] + [
        even[n] - odd[n] for n in range(half - 1, -1, -1)
    ]


def prep_kernel(coeffs, profile, klass, target, decay, source, onehot):
    levels, pairs = decay.shape[:2]
    fields = profile.shape[0]
    tile = decay.shape[2:]
    rows, lanes = klass.shape
    sub, lane = iotas(tile)
    low = sub < rows
    kind = jnp.concatenate([klass[...], klass[...]], axis=0)
    is_two = kind == 2
    is_one = kind == 1

    def by_class(which, f):
        return jnp.where(
            is_two,
            coeffs[which, 2, f] * 0.25,
            jnp.where(is_one, coeffs[which, 1, f] * 0.5, coeffs[which, 0, f]),
        )

    for p in range(pairs):
        f1 = 2 * p
        f2 = min(2 * p + 1, fields - 1)
        diffusion = jnp.where(low, by_class(0, f1), by_class(0, f2))
        relax = jnp.where(low, by_class(1, f1), by_class(1, f2))
        waves = cosine_sums([jnp.where(low, profile[f1, l], profile[f2, l]) for l in range(levels)])
        for m in range(levels):
            rate = relax + diffusion * (2.0 - 2.0 * math.cos(math.pi * m / levels))
            once = 1.0 / (1.0 + rate)
            square = once * once
            twice = once + square
            steps = jnp.where(is_two, twice + twice * square, jnp.where(is_one, twice, once))
            steps = steps * ((1.0 if m == 0 else 2.0) / levels)
            decay[m, p] = steps * rate
            source[m, p] = steps * relax * waves[m]
    low_part = target[...] & (lanes - 1)
    slot, _ = iotas((lanes, lanes))
    for r in range(rows):
        hit = jnp.where(slot == low_part[r : r + 1], 1.0, 0.0)
        onehot[r * lanes : (r + 1) * lanes, :] = jnp.transpose(hit).astype(jnp.bfloat16)


def combine(coefs, center, east, west, north, south):
    return (
        coefs[0] * center
        + (coefs[1] * east + coefs[2] * west)
        + (coefs[3] * north + coefs[4] * south)
    )


def coefficients(here_x, west_x, here_y, south_y):
    return (
        1.0
        - jnp.maximum(here_x, 0.0)
        + jnp.minimum(west_x, 0.0)
        - jnp.maximum(here_y, 0.0)
        + jnp.minimum(south_y, 0.0),
        jnp.maximum(-here_x, 0.0),
        jnp.maximum(west_x, 0.0),
        jnp.maximum(-here_y, 0.0),
        jnp.maximum(south_y, 0.0),
    )


def side_by_side(value, place):
    return jnp.where(place == 3, lane_roll(value, -2), value)


def beside(edge, edge_west, edge_east, slot, place):
    from_east = (place == 2) | (place == 3)
    from_west = (place == 4) | (place == 5)
    return jnp.where(
        from_east, edge_east[slot], jnp.where(from_west, edge_west[slot], edge[slot])
    )


def spread(value, levels):
    lanes = value.shape[1]
    rows = value.shape[0] // 2
    group = lanes // levels
    sub, lane = iotas(value.shape)
    value = side_by_side(value, lane % group)
    value = jnp.where(sub < rows, value, sub_roll(lane_roll(value, -group), rows))
    return [lane_roll(value, -(2 * group * k + 3)) for k in range(levels // 2)]


def shift_kernel(levels, tracers, edge, edge_west, edge_east, east, west):
    pairs = levels // 2
    tile = tracers.shape[1:]
    lanes = tile[1]
    lane = iotas(tile)[1]
    place = lane % (lanes // levels)
    for f in range(tracers.shape[0] // pairs):
        for k, sides in enumerate(spread(beside(edge, edge_west, edge_east, f, place), levels)):
            own = tracers[f * pairs + k]
            east[f * pairs + k] = jnp.where(lane == lanes - 1, sides, lane_roll(own, -1))
            west[f * pairs + k] = jnp.where(lane == 0, sides, lane_roll(own, 1))


def next_kernel(levels, cx, edge, edge_west, edge_east, next_sides, west_x, sides_y):
    pairs = levels // 2
    fields = next_sides.shape[0] // pairs
    tile = cx.shape[1:]
    rows = tile[0] // 2
    sub, lane = iotas(tile)
    place = lane % (tile[1] // levels)

    def own_rows(slot):
        value = beside(edge, edge_west, edge_east, slot, place)
        return jnp.where(sub < rows, value, 0.0)

    edge_x = own_rows(fields)
    edge_y = own_rows(fields + 1)
    coefs = coefficients(edge_x, lane_roll(edge_x, 1), edge_y, sub_roll(edge_y, 1))
    for k, sides in enumerate(spread(edge_x, levels)):
        west_x[k] = jnp.where(lane == 0, sides, lane_roll(cx[k], 1))
    for k, sides in enumerate(spread(edge_y, levels)):
        sides_y[k] = sides
    for f in range(fields):
        raw = own_rows(f)
        moved = combine(
            coefs,
            raw,
            lane_roll(raw, -1),
            lane_roll(raw, 1),
            sub_roll(raw, -1),
            sub_roll(raw, 1),
        )
        for k, sides in enumerate(spread(moved, levels)):
            next_sides[f * pairs + k] = sides


def turned(value):
    rows = value.shape[0] // 2
    up, down = sub_roll(value, rows - 1), sub_roll(value, 1 - rows)
    return ((up, down), (down, up))


def corner_kernel(
    levels, sides_y, corner_sw, corner_se, corner_nw, corner_ne, corners, shares
):
    half = levels // 4
    tile = corner_sw.shape
    rows = tile[0] // 2
    sub, lane = iotas(tile)
    local = sub % rows
    odd_sub = sub % 2 == 1
    bottom = local == 0
    top = local == rows - 1
    even_lane = lane % 2 == 0
    dense = jnp.where(
        odd_sub,
        jnp.where(even_lane, lane_roll(corner_se[...], -1), lane_roll(corner_sw[...], 1)),
        jnp.where(even_lane, lane_roll(corner_ne[...], -1), lane_roll(corner_nw[...], 1)),
    )
    count = corners.shape[0]
    for i in range(count):
        corners[i] = lane_roll(dense, -(2 * i + 1))
    for k in range(half):
        places = turned(lane_roll(dense, -(2 * (count + k) + 1)))
        for i in range(2):
            j = 2 * k + i
            south_face = places[i][1]
            shares[j, 0] = jnp.where(bottom, jnp.minimum(south_face, 0.0), 0.0)
            shares[j, 1] = jnp.where(
                bottom,
                jnp.maximum(south_face, 0.0),
                jnp.where(top, jnp.maximum(-sides_y[j], 0.0), 0.0),
            )


def transport_and_solve(
    fields,
    levels,
    tracers,
    cx,
    cy,
    from_south,
    from_north,
    east,
    west,
    next_sides,
    west_x,
    corners,
    shares,
    decay,
    source,
    changes,
    starts,
    own_coefs,
    halo_coefs,
):
    pairs = levels // 2
    half = pairs // 2
    tile = tracers.shape[1:]
    rows = tile[0] // 2
    lanes = tile[1]
    group = lanes // levels
    sub, lane = iotas(tile)
    local = sub % rows
    low = sub < rows
    first_lane = lane == 0
    last_lane = lane == lanes - 1
    odd_sub = sub % 2 == 1
    bottom = local == 0
    top = local == rows - 1
    in_first = bottom | top


    def inner_rows(first, second):
        (first_up, first_down), _ = turned(first)
        (second_up, second_down), _ = turned(second)
        return (
            jnp.where(in_first, first_up, second_down),
            jnp.where(in_first, first_down, second_up),
        )

    base = fields * half
    count = pairs // rows
    for k in range(half):
        quad, t = 2 * k // rows, 2 * k % rows
        packed_south = from_south[base + quad]
        packed_south_y = from_south[base + count + quad]
        packed_north = from_north[base + quad]
        south_x = jnp.where(in_first, sub_roll(packed_south, t), sub_roll(packed_south, 3 + t))
        south_y = jnp.where(
            in_first, sub_roll(packed_south_y, t), sub_roll(packed_south_y, 3 + t)
        )
        north_x = jnp.where(in_first, sub_roll(packed_north, -t), sub_roll(packed_north, 5 - t))
        halo_x = jnp.where(odd_sub, south_x, north_x)
        halo_west = jnp.where(
            first_lane, corners[fields * half + k], lane_roll(halo_x, 1)
        )
        _, inner_top = inner_rows(cy[2 * k], cy[2 * k + 1])
        face = jnp.where(odd_sub, -south_y, inner_top)
        halo_coefs[k, 0] = (
            1.0
            - jnp.maximum(halo_x, 0.0)
            + jnp.minimum(halo_west, 0.0)
            + jnp.minimum(face, 0.0)
        )
        halo_coefs[k, 1] = jnp.maximum(-halo_x, 0.0)
        halo_coefs[k, 2] = jnp.maximum(halo_west, 0.0)
        halo_coefs[k, 3] = jnp.maximum(face, 0.0)
        places = turned(south_y)
        for i in range(2):
            j = 2 * k + i
            below = jnp.where(bottom, places[i][1], sub_roll(cy[j], 1))
            for c, value in enumerate(coefficients(cx[j], west_x[j], cy[j], below)):
                own_coefs[j, c] = value

    def advect(f, k, own_set, halo_set):
        message_south = from_south[f * half + k]
        message_north = from_north[f * half + k]
        slots = (f * pairs + 2 * k, f * pairs + 2 * k + 1)
        own = [tracers[slot] for slot in slots]
        own_east = [east[slot] for slot in slots]
        own_west = [west[slot] for slot in slots]
        sides = corners[f * half + k]
        halo = jnp.where(odd_sub, message_south, message_north)
        inner_bottom, inner_top = inner_rows(*own)
        flux = jnp.where(odd_sub, sub_roll(message_south, 1), sub_roll(message_north, -1))
        next_halo = (
            halo_set[0] * halo
            + (
                halo_set[1] * jnp.where(last_lane, sides, lane_roll(halo, -1))
                + halo_set[2] * jnp.where(first_lane, sides, lane_roll(halo, 1))
            )
            + (halo_set[3] * jnp.where(odd_sub, inner_bottom, inner_top) + flux)
        )
        places, next_places, side_places = turned(halo), turned(next_halo), turned(sides)
        results = []
        for i in range(2):
            north, south = places[i]
            once = combine(
                own_set[i],
                own[i],
                own_east[i],
                own_west[i],
                jnp.where(top, north, sub_roll(own[i], -1)),
                jnp.where(bottom, south, sub_roll(own[i], 1)),
            )
            side_north, side_south = side_places[i]
            next_column = (
                next_sides[slots[i]]
                + own_set[i][5] * jnp.where(first_lane, own_west[i], own_east[i])
                + own_set[i][6] * jnp.where(bottom, side_south, side_north)
            )
            north, south = next_places[i]
            results.append(
                combine(
                    own_set[i],
                    once,
                    jnp.where(last_lane, next_column, lane_roll(once, -1)),
                    jnp.where(first_lane, next_column, lane_roll(once, 1)),
                    jnp.where(top, north, sub_roll(once, -1)),
                    jnp.where(bottom, south, sub_roll(once, 1)),
                )
            )
        return results

    def transport(p):
        f1 = 2 * p
        f2 = jnp.minimum(f1 + 1, fields - 1)
        columns = []
        for k in range(half):
            own_set = [
                [own_coefs[2 * k + i, c] for c in range(5)]
                + [shares[2 * k + i, c] for c in range(2)]
                for i in range(2)
            ]
            halo_set = [halo_coefs[k, c] for c in range(4)]
            for one, two in zip(
                advect(f1, k, own_set, halo_set), advect(f2, k, own_set, halo_set)
            ):
                columns.append(jnp.where(low, one, sub_roll(two, rows)))
                columns.append(jnp.where(low, sub_roll(one, rows), two))
        return tuple(columns)

    def solve(p, columns):
        waves = cosine_sums(columns)
        change = [source[m, p] - decay[m, p] * waves[m] for m in range(levels)]
        square = change[1] * change[1]
        for m in range(2, levels):
            square = square + change[m] * change[m]
        square = (change[0] * change[0]) * float(levels) + square * (0.5 * levels)
        for m in range(levels):
            changes[m, p] = change[m]
            starts[m, p] = columns[m]
        return jnp.where(low | (2 * p + 1 < fields), square, 0.0)

    def pair_step(p, carried):
        total, columns = carried
        following = transport(p)
        return total + solve(p - 1, columns), following

    field_pairs = (fields + 1) // 2
    total, columns = lax.fori_loop(
        1, field_pairs, pair_step, (jnp.zeros(tile, F32), transport(0))
    )
    return total + solve(field_pairs - 1, columns)


def main_kernel(fields, levels, *refs):
    inputs, (target, onehot), (changes, starts, placed), coefs = (
        refs[:13],
        refs[13:15],
        refs[15:18],
        refs[18:],
    )
    rows, lanes = target.shape
    total = transport_and_solve(fields, levels, *inputs, changes, starts, *coefs)

    heat = (total + sub_roll(total, rows)) * (1.0 / (fields * levels))
    first = heat.astype(jnp.bfloat16).astype(F32)
    rest = heat - first
    second = rest.astype(jnp.bfloat16).astype(F32)
    third = rest - second
    spans = placed.shape[0]
    slot_row, _ = iotas((spans, lanes))
    high = lax.shift_right_logical(target[...], lanes.bit_length() - 1)
    hits = [slot_row == high[r : r + 1] for r in range(rows)]
    left = jnp.concatenate(
        [
            jnp.concatenate(
                [
                    jnp.where(hits[r], part[r : r + 1], 0.0).astype(jnp.bfloat16)
                    for r in range(rows)
                ],
                axis=1,
            )
            for part in (first, second, third)
        ],
        axis=0,
    )
    result = jnp.dot(left, onehot[...], preferred_element_type=F32)
    placed[...] = result[:spans] + result[spans : 2 * spans] + result[2 * spans :]


def state_kernel(fields, changes, starts, state):
    levels, field_pairs = changes.shape[:2]
    tile = changes.shape[2:]
    rows = tile[0] // 2
    pairs = levels // 2
    low = iotas(tile)[0] < rows

    def one_pair(p, carried):
        f1 = 2 * p
        f2 = jnp.minimum(f1 + 1, fields - 1)
        change = cosine_series([changes[m, p] for m in range(levels)])
        for k in range(pairs):
            even, odd = (starts[l, p] + change[l] for l in (2 * k, 2 * k + 1))
            state[f1 * pairs + k] = jnp.where(low, even, sub_roll(odd, rows))
            state[f2 * pairs + k] = jnp.where(low, sub_roll(even, rows), odd)
        return carried

    lax.fori_loop(0, field_pairs, one_pair, 0)


def finish_kernel(parts, total):
    value = parts[0]
    for i in range(1, parts.shape[0]):
        value = value + parts[i]
    total[...] = value


def body(tracers, courant_x, courant_y, physics_ref, class_coeffs, span_target, cloud_class):
    fields, levels, rows, cols = tracers.shape
    wide = lax.axis_size("wide")
    narrow = lax.axis_size("narrow")
    pairs = levels // 2
    half = pairs // 2
    tile = (2 * rows, cols)
    field_pairs = (fields + 1) // 2
    flat = tracers.reshape(fields * pairs, *tile)
    cx = courant_x.reshape(pairs, *tile)
    cy = courant_y.reshape(pairs, *tile)
    quads = pairs // rows

    def array(*shape, dtype=F32):
        return jax.ShapeDtypeStruct(shape, dtype)

    flat, cx, cy, north = pl.pallas_call(
        functools.partial(pack_north_kernel, levels),
        out_shape=(
            array(fields * pairs, *tile),
            array(pairs, *tile),
            array(pairs, *tile),
            array(fields * half + 2 * quads, *tile),
        ),
        in_specs=[HBM] * 3,
        out_specs=[VMEM] * 4,
        scratch_shapes=[pltpu.SemaphoreType.DMA((3,))],
        compiler_params=PARAMS,
    )(*(pltpu.with_memory_space_constraint(x, pltpu.HBM) for x in (flat, cx, cy)))
    edge, corner, south = pl.pallas_call(
        functools.partial(pack_edges_kernel, levels),
        out_shape=(
            array(fields + 2, *tile),
            array(*tile),
            array(fields * half + quads, *tile),
        ),
        in_specs=[VMEM] * 3,
        out_specs=[VMEM] * 3,
        compiler_params=PARAMS,
    )(flat, cx, cy)

    def send(value, up, right):
        pairs_ = []
        for w in range(wide):
            for n in range(narrow):
                to = ((w + up) % wide) * narrow + (n + right) % narrow
                pairs_.append((w * narrow + n, to))
        return lax.ppermute(value, ("wide", "narrow"), pairs_)

    def to_both_sides(value, up):
        from_west = send(value, up, 1)
        from_east = from_west if narrow == 2 else send(value, up, -1)
        return from_west, from_east

    from_south = send(north, 1, 0)
    from_north = send(south, -1, 0)
    edge_west, edge_east = to_both_sides(edge, 0)
    corner_sw, corner_se = to_both_sides(corner, 1)
    corner_nw, corner_ne = to_both_sides(corner, -1)

    decay, source, onehot = pl.pallas_call(
        prep_kernel,
        out_shape=(array(levels, field_pairs, *tile),) * 2
        + (array(rows * cols, cols, dtype=jnp.bfloat16),),
        in_specs=[SMEM, SMEM, VMEM, VMEM],
        out_specs=[VMEM] * 3,
        cost_estimate=pl.CostEstimate(flops=4000000, bytes_accessed=2000000, transcendentals=0),
        compiler_params=PARAMS,
    )(class_coeffs, physics_ref, cloud_class, span_target)

    shifted = pl.pallas_call(
        functools.partial(shift_kernel, levels),
        out_shape=(array(fields * pairs, *tile),) * 2,
        in_specs=[VMEM] * 4,
        out_specs=[VMEM] * 2,
        compiler_params=PARAMS,
    )(flat, edge, edge_west, edge_east)
    next_sides, west_x, sides_y = pl.pallas_call(
        functools.partial(next_kernel, levels),
        out_shape=(array(fields * pairs, *tile),) + (array(pairs, *tile),) * 2,
        in_specs=[VMEM] * 4,
        out_specs=[VMEM] * 3,
        compiler_params=PARAMS,
    )(cx, edge, edge_west, edge_east)
    corners, shares = pl.pallas_call(
        functools.partial(corner_kernel, levels),
        out_shape=(array((fields + 1) * half, *tile), array(pairs, 2, *tile)),
        in_specs=[VMEM] * 5,
        out_specs=[VMEM] * 2,
        compiler_params=PARAMS,
    )(sides_y, corner_sw, corner_se, corner_nw, corner_ne)
    changes, starts, placed = pl.pallas_call(
        functools.partial(main_kernel, fields, levels),
        out_shape=(
            array(levels, field_pairs, *tile),
            array(levels, field_pairs, *tile),
            pltpu.VMEM((wide * rows, cols), F32),
        ),
        in_specs=[VMEM] * 15,
        out_specs=[VMEM] * 3,
        scratch_shapes=[
            pltpu.VMEM((pairs, 5) + tile, F32),
            pltpu.VMEM((half, 4) + tile, F32),
        ],
        compiler_params=PARAMS,
    )(
        flat,
        cx,
        cy,
        from_south,
        from_north,
        *shifted,
        next_sides,
        west_x,
        corners,
        shares,
        decay,
        source,
        span_target,
        onehot,
    )
    received = lax.all_to_all(
        placed.reshape(wide, rows, cols), "wide", split_axis=0, concat_axis=0, tiled=True
    )
    state = pl.pallas_call(
        functools.partial(state_kernel, fields),
        out_shape=array(fields * pairs, *tile),
        in_specs=[VMEM] * 2,
        out_specs=VMEM,
        cost_estimate=pl.CostEstimate(flops=0, bytes_accessed=40000000, transcendentals=0),
        compiler_params=PARAMS,
    )(changes, starts)
    span_diag = pl.pallas_call(
        finish_kernel,
        out_shape=array(rows, cols),
        in_specs=[VMEM],
        out_specs=VMEM,
        compiler_params=PARAMS,
    )(received)
    return state.reshape(fields, levels, rows, cols), span_diag


def solution(mesh):
    return jax.shard_map(
        body,
        mesh=mesh,
        in_specs=(
            P(None, None, "wide", "narrow"),
            P(None, "wide", "narrow"),
            P(None, "wide", "narrow"),
            P(),
            P(),
            P("wide", "narrow"),
            P("wide", "narrow"),
        ),
        out_specs=(P(None, None, "wide", "narrow"), P("wide", "narrow")),
        check_vma=False,
    )
```

```python
import functools
import math

import jax
import jax.numpy as jnp
from jax import lax
from jax.experimental import pallas as pl
from jax.experimental.pallas import tpu as pltpu
from jax.sharding import PartitionSpec as P

VMEM = pl.BlockSpec(memory_space=pltpu.VMEM)
HBM = pl.BlockSpec(memory_space=pltpu.HBM)
SMEM = pl.BlockSpec(memory_space=pltpu.SMEM)
F32 = jnp.float32
PARAMS = pltpu.CompilerParams(vmem_limit_bytes=12 * 1024 * 1024)


def sub_roll(value, shift):
    shift = shift % value.shape[0]
    return value if shift == 0 else pltpu.roll(value, shift, 0)


def lane_roll(value, shift):
    shift = shift % value.shape[1]
    return value if shift == 0 else pltpu.roll(value, shift, 1)


def iotas(shape):
    return lax.broadcasted_iota(jnp.int32, shape, 0), lax.broadcasted_iota(jnp.int32, shape, 1)


def one_row(vectors, row, step):
    rows = vectors[0].shape[0] // 2
    local = iotas(vectors[0].shape)[0] % rows
    packed = []
    for start in range(0, len(vectors), rows):
        total = vectors[start]
        for t in range(1, rows):
            total = jnp.where(
                local == row + step * t, sub_roll(vectors[start + t], step * t), total
            )
        packed.append(total)
    return packed


def inner_flux(value, courant):
    return jnp.maximum(courant, 0.0) * value + jnp.minimum(courant, 0.0) * sub_roll(value, -1)


def northward_rows(value, courant):
    local = iotas(value.shape)[0] % (value.shape[0] // 2)
    return jnp.where(local == 2, inner_flux(value, courant), value)


def southward_rows(value, courant):
    local = iotas(value.shape)[0] % (value.shape[0] // 2)
    return jnp.where(local == 1, sub_roll(-inner_flux(value, courant), 1), value)


def pack_north_kernel(levels, tracers_in, cx_in, cy_in, tracers, cx, cy, north, semaphores):
    copies = [
        pltpu.make_async_copy(source, into, semaphores.at[i])
        for i, (source, into) in enumerate(((tracers_in, tracers), (cx_in, cx), (cy_in, cy)))
    ]
    for copy in copies:
        copy.start()
    for copy in copies:
        copy.wait()
    pairs = levels // 2
    half = pairs // 2
    tile = tracers.shape[1:]
    rows = tile[0] // 2
    upper = iotas(tile)[0] % rows >= rows // 2
    fields = tracers.shape[0] // pairs
    for f in range(fields):
        for k in range(half):
            one, two = (
                northward_rows(tracers[f * pairs + j], cy[j]) for j in (2 * k, 2 * k + 1)
            )
            north[f * half + k] = jnp.where(upper, one, sub_roll(two, 2))
    courant = one_row([cx[k] for k in range(pairs)], rows - 1, -1)
    courant += one_row([cy[k] for k in range(pairs)], rows - 1, -1)
    for k, value in enumerate(courant):
        north[fields * half + k] = value


def pack_edges_kernel(levels, tracers, cx, cy, edge, corner, south_rows):
    pairs = levels // 2
    half = pairs // 2
    fields = tracers.shape[0] // pairs
    tile = tracers.shape[1:]
    rows = tile[0] // 2
    lanes = tile[1]
    group = lanes // levels
    sub, lane = iotas(tile)
    upper = sub % rows >= rows // 2
    odd_sub = sub % 2 == 1
    corners = [jnp.zeros(tile, F32)]

    def pack_edge(vectors, slot):
        total = lane_roll(vectors[0], 2)
        for k in range(1, pairs):
            total = jnp.where(
                lane // (2 * group) == k, lane_roll(vectors[k], 2 + 2 * group * k), total
            )
        total = jnp.where(
            lane % (2 * group) < group, total, sub_roll(lane_roll(total, group), rows)
        )
        edge[slot] = jnp.where(lane % group < group // 2, total, lane_roll(total, group // 2))
        for k in range(half):
            one, two = vectors[2 * k], vectors[2 * k + 1]
            place = slot * half + k
            north = jnp.where(upper, one, sub_roll(two, 2))
            south = jnp.where(upper, sub_roll(two, -2), one)
            if slot < fields:
                first = southward_rows(one, cy[2 * k])
                second = southward_rows(two, cy[2 * k + 1])
                south_rows[place] = jnp.where(upper, sub_roll(second, -2), first)
            value = lane_roll(jnp.where(odd_sub, north, south), 2 * place + 1)
            corners[0] = jnp.where(lane // 2 == place, value, corners[0])

    for f in range(fields):
        pack_edge([tracers[f * pairs + k] for k in range(pairs)], f)
    pack_edge([cx[k] for k in range(pairs)], fields)
    pack_edge([cy[k] for k in range(pairs)], fields + 1)
    corner[...] = corners[0]
    for k, value in enumerate(one_row([cx[k] for k in range(pairs)], 0, 1)):
        south_rows[fields * half + k] = value


def cosine_sums(values):
    count = len(values)
    if count == 1:
        return values
    half = count // 2
    plus = [values[n] + values[count - 1 - n] for n in range(half)]
    minus = [
        (values[n] - values[count - 1 - n])
        * (0.5 / math.cos(math.pi * (2 * n + 1) / (2 * count)))
        for n in range(half)
    ]
    even = cosine_sums(plus)
    odd = cosine_sums(minus)
    result = []
    for k in range(half):
        result.append(even[k])
        result.append(odd[k] + odd[k + 1] if k + 1 < half else odd[k])
    return result


def cosine_series(values):
    count = len(values)
    if count == 1:
        return values
    half = count // 2
    odd_in = [values[2 * k + 1] + values[2 * k - 1] if k else values[1] for k in range(half)]
    even = cosine_series(values[0::2])
    odd = cosine_series(odd_in)
    odd = [
        odd[n] * (0.5 / math.cos(math.pi * (2 * n + 1) / (2 * count))) for n in range(half)
    ]
    return [even[n] + odd[n] for n in range(half)] + [
        even[n] - odd[n] for n in range(half - 1, -1, -1)
    ]


def prep_kernel(coeffs, profile, klass, target, decay, source, onehot):
    levels, pairs = decay.shape[:2]
    fields = profile.shape[0]
    tile = decay.shape[2:]
    rows, lanes = klass.shape
    sub, lane = iotas(tile)
    low = sub < rows
    kind = jnp.concatenate([klass[...], klass[...]], axis=0)
    is_two = kind == 2
    is_one = kind == 1

    def by_class(which, f):
        return jnp.where(
            is_two,
            coeffs[which, 2, f] * 0.25,
            jnp.where(is_one, coeffs[which, 1, f] * 0.5, coeffs[which, 0, f]),
        )

    for p in range(pairs):
        f1 = 2 * p
        f2 = min(2 * p + 1, fields - 1)
        diffusion = jnp.where(low, by_class(0, f1), by_class(0, f2))
        relax = jnp.where(low, by_class(1, f1), by_class(1, f2))
        waves = cosine_sums([jnp.where(low, profile[f1, l], profile[f2, l]) for l in range(levels)])
        for m in range(levels):
            rate = relax + diffusion * (2.0 - 2.0 * math.cos(math.pi * m / levels))
            once = 1.0 / (1.0 + rate)
            square = once * once
            twice = once + square
            steps = jnp.where(is_two, twice + twice * square, jnp.where(is_one, twice, once))
            steps = steps * ((1.0 if m == 0 else 2.0) / levels)
            decay[m, p] = steps * rate
            source[m, p] = steps * relax * waves[m]
    low_part = target[...] & (lanes - 1)
    slot, _ = iotas((lanes, lanes))
    for r in range(rows):
        hit = jnp.where(slot == low_part[r : r + 1], 1.0, 0.0)
        onehot[r * lanes : (r + 1) * lanes, :] = jnp.transpose(hit).astype(jnp.bfloat16)


def combine(coefs, center, east, west, north, south):
    return (
        coefs[0] * center
        + (coefs[1] * east + coefs[2] * west)
        + (coefs[3] * north + coefs[4] * south)
    )


def coefficients(here_x, west_x, here_y, south_y):
    return (
        1.0
        - jnp.maximum(here_x, 0.0)
        + jnp.minimum(west_x, 0.0)
        - jnp.maximum(here_y, 0.0)
        + jnp.minimum(south_y, 0.0),
        jnp.maximum(-here_x, 0.0),
        jnp.maximum(west_x, 0.0),
        jnp.maximum(-here_y, 0.0),
        jnp.maximum(south_y, 0.0),
    )


def side_by_side(value, place):
    return jnp.where(place == 3, lane_roll(value, -2), value)


def beside(edge, edge_west, edge_east, slot, place):
    from_east = (place == 2) | (place == 3)
    from_west = (place == 4) | (place == 5)
    return jnp.where(
        from_east, edge_east[slot], jnp.where(from_west, edge_west[slot], edge[slot])
    )


def spread(value, levels):
    lanes = value.shape[1]
    rows = value.shape[0] // 2
    group = lanes // levels
    sub, lane = iotas(value.shape)
    value = side_by_side(value, lane % group)
    value = jnp.where(sub < rows, value, sub_roll(lane_roll(value, -group), rows))
    return [lane_roll(value, -(2 * group * k + 3)) for k in range(levels // 2)]


def shift_kernel(levels, tracers, edge, edge_west, edge_east, east, west):
    pairs = levels // 2
    tile = tracers.shape[1:]
    lanes = tile[1]
    lane = iotas(tile)[1]
    place = lane % (lanes // levels)
    for f in range(tracers.shape[0] // pairs):
        for k, sides in enumerate(spread(beside(edge, edge_west, edge_east, f, place), levels)):
            own = tracers[f * pairs + k]
            east[f * pairs + k] = jnp.where(lane == lanes - 1, sides, lane_roll(own, -1))
            west[f * pairs + k] = jnp.where(lane == 0, sides, lane_roll(own, 1))


def next_kernel(levels, cx, edge, edge_west, edge_east, next_sides, west_x, sides_y):
    pairs = levels // 2
    fields = next_sides.shape[0] // pairs
    tile = cx.shape[1:]
    rows = tile[0] // 2
    sub, lane = iotas(tile)
    place = lane % (tile[1] // levels)

    def own_rows(slot):
        value = beside(edge, edge_west, edge_east, slot, place)
        return jnp.where(sub < rows, value, 0.0)

    edge_x = own_rows(fields)
    edge_y = own_rows(fields + 1)
    coefs = coefficients(edge_x, lane_roll(edge_x, 1), edge_y, sub_roll(edge_y, 1))
    for k, sides in enumerate(spread(edge_x, levels)):
        west_x[k] = jnp.where(lane == 0, sides, lane_roll(cx[k], 1))
    for k, sides in enumerate(spread(edge_y, levels)):
        sides_y[k] = sides
    for f in range(fields):
        raw = own_rows(f)
        moved = combine(
            coefs,
            raw,
            lane_roll(raw, -1),
            lane_roll(raw, 1),
            sub_roll(raw, -1),
            sub_roll(raw, 1),
        )
        for k, sides in enumerate(spread(moved, levels)):
            next_sides[f * pairs + k] = sides


def turned(value):
    rows = value.shape[0] // 2
    up, down = sub_roll(value, rows - 1), sub_roll(value, 1 - rows)
    return ((up, down), (down, up))


def corner_kernel(
    levels, sides_y, corner_sw, corner_se, corner_nw, corner_ne, corners, shares
):
    half = levels // 4
    tile = corner_sw.shape
    rows = tile[0] // 2
    sub, lane = iotas(tile)
    local = sub % rows
    odd_sub = sub % 2 == 1
    bottom = local == 0
    top = local == rows - 1
    even_lane = lane % 2 == 0
    dense = jnp.where(
        odd_sub,
        jnp.where(even_lane, lane_roll(corner_se[...], -1), lane_roll(corner_sw[...], 1)),
        jnp.where(even_lane, lane_roll(corner_ne[...], -1), lane_roll(corner_nw[...], 1)),
    )
    count = corners.shape[0]
    for i in range(count):
        corners[i] = lane_roll(dense, -(2 * i + 1))
    for k in range(half):
        places = turned(lane_roll(dense, -(2 * (count + k) + 1)))
        for i in range(2):
            j = 2 * k + i
            south_face = places[i][1]
            shares[j, 0] = jnp.where(bottom, jnp.minimum(south_face, 0.0), 0.0)
            shares[j, 1] = jnp.where(
                bottom,
                jnp.maximum(south_face, 0.0),
                jnp.where(top, jnp.maximum(-sides_y[j], 0.0), 0.0),
            )


def transport_and_solve(
    fields,
    levels,
    tracers,
    cx,
    cy,
    from_south,
    from_north,
    east,
    west,
    next_sides,
    west_x,
    corners,
    shares,
    decay,
    source,
    state,
    own_coefs,
    halo_coefs,
):
    pairs = levels // 2
    half = pairs // 2
    tile = tracers.shape[1:]
    rows = tile[0] // 2
    lanes = tile[1]
    group = lanes // levels
    sub, lane = iotas(tile)
    local = sub % rows
    low = sub < rows
    first_lane = lane == 0
    last_lane = lane == lanes - 1
    odd_sub = sub % 2 == 1
    bottom = local == 0
    top = local == rows - 1
    in_first = bottom | top


    def inner_rows(first, second):
        (first_up, first_down), _ = turned(first)
        (second_up, second_down), _ = turned(second)
        return (
            jnp.where(in_first, first_up, second_down),
            jnp.where(in_first, first_down, second_up),
        )

    base = fields * half
    count = pairs // rows
    for k in range(half):
        quad, t = 2 * k // rows, 2 * k % rows
        packed_south = from_south[base + quad]
        packed_south_y = from_south[base + count + quad]
        packed_north = from_north[base + quad]
        south_x = jnp.where(in_first, sub_roll(packed_south, t), sub_roll(packed_south, 3 + t))
        south_y = jnp.where(
            in_first, sub_roll(packed_south_y, t), sub_roll(packed_south_y, 3 + t)
        )
        north_x = jnp.where(in_first, sub_roll(packed_north, -t), sub_roll(packed_north, 5 - t))
        halo_x = jnp.where(odd_sub, south_x, north_x)
        halo_west = jnp.where(
            first_lane, corners[fields * half + k], lane_roll(halo_x, 1)
        )
        _, inner_top = inner_rows(cy[2 * k], cy[2 * k + 1])
        face = jnp.where(odd_sub, -south_y, inner_top)
        halo_coefs[k, 0] = (
            1.0
            - jnp.maximum(halo_x, 0.0)
            + jnp.minimum(halo_west, 0.0)
            + jnp.minimum(face, 0.0)
        )
        halo_coefs[k, 1] = jnp.maximum(-halo_x, 0.0)
        halo_coefs[k, 2] = jnp.maximum(halo_west, 0.0)
        halo_coefs[k, 3] = jnp.maximum(face, 0.0)
        places = turned(south_y)
        for i in range(2):
            j = 2 * k + i
            below = jnp.where(bottom, places[i][1], sub_roll(cy[j], 1))
            for c, value in enumerate(coefficients(cx[j], west_x[j], cy[j], below)):
                own_coefs[j, c] = value

    def advect(f, k, own_set, halo_set):
        message_south = from_south[f * half + k]
        message_north = from_north[f * half + k]
        slots = (f * pairs + 2 * k, f * pairs + 2 * k + 1)
        own = [tracers[slot] for slot in slots]
        own_east = [east[slot] for slot in slots]
        own_west = [west[slot] for slot in slots]
        sides = corners[f * half + k]
        halo = jnp.where(odd_sub, message_south, message_north)
        inner_bottom, inner_top = inner_rows(*own)
        flux = jnp.where(odd_sub, sub_roll(message_south, 1), sub_roll(message_north, -1))
        next_halo = (
            halo_set[0] * halo
            + (
                halo_set[1] * jnp.where(last_lane, sides, lane_roll(halo, -1))
                + halo_set[2] * jnp.where(first_lane, sides, lane_roll(halo, 1))
            )
            + (halo_set[3] * jnp.where(odd_sub, inner_bottom, inner_top) + flux)
        )
        places, next_places, side_places = turned(halo), turned(next_halo), turned(sides)
        results = []
        for i in range(2):
            north, south = places[i]
            once = combine(
                own_set[i],
                own[i],
                own_east[i],
                own_west[i],
                jnp.where(top, north, sub_roll(own[i], -1)),
                jnp.where(bottom, south, sub_roll(own[i], 1)),
            )
            side_north, side_south = side_places[i]
            next_column = (
                next_sides[slots[i]]
                + own_set[i][5] * jnp.where(first_lane, own_west[i], own_east[i])
                + own_set[i][6] * jnp.where(bottom, side_south, side_north)
            )
            north, south = next_places[i]
            results.append(
                combine(
                    own_set[i],
                    once,
                    jnp.where(last_lane, next_column, lane_roll(once, -1)),
                    jnp.where(first_lane, next_column, lane_roll(once, 1)),
                    jnp.where(top, north, sub_roll(once, -1)),
                    jnp.where(bottom, south, sub_roll(once, 1)),
                )
            )
        return results

    def transport(p):
        f1 = 2 * p
        f2 = jnp.minimum(f1 + 1, fields - 1)
        columns = []
        for k in range(half):
            own_set = [
                [own_coefs[2 * k + i, c] for c in range(5)]
                + [shares[2 * k + i, c] for c in range(2)]
                for i in range(2)
            ]
            halo_set = [halo_coefs[k, c] for c in range(4)]
            for one, two in zip(
                advect(f1, k, own_set, halo_set), advect(f2, k, own_set, halo_set)
            ):
                columns.append(jnp.where(low, one, sub_roll(two, rows)))
                columns.append(jnp.where(low, sub_roll(one, rows), two))
        return tuple(columns)

    def solve(p, columns):
        f1 = 2 * p
        f2 = jnp.minimum(f1 + 1, fields - 1)
        waves = cosine_sums(columns)
        change = cosine_series([source[m, p] - decay[m, p] * waves[m] for m in range(levels)])
        square = change[0] * change[0]
        for l in range(1, levels):
            square = square + change[l] * change[l]
        for k in range(pairs):
            even, odd = (columns[l] + change[l] for l in (2 * k, 2 * k + 1))
            state[f1 * pairs + k] = jnp.where(low, even, sub_roll(odd, rows))
            state[f2 * pairs + k] = jnp.where(low, sub_roll(even, rows), odd)
        return jnp.where(low | (f1 + 1 < fields), square, 0.0)

    def pair_step(p, carried):
        total, columns = carried
        following = transport(p)
        return total + solve(p - 1, columns), following

    field_pairs = (fields + 1) // 2
    total, columns = lax.fori_loop(
        1, field_pairs, pair_step, (jnp.zeros(tile, F32), transport(0)), unroll=2
    )
    return total + solve(field_pairs - 1, columns)


def main_kernel(fields, levels, *refs):
    inputs, (target, onehot), (state, placed), coefs = refs[:13], refs[13:15], refs[15:17], refs[17:]
    rows, lanes = target.shape
    total = transport_and_solve(fields, levels, *inputs, state, *coefs)

    heat = (total + sub_roll(total, rows)) * (1.0 / (fields * levels))
    first = heat.astype(jnp.bfloat16).astype(F32)
    rest = heat - first
    second = rest.astype(jnp.bfloat16).astype(F32)
    third = rest - second
    spans = placed.shape[0]
    slot_row, _ = iotas((spans, lanes))
    high = lax.shift_right_logical(target[...], lanes.bit_length() - 1)
    hits = [slot_row == high[r : r + 1] for r in range(rows)]
    left = jnp.concatenate(
        [
            jnp.concatenate(
                [
                    jnp.where(hits[r], part[r : r + 1], 0.0).astype(jnp.bfloat16)
                    for r in range(rows)
                ],
                axis=1,
            )
            for part in (first, second, third)
        ],
        axis=0,
    )
    result = jnp.dot(left, onehot[...], preferred_element_type=F32)
    placed[...] = result[:spans] + result[spans : 2 * spans] + result[2 * spans :]


def finish_kernel(parts, state, total_out, state_out, total, semaphores):
    copy_state = pltpu.make_async_copy(state, state_out, semaphores.at[0])
    copy_state.start()
    value = parts[0]
    for i in range(1, parts.shape[0]):
        value = value + parts[i]
    total[...] = value
    copy_total = pltpu.make_async_copy(total, total_out, semaphores.at[1])
    copy_total.start()
    copy_state.wait()
    copy_total.wait()


def body(tracers, courant_x, courant_y, physics_ref, class_coeffs, span_target, cloud_class):
    fields, levels, rows, cols = tracers.shape
    wide = lax.axis_size("wide")
    narrow = lax.axis_size("narrow")
    pairs = levels // 2
    half = pairs // 2
    tile = (2 * rows, cols)
    field_pairs = (fields + 1) // 2
    flat = tracers.reshape(fields * pairs, *tile)
    cx = courant_x.reshape(pairs, *tile)
    cy = courant_y.reshape(pairs, *tile)
    quads = pairs // rows

    def array(*shape, dtype=F32):
        return jax.ShapeDtypeStruct(shape, dtype)

    flat, cx, cy, north = pl.pallas_call(
        functools.partial(pack_north_kernel, levels),
        out_shape=(
            array(fields * pairs, *tile),
            array(pairs, *tile),
            array(pairs, *tile),
            array(fields * half + 2 * quads, *tile),
        ),
        in_specs=[HBM] * 3,
        out_specs=[VMEM] * 4,
        scratch_shapes=[pltpu.SemaphoreType.DMA((3,))],
        compiler_params=PARAMS,
    )(*(pltpu.with_memory_space_constraint(x, pltpu.HBM) for x in (flat, cx, cy)))
    edge, corner, south = pl.pallas_call(
        functools.partial(pack_edges_kernel, levels),
        out_shape=(
            array(fields + 2, *tile),
            array(*tile),
            array(fields * half + quads, *tile),
        ),
        in_specs=[VMEM] * 3,
        out_specs=[VMEM] * 3,
        compiler_params=PARAMS,
    )(flat, cx, cy)

    def send(value, up, right):
        pairs_ = []
        for w in range(wide):
            for n in range(narrow):
                to = ((w + up) % wide) * narrow + (n + right) % narrow
                pairs_.append((w * narrow + n, to))
        return lax.ppermute(value, ("wide", "narrow"), pairs_)

    def to_both_sides(value, up):
        from_west = send(value, up, 1)
        from_east = from_west if narrow == 2 else send(value, up, -1)
        return from_west, from_east

    from_south = send(north, 1, 0)
    from_north = send(south, -1, 0)
    edge_west, edge_east = to_both_sides(edge, 0)
    corner_sw, corner_se = to_both_sides(corner, 1)
    corner_nw, corner_ne = to_both_sides(corner, -1)

    decay, source, onehot = pl.pallas_call(
        prep_kernel,
        out_shape=(array(levels, field_pairs, *tile),) * 2
        + (array(rows * cols, cols, dtype=jnp.bfloat16),),
        in_specs=[SMEM, SMEM, VMEM, VMEM],
        out_specs=[VMEM] * 3,
        cost_estimate=pl.CostEstimate(flops=4000000, bytes_accessed=2000000, transcendentals=0),
        compiler_params=PARAMS,
    )(class_coeffs, physics_ref, cloud_class, span_target)

    shifted = pl.pallas_call(
        functools.partial(shift_kernel, levels),
        out_shape=(array(fields * pairs, *tile),) * 2,
        in_specs=[VMEM] * 4,
        out_specs=[VMEM] * 2,
        compiler_params=PARAMS,
    )(flat, edge, edge_west, edge_east)
    next_sides, west_x, sides_y = pl.pallas_call(
        functools.partial(next_kernel, levels),
        out_shape=(array(fields * pairs, *tile),) + (array(pairs, *tile),) * 2,
        in_specs=[VMEM] * 4,
        out_specs=[VMEM] * 3,
        compiler_params=PARAMS,
    )(cx, edge, edge_west, edge_east)
    corners, shares = pl.pallas_call(
        functools.partial(corner_kernel, levels),
        out_shape=(array((fields + 1) * half, *tile), array(pairs, 2, *tile)),
        in_specs=[VMEM] * 5,
        out_specs=[VMEM] * 2,
        compiler_params=PARAMS,
    )(sides_y, corner_sw, corner_se, corner_nw, corner_ne)
    state, placed = pl.pallas_call(
        functools.partial(main_kernel, fields, levels),
        out_shape=(array(fields * pairs, *tile), array(wide * rows, cols)),
        in_specs=[VMEM] * 15,
        out_specs=[VMEM] * 2,
        scratch_shapes=[
            pltpu.VMEM((pairs, 5) + tile, F32),
            pltpu.VMEM((half, 4) + tile, F32),
        ],
        compiler_params=PARAMS,
    )(
        flat,
        cx,
        cy,
        from_south,
        from_north,
        *shifted,
        next_sides,
        west_x,
        corners,
        shares,
        decay,
        source,
        span_target,
        onehot,
    )
    received = lax.all_to_all(
        placed.reshape(wide, rows, cols), "wide", split_axis=0, concat_axis=0, tiled=True
    )
    span_diag, state = pl.pallas_call(
        finish_kernel,
        out_shape=(array(rows, cols), array(fields * pairs, *tile)),
        in_specs=[VMEM] * 2,
        out_specs=[HBM] * 2,
        scratch_shapes=[pltpu.VMEM((rows, cols), F32), pltpu.SemaphoreType.DMA((2,))],
        compiler_params=PARAMS,
    )(received, state)
    return state.reshape(fields, levels, rows, cols), span_diag


def solution(mesh):
    return jax.shard_map(
        body,
        mesh=mesh,
        in_specs=(
            P(None, None, "wide", "narrow"),
            P(None, "wide", "narrow"),
            P(None, "wide", "narrow"),
            P(),
            P(),
            P("wide", "narrow"),
            P("wide", "narrow"),
        ),
        out_specs=(P(None, None, "wide", "narrow"), P("wide", "narrow")),
        check_vma=False,
    )
```

```python
import functools
import math

import jax
import jax.numpy as jnp
from jax import lax
from jax.experimental import pallas as pl
from jax.experimental.pallas import tpu as pltpu
from jax.sharding import PartitionSpec as P

VMEM = pl.BlockSpec(memory_space=pltpu.VMEM)
HBM = pl.BlockSpec(memory_space=pltpu.HBM)
SMEM = pl.BlockSpec(memory_space=pltpu.SMEM)
F32 = jnp.float32
PARAMS = pltpu.CompilerParams(vmem_limit_bytes=12 * 1024 * 1024)


def sub_roll(value, shift):
    shift = shift % value.shape[0]
    return value if shift == 0 else pltpu.roll(value, shift, 0)


def lane_roll(value, shift):
    shift = shift % value.shape[1]
    return value if shift == 0 else pltpu.roll(value, shift, 1)


def iotas(shape):
    return lax.broadcasted_iota(jnp.int32, shape, 0), lax.broadcasted_iota(jnp.int32, shape, 1)


def one_row(vectors, row, step):
    rows = vectors[0].shape[0] // 2
    local = iotas(vectors[0].shape)[0] % rows
    packed = []
    for start in range(0, len(vectors), rows):
        total = vectors[start]
        for t in range(1, rows):
            total = jnp.where(
                local == row + step * t, sub_roll(vectors[start + t], step * t), total
            )
        packed.append(total)
    return packed


def inner_flux(value, courant):
    return jnp.maximum(courant, 0.0) * value + jnp.minimum(courant, 0.0) * sub_roll(value, -1)


def northward_rows(value, courant):
    local = iotas(value.shape)[0] % (value.shape[0] // 2)
    return jnp.where(local == 2, inner_flux(value, courant), value)


def southward_rows(value, courant):
    local = iotas(value.shape)[0] % (value.shape[0] // 2)
    return jnp.where(local == 1, sub_roll(-inner_flux(value, courant), 1), value)


def pack_north_kernel(levels, tracers_in, cx_in, cy_in, tracers, cx, cy, north, semaphores):
    copies = [
        pltpu.make_async_copy(source, into, semaphores.at[i])
        for i, (source, into) in enumerate(((tracers_in, tracers), (cx_in, cx), (cy_in, cy)))
    ]
    for copy in copies:
        copy.start()
    for copy in copies:
        copy.wait()
    pairs = levels // 2
    half = pairs // 2
    tile = tracers.shape[1:]
    rows = tile[0] // 2
    upper = iotas(tile)[0] % rows >= rows // 2
    fields = tracers.shape[0] // pairs
    for f in range(fields):
        for k in range(half):
            one, two = (
                northward_rows(tracers[f * pairs + j], cy[j]) for j in (2 * k, 2 * k + 1)
            )
            north[f * half + k] = jnp.where(upper, one, sub_roll(two, 2))
    courant = one_row([cx[k] for k in range(pairs)], rows - 1, -1)
    courant += one_row([cy[k] for k in range(pairs)], rows - 1, -1)
    for k, value in enumerate(courant):
        north[fields * half + k] = value


def pack_edges_kernel(levels, tracers, cx, cy, edge, corner, south_rows):
    pairs = levels // 2
    half = pairs // 2
    fields = tracers.shape[0] // pairs
    tile = tracers.shape[1:]
    rows = tile[0] // 2
    lanes = tile[1]
    group = lanes // levels
    sub, lane = iotas(tile)
    upper = sub % rows >= rows // 2
    odd_sub = sub % 2 == 1
    corners = [jnp.zeros(tile, F32)]

    def pack_edge(vectors, slot):
        total = lane_roll(vectors[0], 2)
        for k in range(1, pairs):
            total = jnp.where(
                lane // (2 * group) == k, lane_roll(vectors[k], 2 + 2 * group * k), total
            )
        total = jnp.where(
            lane % (2 * group) < group, total, sub_roll(lane_roll(total, group), rows)
        )
        edge[slot] = jnp.where(lane % group < group // 2, total, lane_roll(total, group // 2))
        for k in range(half):
            one, two = vectors[2 * k], vectors[2 * k + 1]
            place = slot * half + k
            north = jnp.where(upper, one, sub_roll(two, 2))
            south = jnp.where(upper, sub_roll(two, -2), one)
            if slot < fields:
                first = southward_rows(one, cy[2 * k])
                second = southward_rows(two, cy[2 * k + 1])
                south_rows[place] = jnp.where(upper, sub_roll(second, -2), first)
            value = lane_roll(jnp.where(odd_sub, north, south), 2 * place + 1)
            corners[0] = jnp.where(lane // 2 == place, value, corners[0])

    for f in range(fields):
        pack_edge([tracers[f * pairs + k] for k in range(pairs)], f)
    pack_edge([cx[k] for k in range(pairs)], fields)
    pack_edge([cy[k] for k in range(pairs)], fields + 1)
    corner[...] = corners[0]
    for k, value in enumerate(one_row([cx[k] for k in range(pairs)], 0, 1)):
        south_rows[fields * half + k] = value


def cosine_sums(values):
    count = len(values)
    if count == 1:
        return values
    half = count // 2
    plus = [values[n] + values[count - 1 - n] for n in range(half)]
    minus = [
        (values[n] - values[count - 1 - n])
        * (0.5 / math.cos(math.pi * (2 * n + 1) / (2 * count)))
        for n in range(half)
    ]
    even = cosine_sums(plus)
    odd = cosine_sums(minus)
    result = []
    for k in range(half):
        result.append(even[k])
        result.append(odd[k] + odd[k + 1] if k + 1 < half else odd[k])
    return result


def cosine_series(values):
    count = len(values)
    if count == 1:
        return values
    half = count // 2
    odd_in = [values[2 * k + 1] + values[2 * k - 1] if k else values[1] for k in range(half)]
    even = cosine_series(values[0::2])
    odd = cosine_series(odd_in)
    odd = [
        odd[n] * (0.5 / math.cos(math.pi * (2 * n + 1) / (2 * count))) for n in range(half)
    ]
    return [even[n] + odd[n] for n in range(half)] + [
        even[n] - odd[n] for n in range(half - 1, -1, -1)
    ]


def prep_kernel(coeffs, profile, klass, target, decay, source, onehot):
    levels, pairs = decay.shape[:2]
    fields = profile.shape[0]
    tile = decay.shape[2:]
    rows, lanes = klass.shape
    sub, lane = iotas(tile)
    low = sub < rows
    kind = jnp.concatenate([klass[...], klass[...]], axis=0)
    is_two = kind == 2
    is_one = kind == 1

    def by_class(which, f):
        return jnp.where(
            is_two,
            coeffs[which, 2, f] * 0.25,
            jnp.where(is_one, coeffs[which, 1, f] * 0.5, coeffs[which, 0, f]),
        )

    for p in range(pairs):
        f1 = 2 * p
        f2 = min(2 * p + 1, fields - 1)
        diffusion = jnp.where(low, by_class(0, f1), by_class(0, f2))
        relax = jnp.where(low, by_class(1, f1), by_class(1, f2))
        waves = cosine_sums([jnp.where(low, profile[f1, l], profile[f2, l]) for l in range(levels)])
        for m in range(levels):
            rate = relax + diffusion * (2.0 - 2.0 * math.cos(math.pi * m / levels))
            once = 1.0 / (1.0 + rate)
            square = once * once
            twice = once + square
            steps = jnp.where(is_two, twice + twice * square, jnp.where(is_one, twice, once))
            steps = steps * ((1.0 if m == 0 else 2.0) / levels)
            decay[m, p] = steps * rate
            source[m, p] = steps * relax * waves[m]
    low_part = target[...] & (lanes - 1)
    slot, _ = iotas((lanes, lanes))
    for r in range(rows):
        hit = jnp.where(slot == low_part[r : r + 1], 1.0, 0.0)
        onehot[r * lanes : (r + 1) * lanes, :] = jnp.transpose(hit).astype(jnp.bfloat16)


def combine(coefs, center, east, west, north, south):
    return (
        coefs[0] * center
        + (coefs[1] * east + coefs[2] * west)
        + (coefs[3] * north + coefs[4] * south)
    )


def coefficients(here_x, west_x, here_y, south_y):
    return (
        1.0
        - jnp.maximum(here_x, 0.0)
        + jnp.minimum(west_x, 0.0)
        - jnp.maximum(here_y, 0.0)
        + jnp.minimum(south_y, 0.0),
        jnp.maximum(-here_x, 0.0),
        jnp.maximum(west_x, 0.0),
        jnp.maximum(-here_y, 0.0),
        jnp.maximum(south_y, 0.0),
    )


def side_by_side(value, place):
    return jnp.where(place == 3, lane_roll(value, -2), value)


def beside(edge, edge_west, edge_east, slot, place):
    from_east = (place == 2) | (place == 3)
    from_west = (place == 4) | (place == 5)
    return jnp.where(
        from_east, edge_east[slot], jnp.where(from_west, edge_west[slot], edge[slot])
    )


def spread(value, levels):
    lanes = value.shape[1]
    rows = value.shape[0] // 2
    group = lanes // levels
    sub, lane = iotas(value.shape)
    value = side_by_side(value, lane % group)
    value = jnp.where(sub < rows, value, sub_roll(lane_roll(value, -group), rows))
    return [lane_roll(value, -(2 * group * k + 3)) for k in range(levels // 2)]


def shift_kernel(levels, tracers, edge, edge_west, edge_east, east, west):
    pairs = levels // 2
    tile = tracers.shape[1:]
    lanes = tile[1]
    lane = iotas(tile)[1]
    place = lane % (lanes // levels)
    for f in range(tracers.shape[0] // pairs):
        for k, sides in enumerate(spread(beside(edge, edge_west, edge_east, f, place), levels)):
            own = tracers[f * pairs + k]
            east[f * pairs + k] = jnp.where(lane == lanes - 1, sides, lane_roll(own, -1))
            west[f * pairs + k] = jnp.where(lane == 0, sides, lane_roll(own, 1))


def next_kernel(levels, cx, edge, edge_west, edge_east, next_sides, west_x, sides_y):
    pairs = levels // 2
    fields = next_sides.shape[0] // pairs
    tile = cx.shape[1:]
    rows = tile[0] // 2
    sub, lane = iotas(tile)
    place = lane % (tile[1] // levels)

    def own_rows(slot):
        value = beside(edge, edge_west, edge_east, slot, place)
        return jnp.where(sub < rows, value, 0.0)

    edge_x = own_rows(fields)
    edge_y = own_rows(fields + 1)
    coefs = coefficients(edge_x, lane_roll(edge_x, 1), edge_y, sub_roll(edge_y, 1))
    for k, sides in enumerate(spread(edge_x, levels)):
        west_x[k] = jnp.where(lane == 0, sides, lane_roll(cx[k], 1))
    for k, sides in enumerate(spread(edge_y, levels)):
        sides_y[k] = sides
    for f in range(fields):
        raw = own_rows(f)
        moved = combine(
            coefs,
            raw,
            lane_roll(raw, -1),
            lane_roll(raw, 1),
            sub_roll(raw, -1),
            sub_roll(raw, 1),
        )
        for k, sides in enumerate(spread(moved, levels)):
            next_sides[f * pairs + k] = sides


def turned(value):
    rows = value.shape[0] // 2
    up, down = sub_roll(value, rows - 1), sub_roll(value, 1 - rows)
    return ((up, down), (down, up))


def corner_kernel(
    levels, sides_y, corner_sw, corner_se, corner_nw, corner_ne, corners, shares
):
    half = levels // 4
    tile = corner_sw.shape
    rows = tile[0] // 2
    sub, lane = iotas(tile)
    local = sub % rows
    odd_sub = sub % 2 == 1
    bottom = local == 0
    top = local == rows - 1
    even_lane = lane % 2 == 0
    dense = jnp.where(
        odd_sub,
        jnp.where(even_lane, lane_roll(corner_se[...], -1), lane_roll(corner_sw[...], 1)),
        jnp.where(even_lane, lane_roll(corner_ne[...], -1), lane_roll(corner_nw[...], 1)),
    )
    count = corners.shape[0]
    for i in range(count):
        corners[i] = lane_roll(dense, -(2 * i + 1))
    for k in range(half):
        places = turned(lane_roll(dense, -(2 * (count + k) + 1)))
        for i in range(2):
            j = 2 * k + i
            south_face = places[i][1]
            shares[j, 0] = jnp.where(bottom, jnp.minimum(south_face, 0.0), 0.0)
            shares[j, 1] = jnp.where(
                bottom,
                jnp.maximum(south_face, 0.0),
                jnp.where(top, jnp.maximum(-sides_y[j], 0.0), 0.0),
            )


def transport_and_solve(
    fields,
    levels,
    tracers,
    cx,
    cy,
    from_south,
    from_north,
    east,
    west,
    next_sides,
    west_x,
    corners,
    shares,
    decay,
    source,
    state,
    own_coefs,
    halo_coefs,
):
    pairs = levels // 2
    half = pairs // 2
    tile = tracers.shape[1:]
    rows = tile[0] // 2
    lanes = tile[1]
    group = lanes // levels
    sub, lane = iotas(tile)
    local = sub % rows
    low = sub < rows
    first_lane = lane == 0
    last_lane = lane == lanes - 1
    odd_sub = sub % 2 == 1
    bottom = local == 0
    top = local == rows - 1
    in_first = bottom | top


    def inner_rows(first, second):
        (first_up, first_down), _ = turned(first)
        (second_up, second_down), _ = turned(second)
        return (
            jnp.where(in_first, first_up, second_down),
            jnp.where(in_first, first_down, second_up),
        )

    base = fields * half
    count = pairs // rows
    for k in range(half):
        quad, t = 2 * k // rows, 2 * k % rows
        packed_south = from_south[base + quad]
        packed_south_y = from_south[base + count + quad]
        packed_north = from_north[base + quad]
        south_x = jnp.where(in_first, sub_roll(packed_south, t), sub_roll(packed_south, 3 + t))
        south_y = jnp.where(
            in_first, sub_roll(packed_south_y, t), sub_roll(packed_south_y, 3 + t)
        )
        north_x = jnp.where(in_first, sub_roll(packed_north, -t), sub_roll(packed_north, 5 - t))
        halo_x = jnp.where(odd_sub, south_x, north_x)
        halo_west = jnp.where(
            first_lane, corners[fields * half + k], lane_roll(halo_x, 1)
        )
        _, inner_top = inner_rows(cy[2 * k], cy[2 * k + 1])
        face = jnp.where(odd_sub, -south_y, inner_top)
        halo_coefs[k, 0] = (
            1.0
            - jnp.maximum(halo_x, 0.0)
            + jnp.minimum(halo_west, 0.0)
            + jnp.minimum(face, 0.0)
        )
        halo_coefs[k, 1] = jnp.maximum(-halo_x, 0.0)
        halo_coefs[k, 2] = jnp.maximum(halo_west, 0.0)
        halo_coefs[k, 3] = jnp.maximum(face, 0.0)
        places = turned(south_y)
        for i in range(2):
            j = 2 * k + i
            below = jnp.where(bottom, places[i][1], sub_roll(cy[j], 1))
            for c, value in enumerate(coefficients(cx[j], west_x[j], cy[j], below)):
                own_coefs[j, c] = value

    def advect(f, k, own_set, halo_set):
        message_south = from_south[f * half + k]
        message_north = from_north[f * half + k]
        slots = (f * pairs + 2 * k, f * pairs + 2 * k + 1)
        own = [tracers[slot] for slot in slots]
        own_east = [east[slot] for slot in slots]
        own_west = [west[slot] for slot in slots]
        sides = corners[f * half + k]
        halo = jnp.where(odd_sub, message_south, message_north)
        inner_bottom, inner_top = inner_rows(*own)
        flux = jnp.where(odd_sub, sub_roll(message_south, 1), sub_roll(message_north, -1))
        next_halo = (
            halo_set[0] * halo
            + (
                halo_set[1] * jnp.where(last_lane, sides, lane_roll(halo, -1))
                + halo_set[2] * jnp.where(first_lane, sides, lane_roll(halo, 1))
            )
            + (halo_set[3] * jnp.where(odd_sub, inner_bottom, inner_top) + flux)
        )
        places, next_places, side_places = turned(halo), turned(next_halo), turned(sides)
        results = []
        for i in range(2):
            north, south = places[i]
            once = combine(
                own_set[i],
                own[i],
                own_east[i],
                own_west[i],
                jnp.where(top, north, sub_roll(own[i], -1)),
                jnp.where(bottom, south, sub_roll(own[i], 1)),
            )
            side_north, side_south = side_places[i]
            next_column = (
                next_sides[slots[i]]
                + own_set[i][5] * jnp.where(first_lane, own_west[i], own_east[i])
                + own_set[i][6] * jnp.where(bottom, side_south, side_north)
            )
            north, south = next_places[i]
            results.append(
                combine(
                    own_set[i],
                    once,
                    jnp.where(last_lane, next_column, lane_roll(once, -1)),
                    jnp.where(first_lane, next_column, lane_roll(once, 1)),
                    jnp.where(top, north, sub_roll(once, -1)),
                    jnp.where(bottom, south, sub_roll(once, 1)),
                )
            )
        return results

    def transport(p):
        f1 = 2 * p
        f2 = jnp.minimum(f1 + 1, fields - 1)
        columns = []
        for k in range(half):
            own_set = [
                [own_coefs[2 * k + i, c] for c in range(5)]
                + [shares[2 * k + i, c] for c in range(2)]
                for i in range(2)
            ]
            halo_set = [halo_coefs[k, c] for c in range(4)]
            for one, two in zip(
                advect(f1, k, own_set, halo_set), advect(f2, k, own_set, halo_set)
            ):
                columns.append(jnp.where(low, one, sub_roll(two, rows)))
                columns.append(jnp.where(low, sub_roll(one, rows), two))
        return tuple(columns)

    def solve(p, columns):
        f1 = 2 * p
        f2 = jnp.minimum(f1 + 1, fields - 1)
        waves = cosine_sums(columns)
        modes = [source[m, p] - decay[m, p] * waves[m] for m in range(levels)]
        square = modes[1] * modes[1]
        for m in range(2, levels):
            square = square + modes[m] * modes[m]
        square = (modes[0] * modes[0]) * float(levels) + square * (0.5 * levels)
        change = cosine_series(modes)
        for k in range(pairs):
            even, odd = (columns[l] + change[l] for l in (2 * k, 2 * k + 1))
            state[f1 * pairs + k] = jnp.where(low, even, sub_roll(odd, rows))
            state[f2 * pairs + k] = jnp.where(low, sub_roll(even, rows), odd)
        return jnp.where(low | (f1 + 1 < fields), square, 0.0)

    def pair_step(p, carried):
        total, columns = carried
        following = transport(p)
        return total + solve(p - 1, columns), following

    field_pairs = (fields + 1) // 2
    total, columns = lax.fori_loop(
        1, field_pairs, pair_step, (jnp.zeros(tile, F32), transport(0))
    )
    return total + solve(field_pairs - 1, columns)


def main_kernel(fields, levels, *refs):
    inputs, (target, onehot), (state, placed), coefs = refs[:13], refs[13:15], refs[15:17], refs[17:]
    rows, lanes = target.shape
    total = transport_and_solve(fields, levels, *inputs, state, *coefs)

    heat = (total + sub_roll(total, rows)) * (1.0 / (fields * levels))
    first = heat.astype(jnp.bfloat16).astype(F32)
    rest = heat - first
    second = rest.astype(jnp.bfloat16).astype(F32)
    third = rest - second
    spans = placed.shape[0]
    slot_row, _ = iotas((spans, lanes))
    high = lax.shift_right_logical(target[...], lanes.bit_length() - 1)
    hits = [slot_row == high[r : r + 1] for r in range(rows)]
    left = jnp.concatenate(
        [
            jnp.concatenate(
                [
                    jnp.where(hits[r], part[r : r + 1], 0.0).astype(jnp.bfloat16)
                    for r in range(rows)
                ],
                axis=1,
            )
            for part in (first, second, third)
        ],
        axis=0,
    )
    result = jnp.dot(left, onehot[...], preferred_element_type=F32)
    placed[...] = result[:spans] + result[spans : 2 * spans] + result[2 * spans :]


def finish_kernel(parts, state, total_out, state_out, total, semaphores):
    copy_state = pltpu.make_async_copy(state, state_out, semaphores.at[0])
    copy_state.start()
    value = parts[0]
    for i in range(1, parts.shape[0]):
        value = value + parts[i]
    total[...] = value
    copy_total = pltpu.make_async_copy(total, total_out, semaphores.at[1])
    copy_total.start()
    copy_state.wait()
    copy_total.wait()


def body(tracers, courant_x, courant_y, physics_ref, class_coeffs, span_target, cloud_class):
    fields, levels, rows, cols = tracers.shape
    wide = lax.axis_size("wide")
    narrow = lax.axis_size("narrow")
    pairs = levels // 2
    half = pairs // 2
    tile = (2 * rows, cols)
    field_pairs = (fields + 1) // 2
    flat = tracers.reshape(fields * pairs, *tile)
    cx = courant_x.reshape(pairs, *tile)
    cy = courant_y.reshape(pairs, *tile)
    quads = pairs // rows

    def array(*shape, dtype=F32):
        return jax.ShapeDtypeStruct(shape, dtype)

    flat, cx, cy, north = pl.pallas_call(
        functools.partial(pack_north_kernel, levels),
        out_shape=(
            array(fields * pairs, *tile),
            array(pairs, *tile),
            array(pairs, *tile),
            array(fields * half + 2 * quads, *tile),
        ),
        in_specs=[HBM] * 3,
        out_specs=[VMEM] * 4,
        scratch_shapes=[pltpu.SemaphoreType.DMA((3,))],
        compiler_params=PARAMS,
    )(*(pltpu.with_memory_space_constraint(x, pltpu.HBM) for x in (flat, cx, cy)))
    edge, corner, south = pl.pallas_call(
        functools.partial(pack_edges_kernel, levels),
        out_shape=(
            array(fields + 2, *tile),
            array(*tile),
            array(fields * half + quads, *tile),
        ),
        in_specs=[VMEM] * 3,
        out_specs=[VMEM] * 3,
        compiler_params=PARAMS,
    )(flat, cx, cy)

    def send(value, up, right):
        pairs_ = []
        for w in range(wide):
            for n in range(narrow):
                to = ((w + up) % wide) * narrow + (n + right) % narrow
                pairs_.append((w * narrow + n, to))
        return lax.ppermute(value, ("wide", "narrow"), pairs_)

    def to_both_sides(value, up):
        from_west = send(value, up, 1)
        from_east = from_west if narrow == 2 else send(value, up, -1)
        return from_west, from_east

    from_south = send(north, 1, 0)
    from_north = send(south, -1, 0)
    edge_west, edge_east = to_both_sides(edge, 0)
    corner_sw, corner_se = to_both_sides(corner, 1)
    corner_nw, corner_ne = to_both_sides(corner, -1)

    decay, source, onehot = pl.pallas_call(
        prep_kernel,
        out_shape=(array(levels, field_pairs, *tile),) * 2
        + (array(rows * cols, cols, dtype=jnp.bfloat16),),
        in_specs=[SMEM, SMEM, VMEM, VMEM],
        out_specs=[VMEM] * 3,
        cost_estimate=pl.CostEstimate(flops=4000000, bytes_accessed=2000000, transcendentals=0),
        compiler_params=PARAMS,
    )(class_coeffs, physics_ref, cloud_class, span_target)

    shifted = pl.pallas_call(
        functools.partial(shift_kernel, levels),
        out_shape=(array(fields * pairs, *tile),) * 2,
        in_specs=[VMEM] * 4,
        out_specs=[VMEM] * 2,
        compiler_params=PARAMS,
    )(flat, edge, edge_west, edge_east)
    next_sides, west_x, sides_y = pl.pallas_call(
        functools.partial(next_kernel, levels),
        out_shape=(array(fields * pairs, *tile),) + (array(pairs, *tile),) * 2,
        in_specs=[VMEM] * 4,
        out_specs=[VMEM] * 3,
        compiler_params=PARAMS,
    )(cx, edge, edge_west, edge_east)
    corners, shares = pl.pallas_call(
        functools.partial(corner_kernel, levels),
        out_shape=(array((fields + 1) * half, *tile), array(pairs, 2, *tile)),
        in_specs=[VMEM] * 5,
        out_specs=[VMEM] * 2,
        compiler_params=PARAMS,
    )(sides_y, corner_sw, corner_se, corner_nw, corner_ne)
    state, placed = pl.pallas_call(
        functools.partial(main_kernel, fields, levels),
        out_shape=(array(fields * pairs, *tile), array(wide * rows, cols)),
        in_specs=[VMEM] * 15,
        out_specs=[VMEM] * 2,
        scratch_shapes=[
            pltpu.VMEM((pairs, 5) + tile, F32),
            pltpu.VMEM((half, 4) + tile, F32),
        ],
        compiler_params=PARAMS,
    )(
        flat,
        cx,
        cy,
        from_south,
        from_north,
        *shifted,
        next_sides,
        west_x,
        corners,
        shares,
        decay,
        source,
        span_target,
        onehot,
    )
    received = lax.all_to_all(
        placed.reshape(wide, rows, cols), "wide", split_axis=0, concat_axis=0, tiled=True
    )
    span_diag, state = pl.pallas_call(
        finish_kernel,
        out_shape=(array(rows, cols), array(fields * pairs, *tile)),
        in_specs=[VMEM] * 2,
        out_specs=[HBM] * 2,
        scratch_shapes=[pltpu.VMEM((rows, cols), F32), pltpu.SemaphoreType.DMA((2,))],
        compiler_params=PARAMS,
    )(received, state)
    return state.reshape(fields, levels, rows, cols), span_diag


def solution(mesh):
    return jax.shard_map(
        body,
        mesh=mesh,
        in_specs=(
            P(None, None, "wide", "narrow"),
            P(None, "wide", "narrow"),
            P(None, "wide", "narrow"),
            P(),
            P(),
            P("wide", "narrow"),
            P("wide", "narrow"),
        ),
        out_specs=(P(None, None, "wide", "narrow"), P("wide", "narrow")),
        check_vma=False,
    )
```

```python
import functools
import math

import jax
import jax.numpy as jnp
from jax import lax
from jax.experimental import pallas as pl
from jax.experimental.pallas import tpu as pltpu
from jax.sharding import PartitionSpec as P

VMEM = pl.BlockSpec(memory_space=pltpu.VMEM)
HBM = pl.BlockSpec(memory_space=pltpu.HBM)
SMEM = pl.BlockSpec(memory_space=pltpu.SMEM)
F32 = jnp.float32
PARAMS = pltpu.CompilerParams(vmem_limit_bytes=12 * 1024 * 1024)


def sub_roll(value, shift):
    shift = shift % value.shape[0]
    return value if shift == 0 else pltpu.roll(value, shift, 0)


def lane_roll(value, shift):
    shift = shift % value.shape[1]
    return value if shift == 0 else pltpu.roll(value, shift, 1)


def iotas(shape):
    return lax.broadcasted_iota(jnp.int32, shape, 0), lax.broadcasted_iota(jnp.int32, shape, 1)


def one_row(vectors, row, step):
    rows = vectors[0].shape[0] // 2
    local = iotas(vectors[0].shape)[0] % rows
    packed = []
    for start in range(0, len(vectors), rows):
        total = vectors[start]
        for t in range(1, rows):
            total = jnp.where(
                local == row + step * t, sub_roll(vectors[start + t], step * t), total
            )
        packed.append(total)
    return packed


def inner_flux(value, courant):
    return jnp.maximum(courant, 0.0) * value + jnp.minimum(courant, 0.0) * sub_roll(value, -1)


def northward_rows(value, courant):
    local = iotas(value.shape)[0] % (value.shape[0] // 2)
    return jnp.where(local == 2, inner_flux(value, courant), value)


def southward_rows(value, courant):
    local = iotas(value.shape)[0] % (value.shape[0] // 2)
    return jnp.where(local == 1, sub_roll(-inner_flux(value, courant), 1), value)


def pack_north_kernel(levels, tracers_in, cx_in, cy_in, tracers, cx, cy, north, semaphores):
    copies = [
        pltpu.make_async_copy(source, into, semaphores.at[i])
        for i, (source, into) in enumerate(((tracers_in, tracers), (cx_in, cx), (cy_in, cy)))
    ]
    for copy in copies:
        copy.start()
    for copy in copies:
        copy.wait()
    pairs = levels // 2
    half = pairs // 2
    tile = tracers.shape[1:]
    rows = tile[0] // 2
    upper = iotas(tile)[0] % rows >= rows // 2
    fields = tracers.shape[0] // pairs
    for f in range(fields):
        for k in range(half):
            one, two = (
                northward_rows(tracers[f * pairs + j], cy[j]) for j in (2 * k, 2 * k + 1)
            )
            north[f * half + k] = jnp.where(upper, one, sub_roll(two, 2))
    courant = one_row([cx[k] for k in range(pairs)], rows - 1, -1)
    courant += one_row([cy[k] for k in range(pairs)], rows - 1, -1)
    for k, value in enumerate(courant):
        north[fields * half + k] = value


def pack_edges_kernel(levels, tracers, cx, cy, edge, corner, south_rows):
    pairs = levels // 2
    half = pairs // 2
    fields = tracers.shape[0] // pairs
    tile = tracers.shape[1:]
    rows = tile[0] // 2
    lanes = tile[1]
    group = lanes // levels
    sub, lane = iotas(tile)
    upper = sub % rows >= rows // 2
    odd_sub = sub % 2 == 1
    corners = [jnp.zeros(tile, F32)]

    def pack_edge(vectors, slot):
        total = lane_roll(vectors[0], 2)
        for k in range(1, pairs):
            total = jnp.where(
                lane // (2 * group) == k, lane_roll(vectors[k], 2 + 2 * group * k), total
            )
        total = jnp.where(
            lane % (2 * group) < group, total, sub_roll(lane_roll(total, group), rows)
        )
        edge[slot] = jnp.where(lane % group < group // 2, total, lane_roll(total, group // 2))
        for k in range(half):
            one, two = vectors[2 * k], vectors[2 * k + 1]
            place = slot * half + k
            north = jnp.where(upper, one, sub_roll(two, 2))
            south = jnp.where(upper, sub_roll(two, -2), one)
            if slot < fields:
                first = southward_rows(one, cy[2 * k])
                second = southward_rows(two, cy[2 * k + 1])
                south_rows[place] = jnp.where(upper, sub_roll(second, -2), first)
            value = lane_roll(jnp.where(odd_sub, north, south), 2 * place + 1)
            corners[0] = jnp.where(lane // 2 == place, value, corners[0])

    for f in range(fields):
        pack_edge([tracers[f * pairs + k] for k in range(pairs)], f)
    pack_edge([cx[k] for k in range(pairs)], fields)
    pack_edge([cy[k] for k in range(pairs)], fields + 1)
    corner[...] = corners[0]
    for k, value in enumerate(one_row([cx[k] for k in range(pairs)], 0, 1)):
        south_rows[fields * half + k] = value


def cosine_sums(values):
    count = len(values)
    if count == 1:
        return values
    half = count // 2
    plus = [values[n] + values[count - 1 - n] for n in range(half)]
    minus = [
        (values[n] - values[count - 1 - n])
        * (0.5 / math.cos(math.pi * (2 * n + 1) / (2 * count)))
        for n in range(half)
    ]
    even = cosine_sums(plus)
    odd = cosine_sums(minus)
    result = []
    for k in range(half):
        result.append(even[k])
        result.append(odd[k] + odd[k + 1] if k + 1 < half else odd[k])
    return result


def cosine_series(values):
    count = len(values)
    if count == 1:
        return values
    half = count // 2
    odd_in = [values[2 * k + 1] + values[2 * k - 1] if k else values[1] for k in range(half)]
    even = cosine_series(values[0::2])
    odd = cosine_series(odd_in)
    odd = [
        odd[n] * (0.5 / math.cos(math.pi * (2 * n + 1) / (2 * count))) for n in range(half)
    ]
    return [even[n] + odd[n] for n in range(half)] + [
        even[n] - odd[n] for n in range(half - 1, -1, -1)
    ]


def prep_kernel(coeffs, profile, klass, target, decay, source, onehot):
    levels, pairs = decay.shape[:2]
    fields = profile.shape[0]
    tile = decay.shape[2:]
    rows, lanes = klass.shape
    sub, lane = iotas(tile)
    low = sub < rows
    kind = jnp.concatenate([klass[...], klass[...]], axis=0)
    is_two = kind == 2
    is_one = kind == 1

    def by_class(which, f):
        return jnp.where(
            is_two,
            coeffs[which, 2, f] * 0.25,
            jnp.where(is_one, coeffs[which, 1, f] * 0.5, coeffs[which, 0, f]),
        )

    for p in range(pairs):
        f1 = 2 * p
        f2 = min(2 * p + 1, fields - 1)
        diffusion = jnp.where(low, by_class(0, f1), by_class(0, f2))
        relax = jnp.where(low, by_class(1, f1), by_class(1, f2))
        waves = cosine_sums([jnp.where(low, profile[f1, l], profile[f2, l]) for l in range(levels)])
        for m in range(levels):
            rate = relax + diffusion * (2.0 - 2.0 * math.cos(math.pi * m / levels))
            once = 1.0 / (1.0 + rate)
            square = once * once
            twice = once + square
            steps = jnp.where(is_two, twice + twice * square, jnp.where(is_one, twice, once))
            steps = steps * ((1.0 if m == 0 else 2.0) / levels)
            decay[m, p] = steps * rate
            source[m, p] = steps * relax * waves[m]
    low_part = target[...] & (lanes - 1)
    slot, _ = iotas((lanes, lanes))
    for r in range(rows):
        hit = jnp.where(slot == low_part[r : r + 1], 1.0, 0.0)
        onehot[r * lanes : (r + 1) * lanes, :] = jnp.transpose(hit).astype(jnp.bfloat16)


def combine(coefs, center, east, west, north, south):
    return (
        coefs[0] * center
        + (coefs[1] * east + coefs[2] * west)
        + (coefs[3] * north + coefs[4] * south)
    )


def coefficients(here_x, west_x, here_y, south_y):
    return (
        1.0
        - jnp.maximum(here_x, 0.0)
        + jnp.minimum(west_x, 0.0)
        - jnp.maximum(here_y, 0.0)
        + jnp.minimum(south_y, 0.0),
        jnp.maximum(-here_x, 0.0),
        jnp.maximum(west_x, 0.0),
        jnp.maximum(-here_y, 0.0),
        jnp.maximum(south_y, 0.0),
    )


def side_by_side(value, place):
    return jnp.where(place == 3, lane_roll(value, -2), value)


def beside(edge, edge_west, edge_east, slot, place):
    from_east = (place == 2) | (place == 3)
    from_west = (place == 4) | (place == 5)
    return jnp.where(
        from_east, edge_east[slot], jnp.where(from_west, edge_west[slot], edge[slot])
    )


def spread(value, levels):
    lanes = value.shape[1]
    rows = value.shape[0] // 2
    group = lanes // levels
    sub, lane = iotas(value.shape)
    value = side_by_side(value, lane % group)
    value = jnp.where(sub < rows, value, sub_roll(lane_roll(value, -group), rows))
    return [lane_roll(value, -(2 * group * k + 3)) for k in range(levels // 2)]


def shift_kernel(levels, tracers, edge, edge_west, edge_east, east, west):
    pairs = levels // 2
    tile = tracers.shape[1:]
    lanes = tile[1]
    lane = iotas(tile)[1]
    place = lane % (lanes // levels)
    for f in range(tracers.shape[0] // pairs):
        for k, sides in enumerate(spread(beside(edge, edge_west, edge_east, f, place), levels)):
            own = tracers[f * pairs + k]
            east[f * pairs + k] = jnp.where(lane == lanes - 1, sides, lane_roll(own, -1))
            west[f * pairs + k] = jnp.where(lane == 0, sides, lane_roll(own, 1))


def next_kernel(levels, cx, edge, edge_west, edge_east, next_sides, west_x, sides_y):
    pairs = levels // 2
    fields = next_sides.shape[0] // pairs
    tile = cx.shape[1:]
    rows = tile[0] // 2
    sub, lane = iotas(tile)
    place = lane % (tile[1] // levels)

    def own_rows(slot):
        value = beside(edge, edge_west, edge_east, slot, place)
        return jnp.where(sub < rows, value, 0.0)

    edge_x = own_rows(fields)
    edge_y = own_rows(fields + 1)
    coefs = coefficients(edge_x, lane_roll(edge_x, 1), edge_y, sub_roll(edge_y, 1))
    for k, sides in enumerate(spread(edge_x, levels)):
        west_x[k] = jnp.where(lane == 0, sides, lane_roll(cx[k], 1))
    for k, sides in enumerate(spread(edge_y, levels)):
        sides_y[k] = sides
    for f in range(fields):
        raw = own_rows(f)
        moved = combine(
            coefs,
            raw,
            lane_roll(raw, -1),
            lane_roll(raw, 1),
            sub_roll(raw, -1),
            sub_roll(raw, 1),
        )
        for k, sides in enumerate(spread(moved, levels)):
            next_sides[f * pairs + k] = sides


def turned(value):
    rows = value.shape[0] // 2
    up, down = sub_roll(value, rows - 1), sub_roll(value, 1 - rows)
    return ((up, down), (down, up))


def corner_kernel(
    levels, sides_y, corner_sw, corner_se, corner_nw, corner_ne, corners, shares
):
    half = levels // 4
    tile = corner_sw.shape
    rows = tile[0] // 2
    sub, lane = iotas(tile)
    local = sub % rows
    odd_sub = sub % 2 == 1
    bottom = local == 0
    top = local == rows - 1
    even_lane = lane % 2 == 0
    dense = jnp.where(
        odd_sub,
        jnp.where(even_lane, lane_roll(corner_se[...], -1), lane_roll(corner_sw[...], 1)),
        jnp.where(even_lane, lane_roll(corner_ne[...], -1), lane_roll(corner_nw[...], 1)),
    )
    count = corners.shape[0]
    for i in range(count):
        corners[i] = lane_roll(dense, -(2 * i + 1))
    for k in range(half):
        places = turned(lane_roll(dense, -(2 * (count + k) + 1)))
        for i in range(2):
            j = 2 * k + i
            south_face = places[i][1]
            shares[j, 0] = jnp.where(bottom, jnp.minimum(south_face, 0.0), 0.0)
            shares[j, 1] = jnp.where(
                bottom,
                jnp.maximum(south_face, 0.0),
                jnp.where(top, jnp.maximum(-sides_y[j], 0.0), 0.0),
            )


def transport_and_solve(
    fields,
    levels,
    tracers,
    cx,
    cy,
    from_south,
    from_north,
    east,
    west,
    next_sides,
    west_x,
    corners,
    shares,
    decay,
    source,
    state,
    own_coefs,
    halo_coefs,
):
    pairs = levels // 2
    half = pairs // 2
    tile = tracers.shape[1:]
    rows = tile[0] // 2
    lanes = tile[1]
    group = lanes // levels
    sub, lane = iotas(tile)
    local = sub % rows
    low = sub < rows
    first_lane = lane == 0
    last_lane = lane == lanes - 1
    odd_sub = sub % 2 == 1
    bottom = local == 0
    top = local == rows - 1
    in_first = bottom | top


    def inner_rows(first, second):
        (first_up, first_down), _ = turned(first)
        (second_up, second_down), _ = turned(second)
        return (
            jnp.where(in_first, first_up, second_down),
            jnp.where(in_first, first_down, second_up),
        )

    base = fields * half
    count = pairs // rows
    for k in range(half):
        quad, t = 2 * k // rows, 2 * k % rows
        packed_south = from_south[base + quad]
        packed_south_y = from_south[base + count + quad]
        packed_north = from_north[base + quad]
        south_x = jnp.where(in_first, sub_roll(packed_south, t), sub_roll(packed_south, 3 + t))
        south_y = jnp.where(
            in_first, sub_roll(packed_south_y, t), sub_roll(packed_south_y, 3 + t)
        )
        north_x = jnp.where(in_first, sub_roll(packed_north, -t), sub_roll(packed_north, 5 - t))
        halo_x = jnp.where(odd_sub, south_x, north_x)
        halo_west = jnp.where(
            first_lane, corners[fields * half + k], lane_roll(halo_x, 1)
        )
        _, inner_top = inner_rows(cy[2 * k], cy[2 * k + 1])
        face = jnp.where(odd_sub, -south_y, inner_top)
        halo_coefs[k, 0] = (
            1.0
            - jnp.maximum(halo_x, 0.0)
            + jnp.minimum(halo_west, 0.0)
            + jnp.minimum(face, 0.0)
        )
        halo_coefs[k, 1] = jnp.maximum(-halo_x, 0.0)
        halo_coefs[k, 2] = jnp.maximum(halo_west, 0.0)
        halo_coefs[k, 3] = jnp.maximum(face, 0.0)
        places = turned(south_y)
        for i in range(2):
            j = 2 * k + i
            below = jnp.where(bottom, places[i][1], sub_roll(cy[j], 1))
            for c, value in enumerate(coefficients(cx[j], west_x[j], cy[j], below)):
                own_coefs[j, c] = value

    def advect(f, k, own_set, halo_set):
        message_south = from_south[f * half + k]
        message_north = from_north[f * half + k]
        slots = (f * pairs + 2 * k, f * pairs + 2 * k + 1)
        own = [tracers[slot] for slot in slots]
        own_east = [east[slot] for slot in slots]
        own_west = [west[slot] for slot in slots]
        sides = corners[f * half + k]
        halo = jnp.where(odd_sub, message_south, message_north)
        inner_bottom, inner_top = inner_rows(*own)
        flux = jnp.where(odd_sub, sub_roll(message_south, 1), sub_roll(message_north, -1))
        next_halo = (
            halo_set[0] * halo
            + (
                halo_set[1] * jnp.where(last_lane, sides, lane_roll(halo, -1))
                + halo_set[2] * jnp.where(first_lane, sides, lane_roll(halo, 1))
            )
            + (halo_set[3] * jnp.where(odd_sub, inner_bottom, inner_top) + flux)
        )
        places, next_places, side_places = turned(halo), turned(next_halo), turned(sides)
        results = []
        for i in range(2):
            north, south = places[i]
            once = combine(
                own_set[i],
                own[i],
                own_east[i],
                own_west[i],
                jnp.where(top, north, sub_roll(own[i], -1)),
                jnp.where(bottom, south, sub_roll(own[i], 1)),
            )
            side_north, side_south = side_places[i]
            next_column = (
                next_sides[slots[i]]
                + own_set[i][5] * jnp.where(first_lane, own_west[i], own_east[i])
                + own_set[i][6] * jnp.where(bottom, side_south, side_north)
            )
            north, south = next_places[i]
            results.append(
                combine(
                    own_set[i],
                    once,
                    jnp.where(last_lane, next_column, lane_roll(once, -1)),
                    jnp.where(first_lane, next_column, lane_roll(once, 1)),
                    jnp.where(top, north, sub_roll(once, -1)),
                    jnp.where(bottom, south, sub_roll(once, 1)),
                )
            )
        return results

    def transport(p):
        f1 = 2 * p
        f2 = jnp.minimum(f1 + 1, fields - 1)
        columns = []
        for k in range(half):
            own_set = [
                [own_coefs[2 * k + i, c] for c in range(5)]
                + [shares[2 * k + i, c] for c in range(2)]
                for i in range(2)
            ]
            halo_set = [halo_coefs[k, c] for c in range(4)]
            for one, two in zip(
                advect(f1, k, own_set, halo_set), advect(f2, k, own_set, halo_set)
            ):
                columns.append(jnp.where(low, one, sub_roll(two, rows)))
                columns.append(jnp.where(low, sub_roll(one, rows), two))
        return tuple(columns)

    def solve(p, columns):
        f1 = 2 * p
        f2 = jnp.minimum(f1 + 1, fields - 1)
        waves = cosine_sums(columns)
        modes = [source[m, p] - decay[m, p] * waves[m] for m in range(levels)]
        square = modes[1] * modes[1]
        for m in range(2, levels):
            square = square + modes[m] * modes[m]
        square = (modes[0] * modes[0]) * float(levels) + square * (0.5 * levels)
        change = cosine_series(modes)
        for k in range(pairs):
            even, odd = (columns[l] + change[l] for l in (2 * k, 2 * k + 1))
            state[f1 * pairs + k] = jnp.where(low, even, sub_roll(odd, rows))
            state[f2 * pairs + k] = jnp.where(low, sub_roll(even, rows), odd)
        return jnp.where(low | (f1 + 1 < fields), square, 0.0)

    def pair_step(p, carried):
        total, columns = carried
        following = transport(p)
        return total + solve(p - 1, columns), following

    field_pairs = (fields + 1) // 2
    total, columns = lax.fori_loop(
        1, field_pairs, pair_step, (jnp.zeros(tile, F32), transport(0)), unroll=2
    )
    return total + solve(field_pairs - 1, columns)


def main_kernel(fields, levels, *refs):
    inputs, (target, onehot), (state, placed), coefs = refs[:13], refs[13:15], refs[15:17], refs[17:]
    rows, lanes = target.shape
    total = transport_and_solve(fields, levels, *inputs, state, *coefs)

    heat = (total + sub_roll(total, rows)) * (1.0 / (fields * levels))
    first = heat.astype(jnp.bfloat16).astype(F32)
    rest = heat - first
    second = rest.astype(jnp.bfloat16).astype(F32)
    third = rest - second
    spans = placed.shape[0]
    slot_row, _ = iotas((spans, lanes))
    high = lax.shift_right_logical(target[...], lanes.bit_length() - 1)
    hits = [slot_row == high[r : r + 1] for r in range(rows)]
    left = jnp.concatenate(
        [
            jnp.concatenate(
                [
                    jnp.where(hits[r], part[r : r + 1], 0.0).astype(jnp.bfloat16)
                    for r in range(rows)
                ],
                axis=1,
            )
            for part in (first, second, third)
        ],
        axis=0,
    )
    result = jnp.dot(left, onehot[...], preferred_element_type=F32)
    placed[...] = result[:spans] + result[spans : 2 * spans] + result[2 * spans :]


def finish_kernel(parts, state, total_out, state_out, total, semaphores):
    copy_state = pltpu.make_async_copy(state, state_out, semaphores.at[0])
    copy_state.start()
    value = parts[0]
    for i in range(1, parts.shape[0]):
        value = value + parts[i]
    total[...] = value
    copy_total = pltpu.make_async_copy(total, total_out, semaphores.at[1])
    copy_total.start()
    copy_state.wait()
    copy_total.wait()


def body(tracers, courant_x, courant_y, physics_ref, class_coeffs, span_target, cloud_class):
    fields, levels, rows, cols = tracers.shape
    wide = lax.axis_size("wide")
    narrow = lax.axis_size("narrow")
    pairs = levels // 2
    half = pairs // 2
    tile = (2 * rows, cols)
    field_pairs = (fields + 1) // 2
    flat = tracers.reshape(fields * pairs, *tile)
    cx = courant_x.reshape(pairs, *tile)
    cy = courant_y.reshape(pairs, *tile)
    quads = pairs // rows

    def array(*shape, dtype=F32):
        return jax.ShapeDtypeStruct(shape, dtype)

    flat, cx, cy, north = pl.pallas_call(
        functools.partial(pack_north_kernel, levels),
        out_shape=(
            array(fields * pairs, *tile),
            array(pairs, *tile),
            array(pairs, *tile),
            array(fields * half + 2 * quads, *tile),
        ),
        in_specs=[HBM] * 3,
        out_specs=[VMEM] * 4,
        scratch_shapes=[pltpu.SemaphoreType.DMA((3,))],
        compiler_params=PARAMS,
    )(*(pltpu.with_memory_space_constraint(x, pltpu.HBM) for x in (flat, cx, cy)))
    edge, corner, south = pl.pallas_call(
        functools.partial(pack_edges_kernel, levels),
        out_shape=(
            array(fields + 2, *tile),
            array(*tile),
            array(fields * half + quads, *tile),
        ),
        in_specs=[VMEM] * 3,
        out_specs=[VMEM] * 3,
        compiler_params=PARAMS,
    )(flat, cx, cy)

    def send(value, up, right):
        pairs_ = []
        for w in range(wide):
            for n in range(narrow):
                to = ((w + up) % wide) * narrow + (n + right) % narrow
                pairs_.append((w * narrow + n, to))
        return lax.ppermute(value, ("wide", "narrow"), pairs_)

    def to_both_sides(value, up):
        from_west = send(value, up, 1)
        from_east = from_west if narrow == 2 else send(value, up, -1)
        return from_west, from_east

    from_south = send(north, 1, 0)
    from_north = send(south, -1, 0)
    edge_west, edge_east = to_both_sides(edge, 0)
    corner_sw, corner_se = to_both_sides(corner, 1)
    corner_nw, corner_ne = to_both_sides(corner, -1)

    decay, source, onehot = pl.pallas_call(
        prep_kernel,
        out_shape=(array(levels, field_pairs, *tile),) * 2
        + (array(rows * cols, cols, dtype=jnp.bfloat16),),
        in_specs=[SMEM, SMEM, VMEM, VMEM],
        out_specs=[VMEM] * 3,
        cost_estimate=pl.CostEstimate(flops=4000000, bytes_accessed=2000000, transcendentals=0),
        compiler_params=PARAMS,
    )(class_coeffs, physics_ref, cloud_class, span_target)

    shifted = pl.pallas_call(
        functools.partial(shift_kernel, levels),
        out_shape=(array(fields * pairs, *tile),) * 2,
        in_specs=[VMEM] * 4,
        out_specs=[VMEM] * 2,
        compiler_params=PARAMS,
    )(flat, edge, edge_west, edge_east)
    next_sides, west_x, sides_y = pl.pallas_call(
        functools.partial(next_kernel, levels),
        out_shape=(array(fields * pairs, *tile),) + (array(pairs, *tile),) * 2,
        in_specs=[VMEM] * 4,
        out_specs=[VMEM] * 3,
        compiler_params=PARAMS,
    )(cx, edge, edge_west, edge_east)
    corners, shares = pl.pallas_call(
        functools.partial(corner_kernel, levels),
        out_shape=(array((fields + 1) * half, *tile), array(pairs, 2, *tile)),
        in_specs=[VMEM] * 5,
        out_specs=[VMEM] * 2,
        compiler_params=PARAMS,
    )(sides_y, corner_sw, corner_se, corner_nw, corner_ne)
    state, placed = pl.pallas_call(
        functools.partial(main_kernel, fields, levels),
        out_shape=(array(fields * pairs, *tile), array(wide * rows, cols)),
        in_specs=[VMEM] * 15,
        out_specs=[VMEM] * 2,
        scratch_shapes=[
            pltpu.VMEM((pairs, 5) + tile, F32),
            pltpu.VMEM((half, 4) + tile, F32),
        ],
        compiler_params=PARAMS,
    )(
        flat,
        cx,
        cy,
        from_south,
        from_north,
        *shifted,
        next_sides,
        west_x,
        corners,
        shares,
        decay,
        source,
        span_target,
        onehot,
    )
    received = lax.all_to_all(
        placed.reshape(wide, rows, cols), "wide", split_axis=0, concat_axis=0, tiled=True
    )
    span_diag, state = pl.pallas_call(
        finish_kernel,
        out_shape=(array(rows, cols), array(fields * pairs, *tile)),
        in_specs=[VMEM] * 2,
        out_specs=[HBM] * 2,
        scratch_shapes=[pltpu.VMEM((rows, cols), F32), pltpu.SemaphoreType.DMA((2,))],
        compiler_params=PARAMS,
    )(received, state)
    return state.reshape(fields, levels, rows, cols), span_diag


def solution(mesh):
    return jax.shard_map(
        body,
        mesh=mesh,
        in_specs=(
            P(None, None, "wide", "narrow"),
            P(None, "wide", "narrow"),
            P(None, "wide", "narrow"),
            P(),
            P(),
            P("wide", "narrow"),
            P("wide", "narrow"),
        ),
        out_specs=(P(None, None, "wide", "narrow"), P("wide", "narrow")),
        check_vma=False,
    )
```
